32 devices in a mesh: lon: 16 (over z, x, core), lat: 2 (over y).
Axes of the slice: x: 2, y: 2, z: 4, core: 2. Of those that a mesh axis runs over, the one named last changes fastest.
Arguments:
- initial_state: float32 [4, 10, 32, 2048], P(None, None, 'lat', 'lon'), may hold values from -6 to 6
- land_mask: int32 [10, 32, 2048], P(None, 'lat', 'lon'), may hold values from 0 to 1, as said below
- surface_flux: float32 [32, 2048], P('lat', 'lon'), may hold values from 0 to 10, as said below
- weight_in: float32 [40, 64], replicated, may hold values from -1 to 1
- bias_in: float32 [64], replicated, may hold values from -3 to 3
- weight_mid: float32 [64, 64], replicated, may hold values from -0.75 to 0.75
- bias_mid: float32 [64], replicated, may hold values from -3 to 3
- weight_out: float32 [64, 40], replicated, may hold values from -0.75 to 0.75
- bias_out: float32 [40], replicated, may hold values from -3 to 3
- cotangent: float32 [4, 10, 32, 2048], P(None, None, 'lat', 'lon'), may hold values from -6 to 6
Outputs:
- final_state: float32 [4, 10, 32, 2048], P(None, None, 'lat', 'lon')
- state_grad: float32 [4, 10, 32, 2048], P(None, None, 'lat', 'lon')
- grad_weight_in: float32 [40, 64], replicated
- grad_bias_in: float32 [64], replicated
- grad_weight_mid: float32 [64, 64], replicated
- grad_bias_mid: float32 [64], replicated
- grad_weight_out: float32 [64, 40], replicated
- grad_bias_out: float32 [40], replicated
The draws below stay inside these ranges and needn't reach their ends.
Inputs may be any that keep to these rules, and one draw needn't show every extreme that they name: `land_mask`: at every cell the ocean levels are a run from level 0 down; at least one cell is ocean at every level. `surface_flux`: strictly positive.
All inputs are finite; a program needn't handle non-finite values.
Results may differ from the reference program's by a relative error of at most 0.00012.
Values sent between devices are 32-bit elements; how exact they have to be, the bound alone decides.
No kernel may reach another device: no remote copies, remote signals or barrier semaphores. Data moves between devices by JAX's collectives and lax.ppermute only.
A program may use at most 128 MiB of HBM per device.

```python
import math
import jax
import jax.numpy as jnp
from jax import lax

LEV = 10
HID = 64
STEPS = 2
NLAT = 32
NLON = 2048
FEAT = 40


def draw_land_mask(key, part):
    roll_key = jax.random.fold_in(key, 11)
    depth_key = jax.random.fold_in(key, 12)
    col_index = jnp.arange(NLON, dtype=jnp.int32)
    row_index = jnp.arange(NLAT, dtype=jnp.int32)
    lon_odds = 300 + 700 * col_index // NLON
    lat_odds = 300 + 700 * row_index // NLAT
    odds = lat_odds[:, None] * lon_odds[None, :] // 1000
    rolled = jax.random.randint(roll_key, (NLAT, NLON), 0, 1000, dtype=jnp.int32)
    depths = jax.random.randint(depth_key, (NLAT, NLON), 1, LEV + 1, dtype=jnp.int32)
    depths = jnp.where(rolled < odds, depths, 0)
    anchor = (row_index[:, None] == NLAT // 2) & (col_index[None, :] == NLON // 2)
    depths = jnp.where(anchor, LEV, depths)
    levels = jnp.arange(LEV, dtype=jnp.int32)
    return (levels[:, None, None] < depths[None, :, :]).astype(jnp.int32)


def draw_surface_flux(key, part):
    row_key = jax.random.fold_in(key, 21)
    col_key = jax.random.fold_in(key, 22)
    cell_key = jax.random.fold_in(key, 23)
    col_scale = jnp.exp(2.302585 * jax.random.uniform(col_key, (1, NLON), jnp.float32))
    cells = jax.random.uniform(cell_key, (NLAT, NLON), jnp.float32)
    row_scale = jnp.exp(2.302585 * jax.random.uniform(row_key, (NLAT, 1), jnp.float32))
    return row_scale * col_scale * (0.5 + cells) / 15.0


def block_scale(stream_key, extent, cuts, smallest, top_value):
    loudness = 1.0
    for axis_at, shards_of in cuts:
        draws = jax.random.uniform(jax.random.fold_in(jax.random.fold_in(stream_key, 6), axis_at), (shards_of,), jnp.float32, smallest / len(cuts), top_value / len(cuts))
        loudness = loudness * jnp.repeat(jnp.exp(draws), extent[axis_at] // shards_of).reshape((-1,) + (1,) * (len(extent) - 1 - axis_at))
    return loudness


def centred(stream_key, dims, scale, limit, cuts=(), kind=jnp.bfloat16):
    values = jax.random.normal(stream_key, dims, jnp.float32) * scale
    if len(cuts) > 0:
        values = block_scale(stream_key, dims, cuts, -0.22, 0.18) * values
    return jnp.clip(values, min=-limit, max=limit).astype(kind)


def setup_inputs(seed: int = 0) -> dict:
    arg_keys = jax.random.split(jax.random.key(seed), 11)
    return {
        "initial_state": centred(arg_keys[0], (4, LEV, NLAT, NLON), 1.0, 6.0, ((2, 2), (3, 16)), jnp.float32),
        "land_mask": draw_land_mask(jax.random.fold_in(arg_keys[10], 71), 0),
        "surface_flux": draw_surface_flux(jax.random.fold_in(arg_keys[10], 71), 0),
        "weight_in": centred(arg_keys[3], (FEAT, HID), FEAT ** -0.5, 1.0, (), jnp.float32),
        "bias_in": centred(arg_keys[4], (HID,), 0.5, 3.0, (), jnp.float32),
        "weight_mid": centred(arg_keys[5], (HID, HID), HID ** -0.5, 0.75, (), jnp.float32),
        "bias_mid": centred(arg_keys[6], (HID,), 0.5, 3.0, (), jnp.float32),
        "weight_out": centred(arg_keys[7], (HID, FEAT), HID ** -0.5, 0.75, (), jnp.float32),
        "bias_out": centred(arg_keys[8], (FEAT,), 0.5, 3.0, (), jnp.float32),
        "cotangent": centred(arg_keys[9], (4, LEV, NLAT, NLON), 1.0, 6.0, ((2, 2), (3, 16)), jnp.float32),
    }


LAT_LIMIT = 1.2
TIME_STEP = 0.25
PRESSURE_GAIN = 0.5
THERMAL_EXPANSION = 0.2
HALINE_CONTRACTION = 0.8
CORIOLIS = 1.0
VISCOSITY = 0.15
DIFFUSIVITY = 0.1
FRESHWATER = 2.0
HIGHEST = lax.Precision.HIGHEST

def pressure_of(fields):
    return PRESSURE_GAIN * jnp.cumsum(HALINE_CONTRACTION * fields[1] - THERMAL_EXPANSION * fields[0], axis=0)

def combine(center, east_side, west_side, north_side, south_side, press_east, press_west, press_north, press_south, ocean_cells, inv_cos, coriolis):
    half_metric = 0.5 * inv_cos
    slope_x = (east_side - west_side) * half_metric
    slope_y = (north_side - south_side) * 0.5
    laplace = (east_side + west_side - 2.0 * center) * (inv_cos * inv_cos) + (north_side + south_side - 2.0 * center)
    along_u = center[2]
    along_v = center[3]
    mixing = jnp.array([DIFFUSIVITY, DIFFUSIVITY, VISCOSITY, VISCOSITY], jnp.float32).reshape((4,) + (1,) * (center.ndim - 1))
    change = mixing * laplace - (along_u * slope_x + along_v * slope_y)
    force_x = coriolis * along_v - (press_east - press_west) * half_metric
    force_y = -coriolis * along_u - (press_north - press_south) * 0.5
    return ocean_cells * jnp.stack([change[0], change[1], change[2] + force_x, change[3] + force_y])

def latitude_terms(row_index, row_count):
    latitude = LAT_LIMIT * (2.0 * (jnp.clip(row_index, 0.0, row_count - 1.0) + 0.5) / row_count - 1.0)
    return ((1.0 / jnp.cos(latitude))[:, None], (CORIOLIS * jnp.sin(latitude))[:, None])

def east_of(fields):
    return jnp.roll(fields, -1, axis=-1)

def west_of(fields):
    return jnp.roll(fields, 1, axis=-1)

def north_of(fields):
    return jnp.concatenate([fields[..., 1:, :], jnp.zeros_like(fields[..., :1, :])], axis=-2)

def south_of(fields):
    return jnp.concatenate([jnp.zeros_like(fields[..., :1, :]), fields[..., :-1, :]], axis=-2)

def dynamics(fields, ocean_cells, inv_cos, coriolis):
    pressure = pressure_of(fields)

    def one_level(pieces):
        column, level_press, level_ocean = pieces
        return combine(column, east_of(column), west_of(column), north_of(column), south_of(column), east_of(level_press), west_of(level_press), north_of(level_press), south_of(level_press), level_ocean, inv_cos, coriolis)
    per_level = lax.map(jax.checkpoint(one_level), (jnp.moveaxis(fields, 1, 0), pressure, ocean_cells))
    return jnp.moveaxis(per_level, 0, 1)

def three_sections(fields, ocean_cells, inv_cos, coriolis):
    section_one = fields + TIME_STEP * dynamics(fields, ocean_cells, inv_cos, coriolis)
    section_two = 0.75 * fields + 0.25 * (section_one + TIME_STEP * dynamics(section_one, ocean_cells, inv_cos, coriolis))
    return 1.0 / 3.0 * fields + 2.0 / 3.0 * (section_two + TIME_STEP * dynamics(section_two, ocean_cells, inv_cos, coriolis))

def closure(fields, ocean_cells, weights, forcing):
    weight_in, bias_in, weight_mid, bias_mid, weight_out, bias_out = weights
    columns = fields.reshape(weight_in.shape[0], -1)
    hidden = jnp.tanh(jnp.dot(weight_in.T, columns, precision=HIGHEST) + bias_in[:, None])
    hidden = jnp.tanh(jnp.dot(weight_mid.T, hidden, precision=HIGHEST) + bias_mid[:, None])
    output = (jnp.dot(weight_out.T, hidden, precision=HIGHEST) + bias_out[:, None]).reshape(fields.shape)
    output = output.at[1, 0].add(forcing)
    return ocean_cells * output

def reference(initial_state, land_mask, surface_flux, weight_in, bias_in, weight_mid, bias_mid, weight_out, bias_out, cotangent):
    ocean_cells = land_mask.astype(jnp.float32)
    top_ocean = ocean_cells[0]
    mean_flux = jnp.sum(top_ocean * surface_flux) / jnp.sum(top_ocean)
    forcing = -FRESHWATER * (surface_flux - mean_flux)
    inv_cos, coriolis = latitude_terms(jnp.arange(NLAT, dtype=jnp.float32), NLAT)

    def one_step(fields, weights):
        advanced = three_sections(fields, ocean_cells, inv_cos, coriolis)
        return advanced + TIME_STEP * closure(fields, ocean_cells, weights, forcing)
    stepper = jax.checkpoint(one_step)

    def run(source, weights):
        fields = ocean_cells * source
        for step_index in range(STEPS):
            fields = stepper(fields, weights)
        return fields
    weights = (weight_in, bias_in, weight_mid, bias_mid, weight_out, bias_out)
    final_state, pullback = jax.vjp(run, initial_state, weights)
    state_grad, weight_grads = pullback(cotangent)
    grad_scale = 1.0 / math.sqrt(NLAT * NLON)
    return (final_state, state_grad, weight_grads[0] * grad_scale, weight_grads[1] * grad_scale, weight_grads[2] * grad_scale, weight_grads[3] * grad_scale, weight_grads[4] * grad_scale, weight_grads[5] * grad_scale)
```

```python
import math

import jax
import jax.numpy as jnp
from jax import lax
from jax.experimental import pallas as pl
from jax.experimental.pallas import tpu as pltpu
from jax.sharding import PartitionSpec as P

LAT_LIMIT = 1.2
CORIOLIS = 1.0
VISCOSITY = 0.15
DIFFUSIVITY = 0.1

ROWS = 16
COLS = 128
REACH = 11
CREACH = 6
PAD = 12
EXT = 40
WIDE = 2 * COLS
FEATS = 40
HID = 64
PACK = 56
SLOT = 16
F32 = jnp.float32
BF16 = jnp.bfloat16
VMEM = pl.BlockSpec(memory_space=pltpu.VMEM)
SMEM = pl.BlockSpec(memory_space=pltpu.SMEM)
PARAMS = pltpu.CompilerParams(vmem_limit_bytes=44 * 1024 * 1024)


def sds(*shape):
    return jax.ShapeDtypeStruct(shape, F32)


def sub_index(width):
    return lax.broadcasted_iota(jnp.int32, (8, width), 0)


def tile(ref, row, number):
    return ref[row, 8 * number : 8 * number + 8, :]


def slot_pack(pieces, shift_of, width):
    lane = lax.broadcasted_iota(jnp.int32, (8, COLS), 1)
    packed = None
    for slot, piece in enumerate(pieces):
        turned = pltpu.roll(piece, shift_of(slot) % COLS, 1)
        if packed is None:
            packed = turned
        else:
            packed = jnp.where((lane >= slot * width) & (lane < (slot + 1) * width), turned, packed)
    return packed


def pack_kernel(sides, scal, x, mask, flux, cot, *outs):
    own, cown, sums, east, west = outs[:5]
    per_side = [outs[5 + 4 * i : 9 + 4 * i] for i in range(len(sides))]
    for r in range(ROWS):
        first = mask[pl.ds(r, 8, stride=ROWS), :].astype(F32)
        m8 = mask[8 * ROWS + r : 8 * ROWS + r + 1, :].astype(F32)
        m9 = mask[9 * ROWS + r : 9 * ROWS + r + 1, :].astype(F32)
        for t in range(4):
            own[r, 8 * t : 8 * t + 8, :] = x[pl.ds(t * 10 * ROWS + r, 8, stride=ROWS), :] * first
            cown[r, 8 * t : 8 * t + 8, :] = cot[pl.ds(t * 10 * ROWS + r, 8, stride=ROWS), :]
        for level, m in ((8, m8), (9, m9)):
            at = 32 + 4 * (level - 8)
            own[r, at : at + 4, :] = x[pl.ds(level * ROWS + r, 4, stride=10 * ROWS), :] * m
            cown[r, at : at + 4, :] = cot[pl.ds(level * ROWS + r, 4, stride=10 * ROWS), :]
        own[r, 40:48, :] = first
        own[r, 48:49, :] = m8
        own[r, 49:50, :] = m9
        own[r, 50:51, :] = flux[r : r + 1, :]
        own[r, 51:56, :] = jnp.zeros((5, COLS), F32)
    top = mask[0:ROWS, :].astype(F32)
    total = jnp.sum(jnp.sum(top * flux[...], axis=1, keepdims=True), axis=0, keepdims=True)
    count = jnp.sum(jnp.sum(top, axis=1, keepdims=True), axis=0, keepdims=True)
    sums[...] = jnp.where(sub_index(COLS) == 0, total, jnp.where(sub_index(COLS) == 1, count, 0.0))
    for half in range(2):
        for t in range(7):
            rows = [own[8 * half + s, 8 * t : 8 * t + 8, :] for s in range(8)]
            at = half * PACK + 8 * t
            east[at : at + 8, :] = slot_pack(rows, lambda s: SLOT * (s + 1), SLOT)
            west[at : at + 8, :] = slot_pack(rows, lambda s: SLOT * s, SLOT)
    for t in range(5):
        rows = [cown[s, 8 * t : 8 * t + 8, :] for s in range(ROWS)]
        at = 2 * PACK + 8 * t
        east[at : at + 8, :] = slot_pack(rows, lambda s: 8 * (s + 1), 8)
        west[at : at + 8, :] = slot_pack(rows, lambda s: 8 * s, 8)
    for side, (lat_x, lat_c, diag_e, diag_w) in zip(sides, per_side):
        start = {"swap": scal[0], "north": ROWS - REACH, "south": 0}[side]
        cstart = {"swap": scal[1], "north": ROWS - CREACH, "south": 0}[side]
        for n in range(REACH):
            lat_x[n] = own[start + n]
        for n in range(CREACH):
            lat_c[n] = cown[cstart + n]
        for t in range(7):
            rows = [own[start + n, 8 * t : 8 * t + 8, :] for n in range(REACH)]
            diag_e[8 * t : 8 * t + 8, :] = slot_pack(rows, lambda s: REACH * (s + 1), REACH)
            diag_w[8 * t : 8 * t + 8, :] = slot_pack(rows, lambda s: REACH * s, REACH)
        diag_e[PACK : PACK + 40, :] = east[2 * PACK : 2 * PACK + 40, :]
        diag_w[PACK : PACK + 40, :] = west[2 * PACK : 2 * PACK + 40, :]


def split(values):
    high = values.astype(BF16)
    return high, (values - high.astype(F32)).astype(BF16)


def stacked_weights(ref):
    values = ref[...]
    third = values.shape[1] // 3
    high, low = split(values)
    lane = lax.broadcasted_iota(jnp.int32, values.shape, 1)
    return jnp.where(lane < 2 * third, high.astype(F32), low.astype(F32)).astype(BF16)


def product(weights, high, low):
    return jnp.dot(weights, jnp.concatenate([high, low, high], axis=0), preferred_element_type=F32)


def across(a, b):
    dims = (((1,), (1,)), ((), ()))
    dot = lambda p, q: lax.dot_general(p, q, dims, preferred_element_type=F32)
    return dot(a[0], b[0]) + dot(a[0], b[1]) + dot(a[1], b[0])


def to_48(columns):
    return jnp.concatenate([columns, jnp.zeros((8, columns.shape[1]), F32)], axis=0)


def hidden_layers(z, w1, b1, w2, b2):
    h1 = jnp.tanh(product(w1, *z) + b1)
    h1s = split(h1)
    h2 = jnp.tanh(product(w2, *h1s) + b2)
    return h1, h1s, h2


def add_weight_terms(acc, z, h1s, h2s, g1s, g2s, gos):
    ones = jnp.ones((16, z[0].shape[1]), BF16)
    acc[0:48, 0:HID] += across(z, g1s)
    acc[48:112, 0:HID] += across(h1s, g2s)
    acc[112:160, 0:HID] += across(gos, h2s)
    acc[160:176, 0:HID] += ones_rows(ones, g1s)
    acc[176:192, 0:HID] += ones_rows(ones, g2s)
    acc[192:208, 0:48] += ones_rows(ones, gos)


def ones_rows(ones, g):
    dims = (((1,), (1,)), ((), ()))
    dot = lambda q: lax.dot_general(ones, q, dims, preferred_element_type=F32)
    return dot(g[0]) + dot(g[1])


def own_closure_kernel(own, w1, b1, w2, b2, w3, b3, out, h1_out, h2_out):
    k1, k2, k3 = stacked_weights(w1), stacked_weights(w2), stacked_weights(w3)

    def chunk(i, _):
        r = 4 * i
        z = split(to_48(jnp.concatenate([own[r + n, 0:FEATS, :] for n in range(4)], axis=1)))
        h1, h1s, h2 = hidden_layers(z, k1, b1[...], k2, b2[...])
        o = product(k3, *split(h2))[0:FEATS] + b3[...]
        for n in range(4):
            at = slice(n * COLS, (n + 1) * COLS)
            out[r + n] = o[:, at]
            h1_out[r + n] = h1[:, at]
            h2_out[r + n] = h2[:, at]
        return 0

    lax.fori_loop(0, ROWS // 4, chunk, 0)


class Row:
    def __init__(self, width):
        sub = sub_index(width)
        group = sub % 4
        self.sub = sub
        self.is_t = group == 0
        self.is_s = group == 1
        self.is_u = group == 2
        self.is_v = group == 3
        self.low = sub >= 4
        self.k4 = jnp.where(group < 2, DIFFUSIVITY, VISCOSITY).astype(F32)


def derived(k, temp, salt, mixed):
    zero = jnp.zeros_like(temp)
    press = 0.4 * salt - 0.1 * temp
    for by in (1, 2, 4):
        press = press + jnp.where(k.sub >= by, pltpu.roll(press, by, 0), zero)
    deep = jnp.where(k.is_t, 0.4 * pltpu.roll(mixed, 7, 0) - 0.1 * mixed, zero)
    deep = deep + jnp.where(k.low, pltpu.roll(deep, 4, 0), zero)
    deep = deep + pltpu.roll(deep, 1, 0)
    deep = deep + pltpu.roll(deep, 2, 0) + press[7:8, :]
    u4, v4 = deep_velocity(k, mixed)
    return press, deep, u4, v4


def deep_velocity(k, mixed):
    zero = jnp.zeros_like(mixed)
    u4 = jnp.where(k.is_u, mixed, zero)
    u4 = u4 + pltpu.roll(u4, 1, 0)
    u4 = u4 + pltpu.roll(u4, 6, 0)
    v4 = jnp.where(k.is_v, mixed, zero)
    v4 = v4 + pltpu.roll(v4, 7, 0)
    v4 = v4 + pltpu.roll(v4, 6, 0)
    return u4, v4


def put_state(k, ref, row, tiles):
    for t in range(5):
        ref[row, 8 * t : 8 * t + 8, :] = tiles[t]
    for t, values in enumerate(derived(k, tiles[0], tiles[1], tiles[4])):
        ref[row, 40 + 8 * t : 48 + 8 * t, :] = values


def east_of(q):
    return pltpu.roll(q, q.shape[1] - 1, 1)


def west_of(q):
    return pltpu.roll(q, 1, 1)


def tendency_row(k, ref, row, c, f):
    half = 0.5 * c
    c2 = c * c
    u, v = tile(ref, row, 2), tile(ref, row, 3)
    u4, v4 = tile(ref, row, 7), tile(ref, row, 8)
    uh, vh = u * half, v * 0.5
    u4h, v4h = u4 * half, v4 * 0.5
    change = []
    for t in range(5):
        q = tile(ref, row, t)
        e, w = east_of(q), west_of(q)
        n, s = tile(ref, row + 1, t), tile(ref, row - 1, t)
        lap = c2 * (e + w) + (n + s) - (2.0 * c2 + 2.0) * q
        gain = k.k4 if t == 4 else (DIFFUSIVITY if t < 2 else VISCOSITY)
        au, av = (u4h, v4h) if t == 4 else (uh, vh)
        change.append(gain * lap - (au * (e - w) + av * (n - s)))
    p = tile(ref, row, 5)
    change[2] = change[2] + (f * v - half * (east_of(p) - west_of(p)))
    change[3] = change[3] - (f * u + 0.5 * (tile(ref, row + 1, 5) - tile(ref, row - 1, 5)))
    p4 = tile(ref, row, 6)
    zero = jnp.zeros_like(p4)
    fx = f * v4 - half * (east_of(p4) - west_of(p4))
    fy = f * u4 + 0.5 * (tile(ref, row + 1, 6) - tile(ref, row - 1, 6))
    change[4] = change[4] + jnp.where(k.is_u, fx, jnp.where(k.is_v, -fy, zero))
    return change


def adjoint_row(k, ref, aref, row, c, f):
    half = 0.5 * c
    c2 = c * c
    u4 = tile(ref, row, 7)
    qe = [east_of(tile(ref, row, t)) for t in range(5)]
    qw = [west_of(tile(ref, row, t)) for t in range(5)]
    u4e, u4w = east_of(u4), west_of(u4)
    out = []
    to_u = to_v = None
    for t in range(5):
        a = tile(aref, row, t)
        ae, aw = east_of(a), west_of(a)
        an, as_ = tile(aref, row + 1, t), tile(aref, row - 1, t)
        gain = k.k4 if t == 4 else (DIFFUSIVITY if t < 2 else VISCOSITY)
        ue, uw = (u4e, u4w) if t == 4 else (qe[2], qw[2])
        which = 8 if t == 4 else 3
        vn, vs = tile(ref, row + 1, which), tile(ref, row - 1, which)
        lap = c2 * (ae + aw) + (an + as_) - (2.0 * c2 + 2.0) * a
        out.append(gain * lap + half * (ue * ae - uw * aw) + 0.5 * (vn * an - vs * as_))
        px = a * (qe[t] - qw[t])
        py = a * (tile(ref, row + 1, t) - tile(ref, row - 1, t))
        if t < 4:
            to_u = px if to_u is None else to_u + px
            to_v = py if to_v is None else to_v + py
        if t == 2:
            a2, bx = a, half * (ae - aw)
        if t == 3:
            a3, by = a, 0.5 * (an - as_)
        if t == 4:
            a4 = a
            deep_bx, deep_by = half * (ae - aw), 0.5 * (an - as_)
            px4, py4 = px * half, py * 0.5
    out[2] = out[2] - half * to_u - f * a3
    out[3] = out[3] - 0.5 * to_v + f * a2
    zero = jnp.zeros_like(a4)
    sx = px4 + pltpu.roll(px4, 7, 0)
    sx = sx + pltpu.roll(sx, 2, 0)
    sy = py4 + pltpu.roll(py4, 1, 0)
    sy = sy + pltpu.roll(sy, 2, 0)
    at_u = -sx - f * pltpu.roll(a4, 7, 0)
    at_v = f * pltpu.roll(a4, 1, 0) - sy
    deep = jnp.where(k.is_t, pltpu.roll(deep_bx, 6, 0) + pltpu.roll(deep_by, 5, 0), zero)
    deep = deep + jnp.where(k.low, zero, pltpu.roll(deep, 4, 0))
    press = bx + by
    for shift in (1, 2, 4):
        press = press + jnp.where(k.sub < 8 - shift, pltpu.roll(press, 8 - shift, 0), zero)
    press = press + deep[0:1, :]
    out[0] = out[0] - 0.1 * press
    out[1] = out[1] + 0.4 * press
    out[4] = out[4] + jnp.where(
        k.is_t,
        -0.1 * deep,
        jnp.where(k.is_s, 0.4 * pltpu.roll(deep, 1, 0), jnp.where(k.is_u, at_u, at_v)),
    )
    return out


def mask_tile(ref, row, t):
    return tile(ref, row, 1 if t == 4 else 0)


def adjoint_sections(k, cs, fs, bounds, states, masks, abuf, bbuf, hold, store, top):
    state_1, state_2, state_3 = states

    def third(r, _):
        d = adjoint_row(k, state_3, abuf, r, cs[r], fs[r])
        for t in range(5):
            ts = (2.0 / 3.0) * top(r, t) + d[t]
            hold[r, 8 * t : 8 * t + 8, :] = ts
            bbuf[r, 8 * t : 8 * t + 8, :] = 0.0625 * mask_tile(masks, r, t) * ts
        return 0

    def second(r, _):
        d = adjoint_row(k, state_2, bbuf, r, cs[r], fs[r])
        for t in range(5):
            ts = tile(hold, r, t)
            tf = 0.25 * ts + d[t]
            hold[r, 8 * t : 8 * t + 8, :] = (1.0 / 3.0) * top(r, t) + 0.75 * ts + tf
            abuf[r, 8 * t : 8 * t + 8, :] = 0.25 * mask_tile(masks, r, t) * tf
        return 0

    def first(r, _):
        d = adjoint_row(k, state_1, abuf, r, cs[r], fs[r])
        store(r, [tile(hold, r, t) + d[t] for t in range(5)])
        return 0

    lax.fori_loop(*bounds[0], third, 0)
    lax.fori_loop(*bounds[1], second, 0)
    lax.fori_loop(*bounds[2], first, 0)


def unpack(packed, slot_shift, keep):
    turned = pltpu.roll(packed, slot_shift % COLS, 1)
    return jnp.where(keep, turned, 0.0)


def edges(reach):
    lane = lax.broadcasted_iota(jnp.int32, (8, COLS), 1)
    return lane < reach, lane >= COLS - reach


def main_kernel(sides, scal, cs, fs, sums, own, cown, own_m, own_h1, own_h2, east, west, *rest):
    n = len(sides)
    side_refs = [rest[4 * i : 4 * i + 4] for i in range(n)]
    (w1, b1, w2, b2, w3, b3, v1, v2, v3), rest = rest[4 * n : 4 * n + 9], rest[4 * n + 9 :]
    final, grads, lam, from_closure, keep_1, keep_2, keep_3, keep_mask = rest[:8]
    s0, s1, s2, s3, s4, masks, fluxes, cot, outs, gz, abuf, bbuf, hold, acc = rest[8:]
    k = Row(WIDE)
    has_south, has_north = scal[2], scal[3]
    lo = lambda h: PAD - h * has_south
    hi = lambda h: PAD + ROWS + h * has_north

    for ref in (s0, s1, s2, s3, s4, abuf, bbuf):
        for row in (PAD - 1, PAD + ROWS):
            ref[row] = jnp.zeros(ref.shape[1:], F32)

    near_e, near_w = edges(REACH)
    cnear_e, cnear_w = edges(CREACH)

    def put_packed(row, core, halo):
        both = lambda t: jnp.concatenate([core(t), halo(t)], axis=1)
        put_state(k, s0, row, [both(t) for t in range(5)])
        masks[row, 0:8, :] = both(5)
        last = both(6)
        masks[row, 8:16, :] = jnp.where(k.low, last[1:2, :], last[0:1, :])
        fluxes[row] = last

    for r in range(ROWS):
        at = (r // 8) * PACK
        turn = SLOT * (r % 8)

        def halo(t):
            from_e = pltpu.roll(west[at + 8 * t : at + 8 * t + 8, :], -turn % COLS, 1)
            from_w = pltpu.roll(east[at + 8 * t : at + 8 * t + 8, :], -(turn + SLOT) % COLS, 1)
            return jnp.where(near_e, from_e, jnp.where(near_w, from_w, 0.0))

        put_packed(PAD + r, lambda t: own[r, 8 * t : 8 * t + 8, :], halo)
        for t in range(5):
            rows = slice(2 * PACK + 8 * t, 2 * PACK + 8 * t + 8)
            from_e = pltpu.roll(west[rows, :], -8 * r % COLS, 1)
            from_w = pltpu.roll(east[rows, :], -8 * (r + 1) % COLS, 1)
            side = jnp.where(cnear_e, from_e, jnp.where(cnear_w, from_w, 0.0))
            cot[PAD + r, 8 * t : 8 * t + 8, :] = jnp.concatenate(
                [cown[r, 8 * t : 8 * t + 8, :], side], axis=1
            )
    for side, (lat_x, lat_c, diag_e, diag_w) in zip(sides, side_refs):
        base = {"swap": scal[4], "north": 1, "south": PAD + ROWS}[side]
        cbase = {"swap": scal[5], "north": PAD - CREACH, "south": PAD + ROWS}[side]
        crow = {"swap": scal[6], "north": ROWS - CREACH, "south": 0}[side]
        for r in range(REACH):

            def halo(t):
                rows = slice(8 * t, 8 * t + 8)
                from_e = pltpu.roll(diag_w[rows, :], -REACH * r % COLS, 1)
                from_w = pltpu.roll(diag_e[rows, :], -REACH * (r + 1) % COLS, 1)
                return jnp.where(near_e, from_e, jnp.where(near_w, from_w, 0.0))

            put_packed(base + r, lambda t: lat_x[r, 8 * t : 8 * t + 8, :], halo)
        for r in range(CREACH):
            turn = lax.rem(2 * COLS - 8 * (crow + r), COLS)
            turn_w = lax.rem(2 * COLS - 8 * (crow + r + 1), COLS)
            for t in range(5):
                rows = slice(PACK + 8 * t, PACK + 8 * t + 8)
                from_e = pltpu.roll(diag_w[rows, :], turn, 1)
                from_w = pltpu.roll(diag_e[rows, :], turn_w, 1)
                part = jnp.where(cnear_e, from_e, jnp.where(cnear_w, from_w, 0.0))
                cot[cbase + r, 8 * t : 8 * t + 8, :] = jnp.concatenate(
                    [lat_c[r, 8 * t : 8 * t + 8, :], part], axis=1
                )

    k1, k2, k3 = stacked_weights(w1), stacked_weights(w2), stacked_weights(w3)
    q1, q2, q3 = stacked_weights(v1), stacked_weights(v2), stacked_weights(v3)

    def wide_pack(ref, base):
        parts = []
        for t in range(5):
            rows = [ref[base + s, 8 * t : 8 * t + 8, COLS:WIDE] for s in range(8)]
            parts.append(slot_pack(rows, lambda s: 8 + SLOT * s, SLOT))
        return jnp.concatenate(parts, axis=0)

    def wide_unpack(ref, base, values):
        for s in range(8):
            ref[base + s, 0:FEATS, COLS:WIDE] = pltpu.roll(values, -(8 + SLOT * s) % COLS, 1)

    for r in range(ROWS):
        outs[PAD + r, :, 0:COLS] = own_m[r]

    def closure_of(columns):
        z = split(to_48(columns))
        _, _, h2 = hidden_layers(z, k1, b1[...], k2, b2[...])
        return product(k3, *split(h2))[0:FEATS] + b3[...]

    def halo_rows(first):
        o = closure_of(jnp.concatenate([s0[first + i, 0:FEATS, 0:COLS] for i in range(4)], axis=1))
        for i in range(4):
            outs[first + i, :, 0:COLS] = o[:, i * COLS : (i + 1) * COLS]

    @pl.when(has_south == 1)
    def _():
        halo_rows(PAD - 8)
        halo_rows(PAD - 4)

    @pl.when(has_north == 1)
    def _():
        halo_rows(PAD + ROWS)
        halo_rows(PAD + ROWS + 4)

    groups = 3 if sides == ["swap"] else 4
    first = PAD - 8 * has_south
    o = closure_of(jnp.concatenate([wide_pack(s0, first + 8 * g) for g in range(groups)], axis=1))
    for g in range(groups):
        wide_unpack(outs, first + 8 * g, o[:, g * COLS : (g + 1) * COLS])

    def section_1(src, dst):
        def body(r, _):
            d = tendency_row(k, src, r, cs[r], fs[r])
            put_state(
                k, dst, r,
                [tile(src, r, t) + 0.25 * mask_tile(masks, r, t) * d[t] for t in range(5)],
            )
            return 0
        return body

    def section_2(src, mid, dst):
        def body(r, _):
            d = tendency_row(k, mid, r, cs[r], fs[r])
            put_state(
                k, dst, r,
                [
                    0.75 * tile(src, r, t) + 0.25 * tile(mid, r, t)
                    + 0.0625 * mask_tile(masks, r, t) * d[t]
                    for t in range(5)
                ],
            )
            return 0
        return body

    total = jnp.zeros((8, COLS), F32)
    for i in range(sums.shape[0] // 8):
        total = total + sums[8 * i : 8 * i + 8, :]
    mean = total[0:1, 0:1] / total[1:2, 0:1]

    def section_3(src, mid, r):
        d = tendency_row(k, mid, r, cs[r], fs[r])
        new = []
        for t in range(5):
            m = mask_tile(masks, r, t)
            o = tile(outs, r, t)
            if t == 1:
                force = 2.0 * (mean - fluxes[r, 2:3, :])
                o = o + jnp.where(k.sub == 0, force, 0.0)
            new.append(
                (1.0 / 3.0) * tile(src, r, t) + (2.0 / 3.0) * tile(mid, r, t)
                + m * ((1.0 / 6.0) * d[t] + 0.25 * o)
            )
        return new

    def step_1_end(r, _):
        put_state(k, s3, r, section_3(s0, s2, r))
        return 0

    lax.fori_loop(lo(10), hi(10), section_1(s0, s1), 0)
    lax.fori_loop(lo(9), hi(9), section_2(s0, s1, s2), 0)
    lax.fori_loop(lo(8), hi(8), step_1_end, 0)
    for i in range(24):
        at = lo(4) + i
        keep_1[i] = s0[at, 0:FEATS, :]
        keep_2[i] = s1[at, 0:FEATS, :]
        keep_3[i] = s2[at, 0:FEATS, :]
        keep_mask[i] = masks[at]

    acc[...] = jnp.zeros(acc.shape, F32)

    def closure_adjoint(z, h1, h1s, h2, go, with_weights):
        gos = split(to_48(go))
        g2 = product(q3, *gos) * (1.0 - h2 * h2)
        g2s = split(g2)
        g1 = product(q2, *g2s) * (1.0 - h1 * h1)
        g1s = split(g1)
        if with_weights:
            add_weight_terms(acc, z, h1s, split(h2), g1s, g2s, gos)
        return product(q1, *g1s)[0:FEATS]

    def both_ways(columns, go, with_weights):
        z = split(to_48(columns))
        h1, h1s, h2 = hidden_layers(z, k1, b1[...], k2, b2[...])
        o = product(k3, *split(h2))[0:FEATS] + b3[...] if with_weights else None
        return o, closure_adjoint(z, h1, h1s, h2, go, with_weights)

    def masked_core(ref, r):
        m0, m4 = masks[r, 0:8, 0:COLS], masks[r, 8:16, 0:COLS]
        parts = [
            0.25 * (m4 if t == 4 else m0) * ref[r, 8 * t : 8 * t + 8, 0:COLS] for t in range(5)
        ]
        return jnp.concatenate(parts, axis=0)

    def mask_cot(r, _):
        for t in range(5):
            bbuf[r, 8 * t : 8 * t + 8, :] = 0.25 * mask_tile(masks, r, t) * tile(cot, r, t)
            abuf[r, 8 * t : 8 * t + 8, :] = (1.0 / 6.0) * mask_tile(masks, r, t) * tile(cot, r, t)
        return 0

    lax.fori_loop(lo(6), hi(6), mask_cot, 0)

    def core_rows(first, with_weights):
        z = jnp.concatenate([s3[first + i, 0:FEATS, 0:COLS] for i in range(4)], axis=1)
        go = jnp.concatenate([bbuf[first + i, 0:FEATS, 0:COLS] for i in range(4)], axis=1)
        o, back = both_ways(z, go, with_weights)
        for i in range(4):
            at = slice(i * COLS, (i + 1) * COLS)
            if with_weights:
                outs[first + i, :, 0:COLS] = o[:, at]
            gz[first + i, :, 0:COLS] = back[:, at]

    lax.fori_loop(0, ROWS // 4, lambda i, _: (core_rows(PAD + 4 * i, True), 0)[1], 0)

    @pl.when(has_south == 1)
    def _():
        core_rows(PAD - 4, False)

    @pl.when(has_north == 1)
    def _():
        core_rows(PAD + ROWS, False)

    first = lo(4)
    z = jnp.concatenate([wide_pack(s3, first + 8 * g) for g in range(3)], axis=1)
    go = jnp.concatenate([wide_pack(bbuf, first + 8 * g) for g in range(3)], axis=1)
    _, back = both_ways(z, go, False)
    for g in range(3):
        wide_unpack(gz, first + 8 * g, back[:, g * COLS : (g + 1) * COLS])

    lax.fori_loop(lo(7), hi(7), section_1(s3, s1), 0)
    lax.fori_loop(lo(6), hi(6), section_2(s3, s1, s2), 0)

    def last(r, _):
        new = section_3(s3, s2, r)
        put_result(final, r - PAD, [x[:, 0:COLS] for x in new])
        return 0

    lax.fori_loop(PAD, PAD + ROWS, last, 0)

    def store(r, tiles):
        for t in range(5):
            s4[r, 8 * t : 8 * t + 8, :] = tiles[t] + tile(gz, r, t)

    @pl.when(has_south == 0)
    def _():
        bbuf[PAD - 1] = jnp.zeros((FEATS, WIDE), F32)

    @pl.when(has_north == 0)
    def _():
        bbuf[PAD + ROWS] = jnp.zeros((FEATS, WIDE), F32)

    adjoint_sections(
        k, cs, fs, [(lo(h), hi(h)) for h in (5, 4, 3)], (s3, s1, s2), masks, abuf, bbuf, hold,
        store, lambda r, t: tile(cot, r, t),
    )

    def first_step(i, _):
        r = 4 * i
        side = lambda read: jnp.concatenate([read(r + j) for j in range(4)], axis=1)
        z = split(to_48(side(lambda j: own[j, 0:FEATS, :])))
        h1 = side(lambda j: own_h1[j])
        h2 = side(lambda j: own_h2[j])
        go = side(lambda j: masked_core(s4, PAD + j))
        back = closure_adjoint(z, h1, split(h1), h2, go, True)
        for j in range(4):
            from_closure[r + j] = back[:, j * COLS : (j + 1) * COLS]
        return 0

    lax.fori_loop(0, ROWS // 4, first_step, 0)
    for i in range(24):
        lam[i] = s4[lo(4) + i, 0:FEATS, :]
    grads[...] = jnp.zeros(grads.shape, F32)
    grads[0:40, 0:HID] = acc[0:40, 0:HID]
    grads[0:40, HID : 2 * HID] = acc[112:152, 0:HID]
    grads[40:72, 0:HID] = acc[48:80, 0:HID]
    grads[40:72, HID : 2 * HID] = acc[80:112, 0:HID]
    grads[72:73, 0:HID] = acc[160:161, 0:HID]
    grads[72:73, HID : 2 * HID] = acc[176:177, 0:HID]
    grads[73:74, 0:HID] = acc[192:193, 0:HID]


def put_result(ref, row, tiles):
    for t in range(4):
        ref[pl.ds(t * 10 * ROWS + row, 8, stride=ROWS), :] = tiles[t]
    ref[pl.ds(8 * ROWS + row, 4, stride=10 * ROWS), :] = tiles[4][0:4, :]
    ref[pl.ds(9 * ROWS + row, 4, stride=10 * ROWS), :] = tiles[4][4:8, :]


def back_kernel(scal, cs, fs, lam, from_closure, keep_1, keep_2, keep_3, keep_mask, grad, *scratch):
    s0, s1, s2, masks, top, abuf, bbuf, hold = scratch
    k = Row(WIDE)
    has_south, has_north = scal[2], scal[3]
    lo = lambda h: PAD - h * has_south
    hi = lambda h: PAD + ROWS + h * has_north
    for ref in (abuf, bbuf):
        for row in (PAD - 1, PAD + ROWS):
            ref[row] = jnp.zeros((FEATS, WIDE), F32)
    for ref in (s0, s1, s2):
        for row in (PAD - 1, PAD + ROWS):
            ref[row] = jnp.zeros(ref.shape[1:], F32)

    def fill(i, _):
        r = lo(4) + i
        masks[r] = keep_mask[i]
        for src, dst in ((keep_1, s0), (keep_2, s1), (keep_3, s2)):
            dst[r, 0:FEATS, :] = src[i]
            u4, v4 = deep_velocity(k, src[i, 32:40, :])
            dst[r, 56:64, :] = u4
            dst[r, 64:72, :] = v4
        top[r] = lam[i]
        return 0

    lax.fori_loop(0, hi(4) - lo(4), fill, 0)

    def mask_top(r, _):
        for t in range(5):
            abuf[r, 8 * t : 8 * t + 8, :] = (1.0 / 6.0) * mask_tile(masks, r, t) * tile(top, r, t)
        return 0

    lax.fori_loop(lo(3), hi(3), mask_top, 0)

    def store(r, tiles):
        done = []
        for t in range(5):
            m = masks[r, 8:16, 0:COLS] if t == 4 else masks[r, 0:8, 0:COLS]
            done.append(m * (tiles[t][:, 0:COLS] + from_closure[r - PAD, 8 * t : 8 * t + 8, :]))
        put_result(grad, r - PAD, done)

    adjoint_sections(
        k, cs, fs, [(lo(2), hi(2)), (lo(1), hi(1)), (PAD, PAD + ROWS)], (s0, s1, s2), masks,
        abuf, bbuf, hold, store, lambda r, t: tile(top, r, t),
    )


def sum_kernel(parts, scale, gathered, win, bin_, wmid, bmid, wout, bout):
    total = gathered[0:80, :]
    for i in range(1, parts):
        total = total + gathered[80 * i : 80 * i + 80, :]
    total = total * scale
    win[...] = total[0:40, 0:HID]
    wout[...] = total[0:40, HID : 2 * HID]
    wmid[0:32, :] = total[40:72, 0:HID]
    wmid[32:64, :] = total[40:72, HID : 2 * HID]
    bin_[...] = total[72:73, 0:HID]
    bmid[...] = total[72:73, HID : 2 * HID]
    bout[...] = total[73:74, 0:40]


def by_tile(weights):
    fields = weights.reshape(4, 10, -1)
    head = fields[:, :8].reshape(32, -1)
    return jnp.concatenate([head, fields[:, 8], fields[:, 9]], axis=0)


def from_tile(rows):
    head = rows[:32].reshape(4, 8, -1)
    tail = jnp.stack([rows[32:36], rows[36:40]], axis=1)
    return jnp.concatenate([head, tail], axis=1).reshape(40, -1)


def three(w):
    return jnp.concatenate([w, w, w], axis=1)


def pad_cols(w):
    return jnp.pad(w, ((0, 0), (0, 8)))


def latitude_terms(row_index, row_count):
    latitude = LAT_LIMIT * (2.0 * (jnp.clip(row_index, 0.0, row_count - 1.0) + 0.5) / row_count - 1.0)
    return 1.0 / jnp.cos(latitude), CORIOLIS * jnp.sin(latitude)


def on_device(
    initial_state, land_mask, surface_flux, weight_in, bias_in, weight_mid, bias_mid, weight_out, bias_out, cotangent
):
    lat_n, lon_n = lax.axis_size("lat"), lax.axis_size("lon")
    lat_i = lax.axis_index("lat")
    lat_total, lon_total = ROWS * lat_n, COLS * lon_n
    sides = ["swap"] if lat_n == 2 else ["north", "south"]
    is_low = (lat_i == 0).astype(jnp.int32)
    has_south = (lat_i > 0).astype(jnp.int32)
    has_north = (lat_i < lat_n - 1).astype(jnp.int32)
    scal = jnp.stack(
        [
            is_low * (ROWS - REACH),
            is_low * (ROWS - CREACH),
            has_south,
            has_north,
            jnp.where(is_low == 1, PAD + ROWS, 1),
            jnp.where(is_low == 1, PAD + ROWS, PAD - CREACH),
            jnp.where(is_low == 1, 0, ROWS - CREACH),
        ]
    ).astype(jnp.int32)
    rows = (lat_i * ROWS - PAD + jnp.arange(EXT, dtype=jnp.int32)).astype(F32)
    cs, fs = latitude_terms(rows, lat_total)

    packed = pl.pallas_call(
        lambda *refs: pack_kernel(sides, *refs),
        out_shape=[
            sds(ROWS, PACK, COLS), sds(ROWS, FEATS, COLS), sds(8, COLS),
            sds(2 * PACK + 40, COLS), sds(2 * PACK + 40, COLS),
        ]
        + [sds(REACH, PACK, COLS), sds(CREACH, FEATS, COLS), sds(PACK + 40, COLS), sds(PACK + 40, COLS)] * len(sides),
        in_specs=[SMEM] + [VMEM] * 4,
        out_specs=[VMEM] * (5 + 4 * len(sides)),
        compiler_params=PARAMS,
        name="pack_halos",
    )(
        scal,
        initial_state.reshape(40 * ROWS, COLS),
        land_mask.reshape(10 * ROWS, COLS),
        surface_flux,
        cotangent.reshape(40 * ROWS, COLS),
    )
    own, cown, sums, east_pay, west_pay = packed[:5]

    def lat_pairs(side):
        if side == "swap":
            return [(0, 1), (1, 0)]
        if side == "north":
            return [(i, i + 1) for i in range(lat_n - 1)]
        return [(i + 1, i) for i in range(lat_n - 1)]

    def diagonal(side, step):
        return [
            (i * lat_n + a, ((i + step) % lon_n) * lat_n + b)
            for i in range(lon_n)
            for a, b in lat_pairs(side)
        ]

    east_ring = [(i, (i + 1) % lon_n) for i in range(lon_n)]
    west_ring = [((i + 1) % lon_n, i) for i in range(lon_n)]
    received = []
    for i, side in enumerate(sides):
        lat_x, lat_c, diag_e, diag_w = packed[5 + 4 * i : 9 + 4 * i]
        received.append(
            [
                lax.ppermute(lat_x, "lat", lat_pairs(side)),
                lax.ppermute(lat_c, "lat", lat_pairs(side)),
                lax.ppermute(diag_e, ("lon", "lat"), diagonal(side, 1)),
                lax.ppermute(diag_w, ("lon", "lat"), diagonal(side, -1)),
            ]
        )
    from_west = lax.ppermute(east_pay, "lon", east_ring)
    from_east = lax.ppermute(west_pay, "lon", west_ring)
    all_sums = lax.all_gather(sums, ("lon", "lat"), tiled=True)

    w_in, w_out_t = by_tile(weight_in), by_tile(weight_out.T)
    col = lambda b: b.reshape(-1, 1)
    forward = [
        three(pad_cols(w_in.T)), col(bias_in), three(weight_mid.T), col(bias_mid), three(w_out_t), by_tile(col(bias_out)),
    ]
    forward[4] = jnp.pad(forward[4], ((0, 8), (0, 0)))
    backward = [jnp.pad(three(w_in), ((0, 8), (0, 0))), three(weight_mid), three(pad_cols(w_out_t.T))]

    own_m, own_h1, own_h2 = pl.pallas_call(
        own_closure_kernel,
        out_shape=[sds(ROWS, FEATS, COLS), sds(ROWS, HID, COLS), sds(ROWS, HID, COLS)],
        in_specs=[VMEM] * 7,
        out_specs=[VMEM] * 3,
        compiler_params=PARAMS,
        cost_estimate=pl.CostEstimate(flops=10**9, bytes_accessed=2 * 10**6, transcendentals=0),
        name="own_closure",
    )(own, *forward)

    state = pltpu.VMEM((EXT, 72, WIDE), F32)
    plain = pltpu.VMEM((EXT, FEATS, WIDE), F32)
    marks = pltpu.VMEM((EXT, 16, WIDE), F32)
    outs = pl.pallas_call(
        lambda *refs: main_kernel(sides, *refs),
        out_shape=[
            sds(40 * ROWS, COLS), sds(80, COLS), sds(24, FEATS, WIDE), sds(ROWS, FEATS, COLS),
            sds(24, FEATS, WIDE), sds(24, FEATS, WIDE), sds(24, FEATS, WIDE), sds(24, 16, WIDE),
        ],
        in_specs=[SMEM] * 3 + [VMEM] * (8 + 4 * len(sides) + 9),
        out_specs=[VMEM] * 8,
        scratch_shapes=[state] * 5
        + [marks, pltpu.VMEM((EXT, 8, WIDE), F32)]
        + [plain] * 6
        + [pltpu.VMEM((208, HID), F32)],
        compiler_params=PARAMS,
        cost_estimate=pl.CostEstimate(flops=5 * 10**9, bytes_accessed=10**7, transcendentals=0),
        name="steps_and_adjoint",
    )(
        scal, cs, fs, all_sums, own, cown, own_m, own_h1, own_h2, from_west, from_east,
        *[item for side in received for item in side], *forward, *backward,
    )
    final, grads, lam, from_closure, keep_1, keep_2, keep_3, keep_mask = outs
    gathered = lax.all_gather(grads, ("lon", "lat"), tiled=True)

    state_grad = pl.pallas_call(
        back_kernel,
        out_shape=sds(40 * ROWS, COLS),
        in_specs=[SMEM] * 3 + [VMEM] * 6,
        out_specs=VMEM,
        scratch_shapes=[state] * 3 + [marks] + [plain] * 4,
        compiler_params=PARAMS,
        cost_estimate=pl.CostEstimate(flops=3 * 10**9, bytes_accessed=10**7, transcendentals=0),
        name="first_step_adjoint",
    )(scal, cs, fs, lam, from_closure, keep_1, keep_2, keep_3, keep_mask)

    parts = lat_n * lon_n
    scale = 1.0 / math.sqrt(lat_total * lon_total)
    g_in, g_bin, g_mid, g_bmid, g_out, g_bout = pl.pallas_call(
        lambda *refs: sum_kernel(parts, scale, *refs),
        out_shape=[sds(40, HID), sds(1, HID), sds(HID, HID), sds(1, HID), sds(40, HID), sds(1, 40)],
        in_specs=[VMEM],
        out_specs=[VMEM] * 6,
        compiler_params=PARAMS,
        name="sum_weight_grads",
    )(gathered)
    shape = initial_state.shape
    return (
        final.reshape(shape),
        state_grad.reshape(shape),
        from_tile(g_in),
        g_bin.reshape(-1),
        g_mid,
        g_bmid.reshape(-1),
        from_tile(g_out).T,
        from_tile(g_bout.reshape(40, 1)).reshape(-1),
    )


def solution(mesh):
    split_state = P(None, None, "lat", "lon")
    return jax.shard_map(
        on_device,
        mesh=mesh,
        in_specs=(split_state, P(None, "lat", "lon"), P("lat", "lon"), P(), P(), P(), P(), P(), P(), split_state),
        out_specs=(split_state, split_state, P(), P(), P(), P(), P(), P()),
        check_vma=False,
    )
```

```python
import math

import jax
import jax.numpy as jnp
from jax import lax
from jax.experimental import pallas as pl
from jax.experimental.pallas import tpu as pltpu
from jax.sharding import PartitionSpec as P

LAT_LIMIT = 1.2
CORIOLIS = 1.0
VISCOSITY = 0.15
DIFFUSIVITY = 0.1

ROWS = 16
COLS = 128
REACH = 11
CREACH = 6
PAD = 12
EXT = 40
WIDE = 2 * COLS
FEATS = 40
HID = 64
PACK = 56
SLOT = 16
F32 = jnp.float32
BF16 = jnp.bfloat16
VMEM = pl.BlockSpec(memory_space=pltpu.VMEM)
SMEM = pl.BlockSpec(memory_space=pltpu.SMEM)


def params(megabytes):
    return pltpu.CompilerParams(vmem_limit_bytes=megabytes * 1024 * 1024)


def sds(*shape):
    return jax.ShapeDtypeStruct(shape, F32)


def sub_index(width):
    return lax.broadcasted_iota(jnp.int32, (8, width), 0)


def tile(ref, row, number):
    return ref[row, 8 * number : 8 * number + 8, :]


def slot_pack(pieces, shift_of, width):
    lane = lax.broadcasted_iota(jnp.int32, (8, COLS), 1)
    packed = None
    for slot, piece in enumerate(pieces):
        turned = pltpu.roll(piece, shift_of(slot) % COLS, 1)
        if packed is None:
            packed = turned
        else:
            packed = jnp.where((lane >= slot * width) & (lane < (slot + 1) * width), turned, packed)
    return packed


def pack_kernel(sides, scal, x_hbm, mask_hbm, flux_hbm, cot_hbm, *outs):
    x, mask, flux, cot, sems = outs[-5:]
    own, cown, sums, east, west = outs[:5]
    per_side = [outs[5 + 4 * i : 9 + 4 * i] for i in range(len(sides))]
    pairs = ((mask_hbm, mask), (x_hbm, x), (flux_hbm, flux), (cot_hbm, cot))
    copies = [pltpu.make_async_copy(a, b, sems.at[i]) for i, (a, b) in enumerate(pairs)]
    for copy in copies:
        copy.start()
    for copy in copies:
        copy.wait()
    for r in range(ROWS):
        first = mask[pl.ds(r, 8, stride=ROWS), :].astype(F32)
        m8 = mask[8 * ROWS + r : 8 * ROWS + r + 1, :].astype(F32)
        m9 = mask[9 * ROWS + r : 9 * ROWS + r + 1, :].astype(F32)
        for t in range(4):
            own[r, 8 * t : 8 * t + 8, :] = x[pl.ds(t * 10 * ROWS + r, 8, stride=ROWS), :] * first
            cown[r, 8 * t : 8 * t + 8, :] = cot[pl.ds(t * 10 * ROWS + r, 8, stride=ROWS), :]
        for level, m in ((8, m8), (9, m9)):
            at = 32 + 4 * (level - 8)
            own[r, at : at + 4, :] = x[pl.ds(level * ROWS + r, 4, stride=10 * ROWS), :] * m
            cown[r, at : at + 4, :] = cot[pl.ds(level * ROWS + r, 4, stride=10 * ROWS), :]
        own[r, 40:48, :] = first
        own[r, 48:49, :] = m8
        own[r, 49:50, :] = m9
        own[r, 50:51, :] = flux[r : r + 1, :]
        own[r, 51:56, :] = jnp.zeros((5, COLS), F32)
    top = mask[0:ROWS, :].astype(F32)
    total = jnp.sum(jnp.sum(top * flux[...], axis=1, keepdims=True), axis=0, keepdims=True)
    count = jnp.sum(jnp.sum(top, axis=1, keepdims=True), axis=0, keepdims=True)
    sums[...] = jnp.where(sub_index(COLS) == 0, total, jnp.where(sub_index(COLS) == 1, count, 0.0))
    for half in range(2):
        for t in range(7):
            rows = [own[8 * half + s, 8 * t : 8 * t + 8, :] for s in range(8)]
            at = half * PACK + 8 * t
            east[at : at + 8, :] = slot_pack(rows, lambda s: SLOT * (s + 1), SLOT)
            west[at : at + 8, :] = slot_pack(rows, lambda s: SLOT * s, SLOT)
    for t in range(5):
        rows = [cown[s, 8 * t : 8 * t + 8, :] for s in range(ROWS)]
        at = 2 * PACK + 8 * t
        east[at : at + 8, :] = slot_pack(rows, lambda s: 8 * (s + 1), 8)
        west[at : at + 8, :] = slot_pack(rows, lambda s: 8 * s, 8)
    for side, (lat_x, lat_c, diag_e, diag_w) in zip(sides, per_side):
        start = {"swap": scal[0], "north": ROWS - REACH, "south": 0}[side]
        cstart = {"swap": scal[1], "north": ROWS - CREACH, "south": 0}[side]
        for n in range(REACH):
            lat_x[n] = own[start + n]
        for n in range(CREACH):
            lat_c[n] = cown[cstart + n]
        for t in range(7):
            rows = [own[start + n, 8 * t : 8 * t + 8, :] for n in range(REACH)]
            diag_e[8 * t : 8 * t + 8, :] = slot_pack(rows, lambda s: REACH * (s + 1), REACH)
            diag_w[8 * t : 8 * t + 8, :] = slot_pack(rows, lambda s: REACH * s, REACH)
        diag_e[PACK : PACK + 40, :] = east[2 * PACK : 2 * PACK + 40, :]
        diag_w[PACK : PACK + 40, :] = west[2 * PACK : 2 * PACK + 40, :]


def split(values):
    high = values.astype(BF16)
    return high, (values - high.astype(F32)).astype(BF16)


def stacked_weights(ref):
    values = ref[...]
    third = values.shape[1] // 3
    high, low = split(values)
    lane = lax.broadcasted_iota(jnp.int32, values.shape, 1)
    return jnp.where(lane < 2 * third, high.astype(F32), low.astype(F32)).astype(BF16)


def product(weights, high, low):
    return jnp.dot(weights, jnp.concatenate([high, low, high], axis=0), preferred_element_type=F32)


def across(a, b):
    dims = (((1,), (1,)), ((), ()))
    dot = lambda p, q: lax.dot_general(p, q, dims, preferred_element_type=F32)
    return dot(a[0], b[0]) + dot(a[0], b[1]) + dot(a[1], b[0])


def to_48(columns):
    return jnp.concatenate([columns, jnp.zeros((8, columns.shape[1]), F32)], axis=0)


def hidden_layers(z, w1, b1, w2, b2):
    h1 = jnp.tanh(product(w1, *z) + b1)
    h1s = split(h1)
    h2 = jnp.tanh(product(w2, *h1s) + b2)
    return h1, h1s, h2


def add_weight_terms(acc, z, h1s, h2s, g1s, g2s, gos):
    ones = jnp.ones((16, z[0].shape[1]), BF16)
    acc[0:48, 0:HID] += across(z, g1s)
    acc[48:112, 0:HID] += across(h1s, g2s)
    acc[112:160, 0:HID] += across(gos, h2s)
    acc[160:176, 0:HID] += ones_rows(ones, g1s)
    acc[176:192, 0:HID] += ones_rows(ones, g2s)
    acc[192:208, 0:48] += ones_rows(ones, gos)


def ones_rows(ones, g):
    dims = (((1,), (1,)), ((), ()))
    dot = lambda q: lax.dot_general(ones, q, dims, preferred_element_type=F32)
    return dot(g[0]) + dot(g[1])


def own_closure_kernel(own, w1, b1, w2, b2, w3, b3, out, h1_out, h2_out):
    k1, k2, k3 = stacked_weights(w1), stacked_weights(w2), stacked_weights(w3)

    def chunk(i, _):
        r = 4 * i
        z = split(to_48(jnp.concatenate([own[r + n, 0:FEATS, :] for n in range(4)], axis=1)))
        h1, h1s, h2 = hidden_layers(z, k1, b1[...], k2, b2[...])
        o = product(k3, *split(h2))[0:FEATS] + b3[...]
        for n in range(4):
            at = slice(n * COLS, (n + 1) * COLS)
            out[r + n] = o[:, at]
            h1_out[r + n] = h1[:, at]
            h2_out[r + n] = h2[:, at]
        return 0

    lax.fori_loop(0, ROWS // 4, chunk, 0)


class Row:
    def __init__(self, width):
        sub = sub_index(width)
        group = sub % 4
        self.sub = sub
        self.is_t = group == 0
        self.is_s = group == 1
        self.is_u = group == 2
        self.is_v = group == 3
        self.low = sub >= 4
        self.k4 = jnp.where(group < 2, DIFFUSIVITY, VISCOSITY).astype(F32)


def derived(k, temp, salt, mixed):
    zero = jnp.zeros_like(temp)
    press = 0.4 * salt - 0.1 * temp
    for by in (1, 2, 4):
        press = press + jnp.where(k.sub >= by, pltpu.roll(press, by, 0), zero)
    deep = jnp.where(k.is_t, 0.4 * pltpu.roll(mixed, 7, 0) - 0.1 * mixed, zero)
    deep = deep + jnp.where(k.low, pltpu.roll(deep, 4, 0), zero)
    deep = deep + pltpu.roll(deep, 1, 0)
    deep = deep + pltpu.roll(deep, 2, 0) + press[7:8, :]
    u4, v4 = deep_velocity(k, mixed)
    return press, deep, u4, v4


def deep_velocity(k, mixed):
    zero = jnp.zeros_like(mixed)
    u4 = jnp.where(k.is_u, mixed, zero)
    u4 = u4 + pltpu.roll(u4, 1, 0)
    u4 = u4 + pltpu.roll(u4, 6, 0)
    v4 = jnp.where(k.is_v, mixed, zero)
    v4 = v4 + pltpu.roll(v4, 7, 0)
    v4 = v4 + pltpu.roll(v4, 6, 0)
    return u4, v4


def put_state(k, ref, row, tiles):
    for t in range(5):
        ref[row, 8 * t : 8 * t + 8, :] = tiles[t]
    for t, values in enumerate(derived(k, tiles[0], tiles[1], tiles[4])):
        ref[row, 40 + 8 * t : 48 + 8 * t, :] = values


def east_of(q):
    return pltpu.roll(q, q.shape[1] - 1, 1)


def west_of(q):
    return pltpu.roll(q, 1, 1)


def tendency_row(k, ref, row, c, f):
    half = 0.5 * c
    c2 = c * c
    u, v = tile(ref, row, 2), tile(ref, row, 3)
    u4, v4 = tile(ref, row, 7), tile(ref, row, 8)
    uh, vh = u * half, v * 0.5
    u4h, v4h = u4 * half, v4 * 0.5
    change = []
    for t in range(5):
        q = tile(ref, row, t)
        e, w = east_of(q), west_of(q)
        n, s = tile(ref, row + 1, t), tile(ref, row - 1, t)
        lap = c2 * (e + w) + (n + s) - (2.0 * c2 + 2.0) * q
        gain = k.k4 if t == 4 else (DIFFUSIVITY if t < 2 else VISCOSITY)
        au, av = (u4h, v4h) if t == 4 else (uh, vh)
        change.append(gain * lap - (au * (e - w) + av * (n - s)))
    p = tile(ref, row, 5)
    change[2] = change[2] + (f * v - half * (east_of(p) - west_of(p)))
    change[3] = change[3] - (f * u + 0.5 * (tile(ref, row + 1, 5) - tile(ref, row - 1, 5)))
    p4 = tile(ref, row, 6)
    zero = jnp.zeros_like(p4)
    fx = f * v4 - half * (east_of(p4) - west_of(p4))
    fy = f * u4 + 0.5 * (tile(ref, row + 1, 6) - tile(ref, row - 1, 6))
    change[4] = change[4] + jnp.where(k.is_u, fx, jnp.where(k.is_v, -fy, zero))
    return change


def adjoint_row(k, ref, aref, row, c, f):
    half = 0.5 * c
    c2 = c * c
    u4 = tile(ref, row, 7)
    qe = [east_of(tile(ref, row, t)) for t in range(5)]
    qw = [west_of(tile(ref, row, t)) for t in range(5)]
    u4e, u4w = east_of(u4), west_of(u4)
    out = []
    to_u = to_v = None
    for t in range(5):
        a = tile(aref, row, t)
        ae, aw = east_of(a), west_of(a)
        an, as_ = tile(aref, row + 1, t), tile(aref, row - 1, t)
        gain = k.k4 if t == 4 else (DIFFUSIVITY if t < 2 else VISCOSITY)
        ue, uw = (u4e, u4w) if t == 4 else (qe[2], qw[2])
        which = 8 if t == 4 else 3
        vn, vs = tile(ref, row + 1, which), tile(ref, row - 1, which)
        lap = c2 * (ae + aw) + (an + as_) - (2.0 * c2 + 2.0) * a
        out.append(gain * lap + half * (ue * ae - uw * aw) + 0.5 * (vn * an - vs * as_))
        px = a * (qe[t] - qw[t])
        py = a * (tile(ref, row + 1, t) - tile(ref, row - 1, t))
        if t < 4:
            to_u = px if to_u is None else to_u + px
            to_v = py if to_v is None else to_v + py
        if t == 2:
            a2, bx = a, half * (ae - aw)
        if t == 3:
            a3, by = a, 0.5 * (an - as_)
        if t == 4:
            a4 = a
            deep_bx, deep_by = half * (ae - aw), 0.5 * (an - as_)
            px4, py4 = px * half, py * 0.5
    out[2] = out[2] - half * to_u - f * a3
    out[3] = out[3] - 0.5 * to_v + f * a2
    zero = jnp.zeros_like(a4)
    sx = px4 + pltpu.roll(px4, 7, 0)
    sx = sx + pltpu.roll(sx, 2, 0)
    sy = py4 + pltpu.roll(py4, 1, 0)
    sy = sy + pltpu.roll(sy, 2, 0)
    at_u = -sx - f * pltpu.roll(a4, 7, 0)
    at_v = f * pltpu.roll(a4, 1, 0) - sy
    deep = jnp.where(k.is_t, pltpu.roll(deep_bx, 6, 0) + pltpu.roll(deep_by, 5, 0), zero)
    deep = deep + jnp.where(k.low, zero, pltpu.roll(deep, 4, 0))
    press = bx + by
    for shift in (1, 2, 4):
        press = press + jnp.where(k.sub < 8 - shift, pltpu.roll(press, 8 - shift, 0), zero)
    press = press + deep[0:1, :]
    out[0] = out[0] - 0.1 * press
    out[1] = out[1] + 0.4 * press
    out[4] = out[4] + jnp.where(
        k.is_t,
        -0.1 * deep,
        jnp.where(k.is_s, 0.4 * pltpu.roll(deep, 1, 0), jnp.where(k.is_u, at_u, at_v)),
    )
    return out


def mask_tile(ref, row, t):
    return tile(ref, row, 1 if t == 4 else 0)


def adjoint_third(k, cs, fs, bounds, state, masks, abuf, top, hold, bbuf):
    def body(r, _):
        d = adjoint_row(k, state, abuf, r, cs[r], fs[r])
        for t in range(5):
            ts = (2.0 / 3.0) * tile(top, r, t) + d[t]
            hold[r, 8 * t : 8 * t + 8, :] = ts
            bbuf[r, 8 * t : 8 * t + 8, :] = 0.0625 * mask_tile(masks, r, t) * ts
        return 0

    lax.fori_loop(*bounds, body, 0)


def adjoint_second(k, cs, fs, bounds, state, masks, bbuf, top, hold, left, abuf):
    def body(r, _):
        d = adjoint_row(k, state, bbuf, r, cs[r], fs[r])
        for t in range(5):
            ts = tile(hold, r, t)
            tf = 0.25 * ts + d[t]
            left[r, 8 * t : 8 * t + 8, :] = (1.0 / 3.0) * tile(top, r, t) + 0.75 * ts + tf
            abuf[r, 8 * t : 8 * t + 8, :] = 0.25 * mask_tile(masks, r, t) * tf
        return 0

    lax.fori_loop(*bounds, body, 0)


def adjoint_first(k, cs, fs, bounds, state, abuf, left, store):
    def body(r, _):
        d = adjoint_row(k, state, abuf, r, cs[r], fs[r])
        store(r, [tile(left, r, t) + d[t] for t in range(5)])
        return 0

    lax.fori_loop(*bounds, body, 0)


def edges(reach):
    lane = lax.broadcasted_iota(jnp.int32, (8, COLS), 1)
    return lane < reach, lane >= COLS - reach


def wide_pack(ref, base):
    parts = []
    for t in range(5):
        rows = [ref[base + s, 8 * t : 8 * t + 8, COLS:WIDE] for s in range(8)]
        parts.append(slot_pack(rows, lambda s: 8 + SLOT * s, SLOT))
    return jnp.concatenate(parts, axis=0)

def wide_unpack(ref, base, values):
    for s in range(8):
        ref[base + s, 0:FEATS, COLS:WIDE] = pltpu.roll(values, -(8 + SLOT * s) % COLS, 1)


def section_1(k, cs, fs, masks, src, dst):
    def body(r, _):
        d = tendency_row(k, src, r, cs[r], fs[r])
        put_state(
            k, dst, r,
            [tile(src, r, t) + 0.25 * mask_tile(masks, r, t) * d[t] for t in range(5)],
        )
        return 0
    return body

def section_2(k, cs, fs, masks, src, mid, dst):
    def body(r, _):
        d = tendency_row(k, mid, r, cs[r], fs[r])
        put_state(
            k, dst, r,
            [
                0.75 * tile(src, r, t) + 0.25 * tile(mid, r, t)
                + 0.0625 * mask_tile(masks, r, t) * d[t]
                for t in range(5)
            ],
        )
        return 0
    return body


def early_kernel(sides, scal, cs, fs, gate, own, cown, own_m, east, west, *rest):
    n = len(sides)
    side_refs = [rest[4 * i : 4 * i + 4] for i in range(n)]
    (w1, b1, w2, b2, w3, b3), rest = rest[4 * n : 4 * n + 6], rest[4 * n + 6 :]
    s0, s1, s2, masks, fluxes, cot, outs = rest
    k = Row(WIDE)
    has_south, has_north = scal[2], scal[3]
    lo = lambda h: PAD - h * has_south
    hi = lambda h: PAD + ROWS + h * has_north

    for ref in (s0, s1, s2):
        for row in (PAD - 1, PAD + ROWS):
            ref[row] = jnp.zeros(ref.shape[1:], F32)

    near_e, near_w = edges(REACH)
    cnear_e, cnear_w = edges(CREACH)

    def put_packed(row, core, halo):
        both = lambda t: jnp.concatenate([core(t), halo(t)], axis=1)
        put_state(k, s0, row, [both(t) for t in range(5)])
        masks[row, 0:8, :] = both(5)
        last = both(6)
        masks[row, 8:16, :] = jnp.where(k.low, last[1:2, :], last[0:1, :])
        fluxes[row] = last

    for r in range(ROWS):
        at = (r // 8) * PACK
        turn = SLOT * (r % 8)

        def halo(t):
            from_e = pltpu.roll(west[at + 8 * t : at + 8 * t + 8, :], -turn % COLS, 1)
            from_w = pltpu.roll(east[at + 8 * t : at + 8 * t + 8, :], -(turn + SLOT) % COLS, 1)
            return jnp.where(near_e, from_e, jnp.where(near_w, from_w, 0.0))

        put_packed(PAD + r, lambda t: own[r, 8 * t : 8 * t + 8, :], halo)
        for t in range(5):
            rows = slice(2 * PACK + 8 * t, 2 * PACK + 8 * t + 8)
            from_e = pltpu.roll(west[rows, :], -8 * r % COLS, 1)
            from_w = pltpu.roll(east[rows, :], -8 * (r + 1) % COLS, 1)
            side = jnp.where(cnear_e, from_e, jnp.where(cnear_w, from_w, 0.0))
            cot[PAD + r, 8 * t : 8 * t + 8, :] = jnp.concatenate(
                [cown[r, 8 * t : 8 * t + 8, :], side], axis=1
            )
    for side, (lat_x, lat_c, diag_e, diag_w) in zip(sides, side_refs):
        base = {"swap": scal[4], "north": 1, "south": PAD + ROWS}[side]
        cbase = {"swap": scal[5], "north": PAD - CREACH, "south": PAD + ROWS}[side]
        crow = {"swap": scal[6], "north": ROWS - CREACH, "south": 0}[side]
        for r in range(REACH):

            def halo(t):
                rows = slice(8 * t, 8 * t + 8)
                from_e = pltpu.roll(diag_w[rows, :], -REACH * r % COLS, 1)
                from_w = pltpu.roll(diag_e[rows, :], -REACH * (r + 1) % COLS, 1)
                return jnp.where(near_e, from_e, jnp.where(near_w, from_w, 0.0))

            put_packed(base + r, lambda t: lat_x[r, 8 * t : 8 * t + 8, :], halo)
        for r in range(CREACH):
            turn = lax.rem(2 * COLS - 8 * (crow + r), COLS)
            turn_w = lax.rem(2 * COLS - 8 * (crow + r + 1), COLS)
            for t in range(5):
                rows = slice(PACK + 8 * t, PACK + 8 * t + 8)
                from_e = pltpu.roll(diag_w[rows, :], turn, 1)
                from_w = pltpu.roll(diag_e[rows, :], turn_w, 1)
                part = jnp.where(cnear_e, from_e, jnp.where(cnear_w, from_w, 0.0))
                cot[cbase + r, 8 * t : 8 * t + 8, :] = jnp.concatenate(
                    [lat_c[r, 8 * t : 8 * t + 8, :], part], axis=1
                )

    k1, k2, k3 = stacked_weights(w1), stacked_weights(w2), stacked_weights(w3)

    for r in range(ROWS):
        outs[PAD + r, :, 0:COLS] = own_m[r]

    def closure_of(columns):
        z = split(to_48(columns))
        _, _, h2 = hidden_layers(z, k1, b1[...], k2, b2[...])
        return product(k3, *split(h2))[0:FEATS] + b3[...]

    def halo_rows(first):
        o = closure_of(jnp.concatenate([s0[first + i, 0:FEATS, 0:COLS] for i in range(4)], axis=1))
        for i in range(4):
            outs[first + i, :, 0:COLS] = o[:, i * COLS : (i + 1) * COLS]

    @pl.when(has_south == 1)
    def _():
        halo_rows(PAD - 8)
        halo_rows(PAD - 4)

    @pl.when(has_north == 1)
    def _():
        halo_rows(PAD + ROWS)
        halo_rows(PAD + ROWS + 4)

    groups = 3 if sides == ["swap"] else 4
    first = PAD - 8 * has_south
    o = closure_of(jnp.concatenate([wide_pack(s0, first + 8 * g) for g in range(groups)], axis=1))
    for g in range(groups):
        wide_unpack(outs, first + 8 * g, o[:, g * COLS : (g + 1) * COLS])

    lax.fori_loop(lo(10), hi(10), section_1(k, cs, fs, masks, s0, s1), 0)
    lax.fori_loop(lo(9), hi(9), section_2(k, cs, fs, masks, s0, s1, s2), 0)


def late_kernel(
    scal, cs, fs, sums, own, own_h1, own_h2, s0, s1, s2, masks, fluxes, cot, outs_in,
    w1, b1, w2, b2, w3, b3, v1, v2, v3, final, grads, s4, abuf, from_closure, *scratch
):
    s3, t1, t2, outs, gz, bbuf, hold, acc = scratch
    k = Row(WIDE)
    has_south, has_north = scal[2], scal[3]
    lo = lambda h: PAD - h * has_south
    hi = lambda h: PAD + ROWS + h * has_north

    for ref in (s3, t1, t2, abuf, bbuf):
        for row in (PAD - 1, PAD + ROWS):
            ref[row] = jnp.zeros(ref.shape[1:], F32)
    k1, k2, k3 = stacked_weights(w1), stacked_weights(w2), stacked_weights(w3)
    q1, q2, q3 = stacked_weights(v1), stacked_weights(v2), stacked_weights(v3)

    mean = sums[0:1, 0:1] / sums[1:2, 0:1]

    def section_3(src, mid, net, r):
        d = tendency_row(k, mid, r, cs[r], fs[r])
        new = []
        for t in range(5):
            m = mask_tile(masks, r, t)
            o = tile(net, r, t)
            if t == 1:
                force = 2.0 * (mean - fluxes[r, 2:3, :])
                o = o + jnp.where(k.sub == 0, force, 0.0)
            new.append(
                (1.0 / 3.0) * tile(src, r, t) + (2.0 / 3.0) * tile(mid, r, t)
                + m * ((1.0 / 6.0) * d[t] + 0.25 * o)
            )
        return new

    def step_1_end(r, _):
        put_state(k, s3, r, section_3(s0, s2, r))
        return 0

    def step_1_end(r, _):
        put_state(k, s3, r, section_3(s0, s2, outs_in, r))
        return 0

    lax.fori_loop(lo(8), hi(8), step_1_end, 0)

    acc[...] = jnp.zeros(acc.shape, F32)

    def closure_adjoint(z, h1, h1s, h2, go, with_weights):
        gos = split(to_48(go))
        g2 = product(q3, *gos) * (1.0 - h2 * h2)
        g2s = split(g2)
        g1 = product(q2, *g2s) * (1.0 - h1 * h1)
        g1s = split(g1)
        if with_weights:
            add_weight_terms(acc, z, h1s, split(h2), g1s, g2s, gos)
        return product(q1, *g1s)[0:FEATS]

    def both_ways(columns, go, with_weights):
        z = split(to_48(columns))
        h1, h1s, h2 = hidden_layers(z, k1, b1[...], k2, b2[...])
        o = product(k3, *split(h2))[0:FEATS] + b3[...] if with_weights else None
        return o, closure_adjoint(z, h1, h1s, h2, go, with_weights)

    def masked_core(ref, r):
        m0, m4 = masks[r, 0:8, 0:COLS], masks[r, 8:16, 0:COLS]
        parts = [
            0.25 * (m4 if t == 4 else m0) * ref[r, 8 * t : 8 * t + 8, 0:COLS] for t in range(5)
        ]
        return jnp.concatenate(parts, axis=0)

    def mask_cot(r, _):
        for t in range(5):
            bbuf[r, 8 * t : 8 * t + 8, :] = 0.25 * mask_tile(masks, r, t) * tile(cot, r, t)
            abuf[r, 8 * t : 8 * t + 8, :] = (1.0 / 6.0) * mask_tile(masks, r, t) * tile(cot, r, t)
        return 0

    lax.fori_loop(lo(6), hi(6), mask_cot, 0)

    def core_rows(first, with_weights):
        z = jnp.concatenate([s3[first + i, 0:FEATS, 0:COLS] for i in range(4)], axis=1)
        go = jnp.concatenate([bbuf[first + i, 0:FEATS, 0:COLS] for i in range(4)], axis=1)
        o, back = both_ways(z, go, with_weights)
        for i in range(4):
            at = slice(i * COLS, (i + 1) * COLS)
            if with_weights:
                outs[first + i, :, 0:COLS] = o[:, at]
            gz[first + i, :, 0:COLS] = back[:, at]

    lax.fori_loop(0, ROWS // 4, lambda i, _: (core_rows(PAD + 4 * i, True), 0)[1], 0)

    @pl.when(has_south == 1)
    def _():
        core_rows(PAD - 4, False)

    @pl.when(has_north == 1)
    def _():
        core_rows(PAD + ROWS, False)

    first = lo(4)
    z = jnp.concatenate([wide_pack(s3, first + 8 * g) for g in range(3)], axis=1)
    go = jnp.concatenate([wide_pack(bbuf, first + 8 * g) for g in range(3)], axis=1)
    _, back = both_ways(z, go, False)
    for g in range(3):
        wide_unpack(gz, first + 8 * g, back[:, g * COLS : (g + 1) * COLS])

    lax.fori_loop(lo(7), hi(7), section_1(k, cs, fs, masks, s3, t1), 0)
    lax.fori_loop(lo(6), hi(6), section_2(k, cs, fs, masks, s3, t1, t2), 0)

    def last(r, _):
        new = section_3(s3, t2, outs, r)
        put_result(final, r - PAD, [x[:, 0:COLS] for x in new])
        return 0

    lax.fori_loop(PAD, PAD + ROWS, last, 0)

    def store(r, tiles):
        for t in range(5):
            s4[r, 8 * t : 8 * t + 8, :] = tiles[t] + tile(gz, r, t)

    adjoint_third(k, cs, fs, (lo(5), hi(5)), t2, masks, abuf, cot, hold, bbuf)
    adjoint_second(k, cs, fs, (lo(4), hi(4)), t1, masks, bbuf, cot, hold, hold, abuf)
    adjoint_first(k, cs, fs, (lo(3), hi(3)), s3, abuf, hold, store)

    def first_step(i, _):
        r = 4 * i
        side = lambda read: jnp.concatenate([read(r + j) for j in range(4)], axis=1)
        z = split(to_48(side(lambda j: own[j, 0:FEATS, :])))
        h1 = side(lambda j: own_h1[j])
        h2 = side(lambda j: own_h2[j])
        go = side(lambda j: masked_core(s4, PAD + j))
        back = closure_adjoint(z, h1, split(h1), h2, go, True)
        for j in range(4):
            from_closure[r + j] = back[:, j * COLS : (j + 1) * COLS]
        return 0

    lax.fori_loop(0, ROWS // 4, first_step, 0)
    for row in (PAD - 1, PAD + ROWS):
        abuf[row] = jnp.zeros((FEATS, WIDE), F32)

    def mask_top(r, _):
        for t in range(5):
            abuf[r, 8 * t : 8 * t + 8, :] = (1.0 / 6.0) * mask_tile(masks, r, t) * tile(s4, r, t)
        return 0

    lax.fori_loop(lo(3), hi(3), mask_top, 0)
    grads[...] = jnp.zeros(grads.shape, F32)
    grads[0:40, 0:HID] = acc[0:40, 0:HID]
    grads[0:40, HID : 2 * HID] = acc[112:152, 0:HID]
    grads[40:72, 0:HID] = acc[48:80, 0:HID]
    grads[40:72, HID : 2 * HID] = acc[80:112, 0:HID]
    grads[72:73, 0:HID] = acc[160:161, 0:HID]
    grads[72:73, HID : 2 * HID] = acc[176:177, 0:HID]
    grads[73:74, 0:HID] = acc[192:193, 0:HID]


def put_result(ref, row, tiles):
    for t in range(4):
        ref[pl.ds(t * 10 * ROWS + row, 8, stride=ROWS), :] = tiles[t]
    ref[pl.ds(8 * ROWS + row, 4, stride=10 * ROWS), :] = tiles[4][0:4, :]
    ref[pl.ds(9 * ROWS + row, 4, stride=10 * ROWS), :] = tiles[4][4:8, :]


def limits(scal, reach):
    return PAD - reach * scal[2], PAD + ROWS + reach * scal[3]


def back_third_kernel(scal, cs, fs, state, masks, abuf, top, hold, bbuf):
    for row in (PAD - 1, PAD + ROWS):
        bbuf[row] = jnp.zeros((FEATS, WIDE), F32)
    adjoint_third(Row(WIDE), cs, fs, limits(scal, 2), state, masks, abuf, top, hold, bbuf)


def back_second_kernel(scal, cs, fs, gate, state, masks, bbuf, top, hold, left, abuf):
    for row in (PAD - 1, PAD + ROWS):
        abuf[row] = jnp.zeros((FEATS, WIDE), F32)
    adjoint_second(Row(WIDE), cs, fs, limits(scal, 1), state, masks, bbuf, top, hold, left, abuf)


def back_first_kernel(scal, cs, fs, gate, state, masks, abuf, left, from_closure, grad):
    def store(r, tiles):
        done = []
        for t in range(5):
            m = masks[r, 8:16, 0:COLS] if t == 4 else masks[r, 0:8, 0:COLS]
            done.append(m * (tiles[t][:, 0:COLS] + from_closure[r - PAD, 8 * t : 8 * t + 8, :]))
        put_result(grad, r - PAD, done)

    adjoint_first(Row(WIDE), cs, fs, (PAD, PAD + ROWS), state, abuf, left, store)


def unpack_kernel(scale, packed, win, bin_, wmid, bmid, wout, bout):
    for ref, lanes in ((win, slice(0, HID)), (wout, slice(HID, 2 * HID))):
        for t in range(4):
            ref[10 * t : 10 * t + 8, :] = packed[8 * t : 8 * t + 8, lanes] * scale
            ref[10 * t + 8 : 10 * t + 9, :] = packed[32 + t : 33 + t, lanes] * scale
            ref[10 * t + 9 : 10 * t + 10, :] = packed[36 + t : 37 + t, lanes] * scale
    wmid[0:32, :] = packed[40:72, 0:HID] * scale
    wmid[32:64, :] = packed[40:72, HID : 2 * HID] * scale
    bin_[...] = packed[72:73, 0:HID] * scale
    bmid[...] = packed[72:73, HID : 2 * HID] * scale
    for t in range(4):
        bout[:, 10 * t : 10 * t + 8] = packed[73:74, 8 * t : 8 * t + 8] * scale
        bout[:, 10 * t + 8 : 10 * t + 9] = packed[73:74, 32 + t : 33 + t] * scale
        bout[:, 10 * t + 9 : 10 * t + 10] = packed[73:74, 36 + t : 37 + t] * scale


def by_tile(weights):
    heads = [weights[10 * t : 10 * t + 8] for t in range(4)]
    tails = [weights[10 * t + level : 10 * t + level + 1] for level in (8, 9) for t in range(4)]
    return jnp.concatenate(heads + tails, axis=0)


def tree_round(x, axis, count, stride):
    group = 4 if (count // stride) % 4 == 0 else 2
    got = [
        lax.ppermute(x, axis, [(i, i ^ (j * stride)) for i in range(count)]) for j in range(1, group)
    ]
    x = x + got[0] if group == 2 else (x + got[0]) + (got[1] + got[2])
    return x, stride * group


def tree_rounds(x, axes):
    for axis, count in axes:
        if count & (count - 1):
            x = lax.psum(x, axis)
            yield x
            continue
        stride = 1
        while stride < count:
            x, stride = tree_round(x, axis, count, stride)
            yield x


def three(w):
    return jnp.concatenate([w, w, w], axis=1)


def pad_cols(w):
    return jnp.pad(w, ((0, 0), (0, 8)))


def latitude_terms(row_index, row_count):
    latitude = LAT_LIMIT * (2.0 * (jnp.clip(row_index, 0.0, row_count - 1.0) + 0.5) / row_count - 1.0)
    return 1.0 / jnp.cos(latitude), CORIOLIS * jnp.sin(latitude)


def on_device(
    initial_state, land_mask, surface_flux, weight_in, bias_in, weight_mid, bias_mid, weight_out, bias_out, cotangent
):
    lat_n, lon_n = lax.axis_size("lat"), lax.axis_size("lon")
    lat_i = lax.axis_index("lat")
    lat_total, lon_total = ROWS * lat_n, COLS * lon_n
    sides = ["swap"] if lat_n == 2 else ["north", "south"]
    is_low = (lat_i == 0).astype(jnp.int32)
    has_south = (lat_i > 0).astype(jnp.int32)
    has_north = (lat_i < lat_n - 1).astype(jnp.int32)
    scal = jnp.stack(
        [
            is_low * (ROWS - REACH),
            is_low * (ROWS - CREACH),
            has_south,
            has_north,
            jnp.where(is_low == 1, PAD + ROWS, 1),
            jnp.where(is_low == 1, PAD + ROWS, PAD - CREACH),
            jnp.where(is_low == 1, 0, ROWS - CREACH),
        ]
    ).astype(jnp.int32)
    rows = (lat_i * ROWS - PAD + jnp.arange(EXT, dtype=jnp.int32)).astype(F32)
    cs, fs = latitude_terms(rows, lat_total)

    packed = pl.pallas_call(
        lambda *refs: pack_kernel(sides, *refs),
        out_shape=[
            sds(ROWS, PACK, COLS), sds(ROWS, FEATS, COLS), sds(8, COLS),
            sds(2 * PACK + 40, COLS), sds(2 * PACK + 40, COLS),
        ]
        + [sds(REACH, PACK, COLS), sds(CREACH, FEATS, COLS), sds(PACK + 40, COLS), sds(PACK + 40, COLS)] * len(sides),
        in_specs=[SMEM] + [pl.BlockSpec(memory_space=pl.ANY)] * 4,
        out_specs=[VMEM] * (5 + 4 * len(sides)),
        scratch_shapes=[
            pltpu.VMEM((40 * ROWS, COLS), F32), pltpu.VMEM((10 * ROWS, COLS), jnp.int32),
            pltpu.VMEM((ROWS, COLS), F32), pltpu.VMEM((40 * ROWS, COLS), F32), pltpu.SemaphoreType.DMA((4,)),
        ],
        compiler_params=params(48),
        name="pack_halos",
    )(
        scal,
        initial_state.reshape(40 * ROWS, COLS),
        land_mask.reshape(10 * ROWS, COLS),
        surface_flux,
        cotangent.reshape(40 * ROWS, COLS),
    )
    own, cown, sums, east_pay, west_pay = packed[:5]

    def lat_pairs(side):
        if side == "swap":
            return [(0, 1), (1, 0)]
        if side == "north":
            return [(i, i + 1) for i in range(lat_n - 1)]
        return [(i + 1, i) for i in range(lat_n - 1)]

    def diagonal(side, step):
        return [
            (i * lat_n + a, ((i + step) % lon_n) * lat_n + b)
            for i in range(lon_n)
            for a, b in lat_pairs(side)
        ]

    east_ring = [(i, (i + 1) % lon_n) for i in range(lon_n)]
    west_ring = [((i + 1) % lon_n, i) for i in range(lon_n)]
    received = []
    for i, side in enumerate(sides):
        lat_x, lat_c, diag_e, diag_w = packed[5 + 4 * i : 9 + 4 * i]
        received.append(
            [
                lax.ppermute(lat_x, "lat", lat_pairs(side)),
                lax.ppermute(lat_c, "lat", lat_pairs(side)),
                lax.ppermute(diag_e, ("lon", "lat"), diagonal(side, 1)),
                lax.ppermute(diag_w, ("lon", "lat"), diagonal(side, -1)),
            ]
        )
    from_west = lax.ppermute(east_pay, "lon", east_ring)
    from_east = lax.ppermute(west_pay, "lon", west_ring)
    axes = (("lon", lon_n), ("lat", lat_n))
    mean_rounds = list(tree_rounds(sums, axes))

    w_in, w_out_t = by_tile(weight_in), by_tile(weight_out.T)
    col = lambda b: b.reshape(-1, 1)
    forward = [
        three(pad_cols(w_in.T)), col(bias_in), three(weight_mid.T), col(bias_mid), three(w_out_t), by_tile(col(bias_out)),
    ]
    forward[4] = jnp.pad(forward[4], ((0, 8), (0, 0)))
    backward = [jnp.pad(three(w_in), ((0, 8), (0, 0))), three(weight_mid), three(pad_cols(w_out_t.T))]

    own_m, own_h1, own_h2 = pl.pallas_call(
        own_closure_kernel,
        out_shape=[sds(ROWS, FEATS, COLS), sds(ROWS, HID, COLS), sds(ROWS, HID, COLS)],
        in_specs=[VMEM] * 7,
        out_specs=[VMEM] * 3,
        compiler_params=params(12),
        cost_estimate=pl.CostEstimate(flops=10**9, bytes_accessed=2 * 10**6, transcendentals=0),
        name="own_closure",
    )(own, *forward)

    geometry = (scal, cs, fs)
    state = sds(EXT, 72, WIDE)
    plain = sds(EXT, FEATS, WIDE)
    marks = sds(EXT, 16, WIDE)
    vmem = lambda shape: pltpu.VMEM(shape.shape, F32)

    def call(kernel, name, out_shape, scratch, args, flops, limit):
        single = not isinstance(out_shape, list)
        return pl.pallas_call(
            kernel,
            out_shape=out_shape,
            in_specs=[SMEM] * 3 + [VMEM] * len(args),
            out_specs=VMEM if single else [VMEM] * len(out_shape),
            scratch_shapes=scratch,
            compiler_params=params(limit),
            cost_estimate=pl.CostEstimate(flops=flops, bytes_accessed=10**7, transcendentals=0),
            name=name,
        )(*geometry, *args)

    s0, s1, s2, masks, fluxes, cot, net = call(
        lambda *refs: early_kernel(sides, *refs), "first_sections",
        [state, state, state, marks, sds(EXT, 8, WIDE), plain, plain], [],
        [mean_rounds[-2], own, cown, own_m, from_west, from_east]
        + [item for side in received for item in side] + forward,
        2 * 10**9, 8,
    )
    final, grads, top, abuf, from_closure = call(
        late_kernel, "steps_and_adjoint",
        [sds(40 * ROWS, COLS), sds(80, COLS), plain, plain, sds(ROWS, FEATS, COLS)],
        [vmem(state)] * 3 + [vmem(plain)] * 4 + [pltpu.VMEM((208, HID), F32)],
        [mean_rounds[-1], own, own_h1, own_h2, s0, s1, s2, masks, fluxes, cot, net] + forward + backward,
        4 * 10**9, 24,
    )
    rounds = list(tree_rounds(grads, axes))
    hold, bbuf = call(
        back_third_kernel, "adjoint_third_section", [plain, plain], [], [s2, masks, abuf, top], 10**9, 8
    )
    left, abuf = call(
        back_second_kernel, "adjoint_second_section", [plain, plain], [],
        [rounds[0], s1, masks, bbuf, top, hold], 10**9, 8,
    )
    state_grad = call(
        back_first_kernel, "adjoint_first_section", sds(40 * ROWS, COLS), [],
        [rounds[1], s0, masks, abuf, left, from_closure], 10**9, 8,
    )

    scale = 1.0 / math.sqrt(lat_total * lon_total)
    g_in, g_bin, g_mid, g_bmid, g_out, g_bout = pl.pallas_call(
        lambda *refs: unpack_kernel(scale, *refs),
        out_shape=[sds(40, HID), sds(1, HID), sds(HID, HID), sds(1, HID), sds(40, HID), sds(1, 40)],
        in_specs=[VMEM],
        out_specs=[VMEM] * 6,
        compiler_params=params(8),
        name="unpack_weight_grads",
    )(rounds[-1])
    shape = initial_state.shape
    return (
        final.reshape(shape),
        state_grad.reshape(shape),
        g_in,
        g_bin.reshape(-1),
        g_mid,
        g_bmid.reshape(-1),
        g_out.T,
        g_bout.reshape(-1),
    )


def solution(mesh):
    split_state = P(None, None, "lat", "lon")
    return jax.shard_map(
        on_device,
        mesh=mesh,
        in_specs=(split_state, P(None, "lat", "lon"), P("lat", "lon"), P(), P(), P(), P(), P(), P(), split_state),
        out_specs=(split_state, split_state, P(), P(), P(), P(), P(), P()),
        check_vma=False,
    )
```

```python
import math

import jax
import jax.numpy as jnp
from jax import lax
from jax.experimental import pallas as pl
from jax.experimental.pallas import tpu as pltpu
from jax.sharding import PartitionSpec as P

LAT_LIMIT = 1.2
CORIOLIS = 1.0
VISCOSITY = 0.15
DIFFUSIVITY = 0.1

ROWS = 16
COLS = 128
REACH = 11
CREACH = 6
PAD = 16
EXT = 48
TURN = 4
WIDE = 2 * COLS
FEATS = 40
HID = 64
PACK = 56
SLOT = 16
F32 = jnp.float32
BF16 = jnp.bfloat16
VMEM = pl.BlockSpec(memory_space=pltpu.VMEM)
SMEM = pl.BlockSpec(memory_space=pltpu.SMEM)


def params(megabytes):
    return pltpu.CompilerParams(vmem_limit_bytes=megabytes * 1024 * 1024)


def sds(*shape):
    return jax.ShapeDtypeStruct(shape, F32)


def sub_index(width):
    return lax.broadcasted_iota(jnp.int32, (8, width), 0)


def tile(ref, row, number):
    return ref[row, 8 * number : 8 * number + 8, :]


def slot_pack(pieces, shift_of, width):
    lane = lax.broadcasted_iota(jnp.int32, (8, COLS), 1)
    packed = None
    for slot, piece in enumerate(pieces):
        turned = pltpu.roll(piece, shift_of(slot) % COLS, 1)
        if packed is None:
            packed = turned
        else:
            packed = jnp.where((lane >= slot * width) & (lane < (slot + 1) * width), turned, packed)
    return packed


def pack_kernel(sides, scal, x_hbm, mask_hbm, flux_hbm, cot_hbm, *outs):
    x, mask, flux, cot, sems = outs[-5:]
    own, cown, sums, east, west = outs[:5]
    per_side = [outs[5 + 4 * i : 9 + 4 * i] for i in range(len(sides))]
    pairs = ((mask_hbm, mask), (x_hbm, x), (flux_hbm, flux), (cot_hbm, cot))
    copies = [pltpu.make_async_copy(a, b, sems.at[i]) for i, (a, b) in enumerate(pairs)]
    for copy in copies:
        copy.start()
    for copy in copies:
        copy.wait()
    for r in range(ROWS):
        first = mask[pl.ds(r, 8, stride=ROWS), :].astype(F32)
        m8 = mask[8 * ROWS + r : 8 * ROWS + r + 1, :].astype(F32)
        m9 = mask[9 * ROWS + r : 9 * ROWS + r + 1, :].astype(F32)
        for t in range(4):
            own[r, 8 * t : 8 * t + 8, :] = x[pl.ds(t * 10 * ROWS + r, 8, stride=ROWS), :] * first
            cown[r, 8 * t : 8 * t + 8, :] = cot[pl.ds(t * 10 * ROWS + r, 8, stride=ROWS), :]
        for level, m in ((8, m8), (9, m9)):
            at = 32 + 4 * (level - 8)
            own[r, at : at + 4, :] = x[pl.ds(level * ROWS + r, 4, stride=10 * ROWS), :] * m
            cown[r, at : at + 4, :] = cot[pl.ds(level * ROWS + r, 4, stride=10 * ROWS), :]
        own[r, 40:48, :] = first
        own[r, 48:49, :] = m8
        own[r, 49:50, :] = m9
        own[r, 50:51, :] = flux[r : r + 1, :]
        own[r, 51:56, :] = jnp.zeros((5, COLS), F32)
    top = mask[0:ROWS, :].astype(F32)
    total = jnp.sum(jnp.sum(top * flux[...], axis=1, keepdims=True), axis=0, keepdims=True)
    count = jnp.sum(jnp.sum(top, axis=1, keepdims=True), axis=0, keepdims=True)
    sums[...] = jnp.where(sub_index(COLS) == 0, total, jnp.where(sub_index(COLS) == 1, count, 0.0))
    for half in range(2):
        for t in range(7):
            rows = [own[8 * half + s, 8 * t : 8 * t + 8, :] for s in range(8)]
            at = half * PACK + 8 * t
            east[at : at + 8, :] = slot_pack(rows, lambda s: SLOT * (s + 1), SLOT)
            west[at : at + 8, :] = slot_pack(rows, lambda s: SLOT * s, SLOT)
    for t in range(5):
        rows = [cown[s, 8 * t : 8 * t + 8, :] for s in range(ROWS)]
        at = 2 * PACK + 8 * t
        east[at : at + 8, :] = slot_pack(rows, lambda s: 8 * (s + 1), 8)
        west[at : at + 8, :] = slot_pack(rows, lambda s: 8 * s, 8)
    for side, (lat_x, lat_c, diag_e, diag_w) in zip(sides, per_side):
        start = {"swap": scal[0], "north": ROWS - REACH, "south": 0}[side]
        cstart = {"swap": scal[1], "north": ROWS - CREACH, "south": 0}[side]
        for n in range(REACH):
            lat_x[n] = own[start + n]
        for n in range(CREACH):
            lat_c[n] = cown[cstart + n]
        for t in range(7):
            rows = [own[start + n, 8 * t : 8 * t + 8, :] for n in range(REACH)]
            diag_e[8 * t : 8 * t + 8, :] = slot_pack(rows, lambda s: REACH * (s + 1), REACH)
            diag_w[8 * t : 8 * t + 8, :] = slot_pack(rows, lambda s: REACH * s, REACH)
        diag_e[PACK : PACK + 40, :] = east[2 * PACK : 2 * PACK + 40, :]
        diag_w[PACK : PACK + 40, :] = west[2 * PACK : 2 * PACK + 40, :]


def split(values):
    high = values.astype(BF16)
    return high, (values - high.astype(F32)).astype(BF16)


def stacked_weights(ref):
    values = ref[...]
    third = values.shape[1] // 3
    high, low = split(values)
    lane = lax.broadcasted_iota(jnp.int32, values.shape, 1)
    return jnp.where(lane < 2 * third, high.astype(F32), low.astype(F32)).astype(BF16)


def product(weights, high, low):
    return jnp.dot(weights, jnp.concatenate([high, low, high], axis=0), preferred_element_type=F32)


def across(a, b):
    dims = (((1,), (1,)), ((), ()))
    dot = lambda p, q: lax.dot_general(p, q, dims, preferred_element_type=F32)
    return dot(a[0], b[0]) + dot(a[0], b[1]) + dot(a[1], b[0])


def to_48(columns):
    return jnp.concatenate([columns, jnp.zeros((8, columns.shape[1]), F32)], axis=0)


def hidden_layers(z, w1, b1, w2, b2):
    h1 = jnp.tanh(product(w1, *z) + b1)
    h1s = split(h1)
    h2 = jnp.tanh(product(w2, *h1s) + b2)
    return h1, h1s, h2


def add_weight_terms(acc, z, h1s, h2s, g1s, g2s, gos):
    ones = jnp.ones((16, z[0].shape[1]), BF16)
    acc[0:48, 0:HID] += across(z, g1s)
    acc[48:112, 0:HID] += across(h1s, g2s)
    acc[112:160, 0:HID] += across(gos, h2s)
    acc[160:176, 0:HID] += ones_rows(ones, g1s)
    acc[176:192, 0:HID] += ones_rows(ones, g2s)
    acc[192:208, 0:48] += ones_rows(ones, gos)


def ones_rows(ones, g):
    dims = (((1,), (1,)), ((), ()))
    dot = lambda q: lax.dot_general(ones, q, dims, preferred_element_type=F32)
    return dot(g[0]) + dot(g[1])


def own_closure_kernel(own, w1, b1, w2, b2, w3, b3, out, h1_out, h2_out):
    k1, k2, k3 = stacked_weights(w1), stacked_weights(w2), stacked_weights(w3)

    for r in range(0, ROWS, 8):
        z = split(to_48(jnp.concatenate([own[r + n, 0:FEATS, :] for n in range(8)], axis=1)))
        h1, h1s, h2 = hidden_layers(z, k1, b1[...], k2, b2[...])
        o = product(k3, *split(h2))[0:FEATS] + b3[...]
        for n in range(8):
            at = slice(n * COLS, (n + 1) * COLS)
            out[r + n] = o[:, at]
            h1_out[r + n] = h1[:, at]
            h2_out[r + n] = h2[:, at]


class Row:
    def __init__(self, width):
        sub = sub_index(width)
        group = sub % 4
        self.sub = sub
        self.is_t = group == 0
        self.is_s = group == 1
        self.is_u = group == 2
        self.is_v = group == 3
        self.low = sub >= 4
        self.k4 = jnp.where(group < 2, DIFFUSIVITY, VISCOSITY).astype(F32)


def derived(k, temp, salt, mixed):
    zero = jnp.zeros_like(temp)
    press = 0.4 * salt - 0.1 * temp
    for by in (1, 2, 4):
        press = press + jnp.where(k.sub >= by, pltpu.roll(press, by, 0), zero)
    deep = jnp.where(k.is_t, 0.4 * pltpu.roll(mixed, 7, 0) - 0.1 * mixed, zero)
    deep = deep + jnp.where(k.low, pltpu.roll(deep, 4, 0), zero)
    deep = deep + pltpu.roll(deep, 1, 0)
    deep = deep + pltpu.roll(deep, 2, 0) + press[7:8, :]
    u4, v4 = deep_velocity(k, mixed)
    return press, deep, u4, v4


def deep_velocity(k, mixed):
    zero = jnp.zeros_like(mixed)
    u4 = jnp.where(k.is_u, mixed, zero)
    u4 = u4 + pltpu.roll(u4, 1, 0)
    u4 = u4 + pltpu.roll(u4, 6, 0)
    v4 = jnp.where(k.is_v, mixed, zero)
    v4 = v4 + pltpu.roll(v4, 7, 0)
    v4 = v4 + pltpu.roll(v4, 6, 0)
    return u4, v4


def put_state(k, ref, row, tiles):
    for t in range(5):
        ref[row, 8 * t : 8 * t + 8, :] = tiles[t]
    for t, values in enumerate(derived(k, tiles[0], tiles[1], tiles[4])):
        ref[row, 40 + 8 * t : 48 + 8 * t, :] = values


def east_of(q):
    return pltpu.roll(q, q.shape[1] - 1, 1)


def west_of(q):
    return pltpu.roll(q, 1, 1)


def tendency_row(k, ref, row, c, f):
    half = 0.5 * c
    c2 = c * c
    u, v = tile(ref, row, 2), tile(ref, row, 3)
    u4, v4 = tile(ref, row, 7), tile(ref, row, 8)
    uh, vh = u * half, v * 0.5
    u4h, v4h = u4 * half, v4 * 0.5
    change = []
    for t in range(5):
        q = tile(ref, row, t)
        e, w = east_of(q), west_of(q)
        n, s = tile(ref, row + 1, t), tile(ref, row - 1, t)
        lap = c2 * (e + w) + (n + s) - (2.0 * c2 + 2.0) * q
        gain = k.k4 if t == 4 else (DIFFUSIVITY if t < 2 else VISCOSITY)
        au, av = (u4h, v4h) if t == 4 else (uh, vh)
        change.append(gain * lap - (au * (e - w) + av * (n - s)))
    p = tile(ref, row, 5)
    change[2] = change[2] + (f * v - half * (east_of(p) - west_of(p)))
    change[3] = change[3] - (f * u + 0.5 * (tile(ref, row + 1, 5) - tile(ref, row - 1, 5)))
    p4 = tile(ref, row, 6)
    zero = jnp.zeros_like(p4)
    fx = f * v4 - half * (east_of(p4) - west_of(p4))
    fy = f * u4 + 0.5 * (tile(ref, row + 1, 6) - tile(ref, row - 1, 6))
    change[4] = change[4] + jnp.where(k.is_u, fx, jnp.where(k.is_v, -fy, zero))
    return change


def adjoint_row(k, ref, aref, row, c, f):
    half = 0.5 * c
    c2 = c * c
    u4 = tile(ref, row, 7)
    qe = [east_of(tile(ref, row, t)) for t in range(5)]
    qw = [west_of(tile(ref, row, t)) for t in range(5)]
    u4e, u4w = east_of(u4), west_of(u4)
    out = []
    to_u = to_v = None
    for t in range(5):
        a = tile(aref, row, t)
        ae, aw = east_of(a), west_of(a)
        an, as_ = tile(aref, row + 1, t), tile(aref, row - 1, t)
        gain = k.k4 if t == 4 else (DIFFUSIVITY if t < 2 else VISCOSITY)
        ue, uw = (u4e, u4w) if t == 4 else (qe[2], qw[2])
        which = 8 if t == 4 else 3
        vn, vs = tile(ref, row + 1, which), tile(ref, row - 1, which)
        lap = c2 * (ae + aw) + (an + as_) - (2.0 * c2 + 2.0) * a
        out.append(gain * lap + half * (ue * ae - uw * aw) + 0.5 * (vn * an - vs * as_))
        px = a * (qe[t] - qw[t])
        py = a * (tile(ref, row + 1, t) - tile(ref, row - 1, t))
        if t < 4:
            to_u = px if to_u is None else to_u + px
            to_v = py if to_v is None else to_v + py
        if t == 2:
            a2, bx = a, half * (ae - aw)
        if t == 3:
            a3, by = a, 0.5 * (an - as_)
        if t == 4:
            a4 = a
            deep_bx, deep_by = half * (ae - aw), 0.5 * (an - as_)
            px4, py4 = px * half, py * 0.5
    out[2] = out[2] - half * to_u - f * a3
    out[3] = out[3] - 0.5 * to_v + f * a2
    zero = jnp.zeros_like(a4)
    sx = px4 + pltpu.roll(px4, 7, 0)
    sx = sx + pltpu.roll(sx, 2, 0)
    sy = py4 + pltpu.roll(py4, 1, 0)
    sy = sy + pltpu.roll(sy, 2, 0)
    at_u = -sx - f * pltpu.roll(a4, 7, 0)
    at_v = f * pltpu.roll(a4, 1, 0) - sy
    deep = jnp.where(k.is_t, pltpu.roll(deep_bx, 6, 0) + pltpu.roll(deep_by, 5, 0), zero)
    deep = deep + jnp.where(k.low, zero, pltpu.roll(deep, 4, 0))
    press = bx + by
    for shift in (1, 2, 4):
        press = press + jnp.where(k.sub < 8 - shift, pltpu.roll(press, 8 - shift, 0), zero)
    press = press + deep[0:1, :]
    out[0] = out[0] - 0.1 * press
    out[1] = out[1] + 0.4 * press
    out[4] = out[4] + jnp.where(
        k.is_t,
        -0.1 * deep,
        jnp.where(k.is_s, 0.4 * pltpu.roll(deep, 1, 0), jnp.where(k.is_u, at_u, at_v)),
    )
    return out


def for_rows(scal, reach, body):
    low, high = PAD - reach * scal[2], PAD + ROWS + reach * scal[3]
    turns = lax.div(high - low + TURN - 1, TURN)
    first = jnp.where(scal[3] == 1, low, high - TURN * turns)

    def turn(i, _):
        for j in range(TURN):
            body(first + TURN * i + j)
        return 0

    lax.fori_loop(0, turns, turn, 0)


def mask_tile(ref, row, t):
    return tile(ref, row, 1 if t == 4 else 0)


def adjoint_third(k, scal, cs, fs, reach, state, masks, abuf, top, hold, bbuf):
    def body(r):
        d = adjoint_row(k, state, abuf, r, cs[r], fs[r])
        for t in range(5):
            ts = (2.0 / 3.0) * tile(top, r, t) + d[t]
            hold[r, 8 * t : 8 * t + 8, :] = ts
            bbuf[r, 8 * t : 8 * t + 8, :] = 0.0625 * mask_tile(masks, r, t) * ts

    for_rows(scal, reach, body)


def adjoint_second(k, scal, cs, fs, reach, state, masks, bbuf, top, hold, left, abuf):
    def body(r):
        d = adjoint_row(k, state, bbuf, r, cs[r], fs[r])
        for t in range(5):
            ts = tile(hold, r, t)
            tf = 0.25 * ts + d[t]
            left[r, 8 * t : 8 * t + 8, :] = (1.0 / 3.0) * tile(top, r, t) + 0.75 * ts + tf
            abuf[r, 8 * t : 8 * t + 8, :] = 0.25 * mask_tile(masks, r, t) * tf

    for_rows(scal, reach, body)


def adjoint_first(k, scal, cs, fs, reach, state, abuf, left, store):
    def body(r):
        d = adjoint_row(k, state, abuf, r, cs[r], fs[r])
        store(r, [tile(left, r, t) + d[t] for t in range(5)])

    for_rows(scal, reach, body)


def edges(reach):
    lane = lax.broadcasted_iota(jnp.int32, (8, COLS), 1)
    return lane < reach, lane >= COLS - reach


def wide_pack(ref, base):
    parts = []
    for t in range(5):
        rows = [ref[base + s, 8 * t : 8 * t + 8, COLS:WIDE] for s in range(8)]
        parts.append(slot_pack(rows, lambda s: 8 + SLOT * s, SLOT))
    return jnp.concatenate(parts, axis=0)

def wide_unpack(ref, base, values):
    for s in range(8):
        ref[base + s, 0:FEATS, COLS:WIDE] = pltpu.roll(values, -(8 + SLOT * s) % COLS, 1)


def section_1(k, cs, fs, masks, src, dst):
    def body(r):
        d = tendency_row(k, src, r, cs[r], fs[r])
        put_state(
            k, dst, r,
            [tile(src, r, t) + 0.25 * mask_tile(masks, r, t) * d[t] for t in range(5)],
        )
    return body

def section_2(k, cs, fs, masks, src, mid, dst):
    def body(r):
        d = tendency_row(k, mid, r, cs[r], fs[r])
        put_state(
            k, dst, r,
            [
                0.75 * tile(src, r, t) + 0.25 * tile(mid, r, t)
                + 0.0625 * mask_tile(masks, r, t) * d[t]
                for t in range(5)
            ],
        )
    return body


def early_kernel(sides, scal, cs, fs, gate, own, cown, own_m, east, west, *rest):
    n = len(sides)
    side_refs = [rest[4 * i : 4 * i + 4] for i in range(n)]
    (w1, b1, w2, b2, w3, b3), rest = rest[4 * n : 4 * n + 6], rest[4 * n + 6 :]
    s0, s1, s2, masks, fluxes, cot, outs = rest
    k = Row(WIDE)
    has_south, has_north = scal[2], scal[3]
    lo = lambda h: PAD - h * has_south
    hi = lambda h: PAD + ROWS + h * has_north

    for ref in (s0, s1, s2):
        for row in (PAD - 1, PAD + ROWS):
            ref[row] = jnp.zeros(ref.shape[1:], F32)

    near_e, near_w = edges(REACH)
    cnear_e, cnear_w = edges(CREACH)

    def put_packed(row, core, halo):
        both = lambda t: jnp.concatenate([core(t), halo(t)], axis=1)
        put_state(k, s0, row, [both(t) for t in range(5)])
        masks[row, 0:8, :] = both(5)
        last = both(6)
        masks[row, 8:16, :] = jnp.where(k.low, last[1:2, :], last[0:1, :])
        fluxes[row] = last

    for r in range(ROWS):
        at = (r // 8) * PACK
        turn = SLOT * (r % 8)

        def halo(t):
            from_e = pltpu.roll(west[at + 8 * t : at + 8 * t + 8, :], -turn % COLS, 1)
            from_w = pltpu.roll(east[at + 8 * t : at + 8 * t + 8, :], -(turn + SLOT) % COLS, 1)
            return jnp.where(near_e, from_e, jnp.where(near_w, from_w, 0.0))

        put_packed(PAD + r, lambda t: own[r, 8 * t : 8 * t + 8, :], halo)
        for t in range(5):
            rows = slice(2 * PACK + 8 * t, 2 * PACK + 8 * t + 8)
            from_e = pltpu.roll(west[rows, :], -8 * r % COLS, 1)
            from_w = pltpu.roll(east[rows, :], -8 * (r + 1) % COLS, 1)
            side = jnp.where(cnear_e, from_e, jnp.where(cnear_w, from_w, 0.0))
            cot[PAD + r, 8 * t : 8 * t + 8, :] = jnp.concatenate(
                [cown[r, 8 * t : 8 * t + 8, :], side], axis=1
            )
    for side, (lat_x, lat_c, diag_e, diag_w) in zip(sides, side_refs):
        base = {"swap": scal[4], "north": PAD - REACH, "south": PAD + ROWS}[side]
        cbase = {"swap": scal[5], "north": PAD - CREACH, "south": PAD + ROWS}[side]
        crow = {"swap": scal[6], "north": ROWS - CREACH, "south": 0}[side]
        for r in range(REACH):

            def halo(t):
                rows = slice(8 * t, 8 * t + 8)
                from_e = pltpu.roll(diag_w[rows, :], -REACH * r % COLS, 1)
                from_w = pltpu.roll(diag_e[rows, :], -REACH * (r + 1) % COLS, 1)
                return jnp.where(near_e, from_e, jnp.where(near_w, from_w, 0.0))

            put_packed(base + r, lambda t: lat_x[r, 8 * t : 8 * t + 8, :], halo)
        for r in range(CREACH):
            turn = lax.rem(2 * COLS - 8 * (crow + r), COLS)
            turn_w = lax.rem(2 * COLS - 8 * (crow + r + 1), COLS)
            for t in range(5):
                rows = slice(PACK + 8 * t, PACK + 8 * t + 8)
                from_e = pltpu.roll(diag_w[rows, :], turn, 1)
                from_w = pltpu.roll(diag_e[rows, :], turn_w, 1)
                part = jnp.where(cnear_e, from_e, jnp.where(cnear_w, from_w, 0.0))
                cot[cbase + r, 8 * t : 8 * t + 8, :] = jnp.concatenate(
                    [lat_c[r, 8 * t : 8 * t + 8, :], part], axis=1
                )

    k1, k2, k3 = stacked_weights(w1), stacked_weights(w2), stacked_weights(w3)

    for r in range(ROWS):
        outs[PAD + r, :, 0:COLS] = own_m[r]

    def closure_of(columns):
        z = split(to_48(columns))
        _, _, h2 = hidden_layers(z, k1, b1[...], k2, b2[...])
        return product(k3, *split(h2))[0:FEATS] + b3[...]

    def halo_rows(first):
        o = closure_of(jnp.concatenate([s0[first + i, 0:FEATS, 0:COLS] for i in range(8)], axis=1))
        for i in range(8):
            outs[first + i, :, 0:COLS] = o[:, i * COLS : (i + 1) * COLS]

    if sides == ["swap"]:
        groups = 3
        halo_rows(jnp.where(has_south == 1, PAD - 8, PAD + ROWS))
    else:
        groups = 4
        halo_rows(PAD - 8)
        halo_rows(PAD + ROWS)
    first = lo(8)
    o = closure_of(jnp.concatenate([wide_pack(s0, first + 8 * g) for g in range(groups)], axis=1))
    for g in range(groups):
        wide_unpack(outs, first + 8 * g, o[:, g * COLS : (g + 1) * COLS])

    for_rows(scal, 10, section_1(k, cs, fs, masks, s0, s1))
    for_rows(scal, 9, section_2(k, cs, fs, masks, s0, s1, s2))


def late_kernel(
    sides, scal, cs, fs, sums, own, own_h1, own_h2, s0, s1, s2, masks, fluxes, cot, outs_in,
    w1, b1, w2, b2, w3, b3, v1, v2, v3, final, grads, s4, abuf, from_closure, *scratch
):
    s3, t1, t2, outs, gz, bbuf, hold, acc = scratch
    k = Row(WIDE)
    has_south, has_north = scal[2], scal[3]
    lo = lambda h: PAD - h * has_south
    hi = lambda h: PAD + ROWS + h * has_north

    for ref in (s3, t1, t2, abuf, bbuf):
        for row in (PAD - 1, PAD + ROWS):
            ref[row] = jnp.zeros(ref.shape[1:], F32)
    k1, k2, k3 = stacked_weights(w1), stacked_weights(w2), stacked_weights(w3)
    q1, q2, q3 = stacked_weights(v1), stacked_weights(v2), stacked_weights(v3)

    mean = sums[0:1, 0:1] / sums[1:2, 0:1]

    def section_3(src, mid, net, r):
        d = tendency_row(k, mid, r, cs[r], fs[r])
        new = []
        for t in range(5):
            m = mask_tile(masks, r, t)
            o = tile(net, r, t)
            if t == 1:
                force = 2.0 * (mean - fluxes[r, 2:3, :])
                o = o + jnp.where(k.sub == 0, force, 0.0)
            new.append(
                (1.0 / 3.0) * tile(src, r, t) + (2.0 / 3.0) * tile(mid, r, t)
                + m * ((1.0 / 6.0) * d[t] + 0.25 * o)
            )
        return new

    def step_1_end(r):
        put_state(k, s3, r, section_3(s0, s2, r))

    def step_1_end(r):
        put_state(k, s3, r, section_3(s0, s2, outs_in, r))

    for_rows(scal, 8, step_1_end)

    acc[...] = jnp.zeros(acc.shape, F32)

    def closure_adjoint(z, h1, h1s, h2, go, with_weights):
        gos = split(to_48(go))
        g2 = product(q3, *gos) * (1.0 - h2 * h2)
        g2s = split(g2)
        g1 = product(q2, *g2s) * (1.0 - h1 * h1)
        g1s = split(g1)
        if with_weights:
            add_weight_terms(acc, z, h1s, split(h2), g1s, g2s, gos)
        return product(q1, *g1s)[0:FEATS]

    def both_ways(columns, go, with_weights):
        z = split(to_48(columns))
        h1, h1s, h2 = hidden_layers(z, k1, b1[...], k2, b2[...])
        o = product(k3, *split(h2))[0:FEATS] + b3[...] if with_weights else None
        return o, closure_adjoint(z, h1, h1s, h2, go, with_weights)

    def masked_core(ref, r):
        m0, m4 = masks[r, 0:8, 0:COLS], masks[r, 8:16, 0:COLS]
        parts = [
            0.25 * (m4 if t == 4 else m0) * ref[r, 8 * t : 8 * t + 8, 0:COLS] for t in range(5)
        ]
        return jnp.concatenate(parts, axis=0)

    def mask_cot(r):
        for t in range(5):
            bbuf[r, 8 * t : 8 * t + 8, :] = 0.25 * mask_tile(masks, r, t) * tile(cot, r, t)
            abuf[r, 8 * t : 8 * t + 8, :] = (1.0 / 6.0) * mask_tile(masks, r, t) * tile(cot, r, t)

    for_rows(scal, 6, mask_cot)

    for first in range(PAD, PAD + ROWS, 8):
        z = jnp.concatenate([s3[first + i, 0:FEATS, 0:COLS] for i in range(8)], axis=1)
        go = jnp.concatenate([bbuf[first + i, 0:FEATS, 0:COLS] for i in range(8)], axis=1)
        o, back = both_ways(z, go, True)
        for i in range(8):
            at = slice(i * COLS, (i + 1) * COLS)
            outs[first + i, :, 0:COLS] = o[:, at]
            gz[first + i, :, 0:COLS] = back[:, at]

    first = lo(4)
    if sides == ["swap"]:
        rows = [jnp.where(has_south == 1, PAD - 4, PAD + ROWS) + i for i in range(4)]
    else:
        rows = [PAD - 4 + i for i in range(4)] + [PAD + ROWS + i for i in range(4)]
    beyond = lambda ref: jnp.concatenate(
        [ref[r, 0:FEATS, 0:COLS] for r in rows] + [wide_pack(ref, first + 8 * g) for g in range(3)], axis=1
    )
    _, back = both_ways(beyond(s3), beyond(bbuf), False)
    for i, r in enumerate(rows):
        gz[r, :, 0:COLS] = back[:, i * COLS : (i + 1) * COLS]
    for g in range(3):
        at = (len(rows) + g) * COLS
        wide_unpack(gz, first + 8 * g, back[:, at : at + COLS])

    for_rows(scal, 7, section_1(k, cs, fs, masks, s3, t1))
    for_rows(scal, 6, section_2(k, cs, fs, masks, s3, t1, t2))

    def last(r):
        new = section_3(s3, t2, outs, r)
        put_result(final, r - PAD, [x[:, 0:COLS] for x in new])

    for_rows(scal, 0, last)

    def store(r, tiles):
        for t in range(5):
            s4[r, 8 * t : 8 * t + 8, :] = tiles[t] + tile(gz, r, t)

    adjoint_third(k, scal, cs, fs, 5, t2, masks, abuf, cot, hold, bbuf)
    adjoint_second(k, scal, cs, fs, 4, t1, masks, bbuf, cot, hold, t2, abuf)
    adjoint_first(k, scal, cs, fs, 3, s3, abuf, t2, store)

    for r in range(0, ROWS, 8):
        side = lambda read: jnp.concatenate([read(r + j) for j in range(8)], axis=1)
        z = split(to_48(side(lambda j: own[j, 0:FEATS, :])))
        h1 = side(lambda j: own_h1[j])
        h2 = side(lambda j: own_h2[j])
        go = side(lambda j: masked_core(s4, PAD + j))
        back = closure_adjoint(z, h1, split(h1), h2, go, True)
        for j in range(8):
            from_closure[r + j] = back[:, j * COLS : (j + 1) * COLS]

    for row in (PAD - 1, PAD + ROWS):
        abuf[row] = jnp.zeros((FEATS, WIDE), F32)

    def mask_top(r):
        for t in range(5):
            abuf[r, 8 * t : 8 * t + 8, :] = (1.0 / 6.0) * mask_tile(masks, r, t) * tile(s4, r, t)

    for_rows(scal, 3, mask_top)
    grads[...] = jnp.zeros(grads.shape, F32)
    grads[0:40, 0:HID] = acc[0:40, 0:HID]
    grads[0:40, HID : 2 * HID] = acc[112:152, 0:HID]
    grads[40:72, 0:HID] = acc[48:80, 0:HID]
    grads[40:72, HID : 2 * HID] = acc[80:112, 0:HID]
    grads[72:73, 0:HID] = acc[160:161, 0:HID]
    grads[72:73, HID : 2 * HID] = acc[176:177, 0:HID]
    grads[73:74, 0:HID] = acc[192:193, 0:HID]


def put_result(ref, row, tiles):
    for t in range(4):
        ref[pl.ds(t * 10 * ROWS + row, 8, stride=ROWS), :] = tiles[t]
    ref[pl.ds(8 * ROWS + row, 4, stride=10 * ROWS), :] = tiles[4][0:4, :]
    ref[pl.ds(9 * ROWS + row, 4, stride=10 * ROWS), :] = tiles[4][4:8, :]


def back_third_kernel(scal, cs, fs, state, masks, abuf, top, hold, bbuf):
    for row in (PAD - 1, PAD + ROWS):
        bbuf[row] = jnp.zeros((FEATS, WIDE), F32)
    adjoint_third(Row(WIDE), scal, cs, fs, 2, state, masks, abuf, top, hold, bbuf)


def back_second_kernel(scal, cs, fs, gate, state, masks, bbuf, top, hold, left, abuf):
    for row in (PAD - 1, PAD + ROWS):
        abuf[row] = jnp.zeros((FEATS, WIDE), F32)
    adjoint_second(Row(WIDE), scal, cs, fs, 1, state, masks, bbuf, top, hold, left, abuf)


def back_first_kernel(scal, cs, fs, gate, state, masks, abuf, left, from_closure, grad):
    def store(r, tiles):
        done = []
        for t in range(5):
            m = masks[r, 8:16, 0:COLS] if t == 4 else masks[r, 0:8, 0:COLS]
            done.append(m * (tiles[t][:, 0:COLS] + from_closure[r - PAD, 8 * t : 8 * t + 8, :]))
        put_result(grad, r - PAD, done)

    adjoint_first(Row(WIDE), scal, cs, fs, 0, state, abuf, left, store)


def unpack_kernel(scale, packed, win, bin_, wmid, bmid, wout, bout):
    for ref, lanes in ((win, slice(0, HID)), (wout, slice(HID, 2 * HID))):
        for t in range(4):
            ref[10 * t : 10 * t + 8, :] = packed[8 * t : 8 * t + 8, lanes] * scale
            ref[10 * t + 8 : 10 * t + 9, :] = packed[32 + t : 33 + t, lanes] * scale
            ref[10 * t + 9 : 10 * t + 10, :] = packed[36 + t : 37 + t, lanes] * scale
    wmid[0:32, :] = packed[40:72, 0:HID] * scale
    wmid[32:64, :] = packed[40:72, HID : 2 * HID] * scale
    bin_[...] = packed[72:73, 0:HID] * scale
    bmid[...] = packed[72:73, HID : 2 * HID] * scale
    for t in range(4):
        bout[:, 10 * t : 10 * t + 8] = packed[73:74, 8 * t : 8 * t + 8] * scale
        bout[:, 10 * t + 8 : 10 * t + 9] = packed[73:74, 32 + t : 33 + t] * scale
        bout[:, 10 * t + 9 : 10 * t + 10] = packed[73:74, 36 + t : 37 + t] * scale


def by_tile(weights):
    heads = [weights[10 * t : 10 * t + 8] for t in range(4)]
    tails = [weights[10 * t + level : 10 * t + level + 1] for level in (8, 9) for t in range(4)]
    return jnp.concatenate(heads + tails, axis=0)


def tree_round(x, axis, count, stride):
    group = 4 if (count // stride) % 4 == 0 else 2
    got = [
        lax.ppermute(x, axis, [(i, i ^ (j * stride)) for i in range(count)]) for j in range(1, group)
    ]
    x = x + got[0] if group == 2 else (x + got[0]) + (got[1] + got[2])
    return x, stride * group


def tree_rounds(x, axes):
    for axis, count in axes:
        if count & (count - 1):
            x = lax.psum(x, axis)
            yield x
            continue
        stride = 1
        while stride < count:
            x, stride = tree_round(x, axis, count, stride)
            yield x


def three(w):
    return jnp.concatenate([w, w, w], axis=1)


def pad_cols(w):
    return jnp.pad(w, ((0, 0), (0, 8)))


def latitude_terms(row_index, row_count):
    latitude = LAT_LIMIT * (2.0 * (jnp.clip(row_index, 0.0, row_count - 1.0) + 0.5) / row_count - 1.0)
    return 1.0 / jnp.cos(latitude), CORIOLIS * jnp.sin(latitude)


def on_device(
    initial_state, land_mask, surface_flux, weight_in, bias_in, weight_mid, bias_mid, weight_out, bias_out, cotangent
):
    lat_n, lon_n = lax.axis_size("lat"), lax.axis_size("lon")
    lat_i = lax.axis_index("lat")
    lat_total, lon_total = ROWS * lat_n, COLS * lon_n
    sides = ["swap"] if lat_n == 2 else ["north", "south"]
    is_low = (lat_i == 0).astype(jnp.int32)
    has_south = (lat_i > 0).astype(jnp.int32)
    has_north = (lat_i < lat_n - 1).astype(jnp.int32)
    scal = jnp.stack(
        [
            is_low * (ROWS - REACH),
            is_low * (ROWS - CREACH),
            has_south,
            has_north,
            jnp.where(is_low == 1, PAD + ROWS, PAD - REACH),
            jnp.where(is_low == 1, PAD + ROWS, PAD - CREACH),
            jnp.where(is_low == 1, 0, ROWS - CREACH),
        ]
    ).astype(jnp.int32)
    rows = (lat_i * ROWS - PAD + jnp.arange(EXT, dtype=jnp.int32)).astype(F32)
    cs, fs = latitude_terms(rows, lat_total)

    packed = pl.pallas_call(
        lambda *refs: pack_kernel(sides, *refs),
        out_shape=[
            sds(ROWS, PACK, COLS), sds(ROWS, FEATS, COLS), sds(8, COLS),
            sds(2 * PACK + 40, COLS), sds(2 * PACK + 40, COLS),
        ]
        + [sds(REACH, PACK, COLS), sds(CREACH, FEATS, COLS), sds(PACK + 40, COLS), sds(PACK + 40, COLS)] * len(sides),
        in_specs=[SMEM] + [pl.BlockSpec(memory_space=pl.ANY)] * 4,
        out_specs=[VMEM] * (5 + 4 * len(sides)),
        scratch_shapes=[
            pltpu.VMEM((40 * ROWS, COLS), F32), pltpu.VMEM((10 * ROWS, COLS), jnp.int32),
            pltpu.VMEM((ROWS, COLS), F32), pltpu.VMEM((40 * ROWS, COLS), F32), pltpu.SemaphoreType.DMA((4,)),
        ],
        compiler_params=params(48),
        name="pack_halos",
    )(
        scal,
        initial_state.reshape(40 * ROWS, COLS),
        land_mask.reshape(10 * ROWS, COLS),
        surface_flux,
        cotangent.reshape(40 * ROWS, COLS),
    )
    own, cown, sums, east_pay, west_pay = packed[:5]

    def lat_pairs(side):
        if side == "swap":
            return [(0, 1), (1, 0)]
        if side == "north":
            return [(i, i + 1) for i in range(lat_n - 1)]
        return [(i + 1, i) for i in range(lat_n - 1)]

    def diagonal(side, step):
        return [
            (i * lat_n + a, ((i + step) % lon_n) * lat_n + b)
            for i in range(lon_n)
            for a, b in lat_pairs(side)
        ]

    east_ring = [(i, (i + 1) % lon_n) for i in range(lon_n)]
    west_ring = [((i + 1) % lon_n, i) for i in range(lon_n)]
    received = []
    for i, side in enumerate(sides):
        lat_x, lat_c, diag_e, diag_w = packed[5 + 4 * i : 9 + 4 * i]
        received.append(
            [
                lax.ppermute(lat_x, "lat", lat_pairs(side)),
                lax.ppermute(lat_c, "lat", lat_pairs(side)),
                lax.ppermute(diag_e, ("lon", "lat"), diagonal(side, 1)),
                lax.ppermute(diag_w, ("lon", "lat"), diagonal(side, -1)),
            ]
        )
    from_west = lax.ppermute(east_pay, "lon", east_ring)
    from_east = lax.ppermute(west_pay, "lon", west_ring)
    axes = (("lon", lon_n), ("lat", lat_n))
    mean_rounds = list(tree_rounds(sums, axes))

    w_in, w_out_t = by_tile(weight_in), by_tile(weight_out.T)
    col = lambda b: b.reshape(-1, 1)
    forward = [
        three(pad_cols(w_in.T)), col(bias_in), three(weight_mid.T), col(bias_mid), three(w_out_t), by_tile(col(bias_out)),
    ]
    forward[4] = jnp.pad(forward[4], ((0, 8), (0, 0)))
    backward = [jnp.pad(three(w_in), ((0, 8), (0, 0))), three(weight_mid), three(pad_cols(w_out_t.T))]

    own_m, own_h1, own_h2 = pl.pallas_call(
        own_closure_kernel,
        out_shape=[sds(ROWS, FEATS, COLS), sds(ROWS, HID, COLS), sds(ROWS, HID, COLS)],
        in_specs=[VMEM] * 7,
        out_specs=[VMEM] * 3,
        compiler_params=params(12),
        cost_estimate=pl.CostEstimate(flops=10**9, bytes_accessed=2 * 10**6, transcendentals=0),
        name="own_closure",
    )(own, *forward)

    geometry = (scal, cs, fs)
    state = sds(EXT, 72, WIDE)
    plain = sds(EXT, FEATS, WIDE)
    marks = sds(EXT, 16, WIDE)
    vmem = lambda shape: pltpu.VMEM(shape.shape, F32)

    def call(kernel, name, out_shape, scratch, args, flops, limit):
        single = not isinstance(out_shape, list)
        return pl.pallas_call(
            kernel,
            out_shape=out_shape,
            in_specs=[SMEM] * 3 + [VMEM] * len(args),
            out_specs=VMEM if single else [VMEM] * len(out_shape),
            scratch_shapes=scratch,
            compiler_params=params(limit),
            cost_estimate=pl.CostEstimate(flops=flops, bytes_accessed=10**7, transcendentals=0),
            name=name,
        )(*geometry, *args)

    s0, s1, s2, masks, fluxes, cot, net = call(
        lambda *refs: early_kernel(sides, *refs), "first_sections",
        [state, state, state, marks, sds(EXT, 8, WIDE), plain, plain], [],
        [mean_rounds[-2], own, cown, own_m, from_west, from_east]
        + [item for side in received for item in side] + forward,
        2 * 10**9, 8,
    )
    final, grads, top, abuf, from_closure = call(
        lambda *refs: late_kernel(sides, *refs), "steps_and_adjoint",
        [sds(40 * ROWS, COLS), sds(80, COLS), plain, plain, sds(ROWS, FEATS, COLS)],
        [vmem(state)] * 3 + [vmem(plain)] * 4 + [pltpu.VMEM((208, HID), F32)],
        [mean_rounds[-1], own, own_h1, own_h2, s0, s1, s2, masks, fluxes, cot, net] + forward + backward,
        4 * 10**9, 24,
    )
    rounds = list(tree_rounds(grads, axes))
    hold, bbuf = call(
        back_third_kernel, "adjoint_third_section", [plain, plain], [], [s2, masks, abuf, top], 10**9, 8
    )
    left, abuf = call(
        back_second_kernel, "adjoint_second_section", [plain, plain], [],
        [rounds[0], s1, masks, bbuf, top, hold], 10**9, 8,
    )
    state_grad = call(
        back_first_kernel, "adjoint_first_section", sds(40 * ROWS, COLS), [],
        [rounds[1], s0, masks, abuf, left, from_closure], 10**9, 8,
    )

    scale = 1.0 / math.sqrt(lat_total * lon_total)
    g_in, g_bin, g_mid, g_bmid, g_out, g_bout = pl.pallas_call(
        lambda *refs: unpack_kernel(scale, *refs),
        out_shape=[sds(40, HID), sds(1, HID), sds(HID, HID), sds(1, HID), sds(40, HID), sds(1, 40)],
        in_specs=[VMEM],
        out_specs=[VMEM] * 6,
        compiler_params=params(8),
        name="unpack_weight_grads",
    )(rounds[-1])
    shape = initial_state.shape
    return (
        final.reshape(shape),
        state_grad.reshape(shape),
        g_in,
        g_bin.reshape(-1),
        g_mid,
        g_bmid.reshape(-1),
        g_out.T,
        g_bout.reshape(-1),
    )


def solution(mesh):
    split_state = P(None, None, "lat", "lon")
    return jax.shard_map(
        on_device,
        mesh=mesh,
        in_specs=(split_state, P(None, "lat", "lon"), P("lat", "lon"), P(), P(), P(), P(), P(), P(), split_state),
        out_specs=(split_state, split_state, P(), P(), P(), P(), P(), P()),
        check_vma=False,
    )
```

```python
import math

import jax
import jax.numpy as jnp
from jax import lax
from jax.experimental import pallas as pl
from jax.experimental.pallas import tpu as pltpu
from jax.sharding import PartitionSpec as P

LAT_LIMIT = 1.2
CORIOLIS = 1.0
VISCOSITY = 0.15
DIFFUSIVITY = 0.1

ROWS = 16
COLS = 128
REACH = 11
CREACH = 6
PAD = 16
EXT = 48
TURN = 4
WIDE = 2 * COLS
FEATS = 40
HID = 64
PACK = 56
SUMS = 51
SLOT = 16
F32 = jnp.float32
BF16 = jnp.bfloat16
VMEM = pl.BlockSpec(memory_space=pltpu.VMEM)
SMEM = pl.BlockSpec(memory_space=pltpu.SMEM)


def params(megabytes):
    return pltpu.CompilerParams(vmem_limit_bytes=megabytes * 1024 * 1024)


def sds(*shape):
    return jax.ShapeDtypeStruct(shape, F32)


def sub_index(width):
    return lax.broadcasted_iota(jnp.int32, (8, width), 0)


def tile(ref, row, number):
    return ref[row, 8 * number : 8 * number + 8, :]


def slot_pack(pieces, shift_of, width):
    lane = lax.broadcasted_iota(jnp.int32, (8, COLS), 1)
    packed = None
    for slot, piece in enumerate(pieces):
        turned = pltpu.roll(piece, shift_of(slot) % COLS, 1)
        if packed is None:
            packed = turned
        else:
            packed = jnp.where((lane >= slot * width) & (lane < (slot + 1) * width), turned, packed)
    return packed


def pack_kernel(sides, scal, x_hbm, mask_hbm, flux_hbm, cot_hbm, *outs):
    x, mask, flux, cot, sems = outs[-5:]
    own, cown, east, west = outs[:4]
    per_side = [outs[4 + 4 * i : 8 + 4 * i] for i in range(len(sides))]
    pairs = ((mask_hbm, mask), (x_hbm, x), (flux_hbm, flux), (cot_hbm, cot))
    copies = [pltpu.make_async_copy(a, b, sems.at[i]) for i, (a, b) in enumerate(pairs)]
    for copy in copies:
        copy.start()
    for copy in copies:
        copy.wait()
    top = mask[0:ROWS, :].astype(F32)
    total = jnp.sum(jnp.sum(top * flux[...], axis=1, keepdims=True), axis=0, keepdims=True)
    count = jnp.sum(jnp.sum(top, axis=1, keepdims=True), axis=0, keepdims=True)
    tail = jnp.where(sub_index(COLS) == 0, total, jnp.where(sub_index(COLS) == 1, count, 0.0))
    for r in range(ROWS):
        first = mask[pl.ds(r, 8, stride=ROWS), :].astype(F32)
        m8 = mask[8 * ROWS + r : 8 * ROWS + r + 1, :].astype(F32)
        m9 = mask[9 * ROWS + r : 9 * ROWS + r + 1, :].astype(F32)
        for t in range(4):
            own[r, 8 * t : 8 * t + 8, :] = x[pl.ds(t * 10 * ROWS + r, 8, stride=ROWS), :] * first
            cown[r, 8 * t : 8 * t + 8, :] = cot[pl.ds(t * 10 * ROWS + r, 8, stride=ROWS), :]
        for level, m in ((8, m8), (9, m9)):
            at = 32 + 4 * (level - 8)
            own[r, at : at + 4, :] = x[pl.ds(level * ROWS + r, 4, stride=10 * ROWS), :] * m
            cown[r, at : at + 4, :] = cot[pl.ds(level * ROWS + r, 4, stride=10 * ROWS), :]
        own[r, 40:48, :] = first
        own[r, 48:49, :] = m8
        own[r, 49:50, :] = m9
        own[r, 50:51, :] = flux[r : r + 1, :]
        own[r, SUMS:56, :] = tail[0:5, :]
    for half in range(2):
        for t in range(7):
            rows = [own[8 * half + s, 8 * t : 8 * t + 8, :] for s in range(8)]
            at = half * PACK + 8 * t
            east[at : at + 8, :] = slot_pack(rows, lambda s: SLOT * (s + 1), SLOT)
            west[at : at + 8, :] = slot_pack(rows, lambda s: SLOT * s, SLOT)
    for t in range(5):
        rows = [cown[s, 8 * t : 8 * t + 8, :] for s in range(ROWS)]
        at = 2 * PACK + 8 * t
        east[at : at + 8, :] = slot_pack(rows, lambda s: 8 * (s + 1), 8)
        west[at : at + 8, :] = slot_pack(rows, lambda s: 8 * s, 8)
    for side, (lat_x, lat_c, diag_e, diag_w) in zip(sides, per_side):
        start = {"swap": scal[0], "north": ROWS - REACH, "south": 0}[side]
        cstart = {"swap": scal[1], "north": ROWS - CREACH, "south": 0}[side]
        for n in range(REACH):
            lat_x[n] = own[start + n]
        for n in range(CREACH):
            lat_c[n] = cown[cstart + n]
        for t in range(7):
            rows = [own[start + n, 8 * t : 8 * t + 8, :] for n in range(REACH)]
            diag_e[8 * t : 8 * t + 8, :] = slot_pack(rows, lambda s: REACH * (s + 1), REACH)
            diag_w[8 * t : 8 * t + 8, :] = slot_pack(rows, lambda s: REACH * s, REACH)
        diag_e[PACK : PACK + 40, :] = east[2 * PACK : 2 * PACK + 40, :]
        diag_w[PACK : PACK + 40, :] = west[2 * PACK : 2 * PACK + 40, :]


def split(values):
    high = values.astype(BF16)
    return high, (values - high.astype(F32)).astype(BF16)


def stack(out, values, buffer):
    k = values.shape[1]
    rows = slice(0, values.shape[0])
    high, low = split(values)
    buffer[rows, 0:k] = high.astype(F32)
    buffer[rows, k : 2 * k] = high.astype(F32)
    buffer[rows, 2 * k : 3 * k] = low.astype(F32)
    out[...] = buffer[rows, 0 : 3 * k].astype(BF16)


def by_tile(dst, src, lanes):
    for t in range(4):
        dst[8 * t : 8 * t + 8, lanes] = src[10 * t : 10 * t + 8, lanes]
        dst[32 + t : 33 + t, lanes] = src[10 * t + 8 : 10 * t + 9, lanes]
        dst[36 + t : 37 + t, lanes] = src[10 * t + 9 : 10 * t + 10, lanes]


def product(weights, high, low):
    return jnp.dot(weights, jnp.concatenate([high, low, high], axis=0), preferred_element_type=F32)


def across(a, b):
    dims = (((1,), (1,)), ((), ()))
    dot = lambda p, q: lax.dot_general(p, q, dims, preferred_element_type=F32)
    return dot(a[0], b[0]) + dot(a[0], b[1]) + dot(a[1], b[0])


def to_48(columns, first=0.0):
    more = jnp.where(sub_index(columns.shape[1]) == 0, first, 0.0).astype(F32)
    return jnp.concatenate([columns, more], axis=0)


def wide(bias, values):
    return jnp.concatenate([bias[...]] * (values.shape[1] // COLS), axis=1)


def hidden_layers(z, k1, k2, b2):
    h1 = jnp.tanh(product(k1[...], *z))
    h1s = split(h1)
    h2 = product(k2[...], *h1s)
    return h1, h1s, jnp.tanh(h2 + wide(b2, h2))


def last_layer(h2, k3, b3):
    o = product(k3[...], *split(h2))[0:FEATS]
    return o + wide(b3, o)


def add_weight_terms(acc, z, h1s, h2s, g1s, g2s, gos):
    ones = jnp.ones((16, z[0].shape[1]), BF16)
    acc[0:48, 0:HID] += across(z, g1s)
    acc[48:112, 0:HID] += across(h1s, g2s)
    acc[112:160, 0:HID] += across(gos, h2s)
    acc[160:176, 0:HID] += ones_rows(ones, g2s)
    acc[176:192, 0:48] += ones_rows(ones, gos)


def ones_rows(ones, g):
    dims = (((1,), (1,)), ((), ()))
    dot = lambda q: lax.dot_general(ones, q, dims, preferred_element_type=F32)
    return dot(g[0]) + dot(g[1])


def own_closure_kernel(own, *refs):
    raw, (out, h1_out, h2_out, k1, k2, k3, q1, q2, q3, b2, b3) = refs[:6], refs[6:17]
    w_in, w_mid, w_out, b_in, b_mid, b_out = refs[17:23]
    buffer, spare, stacked, sems = refs[23:]
    copies = [pltpu.make_async_copy(a, b, sems.at[i]) for i, (a, b) in enumerate(zip(raw, refs[17:23]))]
    for copy in copies:
        copy.start()
    for copy in copies:
        copy.wait()
    buffer[...] = jnp.zeros(buffer.shape, F32)
    by_tile(buffer, w_in, slice(0, HID))
    buffer[40:41, 0:HID] = b_in[...]
    stack(q1, buffer[0:48, 0:HID], stacked)
    spare[...] = buffer[...].T
    stack(k1, spare[0:HID, 0:48], stacked)
    buffer[0:HID, 0:HID] = w_mid[...]
    buffer[HID : HID + 1, 0:HID] = b_mid[...]
    stack(q2, buffer[0:HID, 0:HID], stacked)
    spare[...] = buffer[...].T
    stack(k2, spare[0:HID, 0:HID], stacked)
    b2[...] = jnp.broadcast_to(spare[0:HID, HID : HID + 1], (HID, COLS))
    buffer[...] = jnp.zeros(buffer.shape, F32)
    buffer[0:HID, 0:FEATS] = w_out[...]
    buffer[HID : HID + 1, 0:FEATS] = b_out[...]
    spare[...] = buffer[...].T
    buffer[...] = jnp.zeros(buffer.shape, F32)
    by_tile(buffer, spare, slice(0, COLS))
    stack(k3, buffer[0:48, 0:HID], stacked)
    b3[...] = jnp.broadcast_to(buffer[0:FEATS, HID : HID + 1], (FEATS, COLS))
    spare[...] = buffer[...].T
    stack(q3, spare[0:HID, 0:48], stacked)

    for r in range(0, ROWS, 8):
        z = split(to_48(jnp.concatenate([own[r + n, 0:FEATS, :] for n in range(8)], axis=1), 1.0))
        h1, h1s, h2 = hidden_layers(z, k1, k2, b2)
        o = last_layer(h2, k3, b3)
        for n in range(8):
            at = slice(n * COLS, (n + 1) * COLS)
            out[r + n] = o[:, at]
            h1_out[r + n] = h1[:, at]
            h2_out[r + n] = h2[:, at]


class Row:
    def __init__(self, width):
        sub = sub_index(width)
        group = sub % 4
        self.sub = sub
        self.is_t = group == 0
        self.is_s = group == 1
        self.is_u = group == 2
        self.is_v = group == 3
        self.low = sub >= 4
        self.k4 = jnp.where(group < 2, DIFFUSIVITY, VISCOSITY).astype(F32)


def derived(k, temp, salt, mixed):
    zero = jnp.zeros_like(temp)
    press = 0.4 * salt - 0.1 * temp
    for by in (1, 2, 4):
        press = press + jnp.where(k.sub >= by, pltpu.roll(press, by, 0), zero)
    deep = jnp.where(k.is_t, 0.4 * pltpu.roll(mixed, 7, 0) - 0.1 * mixed, zero)
    deep = deep + jnp.where(k.low, pltpu.roll(deep, 4, 0), zero)
    deep = deep + pltpu.roll(deep, 1, 0)
    deep = deep + pltpu.roll(deep, 2, 0) + press[7:8, :]
    u4, v4 = deep_velocity(k, mixed)
    return press, deep, u4, v4


def deep_velocity(k, mixed):
    zero = jnp.zeros_like(mixed)
    u4 = jnp.where(k.is_u, mixed, zero)
    u4 = u4 + pltpu.roll(u4, 1, 0)
    u4 = u4 + pltpu.roll(u4, 6, 0)
    v4 = jnp.where(k.is_v, mixed, zero)
    v4 = v4 + pltpu.roll(v4, 7, 0)
    v4 = v4 + pltpu.roll(v4, 6, 0)
    return u4, v4


def put_state(k, ref, row, tiles):
    for t in range(5):
        ref[row, 8 * t : 8 * t + 8, :] = tiles[t]
    for t, values in enumerate(derived(k, tiles[0], tiles[1], tiles[4])):
        ref[row, 40 + 8 * t : 48 + 8 * t, :] = values


def east_of(q):
    return pltpu.roll(q, q.shape[1] - 1, 1)


def west_of(q):
    return pltpu.roll(q, 1, 1)


def tendency_row(k, ref, row, c, f):
    half = 0.5 * c
    c2 = c * c
    u, v = tile(ref, row, 2), tile(ref, row, 3)
    u4, v4 = tile(ref, row, 7), tile(ref, row, 8)
    uh, vh = u * half, v * 0.5
    u4h, v4h = u4 * half, v4 * 0.5
    change = []
    for t in range(5):
        q = tile(ref, row, t)
        e, w = east_of(q), west_of(q)
        n, s = tile(ref, row + 1, t), tile(ref, row - 1, t)
        lap = c2 * (e + w) + (n + s) - (2.0 * c2 + 2.0) * q
        gain = k.k4 if t == 4 else (DIFFUSIVITY if t < 2 else VISCOSITY)
        au, av = (u4h, v4h) if t == 4 else (uh, vh)
        change.append(gain * lap - (au * (e - w) + av * (n - s)))
    p = tile(ref, row, 5)
    change[2] = change[2] + (f * v - half * (east_of(p) - west_of(p)))
    change[3] = change[3] - (f * u + 0.5 * (tile(ref, row + 1, 5) - tile(ref, row - 1, 5)))
    p4 = tile(ref, row, 6)
    zero = jnp.zeros_like(p4)
    fx = f * v4 - half * (east_of(p4) - west_of(p4))
    fy = f * u4 + 0.5 * (tile(ref, row + 1, 6) - tile(ref, row - 1, 6))
    change[4] = change[4] + jnp.where(k.is_u, fx, jnp.where(k.is_v, -fy, zero))
    return change


def adjoint_row(k, ref, aref, row, c, f):
    half = 0.5 * c
    c2 = c * c
    u4 = tile(ref, row, 7)
    qe = [east_of(tile(ref, row, t)) for t in range(5)]
    qw = [west_of(tile(ref, row, t)) for t in range(5)]
    u4e, u4w = east_of(u4), west_of(u4)
    out = []
    to_u = to_v = None
    for t in range(5):
        a = tile(aref, row, t)
        ae, aw = east_of(a), west_of(a)
        an, as_ = tile(aref, row + 1, t), tile(aref, row - 1, t)
        gain = k.k4 if t == 4 else (DIFFUSIVITY if t < 2 else VISCOSITY)
        ue, uw = (u4e, u4w) if t == 4 else (qe[2], qw[2])
        which = 8 if t == 4 else 3
        vn, vs = tile(ref, row + 1, which), tile(ref, row - 1, which)
        lap = c2 * (ae + aw) + (an + as_) - (2.0 * c2 + 2.0) * a
        out.append(gain * lap + half * (ue * ae - uw * aw) + 0.5 * (vn * an - vs * as_))
        px = a * (qe[t] - qw[t])
        py = a * (tile(ref, row + 1, t) - tile(ref, row - 1, t))
        if t < 4:
            to_u = px if to_u is None else to_u + px
            to_v = py if to_v is None else to_v + py
        if t == 2:
            a2, bx = a, half * (ae - aw)
        if t == 3:
            a3, by = a, 0.5 * (an - as_)
        if t == 4:
            a4 = a
            deep_bx, deep_by = half * (ae - aw), 0.5 * (an - as_)
            px4, py4 = px * half, py * 0.5
    out[2] = out[2] - half * to_u - f * a3
    out[3] = out[3] - 0.5 * to_v + f * a2
    zero = jnp.zeros_like(a4)
    sx = px4 + pltpu.roll(px4, 7, 0)
    sx = sx + pltpu.roll(sx, 2, 0)
    sy = py4 + pltpu.roll(py4, 1, 0)
    sy = sy + pltpu.roll(sy, 2, 0)
    at_u = -sx - f * pltpu.roll(a4, 7, 0)
    at_v = f * pltpu.roll(a4, 1, 0) - sy
    deep = jnp.where(k.is_t, pltpu.roll(deep_bx, 6, 0) + pltpu.roll(deep_by, 5, 0), zero)
    deep = deep + jnp.where(k.low, zero, pltpu.roll(deep, 4, 0))
    press = bx + by
    for shift in (1, 2, 4):
        press = press + jnp.where(k.sub < 8 - shift, pltpu.roll(press, 8 - shift, 0), zero)
    press = press + deep[0:1, :]
    out[0] = out[0] - 0.1 * press
    out[1] = out[1] + 0.4 * press
    out[4] = out[4] + jnp.where(
        k.is_t,
        -0.1 * deep,
        jnp.where(k.is_s, 0.4 * pltpu.roll(deep, 1, 0), jnp.where(k.is_u, at_u, at_v)),
    )
    return out


def for_rows(scal, reach, body):
    low, high = PAD - reach * scal[2], PAD + ROWS + reach * scal[3]
    turns = lax.div(high - low + TURN - 1, TURN)
    first = jnp.where(scal[3] == 1, low, high - TURN * turns)

    def turn(i, _):
        for j in range(TURN):
            body(first + TURN * i + j)
        return 0

    lax.fori_loop(0, turns, turn, 0)


def mask_tile(ref, row, t):
    return tile(ref, row, 1 if t == 4 else 0)


def adjoint_third(k, scal, cs, fs, reach, state, masks, abuf, top, hold, bbuf):
    def body(r):
        d = adjoint_row(k, state, abuf, r, cs[r], fs[r])
        for t in range(5):
            ts = (2.0 / 3.0) * tile(top, r, t) + d[t]
            hold[r, 8 * t : 8 * t + 8, :] = ts
            bbuf[r, 8 * t : 8 * t + 8, :] = 0.0625 * mask_tile(masks, r, t) * ts

    for_rows(scal, reach, body)


def adjoint_second(k, scal, cs, fs, reach, state, masks, bbuf, top, hold, left, abuf):
    def body(r):
        d = adjoint_row(k, state, bbuf, r, cs[r], fs[r])
        for t in range(5):
            ts = tile(hold, r, t)
            tf = 0.25 * ts + d[t]
            left[r, 8 * t : 8 * t + 8, :] = (1.0 / 3.0) * tile(top, r, t) + 0.75 * ts + tf
            abuf[r, 8 * t : 8 * t + 8, :] = 0.25 * mask_tile(masks, r, t) * tf

    for_rows(scal, reach, body)


def adjoint_first(k, scal, cs, fs, reach, state, abuf, left, store):
    def body(r):
        d = adjoint_row(k, state, abuf, r, cs[r], fs[r])
        store(r, [tile(left, r, t) + d[t] for t in range(5)])

    for_rows(scal, reach, body)


def edges(reach):
    lane = lax.broadcasted_iota(jnp.int32, (8, COLS), 1)
    return lane < reach, lane >= COLS - reach


def wide_pack(ref, base):
    parts = []
    for t in range(5):
        rows = [ref[base + s, 8 * t : 8 * t + 8, COLS:WIDE] for s in range(8)]
        parts.append(slot_pack(rows, lambda s: 8 + SLOT * s, SLOT))
    return jnp.concatenate(parts, axis=0)

def wide_unpack(ref, base, values):
    for s in range(8):
        ref[base + s, 0:FEATS, COLS:WIDE] = pltpu.roll(values, -(8 + SLOT * s) % COLS, 1)


def section_1(k, cs, fs, masks, src, dst):
    def body(r):
        d = tendency_row(k, src, r, cs[r], fs[r])
        put_state(
            k, dst, r,
            [tile(src, r, t) + 0.25 * mask_tile(masks, r, t) * d[t] for t in range(5)],
        )
    return body

def section_2(k, cs, fs, masks, src, mid, dst):
    def body(r):
        d = tendency_row(k, mid, r, cs[r], fs[r])
        put_state(
            k, dst, r,
            [
                0.75 * tile(src, r, t) + 0.25 * tile(mid, r, t)
                + 0.0625 * mask_tile(masks, r, t) * d[t]
                for t in range(5)
            ],
        )
    return body


def section_3(k, cs, fs, masks, fluxes, mean, src, mid, net, r):
    d = tendency_row(k, mid, r, cs[r], fs[r])
    new = []
    for t in range(5):
        m = mask_tile(masks, r, t)
        o = tile(net, r, t)
        if t == 1:
            force = 2.0 * (mean - fluxes[r, 2:3, :])
            o = o + jnp.where(k.sub == 0, force, 0.0)
        new.append(
            (1.0 / 3.0) * tile(src, r, t) + (2.0 / 3.0) * tile(mid, r, t)
            + m * ((1.0 / 6.0) * d[t] + 0.25 * o)
        )
    return new


def zero_walls(ref):
    for row in (PAD - 1, PAD + ROWS):
        ref[row] = jnp.zeros(ref.shape[1:], F32)


def assemble_kernel(sides, scal, cs, fs, own, own_m, east, west, *rest):
    n = len(sides)
    side_refs = [rest[3 * i : 3 * i + 3] for i in range(n)]
    (k1, k2, k3, b2, b3), rest = rest[3 * n : 3 * n + 5], rest[3 * n + 5 :]
    s0, masks, fluxes, outs, window = rest
    k = Row(WIDE)
    has_south = scal[2]
    lo = lambda h: PAD - h * has_south

    zero_walls(s0)

    near_e, near_w = edges(REACH)

    def put_packed(row, core, halo):
        both = lambda t: jnp.concatenate([core(t), halo(t)], axis=1)
        put_state(k, s0, row, [both(t) for t in range(5)])
        masks[row, 0:8, :] = both(5)
        last = both(6)
        masks[row, 8:16, :] = jnp.where(k.low, last[1:2, :], last[0:1, :])
        fluxes[row] = last

    for r in range(ROWS):
        at = (r // 8) * PACK
        turn = SLOT * (r % 8)

        def halo(t):
            from_e = pltpu.roll(west[at + 8 * t : at + 8 * t + 8, :], -turn % COLS, 1)
            from_w = pltpu.roll(east[at + 8 * t : at + 8 * t + 8, :], -(turn + SLOT) % COLS, 1)
            return jnp.where(near_e, from_e, jnp.where(near_w, from_w, 0.0))

        put_packed(PAD + r, lambda t: own[r, 8 * t : 8 * t + 8, :], halo)
    for side, (lat_x, diag_e, diag_w) in zip(sides, side_refs):
        base = {"swap": scal[4], "north": PAD - REACH, "south": PAD + ROWS}[side]
        for r in range(REACH):

            def halo(t):
                rows = slice(8 * t, 8 * t + 8)
                from_e = pltpu.roll(diag_w[rows, :], -REACH * r % COLS, 1)
                from_w = pltpu.roll(diag_e[rows, :], -REACH * (r + 1) % COLS, 1)
                return jnp.where(near_e, from_e, jnp.where(near_w, from_w, 0.0))

            put_packed(base + r, lambda t: lat_x[r, 8 * t : 8 * t + 8, :], halo)

    of = lambda ref: ref[SUMS : SUMS + 2, :]
    sums = of(own.at[0]) + jnp.broadcast_to(of(east)[:, 0:1], (2, COLS))
    if sides == ["swap"]:
        lat_x, diag_e, _ = side_refs[0]
        sums = sums + (of(lat_x.at[0]) + jnp.broadcast_to(of(diag_e)[:, 0:1], (2, COLS)))
    window[...] = jnp.zeros((8, COLS), F32)
    window[0:2, :] = sums

    for r in range(ROWS):
        outs[PAD + r, :, 0:COLS] = own_m[r]

    def closure_of(columns):
        _, _, h2 = hidden_layers(split(to_48(columns, 1.0)), k1, k2, b2)
        return last_layer(h2, k3, b3)

    def halo_rows(first):
        o = closure_of(jnp.concatenate([s0[first + i, 0:FEATS, 0:COLS] for i in range(8)], axis=1))
        for i in range(8):
            outs[first + i, :, 0:COLS] = o[:, i * COLS : (i + 1) * COLS]

    if sides == ["swap"]:
        groups = 3
        halo_rows(jnp.where(has_south == 1, PAD - 8, PAD + ROWS))
    else:
        groups = 4
        halo_rows(PAD - 8)
        halo_rows(PAD + ROWS)
    first = lo(8)
    o = closure_of(jnp.concatenate([wide_pack(s0, first + 8 * g) for g in range(groups)], axis=1))
    for g in range(groups):
        wide_unpack(outs, first + 8 * g, o[:, g * COLS : (g + 1) * COLS])


def first_section_kernel(scal, cs, fs, s0, masks, s1):
    zero_walls(s1)
    for_rows(scal, 10, section_1(Row(WIDE), cs, fs, masks, s0, s1))


def second_section_kernel(scal, cs, fs, gate, s0, s1, masks, s2):
    zero_walls(s2)
    for_rows(scal, 9, section_2(Row(WIDE), cs, fs, masks, s0, s1, s2))


def last_section_kernel(scal, cs, fs, gate, sums, s3, t2, masks, fluxes, outs, final):
    k = Row(WIDE)
    mean = sums[0:1, 0:1] / sums[1:2, 0:1]

    def last(r):
        new = section_3(k, cs, fs, masks, fluxes, mean, s3, t2, outs, r)
        put_result(final, r - PAD, [x[:, 0:COLS] for x in new])

    for_rows(scal, 0, last)


def late_kernel(
    sides, scal, cs, fs, sums, own, cown, own_h1, own_h2, s0, s2, masks, fluxes, outs_in, east, west, *rest
):
    n = len(sides)
    side_refs = [rest[3 * i : 3 * i + 3] for i in range(n)]
    (k1, k2, k3, q1, q2, q3, b2, b3), rest = rest[3 * n : 3 * n + 8], rest[3 * n + 8 :]
    grads, s4, abuf, from_closure, s3, t2, outs, t1, cot, gz, bbuf, hold, left, acc = rest
    k = Row(WIDE)
    has_south = scal[2]
    lo = lambda h: PAD - h * has_south
    for ref in (s3, t1, t2, abuf, bbuf):
        zero_walls(ref)
    mean = sums[0:1, 0:1] / sums[1:2, 0:1]

    cnear_e, cnear_w = edges(CREACH)
    for r in range(ROWS):
        for t in range(5):
            rows = slice(2 * PACK + 8 * t, 2 * PACK + 8 * t + 8)
            from_e = pltpu.roll(west[rows, :], -8 * r % COLS, 1)
            from_w = pltpu.roll(east[rows, :], -8 * (r + 1) % COLS, 1)
            side = jnp.where(cnear_e, from_e, jnp.where(cnear_w, from_w, 0.0))
            cot[PAD + r, 8 * t : 8 * t + 8, :] = jnp.concatenate(
                [cown[r, 8 * t : 8 * t + 8, :], side], axis=1
            )
    for side, (lat_c, diag_e, diag_w) in zip(sides, side_refs):
        cbase = {"swap": scal[5], "north": PAD - CREACH, "south": PAD + ROWS}[side]
        crow = {"swap": scal[6], "north": ROWS - CREACH, "south": 0}[side]
        for r in range(CREACH):
            turn = lax.rem(2 * COLS - 8 * (crow + r), COLS)
            turn_w = lax.rem(2 * COLS - 8 * (crow + r + 1), COLS)
            for t in range(5):
                rows = slice(PACK + 8 * t, PACK + 8 * t + 8)
                from_e = pltpu.roll(diag_w[rows, :], turn, 1)
                from_w = pltpu.roll(diag_e[rows, :], turn_w, 1)
                part = jnp.where(cnear_e, from_e, jnp.where(cnear_w, from_w, 0.0))
                cot[cbase + r, 8 * t : 8 * t + 8, :] = jnp.concatenate(
                    [lat_c[r, 8 * t : 8 * t + 8, :], part], axis=1
                )


    def step_1_end(r):
        put_state(k, s3, r, section_3(s0, s2, r))

    def step_1_end(r):
        put_state(k, s3, r, section_3(k, cs, fs, masks, fluxes, mean, s0, s2, outs_in, r))

    for_rows(scal, 8, step_1_end)

    acc[...] = jnp.zeros(acc.shape, F32)

    def closure_adjoint(z, h1, h1s, h2, go, with_weights):
        gos = split(to_48(go))
        g2 = product(q3[...], *gos) * (1.0 - h2 * h2)
        g2s = split(g2)
        g1 = product(q2[...], *g2s) * (1.0 - h1 * h1)
        g1s = split(g1)
        if with_weights:
            add_weight_terms(acc, z, h1s, split(h2), g1s, g2s, gos)
        return product(q1[...], *g1s)[0:FEATS]

    def both_ways(columns, go, with_weights):
        z = split(to_48(columns, 1.0))
        h1, h1s, h2 = hidden_layers(z, k1, k2, b2)
        o = last_layer(h2, k3, b3) if with_weights else None
        return o, closure_adjoint(z, h1, h1s, h2, go, with_weights)

    def masked_core(ref, r):
        m0, m4 = masks[r, 0:8, 0:COLS], masks[r, 8:16, 0:COLS]
        parts = [
            0.25 * (m4 if t == 4 else m0) * ref[r, 8 * t : 8 * t + 8, 0:COLS] for t in range(5)
        ]
        return jnp.concatenate(parts, axis=0)

    def mask_cot(r):
        for t in range(5):
            bbuf[r, 8 * t : 8 * t + 8, :] = 0.25 * mask_tile(masks, r, t) * tile(cot, r, t)
            abuf[r, 8 * t : 8 * t + 8, :] = (1.0 / 6.0) * mask_tile(masks, r, t) * tile(cot, r, t)

    for_rows(scal, 6, mask_cot)

    for first in range(PAD, PAD + ROWS, 8):
        z = jnp.concatenate([s3[first + i, 0:FEATS, 0:COLS] for i in range(8)], axis=1)
        go = jnp.concatenate([bbuf[first + i, 0:FEATS, 0:COLS] for i in range(8)], axis=1)
        o, back = both_ways(z, go, True)
        for i in range(8):
            at = slice(i * COLS, (i + 1) * COLS)
            outs[first + i, :, 0:COLS] = o[:, at]
            gz[first + i, :, 0:COLS] = back[:, at]

    first = lo(4)
    if sides == ["swap"]:
        rows = [jnp.where(has_south == 1, PAD - 4, PAD + ROWS) + i for i in range(4)]
    else:
        rows = [PAD - 4 + i for i in range(4)] + [PAD + ROWS + i for i in range(4)]
    beyond = lambda ref: jnp.concatenate(
        [ref[r, 0:FEATS, 0:COLS] for r in rows] + [wide_pack(ref, first + 8 * g) for g in range(3)], axis=1
    )
    _, back = both_ways(beyond(s3), beyond(bbuf), False)
    for i, r in enumerate(rows):
        gz[r, :, 0:COLS] = back[:, i * COLS : (i + 1) * COLS]
    for g in range(3):
        at = (len(rows) + g) * COLS
        wide_unpack(gz, first + 8 * g, back[:, at : at + COLS])

    for_rows(scal, 7, section_1(k, cs, fs, masks, s3, t1))
    for_rows(scal, 6, section_2(k, cs, fs, masks, s3, t1, t2))

    def store(r, tiles):
        for t in range(5):
            s4[r, 8 * t : 8 * t + 8, :] = tiles[t] + tile(gz, r, t)

    adjoint_third(k, scal, cs, fs, 5, t2, masks, abuf, cot, hold, bbuf)
    adjoint_second(k, scal, cs, fs, 4, t1, masks, bbuf, cot, hold, left, abuf)
    adjoint_first(k, scal, cs, fs, 3, s3, abuf, left, store)

    for r in range(0, ROWS, 8):
        side = lambda read: jnp.concatenate([read(r + j) for j in range(8)], axis=1)
        z = split(to_48(side(lambda j: own[j, 0:FEATS, :]), 1.0))
        h1 = side(lambda j: own_h1[j])
        h2 = side(lambda j: own_h2[j])
        go = side(lambda j: masked_core(s4, PAD + j))
        back = closure_adjoint(z, h1, split(h1), h2, go, True)
        for j in range(8):
            from_closure[r + j] = back[:, j * COLS : (j + 1) * COLS]

    zero_walls(abuf)

    def mask_top(r):
        for t in range(5):
            abuf[r, 8 * t : 8 * t + 8, :] = (1.0 / 6.0) * mask_tile(masks, r, t) * tile(s4, r, t)

    for_rows(scal, 3, mask_top)
    grads[...] = jnp.zeros(grads.shape, F32)
    grads[0:40, 0:HID] = acc[0:40, 0:HID]
    grads[0:40, HID : 2 * HID] = acc[112:152, 0:HID]
    grads[40:72, 0:HID] = acc[48:80, 0:HID]
    grads[40:72, HID : 2 * HID] = acc[80:112, 0:HID]
    grads[72:73, 0:HID] = acc[40:41, 0:HID]
    grads[72:73, HID : 2 * HID] = acc[160:161, 0:HID]
    grads[73:74, 0:HID] = acc[176:177, 0:HID]


def put_result(ref, row, tiles):
    for t in range(4):
        ref[pl.ds(t * 10 * ROWS + row, 8, stride=ROWS), :] = tiles[t]
    ref[pl.ds(8 * ROWS + row, 4, stride=10 * ROWS), :] = tiles[4][0:4, :]
    ref[pl.ds(9 * ROWS + row, 4, stride=10 * ROWS), :] = tiles[4][4:8, :]


def back_third_kernel(scal, cs, fs, state, masks, abuf, top, hold, bbuf):
    zero_walls(bbuf)
    adjoint_third(Row(WIDE), scal, cs, fs, 2, state, masks, abuf, top, hold, bbuf)


def back_second_kernel(scal, cs, fs, gate, state, masks, bbuf, top, hold, left, abuf):
    zero_walls(abuf)
    adjoint_second(Row(WIDE), scal, cs, fs, 1, state, masks, bbuf, top, hold, left, abuf)


def back_first_kernel(scal, cs, fs, gate, state, masks, abuf, left, from_closure, grad):
    def store(r, tiles):
        done = []
        for t in range(5):
            m = masks[r, 8:16, 0:COLS] if t == 4 else masks[r, 0:8, 0:COLS]
            done.append(m * (tiles[t][:, 0:COLS] + from_closure[r - PAD, 8 * t : 8 * t + 8, :]))
        put_result(grad, r - PAD, done)

    adjoint_first(Row(WIDE), scal, cs, fs, 0, state, abuf, left, store)


def unpack_kernel(scale, packed, win, bin_, wmid, bmid, wout, bout):
    for ref, lanes in ((win, slice(0, HID)), (wout, slice(HID, 2 * HID))):
        for t in range(4):
            ref[10 * t : 10 * t + 8, :] = packed[8 * t : 8 * t + 8, lanes] * scale
            ref[10 * t + 8 : 10 * t + 9, :] = packed[32 + t : 33 + t, lanes] * scale
            ref[10 * t + 9 : 10 * t + 10, :] = packed[36 + t : 37 + t, lanes] * scale
    wmid[0:32, :] = packed[40:72, 0:HID] * scale
    wmid[32:64, :] = packed[40:72, HID : 2 * HID] * scale
    bin_[...] = packed[72:73, 0:HID] * scale
    bmid[...] = packed[72:73, HID : 2 * HID] * scale
    for t in range(4):
        bout[:, 10 * t : 10 * t + 8] = packed[73:74, 8 * t : 8 * t + 8] * scale
        bout[:, 10 * t + 8 : 10 * t + 9] = packed[73:74, 32 + t : 33 + t] * scale
        bout[:, 10 * t + 9 : 10 * t + 10] = packed[73:74, 36 + t : 37 + t] * scale


def pair_rounds(x, axes):
    rounds = []
    for axis, count in axes:
        if count & (count - 1):
            rounds.append(x := lax.psum(x, axis))
            continue
        stride = 1
        while stride < count:
            x = x + lax.ppermute(x, axis, [(i, i ^ stride) for i in range(count)])
            rounds.append(x)
            stride *= 2
    return rounds


def window_rounds(x, axis, count):
    rounds = [x]
    width = 2
    while width < count:
        x = x + lax.ppermute(x, axis, [(i, (i + width) % count) for i in range(count)])
        rounds.append(x)
        width *= 2
    return rounds


def latitude_terms(row_index, row_count):
    latitude = LAT_LIMIT * (2.0 * (jnp.clip(row_index, 0.0, row_count - 1.0) + 0.5) / row_count - 1.0)
    return 1.0 / jnp.cos(latitude), CORIOLIS * jnp.sin(latitude)


def on_device(
    initial_state, land_mask, surface_flux, weight_in, bias_in, weight_mid, bias_mid, weight_out, bias_out, cotangent
):
    lat_n, lon_n = lax.axis_size("lat"), lax.axis_size("lon")
    lat_i = lax.axis_index("lat")
    lat_total, lon_total = ROWS * lat_n, COLS * lon_n
    sides = ["swap"] if lat_n == 2 else ["north", "south"]
    is_low = (lat_i == 0).astype(jnp.int32)
    has_south = (lat_i > 0).astype(jnp.int32)
    has_north = (lat_i < lat_n - 1).astype(jnp.int32)
    scal = jnp.stack(
        [
            is_low * (ROWS - REACH),
            is_low * (ROWS - CREACH),
            has_south,
            has_north,
            jnp.where(is_low == 1, PAD + ROWS, PAD - REACH),
            jnp.where(is_low == 1, PAD + ROWS, PAD - CREACH),
            jnp.where(is_low == 1, 0, ROWS - CREACH),
        ]
    ).astype(jnp.int32)
    rows = (lat_i * ROWS - PAD + jnp.arange(EXT, dtype=jnp.int32)).astype(F32)
    cs, fs = latitude_terms(rows, lat_total)

    hbm = pl.BlockSpec(memory_space=pltpu.HBM)
    packed = pl.pallas_call(
        lambda *refs: pack_kernel(sides, *refs),
        out_shape=[
            sds(ROWS, PACK, COLS), sds(ROWS, FEATS, COLS), sds(2 * PACK + 40, COLS), sds(2 * PACK + 40, COLS),
        ]
        + [sds(REACH, PACK, COLS), sds(CREACH, FEATS, COLS), sds(PACK + 40, COLS), sds(PACK + 40, COLS)] * len(sides),
        in_specs=[SMEM] + [hbm] * 4,
        out_specs=[VMEM] * (4 + 4 * len(sides)),
        scratch_shapes=[
            pltpu.VMEM((40 * ROWS, COLS), F32), pltpu.VMEM((10 * ROWS, COLS), jnp.int32),
            pltpu.VMEM((ROWS, COLS), F32), pltpu.VMEM((40 * ROWS, COLS), F32), pltpu.SemaphoreType.DMA((4,)),
        ],
        compiler_params=params(8),
        name="pack_halos",
    )(
        scal,
        initial_state.reshape(40 * ROWS, COLS),
        land_mask.reshape(10 * ROWS, COLS),
        surface_flux,
        cotangent.reshape(40 * ROWS, COLS),
    )
    own, cown, east_pay, west_pay = packed[:4]

    def lat_pairs(side):
        if side == "swap":
            return [(0, 1), (1, 0)]
        if side == "north":
            return [(i, i + 1) for i in range(lat_n - 1)]
        return [(i + 1, i) for i in range(lat_n - 1)]

    def diagonal(side, step):
        return [
            (i * lat_n + a, ((i + step) % lon_n) * lat_n + b)
            for i in range(lon_n)
            for a, b in lat_pairs(side)
        ]

    east_ring = [(i, (i + 1) % lon_n) for i in range(lon_n)]
    west_ring = [((i + 1) % lon_n, i) for i in range(lon_n)]
    lat_x, lat_c, diags = [], [], []
    for i, side in enumerate(sides):
        pay_x, pay_c, diag_e, diag_w = packed[4 + 4 * i : 8 + 4 * i]
        lat_x.append(lax.ppermute(pay_x, "lat", lat_pairs(side)))
        diags.append(
            [
                lax.ppermute(diag_e, ("lon", "lat"), diagonal(side, 1)),
                lax.ppermute(diag_w, ("lon", "lat"), diagonal(side, -1)),
            ]
        )
        lat_c.append(lax.ppermute(pay_c, "lat", lat_pairs(side)))
    from_west = lax.ppermute(east_pay, "lon", east_ring)
    from_east = lax.ppermute(west_pay, "lon", west_ring)

    row = lambda b: b.reshape(1, -1)
    raw = (weight_in, weight_mid, weight_out, row(bias_in), row(bias_mid), row(bias_out))
    half = lambda *shape: jax.ShapeDtypeStruct(shape, BF16)
    own_m, own_h1, own_h2, k1, k2, k3, q1, q2, q3, b2, b3 = pl.pallas_call(
        own_closure_kernel,
        out_shape=[
            sds(ROWS, FEATS, COLS), sds(ROWS, HID, COLS), sds(ROWS, HID, COLS),
            half(HID, 144), half(HID, 192), half(48, 192), half(48, 192), half(HID, 192), half(HID, 144),
            sds(HID, COLS), sds(FEATS, COLS),
        ],
        in_specs=[VMEM] + [hbm] * 6,
        out_specs=[VMEM] * 11,
        scratch_shapes=[pltpu.VMEM(w.shape, F32) for w in raw]
        + [pltpu.VMEM((COLS, COLS), F32), pltpu.VMEM((COLS, COLS), F32), pltpu.VMEM((HID, WIDE), F32)]
        + [pltpu.SemaphoreType.DMA((6,))],
        compiler_params=params(12),
        cost_estimate=pl.CostEstimate(flops=10**9, bytes_accessed=2 * 10**6, transcendentals=0),
        name="own_closure",
    )(own, *raw)

    geometry = (scal, cs, fs)
    state = sds(EXT, 72, WIDE)
    plain = sds(EXT, FEATS, WIDE)
    marks = sds(EXT, 16, WIDE)
    vmem = lambda shape: pltpu.VMEM(shape.shape, F32)

    def call(kernel, name, out_shape, scratch, args, flops, limit):
        single = not isinstance(out_shape, list)
        return pl.pallas_call(
            kernel,
            out_shape=out_shape,
            in_specs=[SMEM] * 3 + [VMEM] * len(args),
            out_specs=VMEM if single else [VMEM] * len(out_shape),
            scratch_shapes=scratch,
            compiler_params=params(limit),
            cost_estimate=pl.CostEstimate(flops=flops, bytes_accessed=10**7, transcendentals=0),
            name=name,
        )(*geometry, *args)

    s0, masks, fluxes, net, window = call(
        lambda *refs: assemble_kernel(sides, *refs), "assemble",
        [state, marks, sds(EXT, 8, WIDE), plain, sds(8, COLS)], [],
        [own, own_m, from_west, from_east]
        + [ref for x, diag in zip(lat_x, diags) for ref in (x, *diag)] + [k1, k2, k3, b2, b3],
        2 * 10**9, 8,
    )
    means = window_rounds(window, "lon", lon_n)
    if sides != ["swap"]:
        means += pair_rounds(means[-1], (("lat", lat_n),))
    s1 = call(first_section_kernel, "first_section", state, [], [s0, masks], 10**9, 8)
    s2 = call(second_section_kernel, "second_section", state, [], [means[min(1, len(means) - 1)], s0, s1, masks], 10**9, 8)
    grads, top, abuf, from_closure, s3, t2, net_2 = call(
        lambda *refs: late_kernel(sides, *refs), "steps_and_adjoint",
        [sds(80, COLS), plain, plain, sds(ROWS, FEATS, COLS), state, state, plain],
        [vmem(state)] + [vmem(plain)] * 5 + [pltpu.VMEM((192, HID), F32)],
        [means[-1], own, cown, own_h1, own_h2, s0, s2, masks, fluxes, net, from_west, from_east]
        + [ref for c, diag in zip(lat_c, diags) for ref in (c, *diag)] + [k1, k2, k3, q1, q2, q3, b2, b3],
        4 * 10**9, 18,
    )
    rounds = pair_rounds(grads, (("lat", lat_n), ("lon", lon_n)))
    final = call(
        last_section_kernel, "last_section", sds(40 * ROWS, COLS), [],
        [rounds[min(2, len(rounds) - 1)], means[-1], s3, t2, masks, fluxes, net_2], 10**9, 8,
    )
    hold, bbuf = call(
        back_third_kernel, "adjoint_third_section", [plain, plain], [], [s2, masks, abuf, top], 10**9, 8
    )
    left, abuf = call(
        back_second_kernel, "adjoint_second_section", [plain, plain], [],
        [rounds[0], s1, masks, bbuf, top, hold], 10**9, 8,
    )
    state_grad = call(
        back_first_kernel, "adjoint_first_section", sds(40 * ROWS, COLS), [],
        [rounds[1], s0, masks, abuf, left, from_closure], 10**9, 8,
    )

    scale = 1.0 / math.sqrt(lat_total * lon_total)
    g_in, g_bin, g_mid, g_bmid, g_out, g_bout = pl.pallas_call(
        lambda *refs: unpack_kernel(scale, *refs),
        out_shape=[sds(40, HID), sds(1, HID), sds(HID, HID), sds(1, HID), sds(40, HID), sds(1, 40)],
        in_specs=[VMEM],
        out_specs=[VMEM] * 6,
        compiler_params=params(8),
        name="unpack_weight_grads",
    )(rounds[-1])
    shape = initial_state.shape
    return (
        final.reshape(shape),
        state_grad.reshape(shape),
        g_in,
        g_bin.reshape(-1),
        g_mid,
        g_bmid.reshape(-1),
        g_out.T,
        g_bout.reshape(-1),
    )


def solution(mesh):
    split_state = P(None, None, "lat", "lon")
    return jax.shard_map(
        on_device,
        mesh=mesh,
        in_specs=(split_state, P(None, "lat", "lon"), P("lat", "lon"), P(), P(), P(), P(), P(), P(), split_state),
        out_specs=(split_state, split_state, P(), P(), P(), P(), P(), P()),
        check_vma=False,
    )
```

```python
import math

import jax
import jax.numpy as jnp
from jax import lax
from jax.experimental import pallas as pl
from jax.experimental.pallas import tpu as pltpu
from jax.sharding import PartitionSpec as P

LAT_LIMIT = 1.2
CORIOLIS = 1.0
VISCOSITY = 0.15
DIFFUSIVITY = 0.1

ROWS = 16
COLS = 128
REACH = 11
CREACH = 6
PAD = 16
EXT = 48
TURN = 4
WIDE = 2 * COLS
FEATS = 40
HID = 64
PACK = 56
STRIP = 2 * PACK + 40
LAT_X = REACH * PACK
LAT = LAT_X + CREACH * FEATS
SLOT = 16
F32 = jnp.float32
BF16 = jnp.bfloat16
VMEM = pl.BlockSpec(memory_space=pltpu.VMEM)
SMEM = pl.BlockSpec(memory_space=pltpu.SMEM)


def params(megabytes):
    return pltpu.CompilerParams(vmem_limit_bytes=megabytes * 1024 * 1024)


def sds(*shape):
    return jax.ShapeDtypeStruct(shape, F32)


def sub_index(width):
    return lax.broadcasted_iota(jnp.int32, (8, width), 0)


def tile(ref, row, number):
    return ref[row, 8 * number : 8 * number + 8, :]


def slot_pack(pieces, shift_of, width):
    lane = lax.broadcasted_iota(jnp.int32, (8, COLS), 1)
    packed = None
    for slot, piece in enumerate(pieces):
        turned = pltpu.roll(piece, shift_of(slot) % COLS, 1)
        if packed is None:
            packed = turned
        else:
            packed = jnp.where((lane >= slot * width) & (lane < (slot + 1) * width), turned, packed)
    return packed


def pack_kernel(sides, scal, x_hbm, mask_hbm, flux_hbm, cot_hbm, *outs):
    x, mask, flux, cot, sems = outs[-5:]
    own, cown, east, west, sums = outs[:5]
    per_side = outs[5 : 5 + len(sides)]
    pairs = ((mask_hbm, mask), (x_hbm, x), (flux_hbm, flux), (cot_hbm, cot))
    copies = [pltpu.make_async_copy(a, b, sems.at[i]) for i, (a, b) in enumerate(pairs)]
    for copy in copies:
        copy.start()
    for copy in copies:
        copy.wait()
    top = mask[0:ROWS, :].astype(F32)
    total = jnp.sum(jnp.sum(top * flux[...], axis=1, keepdims=True), axis=0, keepdims=True)
    count = jnp.sum(jnp.sum(top, axis=1, keepdims=True), axis=0, keepdims=True)
    sums[...] = jnp.where(sub_index(COLS) == 0, total, jnp.where(sub_index(COLS) == 1, count, 0.0))
    for r in range(ROWS):
        first = mask[pl.ds(r, 8, stride=ROWS), :].astype(F32)
        m8 = mask[8 * ROWS + r : 8 * ROWS + r + 1, :].astype(F32)
        m9 = mask[9 * ROWS + r : 9 * ROWS + r + 1, :].astype(F32)
        for t in range(4):
            own[r, 8 * t : 8 * t + 8, :] = x[pl.ds(t * 10 * ROWS + r, 8, stride=ROWS), :] * first
            cown[r, 8 * t : 8 * t + 8, :] = cot[pl.ds(t * 10 * ROWS + r, 8, stride=ROWS), :]
        for level, m in ((8, m8), (9, m9)):
            at = 32 + 4 * (level - 8)
            own[r, at : at + 4, :] = x[pl.ds(level * ROWS + r, 4, stride=10 * ROWS), :] * m
            cown[r, at : at + 4, :] = cot[pl.ds(level * ROWS + r, 4, stride=10 * ROWS), :]
        own[r, 40:48, :] = first
        own[r, 48:49, :] = m8
        own[r, 49:50, :] = m9
        own[r, 50:51, :] = flux[r : r + 1, :]
        own[r, 51:56, :] = jnp.zeros((5, COLS), F32)
    for half in range(2):
        for t in range(7):
            rows = [own[8 * half + s, 8 * t : 8 * t + 8, :] for s in range(8)]
            at = half * PACK + 8 * t
            east[at : at + 8, :] = slot_pack(rows, lambda s: SLOT * (s + 1), SLOT)
            west[at : at + 8, :] = slot_pack(rows, lambda s: SLOT * s, SLOT)
    for t in range(5):
        rows = [cown[s, 8 * t : 8 * t + 8, :] for s in range(ROWS)]
        at = 2 * PACK + 8 * t
        east[at : at + 8, :] = slot_pack(rows, lambda s: 8 * (s + 1), 8)
        west[at : at + 8, :] = slot_pack(rows, lambda s: 8 * s, 8)
    for side, lat in zip(sides, per_side):
        start = {"swap": scal[0], "north": ROWS - REACH, "south": 0}[side]
        cstart = {"swap": scal[1], "north": ROWS - CREACH, "south": 0}[side]
        for n in range(REACH):
            lat[PACK * n : PACK * (n + 1), :] = own[start + n]
        for n in range(CREACH):
            lat[LAT_X + FEATS * n : LAT_X + FEATS * (n + 1), :] = cown[cstart + n]


def corner_kernel(sides, scal, east, west, *outs):
    for side, corner in zip(sides, outs):
        start = {"swap": scal[0], "north": ROWS - REACH, "south": 0}[side]
        for at, strip, near in ((0, east, 1), (PACK + 40, west, 0)):
            for t in range(7):
                rows = slice(at + 8 * t, at + 8 * t + 8)
                corner[rows, :] = shift_rows(strip, t, start, near)
            corner[at + PACK : at + PACK + 40, :] = strip[2 * PACK : 2 * PACK + 40, :]


def shift_rows(strip, t, start, near):
    lane = lax.broadcasted_iota(jnp.int32, (8, COLS), 1)
    halves = [strip[8 * t : 8 * t + 8, :], strip[PACK + 8 * t : PACK + 8 * t + 8, :]]
    if isinstance(start, int):
        out = jnp.zeros((8, COLS), F32)
        for n in range(REACH):
            r = start + n
            turn = REACH * n - (SLOT * (r % 8) + near * (SLOT - REACH))
            turned = pltpu.roll(halves[r // 8], turn % COLS, 1)
            out = jnp.where((lane >= REACH * n) & (lane < REACH * (n + 1)), turned, out)
        return out
    low = shift_rows(strip, t, 0, near)
    high = shift_rows(strip, t, ROWS - REACH, near)
    return jnp.where(start == 0, low, high)


def split(values):
    high = values.astype(BF16)
    return high, (values - high.astype(F32)).astype(BF16)


def stack(out, values, buffer):
    k = values.shape[1]
    rows = slice(0, values.shape[0])
    high, low = split(values)
    buffer[rows, 0:k] = high.astype(F32)
    buffer[rows, k : 2 * k] = high.astype(F32)
    buffer[rows, 2 * k : 3 * k] = low.astype(F32)
    out[...] = buffer[rows, 0 : 3 * k].astype(BF16)


def by_tile(dst, src, lanes):
    for t in range(4):
        dst[8 * t : 8 * t + 8, lanes] = src[10 * t : 10 * t + 8, lanes]
        dst[32 + t : 33 + t, lanes] = src[10 * t + 8 : 10 * t + 9, lanes]
        dst[36 + t : 37 + t, lanes] = src[10 * t + 9 : 10 * t + 10, lanes]


def product(weights, high, low):
    return jnp.dot(weights, jnp.concatenate([high, low, high], axis=0), preferred_element_type=F32)


def across(a, b):
    dims = (((1,), (1,)), ((), ()))
    dot = lambda p, q: lax.dot_general(p, q, dims, preferred_element_type=F32)
    return dot(a[0], b[0]) + dot(a[0], b[1]) + dot(a[1], b[0])


def to_48(columns, first=0.0):
    more = jnp.where(sub_index(columns.shape[1]) == 0, first, 0.0).astype(F32)
    return jnp.concatenate([columns, more], axis=0)


def wide(bias, values):
    return jnp.concatenate([bias[...]] * (values.shape[1] // COLS), axis=1)


def hidden_layers(z, k1, k2, b2):
    h1 = jnp.tanh(product(k1[...], *z))
    h1s = split(h1)
    h2 = product(k2[...], *h1s)
    return h1, h1s, jnp.tanh(h2 + wide(b2, h2))


def last_layer(h2, k3, b3):
    o = product(k3[...], *split(h2))[0:FEATS]
    return o + wide(b3, o)


def add_weight_terms(acc, z, h1s, h2s, g1s, g2s, gos):
    ones = jnp.ones((16, z[0].shape[1]), BF16)
    acc[0:48, 0:HID] += across(z, g1s)
    acc[48:112, 0:HID] += across(h1s, g2s)
    acc[112:160, 0:HID] += across(gos, h2s)
    acc[160:176, 0:HID] += ones_rows(ones, g2s)
    acc[176:192, 0:48] += ones_rows(ones, gos)


def ones_rows(ones, g):
    dims = (((1,), (1,)), ((), ()))
    dot = lambda q: lax.dot_general(ones, q, dims, preferred_element_type=F32)
    return dot(g[0]) + dot(g[1])


def own_closure_kernel(own, *refs):
    raw, (out, h1_out, h2_out, k1, k2, k3, q1, q2, q3, b2, b3) = refs[:6], refs[6:17]
    w_in, w_mid, w_out, b_in, b_mid, b_out = refs[17:23]
    buffer, spare, stacked, sems = refs[23:]
    copies = [pltpu.make_async_copy(a, b, sems.at[i]) for i, (a, b) in enumerate(zip(raw, refs[17:23]))]
    for copy in copies:
        copy.start()
    for copy in copies:
        copy.wait()
    buffer[...] = jnp.zeros(buffer.shape, F32)
    by_tile(buffer, w_in, slice(0, HID))
    buffer[40:41, 0:HID] = b_in[...]
    stack(q1, buffer[0:48, 0:HID], stacked)
    spare[...] = buffer[...].T
    stack(k1, spare[0:HID, 0:48], stacked)
    buffer[0:HID, 0:HID] = w_mid[...]
    buffer[HID : HID + 1, 0:HID] = b_mid[...]
    stack(q2, buffer[0:HID, 0:HID], stacked)
    spare[...] = buffer[...].T
    stack(k2, spare[0:HID, 0:HID], stacked)
    b2[...] = jnp.broadcast_to(spare[0:HID, HID : HID + 1], (HID, COLS))
    buffer[...] = jnp.zeros(buffer.shape, F32)
    buffer[0:HID, 0:FEATS] = w_out[...]
    buffer[HID : HID + 1, 0:FEATS] = b_out[...]
    spare[...] = buffer[...].T
    buffer[...] = jnp.zeros(buffer.shape, F32)
    by_tile(buffer, spare, slice(0, COLS))
    stack(k3, buffer[0:48, 0:HID], stacked)
    b3[...] = jnp.broadcast_to(buffer[0:FEATS, HID : HID + 1], (FEATS, COLS))
    spare[...] = buffer[...].T
    stack(q3, spare[0:HID, 0:48], stacked)

    for r in range(0, ROWS, 8):
        z = split(to_48(jnp.concatenate([own[r + n, 0:FEATS, :] for n in range(8)], axis=1), 1.0))
        h1, h1s, h2 = hidden_layers(z, k1, k2, b2)
        o = last_layer(h2, k3, b3)
        for n in range(8):
            at = slice(n * COLS, (n + 1) * COLS)
            out[r + n] = o[:, at]
            h1_out[r + n] = h1[:, at]
            h2_out[r + n] = h2[:, at]


class Row:
    def __init__(self, width):
        sub = sub_index(width)
        group = sub % 4
        self.sub = sub
        self.is_t = group == 0
        self.is_s = group == 1
        self.is_u = group == 2
        self.is_v = group == 3
        self.low = sub >= 4
        self.k4 = jnp.where(group < 2, DIFFUSIVITY, VISCOSITY).astype(F32)


def derived(k, temp, salt, mixed):
    zero = jnp.zeros_like(temp)
    press = 0.4 * salt - 0.1 * temp
    for by in (1, 2, 4):
        press = press + jnp.where(k.sub >= by, pltpu.roll(press, by, 0), zero)
    deep = jnp.where(k.is_t, 0.4 * pltpu.roll(mixed, 7, 0) - 0.1 * mixed, zero)
    deep = deep + jnp.where(k.low, pltpu.roll(deep, 4, 0), zero)
    deep = deep + pltpu.roll(deep, 1, 0)
    deep = deep + pltpu.roll(deep, 2, 0) + press[7:8, :]
    u4, v4 = deep_velocity(k, mixed)
    return press, deep, u4, v4


def deep_velocity(k, mixed):
    zero = jnp.zeros_like(mixed)
    u4 = jnp.where(k.is_u, mixed, zero)
    u4 = u4 + pltpu.roll(u4, 1, 0)
    u4 = u4 + pltpu.roll(u4, 6, 0)
    v4 = jnp.where(k.is_v, mixed, zero)
    v4 = v4 + pltpu.roll(v4, 7, 0)
    v4 = v4 + pltpu.roll(v4, 6, 0)
    return u4, v4


def put_state(k, ref, row, tiles):
    for t in range(5):
        ref[row, 8 * t : 8 * t + 8, :] = tiles[t]
    for t, values in enumerate(derived(k, tiles[0], tiles[1], tiles[4])):
        ref[row, 40 + 8 * t : 48 + 8 * t, :] = values


def east_of(q):
    return pltpu.roll(q, q.shape[1] - 1, 1)


def west_of(q):
    return pltpu.roll(q, 1, 1)


def tendency_row(k, ref, row, c, f):
    half = 0.5 * c
    c2 = c * c
    u, v = tile(ref, row, 2), tile(ref, row, 3)
    u4, v4 = tile(ref, row, 7), tile(ref, row, 8)
    uh, vh = u * half, v * 0.5
    u4h, v4h = u4 * half, v4 * 0.5
    change = []
    for t in range(5):
        q = tile(ref, row, t)
        e, w = east_of(q), west_of(q)
        n, s = tile(ref, row + 1, t), tile(ref, row - 1, t)
        lap = c2 * (e + w) + (n + s) - (2.0 * c2 + 2.0) * q
        gain = k.k4 if t == 4 else (DIFFUSIVITY if t < 2 else VISCOSITY)
        au, av = (u4h, v4h) if t == 4 else (uh, vh)
        change.append(gain * lap - (au * (e - w) + av * (n - s)))
    p = tile(ref, row, 5)
    change[2] = change[2] + (f * v - half * (east_of(p) - west_of(p)))
    change[3] = change[3] - (f * u + 0.5 * (tile(ref, row + 1, 5) - tile(ref, row - 1, 5)))
    p4 = tile(ref, row, 6)
    zero = jnp.zeros_like(p4)
    fx = f * v4 - half * (east_of(p4) - west_of(p4))
    fy = f * u4 + 0.5 * (tile(ref, row + 1, 6) - tile(ref, row - 1, 6))
    change[4] = change[4] + jnp.where(k.is_u, fx, jnp.where(k.is_v, -fy, zero))
    return change


def adjoint_row(k, ref, aref, row, c, f):
    half = 0.5 * c
    c2 = c * c
    u4 = tile(ref, row, 7)
    qe = [east_of(tile(ref, row, t)) for t in range(5)]
    qw = [west_of(tile(ref, row, t)) for t in range(5)]
    u4e, u4w = east_of(u4), west_of(u4)
    out = []
    to_u = to_v = None
    for t in range(5):
        a = tile(aref, row, t)
        ae, aw = east_of(a), west_of(a)
        an, as_ = tile(aref, row + 1, t), tile(aref, row - 1, t)
        gain = k.k4 if t == 4 else (DIFFUSIVITY if t < 2 else VISCOSITY)
        ue, uw = (u4e, u4w) if t == 4 else (qe[2], qw[2])
        which = 8 if t == 4 else 3
        vn, vs = tile(ref, row + 1, which), tile(ref, row - 1, which)
        lap = c2 * (ae + aw) + (an + as_) - (2.0 * c2 + 2.0) * a
        out.append(gain * lap + half * (ue * ae - uw * aw) + 0.5 * (vn * an - vs * as_))
        px = a * (qe[t] - qw[t])
        py = a * (tile(ref, row + 1, t) - tile(ref, row - 1, t))
        if t < 4:
            to_u = px if to_u is None else to_u + px
            to_v = py if to_v is None else to_v + py
        if t == 2:
            a2, bx = a, half * (ae - aw)
        if t == 3:
            a3, by = a, 0.5 * (an - as_)
        if t == 4:
            a4 = a
            deep_bx, deep_by = half * (ae - aw), 0.5 * (an - as_)
            px4, py4 = px * half, py * 0.5
    out[2] = out[2] - half * to_u - f * a3
    out[3] = out[3] - 0.5 * to_v + f * a2
    zero = jnp.zeros_like(a4)
    sx = px4 + pltpu.roll(px4, 7, 0)
    sx = sx + pltpu.roll(sx, 2, 0)
    sy = py4 + pltpu.roll(py4, 1, 0)
    sy = sy + pltpu.roll(sy, 2, 0)
    at_u = -sx - f * pltpu.roll(a4, 7, 0)
    at_v = f * pltpu.roll(a4, 1, 0) - sy
    deep = jnp.where(k.is_t, pltpu.roll(deep_bx, 6, 0) + pltpu.roll(deep_by, 5, 0), zero)
    deep = deep + jnp.where(k.low, zero, pltpu.roll(deep, 4, 0))
    press = bx + by
    for shift in (1, 2, 4):
        press = press + jnp.where(k.sub < 8 - shift, pltpu.roll(press, 8 - shift, 0), zero)
    press = press + deep[0:1, :]
    out[0] = out[0] - 0.1 * press
    out[1] = out[1] + 0.4 * press
    out[4] = out[4] + jnp.where(
        k.is_t,
        -0.1 * deep,
        jnp.where(k.is_s, 0.4 * pltpu.roll(deep, 1, 0), jnp.where(k.is_u, at_u, at_v)),
    )
    return out


def for_rows(scal, reach, body):
    low, high = PAD - reach * scal[2], PAD + ROWS + reach * scal[3]
    turns = lax.div(high - low + TURN - 1, TURN)
    first = jnp.where(scal[3] == 1, low, high - TURN * turns)

    def turn(i, _):
        for j in range(TURN):
            body(first + TURN * i + j)
        return 0

    lax.fori_loop(0, turns, turn, 0)


def mask_tile(ref, row, t):
    return tile(ref, row, 1 if t == 4 else 0)


def adjoint_third(k, scal, cs, fs, reach, state, masks, abuf, top, hold, bbuf):
    def body(r):
        d = adjoint_row(k, state, abuf, r, cs[r], fs[r])
        for t in range(5):
            ts = (2.0 / 3.0) * tile(top, r, t) + d[t]
            hold[r, 8 * t : 8 * t + 8, :] = ts
            bbuf[r, 8 * t : 8 * t + 8, :] = 0.0625 * mask_tile(masks, r, t) * ts

    for_rows(scal, reach, body)


def adjoint_second(k, scal, cs, fs, reach, state, masks, bbuf, top, hold, left, abuf):
    def body(r):
        d = adjoint_row(k, state, bbuf, r, cs[r], fs[r])
        for t in range(5):
            ts = tile(hold, r, t)
            tf = 0.25 * ts + d[t]
            left[r, 8 * t : 8 * t + 8, :] = (1.0 / 3.0) * tile(top, r, t) + 0.75 * ts + tf
            abuf[r, 8 * t : 8 * t + 8, :] = 0.25 * mask_tile(masks, r, t) * tf

    for_rows(scal, reach, body)


def adjoint_first(k, scal, cs, fs, reach, state, abuf, left, store):
    def body(r):
        d = adjoint_row(k, state, abuf, r, cs[r], fs[r])
        store(r, [tile(left, r, t) + d[t] for t in range(5)])

    for_rows(scal, reach, body)


def edges(reach):
    lane = lax.broadcasted_iota(jnp.int32, (8, COLS), 1)
    return lane < reach, lane >= COLS - reach


def wide_pack(ref, base):
    parts = []
    for t in range(5):
        rows = [ref[base + s, 8 * t : 8 * t + 8, COLS:WIDE] for s in range(8)]
        parts.append(slot_pack(rows, lambda s: 8 + SLOT * s, SLOT))
    return jnp.concatenate(parts, axis=0)

def wide_unpack(ref, base, values):
    for s in range(8):
        ref[base + s, 0:FEATS, COLS:WIDE] = pltpu.roll(values, -(8 + SLOT * s) % COLS, 1)


def section_1(k, cs, fs, masks, src, dst):
    def body(r):
        d = tendency_row(k, src, r, cs[r], fs[r])
        put_state(
            k, dst, r,
            [tile(src, r, t) + 0.25 * mask_tile(masks, r, t) * d[t] for t in range(5)],
        )
    return body

def section_2(k, cs, fs, masks, src, mid, dst):
    def body(r):
        d = tendency_row(k, mid, r, cs[r], fs[r])
        put_state(
            k, dst, r,
            [
                0.75 * tile(src, r, t) + 0.25 * tile(mid, r, t)
                + 0.0625 * mask_tile(masks, r, t) * d[t]
                for t in range(5)
            ],
        )
    return body


def section_3(k, cs, fs, masks, fluxes, mean, src, mid, net, r):
    d = tendency_row(k, mid, r, cs[r], fs[r])
    new = []
    for t in range(5):
        m = mask_tile(masks, r, t)
        o = tile(net, r, t)
        if t == 1:
            force = 2.0 * (mean - fluxes[r, 2:3, :])
            o = o + jnp.where(k.sub == 0, force, 0.0)
        new.append(
            (1.0 / 3.0) * tile(src, r, t) + (2.0 / 3.0) * tile(mid, r, t)
            + m * ((1.0 / 6.0) * d[t] + 0.25 * o)
        )
    return new


def zero_walls(ref):
    for row in (PAD - 1, PAD + ROWS):
        ref[row] = jnp.zeros(ref.shape[1:], F32)


def assemble_kernel(sides, scal, cs, fs, gate, own, own_m, east, west, *rest):
    n = len(sides)
    side_refs = [rest[2 * i : 2 * i + 2] for i in range(n)]
    (k1, k2, k3, b2, b3), rest = rest[2 * n : 2 * n + 5], rest[2 * n + 5 :]
    s0, masks, fluxes, outs = rest
    k = Row(WIDE)
    has_south = scal[2]
    lo = lambda h: PAD - h * has_south

    zero_walls(s0)

    near_e, near_w = edges(REACH)

    def put_packed(row, core, halo):
        both = lambda t: jnp.concatenate([core(t), halo(t)], axis=1)
        put_state(k, s0, row, [both(t) for t in range(5)])
        masks[row, 0:8, :] = both(5)
        last = both(6)
        masks[row, 8:16, :] = jnp.where(k.low, last[1:2, :], last[0:1, :])
        fluxes[row] = last

    for r in range(ROWS):
        at = (r // 8) * PACK
        turn = SLOT * (r % 8)

        def halo(t):
            from_e = pltpu.roll(west[at + 8 * t : at + 8 * t + 8, :], -turn % COLS, 1)
            from_w = pltpu.roll(east[at + 8 * t : at + 8 * t + 8, :], -(turn + SLOT) % COLS, 1)
            return jnp.where(near_e, from_e, jnp.where(near_w, from_w, 0.0))

        put_packed(PAD + r, lambda t: own[r, 8 * t : 8 * t + 8, :], halo)
    for side, (lat, corner) in zip(sides, side_refs):
        base = {"swap": scal[4], "north": PAD - REACH, "south": PAD + ROWS}[side]
        for r in range(REACH):

            def halo(t):
                wrows = slice(8 * t, 8 * t + 8)
                erows = slice(PACK + 40 + 8 * t, PACK + 48 + 8 * t)
                from_e = pltpu.roll(corner[erows, :], -REACH * r % COLS, 1)
                from_w = pltpu.roll(corner[wrows, :], -REACH * (r + 1) % COLS, 1)
                return jnp.where(near_e, from_e, jnp.where(near_w, from_w, 0.0))

            put_packed(base + r, lambda t: lat[PACK * r + 8 * t : PACK * r + 8 * t + 8, :], halo)

    for r in range(ROWS):
        outs[PAD + r, :, 0:COLS] = own_m[r]

    def closure_of(columns):
        _, _, h2 = hidden_layers(split(to_48(columns, 1.0)), k1, k2, b2)
        return last_layer(h2, k3, b3)

    def halo_rows(first):
        o = closure_of(jnp.concatenate([s0[first + i, 0:FEATS, 0:COLS] for i in range(8)], axis=1))
        for i in range(8):
            outs[first + i, :, 0:COLS] = o[:, i * COLS : (i + 1) * COLS]

    if sides == ["swap"]:
        groups = 3
        halo_rows(jnp.where(has_south == 1, PAD - 8, PAD + ROWS))
    else:
        groups = 4
        halo_rows(PAD - 8)
        halo_rows(PAD + ROWS)
    first = lo(8)
    o = closure_of(jnp.concatenate([wide_pack(s0, first + 8 * g) for g in range(groups)], axis=1))
    for g in range(groups):
        wide_unpack(outs, first + 8 * g, o[:, g * COLS : (g + 1) * COLS])


def first_section_kernel(scal, cs, fs, s0, masks, s1):
    zero_walls(s1)
    for_rows(scal, 10, section_1(Row(WIDE), cs, fs, masks, s0, s1))


def second_section_kernel(scal, cs, fs, s0, s1, masks, s2):
    zero_walls(s2)
    for_rows(scal, 9, section_2(Row(WIDE), cs, fs, masks, s0, s1, s2))


def last_section_kernel(scal, cs, fs, gate, sums, s3, t2, masks, fluxes, outs, final):
    k = Row(WIDE)
    mean = sums[0:1, 0:1] / sums[1:2, 0:1]

    def last(r):
        new = section_3(k, cs, fs, masks, fluxes, mean, s3, t2, outs, r)
        put_result(final, r - PAD, [x[:, 0:COLS] for x in new])

    for_rows(scal, 0, last)


def late_kernel(
    sides, scal, cs, fs, sums, own, cown, own_h1, own_h2, s0, s2, masks, fluxes, outs_in, east, west, *rest
):
    n = len(sides)
    side_refs = [rest[2 * i : 2 * i + 2] for i in range(n)]
    (k1, k2, k3, q1, q2, q3, b2, b3), rest = rest[2 * n : 2 * n + 8], rest[2 * n + 8 :]
    grads, s4, abuf, from_closure, s3, t2, outs, t1, cot, gz, bbuf, hold, left, acc = rest
    k = Row(WIDE)
    has_south = scal[2]
    lo = lambda h: PAD - h * has_south
    for ref in (s3, t1, t2, abuf, bbuf):
        zero_walls(ref)
    mean = sums[0:1, 0:1] / sums[1:2, 0:1]

    cnear_e, cnear_w = edges(CREACH)
    for r in range(ROWS):
        for t in range(5):
            rows = slice(2 * PACK + 8 * t, 2 * PACK + 8 * t + 8)
            from_e = pltpu.roll(west[rows, :], -8 * r % COLS, 1)
            from_w = pltpu.roll(east[rows, :], -8 * (r + 1) % COLS, 1)
            side = jnp.where(cnear_e, from_e, jnp.where(cnear_w, from_w, 0.0))
            cot[PAD + r, 8 * t : 8 * t + 8, :] = jnp.concatenate(
                [cown[r, 8 * t : 8 * t + 8, :], side], axis=1
            )
    for side, (lat, corner) in zip(sides, side_refs):
        cbase = {"swap": scal[5], "north": PAD - CREACH, "south": PAD + ROWS}[side]
        crow = {"swap": scal[6], "north": ROWS - CREACH, "south": 0}[side]
        for r in range(CREACH):
            turn = lax.rem(2 * COLS - 8 * (crow + r), COLS)
            turn_w = lax.rem(2 * COLS - 8 * (crow + r + 1), COLS)
            for t in range(5):
                wrows = slice(PACK + 8 * t, PACK + 8 * t + 8)
                erows = slice(2 * PACK + 40 + 8 * t, 2 * PACK + 48 + 8 * t)
                from_e = pltpu.roll(corner[erows, :], turn, 1)
                from_w = pltpu.roll(corner[wrows, :], turn_w, 1)
                part = jnp.where(cnear_e, from_e, jnp.where(cnear_w, from_w, 0.0))
                cot[cbase + r, 8 * t : 8 * t + 8, :] = jnp.concatenate(
                    [lat[LAT_X + FEATS * r + 8 * t : LAT_X + FEATS * r + 8 * t + 8, :], part], axis=1
                )


    def step_1_end(r):
        put_state(k, s3, r, section_3(s0, s2, r))

    def step_1_end(r):
        put_state(k, s3, r, section_3(k, cs, fs, masks, fluxes, mean, s0, s2, outs_in, r))

    for_rows(scal, 8, step_1_end)

    acc[...] = jnp.zeros(acc.shape, F32)

    def closure_adjoint(z, h1, h1s, h2, go, with_weights):
        gos = split(to_48(go))
        g2 = product(q3[...], *gos) * (1.0 - h2 * h2)
        g2s = split(g2)
        g1 = product(q2[...], *g2s) * (1.0 - h1 * h1)
        g1s = split(g1)
        if with_weights:
            add_weight_terms(acc, z, h1s, split(h2), g1s, g2s, gos)
        return product(q1[...], *g1s)[0:FEATS]

    def both_ways(columns, go, with_weights):
        z = split(to_48(columns, 1.0))
        h1, h1s, h2 = hidden_layers(z, k1, k2, b2)
        o = last_layer(h2, k3, b3) if with_weights else None
        return o, closure_adjoint(z, h1, h1s, h2, go, with_weights)

    def masked_core(ref, r):
        m0, m4 = masks[r, 0:8, 0:COLS], masks[r, 8:16, 0:COLS]
        parts = [
            0.25 * (m4 if t == 4 else m0) * ref[r, 8 * t : 8 * t + 8, 0:COLS] for t in range(5)
        ]
        return jnp.concatenate(parts, axis=0)

    def mask_cot(r):
        for t in range(5):
            bbuf[r, 8 * t : 8 * t + 8, :] = 0.25 * mask_tile(masks, r, t) * tile(cot, r, t)
            abuf[r, 8 * t : 8 * t + 8, :] = (1.0 / 6.0) * mask_tile(masks, r, t) * tile(cot, r, t)

    for_rows(scal, 6, mask_cot)

    for first in range(PAD, PAD + ROWS, 8):
        z = jnp.concatenate([s3[first + i, 0:FEATS, 0:COLS] for i in range(8)], axis=1)
        go = jnp.concatenate([bbuf[first + i, 0:FEATS, 0:COLS] for i in range(8)], axis=1)
        o, back = both_ways(z, go, True)
        for i in range(8):
            at = slice(i * COLS, (i + 1) * COLS)
            outs[first + i, :, 0:COLS] = o[:, at]
            gz[first + i, :, 0:COLS] = back[:, at]

    first = lo(4)
    if sides == ["swap"]:
        rows = [jnp.where(has_south == 1, PAD - 4, PAD + ROWS) + i for i in range(4)]
    else:
        rows = [PAD - 4 + i for i in range(4)] + [PAD + ROWS + i for i in range(4)]
    beyond = lambda ref: jnp.concatenate(
        [ref[r, 0:FEATS, 0:COLS] for r in rows] + [wide_pack(ref, first + 8 * g) for g in range(3)], axis=1
    )
    _, back = both_ways(beyond(s3), beyond(bbuf), False)
    for i, r in enumerate(rows):
        gz[r, :, 0:COLS] = back[:, i * COLS : (i + 1) * COLS]
    for g in range(3):
        at = (len(rows) + g) * COLS
        wide_unpack(gz, first + 8 * g, back[:, at : at + COLS])

    for_rows(scal, 7, section_1(k, cs, fs, masks, s3, t1))
    for_rows(scal, 6, section_2(k, cs, fs, masks, s3, t1, t2))

    def store(r, tiles):
        for t in range(5):
            s4[r, 8 * t : 8 * t + 8, :] = tiles[t] + tile(gz, r, t)

    adjoint_third(k, scal, cs, fs, 5, t2, masks, abuf, cot, hold, bbuf)
    adjoint_second(k, scal, cs, fs, 4, t1, masks, bbuf, cot, hold, left, abuf)
    adjoint_first(k, scal, cs, fs, 3, s3, abuf, left, store)

    for r in range(0, ROWS, 8):
        side = lambda read: jnp.concatenate([read(r + j) for j in range(8)], axis=1)
        z = split(to_48(side(lambda j: own[j, 0:FEATS, :]), 1.0))
        h1 = side(lambda j: own_h1[j])
        h2 = side(lambda j: own_h2[j])
        go = side(lambda j: masked_core(s4, PAD + j))
        back = closure_adjoint(z, h1, split(h1), h2, go, True)
        for j in range(8):
            from_closure[r + j] = back[:, j * COLS : (j + 1) * COLS]

    zero_walls(abuf)

    def mask_top(r):
        for t in range(5):
            abuf[r, 8 * t : 8 * t + 8, :] = (1.0 / 6.0) * mask_tile(masks, r, t) * tile(s4, r, t)

    for_rows(scal, 3, mask_top)
    grads[...] = jnp.zeros(grads.shape, F32)
    grads[0:40, 0:HID] = acc[0:40, 0:HID]
    grads[0:40, HID : 2 * HID] = acc[112:152, 0:HID]
    grads[40:72, 0:HID] = acc[48:80, 0:HID]
    grads[40:72, HID : 2 * HID] = acc[80:112, 0:HID]
    grads[72:73, 0:HID] = acc[40:41, 0:HID]
    grads[72:73, HID : 2 * HID] = acc[160:161, 0:HID]
    grads[73:74, 0:HID] = acc[176:177, 0:HID]


def put_result(ref, row, tiles):
    for t in range(4):
        ref[pl.ds(t * 10 * ROWS + row, 8, stride=ROWS), :] = tiles[t]
    ref[pl.ds(8 * ROWS + row, 4, stride=10 * ROWS), :] = tiles[4][0:4, :]
    ref[pl.ds(9 * ROWS + row, 4, stride=10 * ROWS), :] = tiles[4][4:8, :]


def back_third_kernel(scal, cs, fs, state, masks, abuf, top, hold, bbuf):
    zero_walls(bbuf)
    adjoint_third(Row(WIDE), scal, cs, fs, 2, state, masks, abuf, top, hold, bbuf)


def back_second_kernel(scal, cs, fs, gate, state, masks, bbuf, top, hold, left, abuf):
    zero_walls(abuf)
    adjoint_second(Row(WIDE), scal, cs, fs, 1, state, masks, bbuf, top, hold, left, abuf)


def back_first_kernel(scal, cs, fs, gate, state, masks, abuf, left, from_closure, grad):
    def store(r, tiles):
        done = []
        for t in range(5):
            m = masks[r, 8:16, 0:COLS] if t == 4 else masks[r, 0:8, 0:COLS]
            done.append(m * (tiles[t][:, 0:COLS] + from_closure[r - PAD, 8 * t : 8 * t + 8, :]))
        put_result(grad, r - PAD, done)

    adjoint_first(Row(WIDE), scal, cs, fs, 0, state, abuf, left, store)


def unpack_kernel(scale, packed, win, bin_, wmid, bmid, wout, bout):
    for ref, lanes in ((win, slice(0, HID)), (wout, slice(HID, 2 * HID))):
        for t in range(4):
            ref[10 * t : 10 * t + 8, :] = packed[8 * t : 8 * t + 8, lanes] * scale
            ref[10 * t + 8 : 10 * t + 9, :] = packed[32 + t : 33 + t, lanes] * scale
            ref[10 * t + 9 : 10 * t + 10, :] = packed[36 + t : 37 + t, lanes] * scale
    wmid[0:32, :] = packed[40:72, 0:HID] * scale
    wmid[32:64, :] = packed[40:72, HID : 2 * HID] * scale
    bin_[...] = packed[72:73, 0:HID] * scale
    bmid[...] = packed[72:73, HID : 2 * HID] * scale
    for t in range(4):
        bout[:, 10 * t : 10 * t + 8] = packed[73:74, 8 * t : 8 * t + 8] * scale
        bout[:, 10 * t + 8 : 10 * t + 9] = packed[73:74, 32 + t : 33 + t] * scale
        bout[:, 10 * t + 9 : 10 * t + 10] = packed[73:74, 36 + t : 37 + t] * scale


def pair_rounds(x, axes):
    rounds = []
    for axis, count in axes:
        if count & (count - 1):
            rounds.append(x := lax.psum(x, axis))
            continue
        stride = 1
        while stride < count:
            x = x + lax.ppermute(x, axis, [(i, i ^ stride) for i in range(count)])
            rounds.append(x)
            stride *= 2
    return rounds


def latitude_terms(row_index, row_count):
    latitude = LAT_LIMIT * (2.0 * (jnp.clip(row_index, 0.0, row_count - 1.0) + 0.5) / row_count - 1.0)
    return 1.0 / jnp.cos(latitude), CORIOLIS * jnp.sin(latitude)


def on_device(
    initial_state, land_mask, surface_flux, weight_in, bias_in, weight_mid, bias_mid, weight_out, bias_out, cotangent
):
    lat_n, lon_n = lax.axis_size("lat"), lax.axis_size("lon")
    lat_i = lax.axis_index("lat")
    lat_total, lon_total = ROWS * lat_n, COLS * lon_n
    sides = ["swap"] if lat_n == 2 else ["north", "south"]
    is_low = (lat_i == 0).astype(jnp.int32)
    has_south = (lat_i > 0).astype(jnp.int32)
    has_north = (lat_i < lat_n - 1).astype(jnp.int32)
    scal = jnp.stack(
        [
            is_low * (ROWS - REACH),
            is_low * (ROWS - CREACH),
            has_south,
            has_north,
            jnp.where(is_low == 1, PAD + ROWS, PAD - REACH),
            jnp.where(is_low == 1, PAD + ROWS, PAD - CREACH),
            jnp.where(is_low == 1, 0, ROWS - CREACH),
        ]
    ).astype(jnp.int32)
    rows = (lat_i * ROWS - PAD + jnp.arange(EXT, dtype=jnp.int32)).astype(F32)
    cs, fs = latitude_terms(rows, lat_total)

    hbm = pl.BlockSpec(memory_space=pltpu.HBM)
    packed = pl.pallas_call(
        lambda *refs: pack_kernel(sides, *refs),
        out_shape=[
            sds(ROWS, PACK, COLS), sds(ROWS, FEATS, COLS), sds(STRIP, COLS), sds(STRIP, COLS), sds(8, COLS),
        ]
        + [sds(LAT, COLS)] * len(sides),
        in_specs=[SMEM] + [hbm] * 4,
        out_specs=[VMEM] * (5 + len(sides)),
        scratch_shapes=[
            pltpu.VMEM((40 * ROWS, COLS), F32), pltpu.VMEM((10 * ROWS, COLS), jnp.int32),
            pltpu.VMEM((ROWS, COLS), F32), pltpu.VMEM((40 * ROWS, COLS), F32), pltpu.SemaphoreType.DMA((4,)),
        ],
        compiler_params=params(56),
        cost_estimate=pl.CostEstimate(flops=10**9, bytes_accessed=3 * 10**6, transcendentals=0),
        name="pack_halos",
    )(
        scal,
        initial_state.reshape(40 * ROWS, COLS),
        land_mask.reshape(10 * ROWS, COLS),
        surface_flux,
        cotangent.reshape(40 * ROWS, COLS),
    )
    own, cown, east_pay, west_pay, sums = packed[:5]

    def lat_pairs(side):
        if side == "swap":
            return [(0, 1), (1, 0)]
        if side == "north":
            return [(i, i + 1) for i in range(lat_n - 1)]
        return [(i + 1, i) for i in range(lat_n - 1)]

    east_ring = [(i, (i + 1) % lon_n) for i in range(lon_n)]
    west_ring = [((i + 1) % lon_n, i) for i in range(lon_n)]
    lats = [lax.ppermute(pay, "lat", lat_pairs(side)) for side, pay in zip(sides, packed[5:])]
    from_west = lax.ppermute(east_pay, "lon", east_ring)
    from_east = lax.ppermute(west_pay, "lon", west_ring)
    corner_pays = pl.pallas_call(
        lambda *refs: corner_kernel(sides, *refs),
        out_shape=[sds(2 * PACK + 80, COLS)] * len(sides),
        in_specs=[SMEM, VMEM, VMEM],
        out_specs=[VMEM] * len(sides),
        compiler_params=params(8),
        cost_estimate=pl.CostEstimate(flops=10**8, bytes_accessed=10**6, transcendentals=0),
        name="pack_corners",
    )(scal, from_west, from_east)
    corners = [lax.ppermute(pay, "lat", lat_pairs(side)) for side, pay in zip(sides, corner_pays)]
    received = [ref for pair in zip(lats, corners) for ref in pair]
    means = pair_rounds(sums, (("lon", lon_n), ("lat", lat_n)))

    row = lambda b: b.reshape(1, -1)
    raw = (weight_in, weight_mid, weight_out, row(bias_in), row(bias_mid), row(bias_out))
    half = lambda *shape: jax.ShapeDtypeStruct(shape, BF16)
    own_m, own_h1, own_h2, k1, k2, k3, q1, q2, q3, b2, b3 = pl.pallas_call(
        own_closure_kernel,
        out_shape=[
            sds(ROWS, FEATS, COLS), sds(ROWS, HID, COLS), sds(ROWS, HID, COLS),
            half(HID, 144), half(HID, 192), half(48, 192), half(48, 192), half(HID, 192), half(HID, 144),
            sds(HID, COLS), sds(FEATS, COLS),
        ],
        in_specs=[VMEM] + [hbm] * 6,
        out_specs=[VMEM] * 11,
        scratch_shapes=[pltpu.VMEM(w.shape, F32) for w in raw]
        + [pltpu.VMEM((COLS, COLS), F32), pltpu.VMEM((COLS, COLS), F32), pltpu.VMEM((HID, WIDE), F32)]
        + [pltpu.SemaphoreType.DMA((6,))],
        compiler_params=params(12),
        cost_estimate=pl.CostEstimate(flops=10**9, bytes_accessed=2 * 10**6, transcendentals=0),
        name="own_closure",
    )(own, *raw)

    geometry = (scal, cs, fs)
    state = sds(EXT, 72, WIDE)
    plain = sds(EXT, FEATS, WIDE)
    marks = sds(EXT, 16, WIDE)
    vmem = lambda shape: pltpu.VMEM(shape.shape, F32)

    def call(kernel, name, out_shape, scratch, args, flops, limit):
        single = not isinstance(out_shape, list)
        return pl.pallas_call(
            kernel,
            out_shape=out_shape,
            in_specs=[SMEM] * 3 + [VMEM] * len(args),
            out_specs=VMEM if single else [VMEM] * len(out_shape),
            scratch_shapes=scratch,
            compiler_params=params(limit),
            cost_estimate=pl.CostEstimate(flops=flops, bytes_accessed=10**7, transcendentals=0),
            name=name,
        )(*geometry, *args)

    s0, masks, fluxes, net = call(
        lambda *refs: assemble_kernel(sides, *refs), "assemble",
        [state, marks, sds(EXT, 8, WIDE), plain], [],
        [means[max(len(means) - 2, 0)], own, own_m, from_west, from_east] + received + [k1, k2, k3, b2, b3],
        2 * 10**9, 8,
    )
    s1 = call(first_section_kernel, "first_section", state, [], [s0, masks], 10**9, 8)
    s2 = call(second_section_kernel, "second_section", state, [], [s0, s1, masks], 10**9, 8)
    grads, top, abuf, from_closure, s3, t2, net_2 = call(
        lambda *refs: late_kernel(sides, *refs), "steps_and_adjoint",
        [sds(80, COLS), plain, plain, sds(ROWS, FEATS, COLS), state, state, plain],
        [vmem(state)] + [vmem(plain)] * 5 + [pltpu.VMEM((192, HID), F32)],
        [means[-1], own, cown, own_h1, own_h2, s0, s2, masks, fluxes, net, from_west, from_east]
        + received + [k1, k2, k3, q1, q2, q3, b2, b3],
        4 * 10**9, 18,
    )
    rounds = pair_rounds(grads, (("lat", lat_n), ("lon", lon_n)))
    final = call(
        last_section_kernel, "last_section", sds(40 * ROWS, COLS), [],
        [rounds[min(2, len(rounds) - 1)], means[-1], s3, t2, masks, fluxes, net_2], 10**9, 8,
    )
    hold, bbuf = call(
        back_third_kernel, "adjoint_third_section", [plain, plain], [], [s2, masks, abuf, top], 10**9, 8
    )
    left, abuf = call(
        back_second_kernel, "adjoint_second_section", [plain, plain], [],
        [rounds[0], s1, masks, bbuf, top, hold], 10**9, 8,
    )
    state_grad = call(
        back_first_kernel, "adjoint_first_section", sds(40 * ROWS, COLS), [],
        [rounds[1], s0, masks, abuf, left, from_closure], 10**9, 8,
    )

    scale = 1.0 / math.sqrt(lat_total * lon_total)
    g_in, g_bin, g_mid, g_bmid, g_out, g_bout = pl.pallas_call(
        lambda *refs: unpack_kernel(scale, *refs),
        out_shape=[sds(40, HID), sds(1, HID), sds(HID, HID), sds(1, HID), sds(40, HID), sds(1, 40)],
        in_specs=[VMEM],
        out_specs=[VMEM] * 6,
        compiler_params=params(8),
        name="unpack_weight_grads",
    )(rounds[-1])
    shape = initial_state.shape
    return (
        final.reshape(shape),
        state_grad.reshape(shape),
        g_in,
        g_bin.reshape(-1),
        g_mid,
        g_bmid.reshape(-1),
        g_out.T,
        g_bout.reshape(-1),
    )


def solution(mesh):
    split_state = P(None, None, "lat", "lon")
    return jax.shard_map(
        on_device,
        mesh=mesh,
        in_specs=(split_state, P(None, "lat", "lon"), P("lat", "lon"), P(), P(), P(), P(), P(), P(), split_state),
        out_specs=(split_state, split_state, P(), P(), P(), P(), P(), P()),
        check_vma=False,
    )
```

```python
import math

import jax
import jax.numpy as jnp
from jax import lax
from jax.experimental import pallas as pl
from jax.experimental.pallas import tpu as pltpu
from jax.sharding import PartitionSpec as P

LAT_LIMIT = 1.2
CORIOLIS = 1.0
VISCOSITY = 0.15
DIFFUSIVITY = 0.1

ROWS = 16
COLS = 128
REACH = 11
CREACH = 6
PAD = 16
EXT = 48
TURN = 4
WIDE = 2 * COLS
FEATS = 40
HID = 64
PACK = 56
STRIP = 2 * PACK + 40
LAT_X = REACH * PACK
LAT = LAT_X + CREACH * FEATS
SLOT = 16
F32 = jnp.float32
BF16 = jnp.bfloat16
VMEM = pl.BlockSpec(memory_space=pltpu.VMEM)
SMEM = pl.BlockSpec(memory_space=pltpu.SMEM)


def params(megabytes):
    return pltpu.CompilerParams(vmem_limit_bytes=megabytes * 1024 * 1024)


def sds(*shape):
    return jax.ShapeDtypeStruct(shape, F32)


def sub_index(width):
    return lax.broadcasted_iota(jnp.int32, (8, width), 0)


def tile(ref, row, number):
    return ref[row, 8 * number : 8 * number + 8, :]


def slot_pack(pieces, shift_of, width):
    lane = lax.broadcasted_iota(jnp.int32, (8, COLS), 1)
    packed = None
    for slot, piece in enumerate(pieces):
        turned = pltpu.roll(piece, shift_of(slot) % COLS, 1)
        if packed is None:
            packed = turned
        else:
            packed = jnp.where((lane >= slot * width) & (lane < (slot + 1) * width), turned, packed)
    return packed


def pack_kernel(sides, x_hbm, mask_hbm, flux_hbm, cot_hbm, *outs):
    x, mask, flux, cot, sems = outs[-5:]
    own, cown, east, west, sums = outs[:5]
    per_side = outs[5 : 5 + len(sides)]
    pairs = ((mask_hbm, mask), (x_hbm, x), (flux_hbm, flux), (cot_hbm, cot))
    copies = [pltpu.make_async_copy(a, b, sems.at[i]) for i, (a, b) in enumerate(pairs)]
    for copy in copies:
        copy.start()
    for copy in copies:
        copy.wait()
    top = mask[0:ROWS, :].astype(F32)
    total = jnp.sum(jnp.sum(top * flux[...], axis=1, keepdims=True), axis=0, keepdims=True)
    count = jnp.sum(jnp.sum(top, axis=1, keepdims=True), axis=0, keepdims=True)
    sums[...] = jnp.where(sub_index(COLS) == 0, total, jnp.where(sub_index(COLS) == 1, count, 0.0))
    for r in range(ROWS):
        first = mask[pl.ds(r, 8, stride=ROWS), :].astype(F32)
        m8 = mask[8 * ROWS + r : 8 * ROWS + r + 1, :].astype(F32)
        m9 = mask[9 * ROWS + r : 9 * ROWS + r + 1, :].astype(F32)
        for t in range(4):
            own[r, 8 * t : 8 * t + 8, :] = x[pl.ds(t * 10 * ROWS + r, 8, stride=ROWS), :] * first
            cown[r, 8 * t : 8 * t + 8, :] = cot[pl.ds(t * 10 * ROWS + r, 8, stride=ROWS), :]
        for level, m in ((8, m8), (9, m9)):
            at = 32 + 4 * (level - 8)
            own[r, at : at + 4, :] = x[pl.ds(level * ROWS + r, 4, stride=10 * ROWS), :] * m
            cown[r, at : at + 4, :] = cot[pl.ds(level * ROWS + r, 4, stride=10 * ROWS), :]
        own[r, 40:48, :] = first
        own[r, 48:49, :] = m8
        own[r, 49:50, :] = m9
        own[r, 50:51, :] = flux[r : r + 1, :]
        own[r, 51:56, :] = jnp.zeros((5, COLS), F32)
    for half in range(2):
        for t in range(7):
            rows = [own[8 * half + s, 8 * t : 8 * t + 8, :] for s in range(8)]
            at = half * PACK + 8 * t
            east[at : at + 8, :] = slot_pack(rows, lambda s: SLOT * (s + 1), SLOT)
            west[at : at + 8, :] = slot_pack(rows, lambda s: SLOT * s, SLOT)
    for t in range(5):
        rows = [cown[s, 8 * t : 8 * t + 8, :] for s in range(ROWS)]
        at = 2 * PACK + 8 * t
        east[at : at + 8, :] = slot_pack(rows, lambda s: 8 * (s + 1), 8)
        west[at : at + 8, :] = slot_pack(rows, lambda s: 8 * s, 8)
    southern = (lax.axis_index("lat") == 0).astype(jnp.int32)
    for side, lat in zip(sides, per_side):
        start = {"swap": southern * (ROWS - REACH), "north": ROWS - REACH, "south": 0}[side]
        cstart = {"swap": southern * (ROWS - CREACH), "north": ROWS - CREACH, "south": 0}[side]
        for n in range(REACH):
            lat[PACK * n : PACK * (n + 1), :] = own[start + n]
        for n in range(CREACH):
            lat[LAT_X + FEATS * n : LAT_X + FEATS * (n + 1), :] = cown[cstart + n]


def corner_kernel(sides, scal, east, west, *outs):
    for side, corner in zip(sides, outs):
        start = {"swap": scal[0], "north": ROWS - REACH, "south": 0}[side]
        for at, strip, near in ((0, east, 1), (PACK + 40, west, 0)):
            for t in range(7):
                rows = slice(at + 8 * t, at + 8 * t + 8)
                corner[rows, :] = shift_rows(strip, t, start, near)
            corner[at + PACK : at + PACK + 40, :] = strip[2 * PACK : 2 * PACK + 40, :]


def shift_rows(strip, t, start, near):
    lane = lax.broadcasted_iota(jnp.int32, (8, COLS), 1)
    halves = [strip[8 * t : 8 * t + 8, :], strip[PACK + 8 * t : PACK + 8 * t + 8, :]]
    if isinstance(start, int):
        out = jnp.zeros((8, COLS), F32)
        for n in range(REACH):
            r = start + n
            turn = REACH * n - (SLOT * (r % 8) + near * (SLOT - REACH))
            turned = pltpu.roll(halves[r // 8], turn % COLS, 1)
            out = jnp.where((lane >= REACH * n) & (lane < REACH * (n + 1)), turned, out)
        return out
    low = shift_rows(strip, t, 0, near)
    high = shift_rows(strip, t, ROWS - REACH, near)
    return jnp.where(start == 0, low, high)


def split(values):
    high = values.astype(BF16)
    return high, (values - high.astype(F32)).astype(BF16)


def stack(out, values, buffer):
    k = values.shape[1]
    rows = slice(0, values.shape[0])
    high, low = split(values)
    buffer[rows, 0:k] = high.astype(F32)
    buffer[rows, k : 2 * k] = high.astype(F32)
    buffer[rows, 2 * k : 3 * k] = low.astype(F32)
    out[...] = buffer[rows, 0 : 3 * k].astype(BF16)


def by_tile(dst, src, lanes):
    for t in range(4):
        dst[8 * t : 8 * t + 8, lanes] = src[10 * t : 10 * t + 8, lanes]
        dst[32 + t : 33 + t, lanes] = src[10 * t + 8 : 10 * t + 9, lanes]
        dst[36 + t : 37 + t, lanes] = src[10 * t + 9 : 10 * t + 10, lanes]


def product(weights, high, low):
    return jnp.dot(weights, jnp.concatenate([high, low, high], axis=0), preferred_element_type=F32)


def across(a, b):
    dims = (((1,), (1,)), ((), ()))
    dot = lambda p, q: lax.dot_general(p, q, dims, preferred_element_type=F32)
    return dot(a[0], b[0]) + dot(a[0], b[1]) + dot(a[1], b[0])


def to_48(columns, first=0.0):
    more = jnp.where(sub_index(columns.shape[1]) == 0, first, 0.0).astype(F32)
    return jnp.concatenate([columns, more], axis=0)


def wide(bias, values):
    return jnp.concatenate([bias[...]] * (values.shape[1] // COLS), axis=1)


def hidden_layers(z, k1, k2, b2):
    h1 = jnp.tanh(product(k1[...], *z))
    h1s = split(h1)
    h2 = product(k2[...], *h1s)
    return h1, h1s, jnp.tanh(h2 + wide(b2, h2))


def last_layer(h2, k3, b3):
    o = product(k3[...], *split(h2))[0:FEATS]
    return o + wide(b3, o)


def add_weight_terms(acc, z, h1s, h2s, g1s, g2s, gos):
    ones = jnp.ones((16, z[0].shape[1]), BF16)
    acc[0:48, 0:HID] += across(z, g1s)
    acc[48:112, 0:HID] += across(h1s, g2s)
    acc[112:160, 0:HID] += across(gos, h2s)
    acc[160:176, 0:HID] += ones_rows(ones, g2s)
    acc[176:192, 0:48] += ones_rows(ones, gos)


def ones_rows(ones, g):
    dims = (((1,), (1,)), ((), ()))
    dot = lambda q: lax.dot_general(ones, q, dims, preferred_element_type=F32)
    return dot(g[0]) + dot(g[1])


def own_closure_kernel(own, *refs):
    raw, (out, h1_out, h2_out, k1, k2, k3, q1, q2, q3, b2, b3) = refs[:6], refs[6:17]
    w_in, w_mid, w_out, b_in, b_mid, b_out = refs[17:23]
    buffer, spare, stacked, sems = refs[23:]
    copies = [pltpu.make_async_copy(a, b, sems.at[i]) for i, (a, b) in enumerate(zip(raw, refs[17:23]))]
    for copy in copies:
        copy.start()
    for copy in copies:
        copy.wait()
    buffer[...] = jnp.zeros(buffer.shape, F32)
    by_tile(buffer, w_in, slice(0, HID))
    buffer[40:41, 0:HID] = b_in[...]
    stack(q1, buffer[0:48, 0:HID], stacked)
    spare[...] = buffer[...].T
    stack(k1, spare[0:HID, 0:48], stacked)
    buffer[0:HID, 0:HID] = w_mid[...]
    buffer[HID : HID + 1, 0:HID] = b_mid[...]
    stack(q2, buffer[0:HID, 0:HID], stacked)
    spare[...] = buffer[...].T
    stack(k2, spare[0:HID, 0:HID], stacked)
    b2[...] = jnp.broadcast_to(spare[0:HID, HID : HID + 1], (HID, COLS))
    buffer[...] = jnp.zeros(buffer.shape, F32)
    buffer[0:HID, 0:FEATS] = w_out[...]
    buffer[HID : HID + 1, 0:FEATS] = b_out[...]
    spare[...] = buffer[...].T
    buffer[...] = jnp.zeros(buffer.shape, F32)
    by_tile(buffer, spare, slice(0, COLS))
    stack(k3, buffer[0:48, 0:HID], stacked)
    b3[...] = jnp.broadcast_to(buffer[0:FEATS, HID : HID + 1], (FEATS, COLS))
    spare[...] = buffer[...].T
    stack(q3, spare[0:HID, 0:48], stacked)

    for r in range(0, ROWS, 8):
        z = split(to_48(jnp.concatenate([own[r + n, 0:FEATS, :] for n in range(8)], axis=1), 1.0))
        h1, h1s, h2 = hidden_layers(z, k1, k2, b2)
        o = last_layer(h2, k3, b3)
        for n in range(8):
            at = slice(n * COLS, (n + 1) * COLS)
            out[r + n] = o[:, at]
            h1_out[r + n] = h1[:, at]
            h2_out[r + n] = h2[:, at]


class Row:
    def __init__(self, width):
        sub = sub_index(width)
        group = sub % 4
        self.sub = sub
        self.is_t = group == 0
        self.is_s = group == 1
        self.is_u = group == 2
        self.is_v = group == 3
        self.low = sub >= 4
        self.k4 = jnp.where(group < 2, DIFFUSIVITY, VISCOSITY).astype(F32)


def put_state(k, ref, row, tiles):
    for t in range(5):
        ref[row, 8 * t : 8 * t + 8, :] = tiles[t]
    press = 0.4 * tiles[1] - 0.1 * tiles[0]
    for by in (1, 2, 4):
        press = press + jnp.where(k.sub >= by, pltpu.roll(press, by, 0), 0.0)
    ref[row, 40:48, :] = press
    deep_8 = ref[row, 47:48, :] + (0.4 * ref[row, 33:34, :] - 0.1 * ref[row, 32:33, :])
    ref[row, 48:49, :] = deep_8
    ref[row, 49:50, :] = deep_8 + (0.4 * ref[row, 37:38, :] - 0.1 * ref[row, 36:37, :])


def deep_pair(k, ref, row, upper, lower):
    return jnp.where(k.low, ref[row, lower : lower + 1, :], ref[row, upper : upper + 1, :])


def deep_u(k, ref, row):
    return deep_pair(k, ref, row, 34, 38)


def deep_v(k, ref, row):
    return deep_pair(k, ref, row, 35, 39)


def deep_p(k, ref, row):
    return deep_pair(k, ref, row, 48, 49)


def east_of(q):
    return pltpu.roll(q, q.shape[1] - 1, 1)


def west_of(q):
    return pltpu.roll(q, 1, 1)


def gain_of(k, t):
    return k.k4 if t == 4 else (DIFFUSIVITY if t < 2 else VISCOSITY)


def tendency_row(k, ref, row, c, f):
    half = 0.5 * c
    c2 = c * c
    u, v = tile(ref, row, 2), tile(ref, row, 3)
    u4, v4 = deep_u(k, ref, row), deep_v(k, ref, row)
    change = []
    for t in range(5):
        gain = gain_of(k, t)
        if t in (0, 2, 4):
            au, av = (half * u4, 0.5 * v4) if t == 4 else (half * u, 0.5 * v)
            along = gain * c2
            at_e, at_w, at_n, at_s = along - au, along + au, gain - av, gain + av
        q = tile(ref, row, t)
        east, west = at_e * east_of(q), at_w * west_of(q)
        north, south = at_n * tile(ref, row + 1, t), at_s * tile(ref, row - 1, t)
        change.append((east + west) + (north + south) - (gain * (2.0 * c2 + 2.0)) * q)
    p = tile(ref, row, 5)
    change[2] = change[2] + (f * v - half * (east_of(p) - west_of(p)))
    change[3] = change[3] - (f * u + 0.5 * (tile(ref, row + 1, 5) - tile(ref, row - 1, 5)))
    p4 = deep_p(k, ref, row)
    fx = f * v4 - half * (east_of(p4) - west_of(p4))
    fy = f * u4 + 0.5 * (deep_p(k, ref, row + 1) - deep_p(k, ref, row - 1))
    change[4] = change[4] + jnp.where(k.is_u, fx, jnp.where(k.is_v, -fy, 0.0))
    return change


def adjoint_row(k, ref, aref, row, c, f):
    half = 0.5 * c
    c2 = c * c
    u4 = deep_u(k, ref, row)
    qe = [east_of(tile(ref, row, t)) for t in range(5)]
    qw = [west_of(tile(ref, row, t)) for t in range(5)]
    out = []
    to_u = to_v = None
    for t in range(5):
        a = tile(aref, row, t)
        ae, aw = east_of(a), west_of(a)
        an, as_ = tile(aref, row + 1, t), tile(aref, row - 1, t)
        gain = gain_of(k, t)
        if t == 0:
            ue, uw = half * qe[2], half * qw[2]
            vn, vs = 0.5 * tile(ref, row + 1, 3), 0.5 * tile(ref, row - 1, 3)
        if t == 4:
            ue, uw = half * east_of(u4), half * west_of(u4)
            vn, vs = 0.5 * deep_v(k, ref, row + 1), 0.5 * deep_v(k, ref, row - 1)
        if t in (0, 2, 4):
            along = gain * c2
            at_e, at_w, at_n, at_s = along + ue, along - uw, gain + vn, gain - vs
        out.append(
            (at_e * ae + at_w * aw) + (at_n * an + at_s * as_) - (gain * (2.0 * c2 + 2.0)) * a
        )
        px = a * (qe[t] - qw[t])
        py = a * (tile(ref, row + 1, t) - tile(ref, row - 1, t))
        if t < 4:
            to_u = px if to_u is None else to_u + px
            to_v = py if to_v is None else to_v + py
        if t == 2:
            a2, bx = a, half * (ae - aw)
        if t == 3:
            a3, by = a, 0.5 * (an - as_)
        if t == 4:
            a4 = a
            deep_bx, deep_by = half * (ae - aw), 0.5 * (an - as_)
            px4, py4 = px * half, py * 0.5
    out[2] = out[2] - half * to_u - f * a3
    out[3] = out[3] - 0.5 * to_v + f * a2
    sx = px4 + pltpu.roll(px4, 7, 0)
    sx = sx + pltpu.roll(sx, 2, 0)
    sy = py4 + pltpu.roll(py4, 1, 0)
    sy = sy + pltpu.roll(sy, 2, 0)
    at_u = -sx - f * pltpu.roll(a4, 7, 0)
    at_v = f * pltpu.roll(a4, 1, 0) - sy
    deep = jnp.where(k.is_t, pltpu.roll(deep_bx, 6, 0) + pltpu.roll(deep_by, 5, 0), 0.0)
    deep = deep + jnp.where(k.low, 0.0, pltpu.roll(deep, 4, 0))
    press = bx + by
    for shift in (1, 2, 4):
        press = press + jnp.where(k.sub < 8 - shift, pltpu.roll(press, 8 - shift, 0), 0.0)
    press = press + deep[0:1, :]
    out[0] = out[0] - 0.1 * press
    out[1] = out[1] + 0.4 * press
    out[4] = out[4] + jnp.where(
        k.is_t,
        -0.1 * deep,
        jnp.where(k.is_s, 0.4 * pltpu.roll(deep, 1, 0), jnp.where(k.is_u, at_u, at_v)),
    )
    return out


def for_rows(scal, reach, body):
    low, high = PAD - reach * scal[2], PAD + ROWS + reach * scal[3]
    turns = lax.div(high - low + TURN - 1, TURN)
    first = jnp.where(scal[3] == 1, low, high - TURN * turns)

    def turn(i, _):
        for j in range(TURN):
            body(first + TURN * i + j)
        return 0

    lax.fori_loop(0, turns, turn, 0)


def mask_tile(ref, row, t):
    return tile(ref, row, 1 if t == 4 else 0)


def adjoint_third(k, scal, cs, fs, reach, state, masks, abuf, top, hold, bbuf):
    def body(r):
        d = adjoint_row(k, state, abuf, r, cs[r], fs[r])
        for t in range(5):
            ts = (2.0 / 3.0) * tile(top, r, t) + d[t]
            hold[r, 8 * t : 8 * t + 8, :] = ts
            bbuf[r, 8 * t : 8 * t + 8, :] = 0.0625 * mask_tile(masks, r, t) * ts

    for_rows(scal, reach, body)


def adjoint_second(k, scal, cs, fs, reach, state, masks, bbuf, top, hold, left, abuf):
    def body(r):
        d = adjoint_row(k, state, bbuf, r, cs[r], fs[r])
        for t in range(5):
            ts = tile(hold, r, t)
            tf = 0.25 * ts + d[t]
            left[r, 8 * t : 8 * t + 8, :] = (1.0 / 3.0) * tile(top, r, t) + 0.75 * ts + tf
            abuf[r, 8 * t : 8 * t + 8, :] = 0.25 * mask_tile(masks, r, t) * tf

    for_rows(scal, reach, body)


def adjoint_first(k, scal, cs, fs, reach, state, abuf, left, store):
    def body(r):
        d = adjoint_row(k, state, abuf, r, cs[r], fs[r])
        store(r, [tile(left, r, t) + d[t] for t in range(5)])

    for_rows(scal, reach, body)


def edges(reach):
    lane = lax.broadcasted_iota(jnp.int32, (8, COLS), 1)
    return lane < reach, lane >= COLS - reach


def wide_pack(ref, base):
    parts = []
    for t in range(5):
        rows = [ref[base + s, 8 * t : 8 * t + 8, COLS:WIDE] for s in range(8)]
        parts.append(slot_pack(rows, lambda s: 8 + SLOT * s, SLOT))
    return jnp.concatenate(parts, axis=0)

def wide_unpack(ref, base, values):
    for s in range(8):
        ref[base + s, 0:FEATS, COLS:WIDE] = pltpu.roll(values, -(8 + SLOT * s) % COLS, 1)


def section_1(k, cs, fs, masks, src, dst):
    def body(r):
        d = tendency_row(k, src, r, cs[r], fs[r])
        put_state(
            k, dst, r,
            [tile(src, r, t) + 0.25 * mask_tile(masks, r, t) * d[t] for t in range(5)],
        )
    return body

def section_2(k, cs, fs, masks, src, mid, dst):
    def body(r):
        d = tendency_row(k, mid, r, cs[r], fs[r])
        put_state(
            k, dst, r,
            [
                0.75 * tile(src, r, t) + 0.25 * tile(mid, r, t)
                + 0.0625 * mask_tile(masks, r, t) * d[t]
                for t in range(5)
            ],
        )
    return body


def section_3(k, cs, fs, masks, fluxes, mean, src, mid, net, r):
    d = tendency_row(k, mid, r, cs[r], fs[r])
    new = []
    for t in range(5):
        m = mask_tile(masks, r, t)
        o = tile(net, r, t)
        if t == 1:
            force = 2.0 * (mean - fluxes[r, 2:3, :])
            o = o + jnp.where(k.sub == 0, force, 0.0)
        new.append(
            (1.0 / 3.0) * tile(src, r, t) + (2.0 / 3.0) * tile(mid, r, t)
            + m * ((1.0 / 6.0) * d[t] + 0.25 * o)
        )
    return new


def zero_walls(ref):
    for row in (PAD - 1, PAD + ROWS):
        ref[row] = jnp.zeros(ref.shape[1:], F32)


def assemble_kernel(sides, scal, cs, fs, own, own_m, east, west, *rest):
    n = len(sides)
    side_refs = [rest[2 * i : 2 * i + 2] for i in range(n)]
    (k1, k2, k3, b2, b3), rest = rest[2 * n : 2 * n + 5], rest[2 * n + 5 :]
    s0, masks, fluxes, outs = rest
    k = Row(WIDE)
    has_south = scal[2]
    lo = lambda h: PAD - h * has_south

    zero_walls(s0)

    near_e, near_w = edges(REACH)

    def put_packed(row, core, halo):
        both = lambda t: jnp.concatenate([core(t), halo(t)], axis=1)
        put_state(k, s0, row, [both(t) for t in range(5)])
        masks[row, 0:8, :] = both(5)
        last = both(6)
        masks[row, 8:16, :] = jnp.where(k.low, last[1:2, :], last[0:1, :])
        fluxes[row] = last

    for r in range(ROWS):
        at = (r // 8) * PACK
        turn = SLOT * (r % 8)

        def halo(t):
            from_e = pltpu.roll(west[at + 8 * t : at + 8 * t + 8, :], -turn % COLS, 1)
            from_w = pltpu.roll(east[at + 8 * t : at + 8 * t + 8, :], -(turn + SLOT) % COLS, 1)
            return jnp.where(near_e, from_e, jnp.where(near_w, from_w, 0.0))

        put_packed(PAD + r, lambda t: own[r, 8 * t : 8 * t + 8, :], halo)
    for side, (lat, corner) in zip(sides, side_refs):
        base = {"swap": scal[4], "north": PAD - REACH, "south": PAD + ROWS}[side]
        for r in range(REACH):

            def halo(t):
                wrows = slice(8 * t, 8 * t + 8)
                erows = slice(PACK + 40 + 8 * t, PACK + 48 + 8 * t)
                from_e = pltpu.roll(corner[erows, :], -REACH * r % COLS, 1)
                from_w = pltpu.roll(corner[wrows, :], -REACH * (r + 1) % COLS, 1)
                return jnp.where(near_e, from_e, jnp.where(near_w, from_w, 0.0))

            put_packed(base + r, lambda t: lat[PACK * r + 8 * t : PACK * r + 8 * t + 8, :], halo)

    for r in range(ROWS):
        outs[PAD + r, :, 0:COLS] = own_m[r]

    def closure_of(columns):
        _, _, h2 = hidden_layers(split(to_48(columns, 1.0)), k1, k2, b2)
        return last_layer(h2, k3, b3)

    def halo_rows(first):
        o = closure_of(jnp.concatenate([s0[first + i, 0:FEATS, 0:COLS] for i in range(8)], axis=1))
        for i in range(8):
            outs[first + i, :, 0:COLS] = o[:, i * COLS : (i + 1) * COLS]

    if sides == ["swap"]:
        groups = 3
        halo_rows(jnp.where(has_south == 1, PAD - 8, PAD + ROWS))
    else:
        groups = 4
        halo_rows(PAD - 8)
        halo_rows(PAD + ROWS)
    first = lo(8)
    o = closure_of(jnp.concatenate([wide_pack(s0, first + 8 * g) for g in range(groups)], axis=1))
    for g in range(groups):
        wide_unpack(outs, first + 8 * g, o[:, g * COLS : (g + 1) * COLS])


def first_section_kernel(scal, cs, fs, s0, masks, s1):
    zero_walls(s1)
    for_rows(scal, 10, section_1(Row(WIDE), cs, fs, masks, s0, s1))


def second_section_kernel(scal, cs, fs, s0, s1, masks, s2):
    zero_walls(s2)
    for_rows(scal, 9, section_2(Row(WIDE), cs, fs, masks, s0, s1, s2))


def last_section_kernel(scal, cs, fs, sums, s3, t2, masks, fluxes, outs, final):
    k = Row(WIDE)
    mean = sums[0:1, 0:1] / sums[1:2, 0:1]

    def last(r):
        new = section_3(k, cs, fs, masks, fluxes, mean, s3, t2, outs, r)
        put_result(final, r - PAD, [x[:, 0:COLS] for x in new])

    for_rows(scal, 0, last)


def late_kernel(
    sides, scal, cs, fs, sums, own, cown, own_h1, own_h2, s0, s2, masks, fluxes, outs_in, east, west, *rest
):
    n = len(sides)
    side_refs = [rest[2 * i : 2 * i + 2] for i in range(n)]
    (k1, k2, k3, q1, q2, q3, b2, b3), rest = rest[2 * n : 2 * n + 8], rest[2 * n + 8 :]
    grads, s4, abuf, from_closure, s3, t2, outs, t1, cot, gz, bbuf, hold, left, acc = rest
    k = Row(WIDE)
    has_south = scal[2]
    lo = lambda h: PAD - h * has_south
    for ref in (s3, t1, t2, abuf, bbuf):
        zero_walls(ref)
    mean = sums[0:1, 0:1] / sums[1:2, 0:1]

    cnear_e, cnear_w = edges(CREACH)
    for r in range(ROWS):
        for t in range(5):
            rows = slice(2 * PACK + 8 * t, 2 * PACK + 8 * t + 8)
            from_e = pltpu.roll(west[rows, :], -8 * r % COLS, 1)
            from_w = pltpu.roll(east[rows, :], -8 * (r + 1) % COLS, 1)
            side = jnp.where(cnear_e, from_e, jnp.where(cnear_w, from_w, 0.0))
            cot[PAD + r, 8 * t : 8 * t + 8, :] = jnp.concatenate(
                [cown[r, 8 * t : 8 * t + 8, :], side], axis=1
            )
    for side, (lat, corner) in zip(sides, side_refs):
        cbase = {"swap": scal[5], "north": PAD - CREACH, "south": PAD + ROWS}[side]
        crow = {"swap": scal[6], "north": ROWS - CREACH, "south": 0}[side]
        for r in range(CREACH):
            turn = lax.rem(2 * COLS - 8 * (crow + r), COLS)
            turn_w = lax.rem(2 * COLS - 8 * (crow + r + 1), COLS)
            for t in range(5):
                wrows = slice(PACK + 8 * t, PACK + 8 * t + 8)
                erows = slice(2 * PACK + 40 + 8 * t, 2 * PACK + 48 + 8 * t)
                from_e = pltpu.roll(corner[erows, :], turn, 1)
                from_w = pltpu.roll(corner[wrows, :], turn_w, 1)
                part = jnp.where(cnear_e, from_e, jnp.where(cnear_w, from_w, 0.0))
                cot[cbase + r, 8 * t : 8 * t + 8, :] = jnp.concatenate(
                    [lat[LAT_X + FEATS * r + 8 * t : LAT_X + FEATS * r + 8 * t + 8, :], part], axis=1
                )


    def step_1_end(r):
        put_state(k, s3, r, section_3(s0, s2, r))

    def step_1_end(r):
        put_state(k, s3, r, section_3(k, cs, fs, masks, fluxes, mean, s0, s2, outs_in, r))

    for_rows(scal, 8, step_1_end)

    acc[...] = jnp.zeros(acc.shape, F32)

    def closure_adjoint(z, h1, h1s, h2, go, with_weights):
        gos = split(to_48(go))
        g2 = product(q3[...], *gos) * (1.0 - h2 * h2)
        g2s = split(g2)
        g1 = product(q2[...], *g2s) * (1.0 - h1 * h1)
        g1s = split(g1)
        if with_weights:
            add_weight_terms(acc, z, h1s, split(h2), g1s, g2s, gos)
        return product(q1[...], *g1s)[0:FEATS]

    def both_ways(columns, go, with_weights):
        z = split(to_48(columns, 1.0))
        h1, h1s, h2 = hidden_layers(z, k1, k2, b2)
        o = last_layer(h2, k3, b3) if with_weights else None
        return o, closure_adjoint(z, h1, h1s, h2, go, with_weights)

    def masked_core(ref, r):
        m0, m4 = masks[r, 0:8, 0:COLS], masks[r, 8:16, 0:COLS]
        parts = [
            0.25 * (m4 if t == 4 else m0) * ref[r, 8 * t : 8 * t + 8, 0:COLS] for t in range(5)
        ]
        return jnp.concatenate(parts, axis=0)

    def mask_cot(r):
        for t in range(5):
            bbuf[r, 8 * t : 8 * t + 8, :] = 0.25 * mask_tile(masks, r, t) * tile(cot, r, t)
            abuf[r, 8 * t : 8 * t + 8, :] = (1.0 / 6.0) * mask_tile(masks, r, t) * tile(cot, r, t)

    for_rows(scal, 6, mask_cot)

    for first in range(PAD, PAD + ROWS, 8):
        z = jnp.concatenate([s3[first + i, 0:FEATS, 0:COLS] for i in range(8)], axis=1)
        go = jnp.concatenate([bbuf[first + i, 0:FEATS, 0:COLS] for i in range(8)], axis=1)
        o, back = both_ways(z, go, True)
        for i in range(8):
            at = slice(i * COLS, (i + 1) * COLS)
            outs[first + i, :, 0:COLS] = o[:, at]
            gz[first + i, :, 0:COLS] = back[:, at]

    first = lo(4)
    if sides == ["swap"]:
        rows = [jnp.where(has_south == 1, PAD - 4, PAD + ROWS) + i for i in range(4)]
    else:
        rows = [PAD - 4 + i for i in range(4)] + [PAD + ROWS + i for i in range(4)]
    beyond = lambda ref: jnp.concatenate(
        [ref[r, 0:FEATS, 0:COLS] for r in rows] + [wide_pack(ref, first + 8 * g) for g in range(3)], axis=1
    )
    _, back = both_ways(beyond(s3), beyond(bbuf), False)
    for i, r in enumerate(rows):
        gz[r, :, 0:COLS] = back[:, i * COLS : (i + 1) * COLS]
    for g in range(3):
        at = (len(rows) + g) * COLS
        wide_unpack(gz, first + 8 * g, back[:, at : at + COLS])

    for_rows(scal, 7, section_1(k, cs, fs, masks, s3, t1))
    for_rows(scal, 6, section_2(k, cs, fs, masks, s3, t1, t2))

    def store(r, tiles):
        for t in range(5):
            s4[r, 8 * t : 8 * t + 8, :] = tiles[t] + tile(gz, r, t)

    adjoint_third(k, scal, cs, fs, 5, t2, masks, abuf, cot, hold, bbuf)
    adjoint_second(k, scal, cs, fs, 4, t1, masks, bbuf, cot, hold, left, abuf)
    adjoint_first(k, scal, cs, fs, 3, s3, abuf, left, store)

    for r in range(0, ROWS, 8):
        side = lambda read: jnp.concatenate([read(r + j) for j in range(8)], axis=1)
        z = split(to_48(side(lambda j: own[j, 0:FEATS, :]), 1.0))
        h1 = side(lambda j: own_h1[j])
        h2 = side(lambda j: own_h2[j])
        go = side(lambda j: masked_core(s4, PAD + j))
        back = closure_adjoint(z, h1, split(h1), h2, go, True)
        for j in range(8):
            from_closure[r + j] = back[:, j * COLS : (j + 1) * COLS]

    zero_walls(abuf)

    def mask_top(r):
        for t in range(5):
            abuf[r, 8 * t : 8 * t + 8, :] = (1.0 / 6.0) * mask_tile(masks, r, t) * tile(s4, r, t)

    for_rows(scal, 3, mask_top)
    grads[...] = jnp.zeros(grads.shape, F32)
    grads[0:40, 0:HID] = acc[0:40, 0:HID]
    grads[0:40, HID : 2 * HID] = acc[112:152, 0:HID]
    grads[40:72, 0:HID] = acc[48:80, 0:HID]
    grads[40:72, HID : 2 * HID] = acc[80:112, 0:HID]
    grads[72:73, 0:HID] = acc[40:41, 0:HID]
    grads[72:73, HID : 2 * HID] = acc[160:161, 0:HID]
    grads[73:74, 0:HID] = acc[176:177, 0:HID]


def put_result(ref, row, tiles):
    for t in range(4):
        ref[pl.ds(t * 10 * ROWS + row, 8, stride=ROWS), :] = tiles[t]
    ref[pl.ds(8 * ROWS + row, 4, stride=10 * ROWS), :] = tiles[4][0:4, :]
    ref[pl.ds(9 * ROWS + row, 4, stride=10 * ROWS), :] = tiles[4][4:8, :]


def back_third_kernel(scal, cs, fs, state, masks, abuf, top, hold, bbuf):
    zero_walls(bbuf)
    adjoint_third(Row(WIDE), scal, cs, fs, 2, state, masks, abuf, top, hold, bbuf)


def back_second_kernel(scal, cs, fs, state, masks, bbuf, top, hold, left, abuf):
    zero_walls(abuf)
    adjoint_second(Row(WIDE), scal, cs, fs, 1, state, masks, bbuf, top, hold, left, abuf)


def back_first_kernel(scal, cs, fs, state, masks, abuf, left, from_closure, grad):
    def store(r, tiles):
        done = []
        for t in range(5):
            m = masks[r, 8:16, 0:COLS] if t == 4 else masks[r, 0:8, 0:COLS]
            done.append(m * (tiles[t][:, 0:COLS] + from_closure[r - PAD, 8 * t : 8 * t + 8, :]))
        put_result(grad, r - PAD, done)

    adjoint_first(Row(WIDE), scal, cs, fs, 0, state, abuf, left, store)


def unpack_kernel(scale, packed, win, bin_, wmid, bmid, wout, bout):
    for ref, lanes in ((win, slice(0, HID)), (wout, slice(HID, 2 * HID))):
        for t in range(4):
            ref[10 * t : 10 * t + 8, :] = packed[8 * t : 8 * t + 8, lanes] * scale
            ref[10 * t + 8 : 10 * t + 9, :] = packed[32 + t : 33 + t, lanes] * scale
            ref[10 * t + 9 : 10 * t + 10, :] = packed[36 + t : 37 + t, lanes] * scale
    wmid[0:32, :] = packed[40:72, 0:HID] * scale
    wmid[32:64, :] = packed[40:72, HID : 2 * HID] * scale
    bin_[...] = packed[72:73, 0:HID] * scale
    bmid[...] = packed[72:73, HID : 2 * HID] * scale
    for t in range(4):
        bout[:, 10 * t : 10 * t + 8] = packed[73:74, 8 * t : 8 * t + 8] * scale
        bout[:, 10 * t + 8 : 10 * t + 9] = packed[73:74, 32 + t : 33 + t] * scale
        bout[:, 10 * t + 9 : 10 * t + 10] = packed[73:74, 36 + t : 37 + t] * scale


def pair_rounds(x, axes, beside=()):
    results = []
    beside = list(beside)

    def wait_for(x):
        if beside:
            results.append(beside.pop(0)(results))
            x, results[-1] = lax.optimization_barrier((x, results[-1]))
        return x

    for axis, count in axes:
        if count & (count - 1):
            x = wait_for(lax.psum(x, axis))
            continue
        for bit in range(count.bit_length() - 1):
            x = x + wait_for(lax.ppermute(x, axis, [(i, i ^ (1 << bit)) for i in range(count)]))
    while beside:
        results.append(beside.pop(0)(results))
    return x, results


def latitude_terms(row_index, row_count):
    latitude = LAT_LIMIT * (2.0 * (jnp.clip(row_index, 0.0, row_count - 1.0) + 0.5) / row_count - 1.0)
    return 1.0 / jnp.cos(latitude), CORIOLIS * jnp.sin(latitude)


def on_device(
    initial_state, land_mask, surface_flux, weight_in, bias_in, weight_mid, bias_mid, weight_out, bias_out, cotangent
):
    lat_n, lon_n = lax.axis_size("lat"), lax.axis_size("lon")
    lat_i = lax.axis_index("lat")
    lat_total, lon_total = ROWS * lat_n, COLS * lon_n
    sides = ["swap"] if lat_n == 2 else ["north", "south"]
    is_low = (lat_i == 0).astype(jnp.int32)
    has_south = (lat_i > 0).astype(jnp.int32)
    has_north = (lat_i < lat_n - 1).astype(jnp.int32)
    scal = jnp.stack(
        [
            is_low * (ROWS - REACH),
            is_low * (ROWS - CREACH),
            has_south,
            has_north,
            jnp.where(is_low == 1, PAD + ROWS, PAD - REACH),
            jnp.where(is_low == 1, PAD + ROWS, PAD - CREACH),
            jnp.where(is_low == 1, 0, ROWS - CREACH),
        ]
    ).astype(jnp.int32)
    rows = (lat_i * ROWS - PAD + jnp.arange(EXT, dtype=jnp.int32)).astype(F32)
    cs, fs = latitude_terms(rows, lat_total)

    hbm = pl.BlockSpec(memory_space=pltpu.HBM)
    packed = pl.pallas_call(
        lambda *refs: pack_kernel(sides, *refs),
        out_shape=[
            sds(ROWS, PACK, COLS), sds(ROWS, FEATS, COLS), sds(STRIP, COLS), sds(STRIP, COLS), sds(8, COLS),
        ]
        + [sds(LAT, COLS)] * len(sides),
        in_specs=[hbm] * 4,
        out_specs=[VMEM] * (5 + len(sides)),
        scratch_shapes=[
            pltpu.VMEM((40 * ROWS, COLS), F32), pltpu.VMEM((10 * ROWS, COLS), jnp.int32),
            pltpu.VMEM((ROWS, COLS), F32), pltpu.VMEM((40 * ROWS, COLS), F32), pltpu.SemaphoreType.DMA((4,)),
        ],
        compiler_params=params(56),
        cost_estimate=pl.CostEstimate(flops=10**9, bytes_accessed=3 * 10**6, transcendentals=0),
        name="pack_halos",
    )(
        initial_state.reshape(40 * ROWS, COLS),
        land_mask.reshape(10 * ROWS, COLS),
        surface_flux,
        cotangent.reshape(40 * ROWS, COLS),
    )
    own, cown, east_pay, west_pay, sums = packed[:5]

    def lat_pairs(side):
        if side == "swap":
            return [(0, 1), (1, 0)]
        if side == "north":
            return [(i, i + 1) for i in range(lat_n - 1)]
        return [(i + 1, i) for i in range(lat_n - 1)]

    east_ring = [(i, (i + 1) % lon_n) for i in range(lon_n)]
    west_ring = [((i + 1) % lon_n, i) for i in range(lon_n)]
    lats = [lax.ppermute(pay, "lat", lat_pairs(side)) for side, pay in zip(sides, packed[5:])]
    from_west = lax.ppermute(east_pay, "lon", east_ring)
    from_east = lax.ppermute(west_pay, "lon", west_ring)
    row = lambda b: b.reshape(1, -1)
    raw = (weight_in, weight_mid, weight_out, row(bias_in), row(bias_mid), row(bias_out))
    half = lambda *shape: jax.ShapeDtypeStruct(shape, BF16)
    own_closure = pl.pallas_call(
        own_closure_kernel,
        out_shape=[
            sds(ROWS, FEATS, COLS), sds(ROWS, HID, COLS), sds(ROWS, HID, COLS),
            half(HID, 144), half(HID, 192), half(48, 192), half(48, 192), half(HID, 192), half(HID, 144),
            sds(HID, COLS), sds(FEATS, COLS),
        ],
        in_specs=[VMEM] + [hbm] * 6,
        out_specs=[VMEM] * 11,
        scratch_shapes=[pltpu.VMEM(w.shape, F32) for w in raw]
        + [pltpu.VMEM((COLS, COLS), F32), pltpu.VMEM((COLS, COLS), F32), pltpu.VMEM((HID, WIDE), F32)]
        + [pltpu.SemaphoreType.DMA((6,))],
        compiler_params=params(12),
        cost_estimate=pl.CostEstimate(flops=10**9, bytes_accessed=2 * 10**6, transcendentals=0),
        name="own_closure",
    )
    pack_corners = pl.pallas_call(
        lambda *refs: corner_kernel(sides, *refs),
        out_shape=[sds(2 * PACK + 80, COLS)] * len(sides),
        in_specs=[SMEM, VMEM, VMEM],
        out_specs=[VMEM] * len(sides),
        compiler_params=params(8),
        cost_estimate=pl.CostEstimate(flops=10**8, bytes_accessed=10**6, transcendentals=0),
        name="pack_corners",
    )
    total, results = pair_rounds(
        sums,
        (("lon", lon_n), ("lat", lat_n)),
        [
            lambda done: sums,
            lambda done: own_closure(own, *raw),
            lambda done: pack_corners(scal, from_west, from_east),
        ],
    )
    corners = [lax.ppermute(pay, "lat", lat_pairs(side)) for side, pay in zip(sides, results[2])]
    received = [ref for pair in zip(lats, corners) for ref in pair]
    own_m, own_h1, own_h2, k1, k2, k3, q1, q2, q3, b2, b3 = results[1]

    geometry = (scal, cs, fs)
    state = sds(EXT, 56, WIDE)
    plain = sds(EXT, FEATS, WIDE)
    marks = sds(EXT, 16, WIDE)
    vmem = lambda shape: pltpu.VMEM(shape.shape, F32)

    def call(kernel, name, out_shape, scratch, args, flops, limit):
        single = not isinstance(out_shape, list)
        return pl.pallas_call(
            kernel,
            out_shape=out_shape,
            in_specs=[SMEM] * 3 + [VMEM] * len(args),
            out_specs=VMEM if single else [VMEM] * len(out_shape),
            scratch_shapes=scratch,
            compiler_params=params(limit),
            cost_estimate=pl.CostEstimate(flops=flops, bytes_accessed=10**7, transcendentals=0),
            name=name,
        )(*geometry, *args)

    s0, masks, fluxes, net = call(
        lambda *refs: assemble_kernel(sides, *refs), "assemble",
        [state, marks, sds(EXT, 8, WIDE), plain], [],
        [own, own_m, from_west, from_east] + received + [k1, k2, k3, b2, b3],
        2 * 10**9, 8,
    )
    s1 = call(first_section_kernel, "first_section", state, [], [s0, masks], 10**9, 8)
    s2 = call(second_section_kernel, "second_section", state, [], [s0, s1, masks], 10**9, 8)
    grads, top, abuf, from_closure, s3, t2, net_2 = call(
        lambda *refs: late_kernel(sides, *refs), "steps_and_adjoint",
        [sds(80, COLS), plain, plain, sds(ROWS, FEATS, COLS), state, state, plain],
        [vmem(state)] + [vmem(plain)] * 5 + [pltpu.VMEM((192, HID), F32)],
        [total, own, cown, own_h1, own_h2, s0, s2, masks, fluxes, net, from_west, from_east]
        + received + [k1, k2, k3, q1, q2, q3, b2, b3],
        4 * 10**9, 18,
    )
    beside = [
        lambda done: call(
            back_third_kernel, "adjoint_third_section", [plain, plain], [], [s2, masks, abuf, top], 10**9, 8
        ),
        lambda done: call(
            back_second_kernel, "adjoint_second_section", [plain, plain], [],
            [s1, masks, done[0][1], top, done[0][0]], 10**9, 8,
        ),
        lambda done: call(
            back_first_kernel, "adjoint_first_section", sds(40 * ROWS, COLS), [],
            [s0, masks, done[1][1], done[1][0], from_closure], 10**9, 8,
        ),
        lambda done: call(
            last_section_kernel, "last_section", sds(40 * ROWS, COLS), [],
            [total, s3, t2, masks, fluxes, net_2], 10**9, 8,
        ),
    ]
    summed, results = pair_rounds(grads, (("lat", lat_n), ("lon", lon_n)), beside)
    state_grad, final = results[2:]

    scale = 1.0 / math.sqrt(lat_total * lon_total)
    g_in, g_bin, g_mid, g_bmid, g_out, g_bout = pl.pallas_call(
        lambda *refs: unpack_kernel(scale, *refs),
        out_shape=[sds(40, HID), sds(1, HID), sds(HID, HID), sds(1, HID), sds(40, HID), sds(1, 40)],
        in_specs=[VMEM],
        out_specs=[VMEM] * 6,
        compiler_params=params(8),
        name="unpack_weight_grads",
    )(summed)
    shape = initial_state.shape
    return (
        final.reshape(shape),
        state_grad.reshape(shape),
        g_in,
        g_bin.reshape(-1),
        g_mid,
        g_bmid.reshape(-1),
        g_out.T,
        g_bout.reshape(-1),
    )


def solution(mesh):
    split_state = P(None, None, "lat", "lon")
    return jax.shard_map(
        on_device,
        mesh=mesh,
        in_specs=(split_state, P(None, "lat", "lon"), P("lat", "lon"), P(), P(), P(), P(), P(), P(), split_state),
        out_specs=(split_state, split_state, P(), P(), P(), P(), P(), P()),
        check_vma=False,
    )
```

```python
import math

import jax
import jax.numpy as jnp
from jax import lax
from jax.experimental import pallas as pl
from jax.experimental.pallas import tpu as pltpu
from jax.sharding import PartitionSpec as P

LAT_LIMIT = 1.2
CORIOLIS = 1.0
VISCOSITY = 0.15
DIFFUSIVITY = 0.1

ROWS = 16
COLS = 128
REACH = 11
CREACH = 6
PAD = 16
EXT = 48
TURN = 4
WIDE = 2 * COLS
FEATS = 40
HID = 64
PACK = 56
STRIP = 2 * PACK + 40
LAT_X = REACH * PACK
LAT = LAT_X + CREACH * FEATS
SLOT = 16
F32 = jnp.float32
BF16 = jnp.bfloat16
VMEM = pl.BlockSpec(memory_space=pltpu.VMEM)
SMEM = pl.BlockSpec(memory_space=pltpu.SMEM)


def params(megabytes):
    return pltpu.CompilerParams(vmem_limit_bytes=megabytes * 1024 * 1024)


def sds(*shape):
    return jax.ShapeDtypeStruct(shape, F32)


def sub_index(width):
    return lax.broadcasted_iota(jnp.int32, (8, width), 0)


def tile(ref, row, number):
    return ref[row, 8 * number : 8 * number + 8, :]


def slot_pack(pieces, shift_of, width):
    lane = lax.broadcasted_iota(jnp.int32, (8, COLS), 1)
    packed = None
    for slot, piece in enumerate(pieces):
        turned = pltpu.roll(piece, shift_of(slot) % COLS, 1)
        if packed is None:
            packed = turned
        else:
            packed = jnp.where((lane >= slot * width) & (lane < (slot + 1) * width), turned, packed)
    return packed


def pack_kernel(sides, x_hbm, mask_hbm, flux_hbm, cot_hbm, *outs):
    x, mask, flux, cot, sems = outs[-5:]
    own, cown, east, west, sums = outs[:5]
    per_side = outs[5 : 5 + len(sides)]
    pairs = ((mask_hbm, mask), (x_hbm, x), (flux_hbm, flux), (cot_hbm, cot))
    copies = [pltpu.make_async_copy(a, b, sems.at[i]) for i, (a, b) in enumerate(pairs)]
    for copy in copies:
        copy.start()
    for copy in copies:
        copy.wait()
    top = mask[0:ROWS, :].astype(F32)
    total = jnp.sum(jnp.sum(top * flux[...], axis=1, keepdims=True), axis=0, keepdims=True)
    count = jnp.sum(jnp.sum(top, axis=1, keepdims=True), axis=0, keepdims=True)
    sums[...] = jnp.where(sub_index(COLS) == 0, total, jnp.where(sub_index(COLS) == 1, count, 0.0))
    for r in range(ROWS):
        first = mask[pl.ds(r, 8, stride=ROWS), :].astype(F32)
        m8 = mask[8 * ROWS + r : 8 * ROWS + r + 1, :].astype(F32)
        m9 = mask[9 * ROWS + r : 9 * ROWS + r + 1, :].astype(F32)
        for t in range(4):
            own[r, 8 * t : 8 * t + 8, :] = x[pl.ds(t * 10 * ROWS + r, 8, stride=ROWS), :] * first
            cown[r, 8 * t : 8 * t + 8, :] = cot[pl.ds(t * 10 * ROWS + r, 8, stride=ROWS), :]
        for level, m in ((8, m8), (9, m9)):
            at = 32 + 4 * (level - 8)
            own[r, at : at + 4, :] = x[pl.ds(level * ROWS + r, 4, stride=10 * ROWS), :] * m
            cown[r, at : at + 4, :] = cot[pl.ds(level * ROWS + r, 4, stride=10 * ROWS), :]
        own[r, 40:48, :] = first
        own[r, 48:49, :] = m8
        own[r, 49:50, :] = m9
        own[r, 50:51, :] = flux[r : r + 1, :]
        own[r, 51:56, :] = jnp.zeros((5, COLS), F32)
    for half in range(2):
        for t in range(7):
            rows = [own[8 * half + s, 8 * t : 8 * t + 8, :] for s in range(8)]
            at = half * PACK + 8 * t
            east[at : at + 8, :] = slot_pack(rows, lambda s: SLOT * (s + 1), SLOT)
            west[at : at + 8, :] = slot_pack(rows, lambda s: SLOT * s, SLOT)
    for t in range(5):
        rows = [cown[s, 8 * t : 8 * t + 8, :] for s in range(ROWS)]
        at = 2 * PACK + 8 * t
        east[at : at + 8, :] = slot_pack(rows, lambda s: 8 * (s + 1), 8)
        west[at : at + 8, :] = slot_pack(rows, lambda s: 8 * s, 8)
    southern = (lax.axis_index("lat") == 0).astype(jnp.int32)
    for side, lat in zip(sides, per_side):
        start = {"swap": southern * (ROWS - REACH), "north": ROWS - REACH, "south": 0}[side]
        cstart = {"swap": southern * (ROWS - CREACH), "north": ROWS - CREACH, "south": 0}[side]
        for n in range(REACH):
            lat[PACK * n : PACK * (n + 1), :] = own[start + n]
        for n in range(CREACH):
            lat[LAT_X + FEATS * n : LAT_X + FEATS * (n + 1), :] = cown[cstart + n]


def corner_kernel(sides, scal, east, west, *outs):
    for side, corner in zip(sides, outs):
        start = {"swap": scal[0], "north": ROWS - REACH, "south": 0}[side]
        for at, strip, near in ((0, east, 1), (PACK + 40, west, 0)):
            for t in range(7):
                rows = slice(at + 8 * t, at + 8 * t + 8)
                corner[rows, :] = shift_rows(strip, t, start, near)
            corner[at + PACK : at + PACK + 40, :] = strip[2 * PACK : 2 * PACK + 40, :]


def shift_rows(strip, t, start, near):
    lane = lax.broadcasted_iota(jnp.int32, (8, COLS), 1)
    halves = [strip[8 * t : 8 * t + 8, :], strip[PACK + 8 * t : PACK + 8 * t + 8, :]]
    if isinstance(start, int):
        out = jnp.zeros((8, COLS), F32)
        for n in range(REACH):
            r = start + n
            turn = REACH * n - (SLOT * (r % 8) + near * (SLOT - REACH))
            turned = pltpu.roll(halves[r // 8], turn % COLS, 1)
            out = jnp.where((lane >= REACH * n) & (lane < REACH * (n + 1)), turned, out)
        return out
    low = shift_rows(strip, t, 0, near)
    high = shift_rows(strip, t, ROWS - REACH, near)
    return jnp.where(start == 0, low, high)


def split(values):
    high = values.astype(BF16)
    return high, (values - high.astype(F32)).astype(BF16)


def stack(out, values, buffer):
    k = values.shape[1]
    rows = slice(0, values.shape[0])
    high, low = split(values)
    buffer[rows, 0:k] = high.astype(F32)
    buffer[rows, k : 2 * k] = high.astype(F32)
    buffer[rows, 2 * k : 3 * k] = low.astype(F32)
    out[...] = buffer[rows, 0 : 3 * k].astype(BF16)


def by_tile(dst, src, lanes):
    for t in range(4):
        dst[8 * t : 8 * t + 8, lanes] = src[10 * t : 10 * t + 8, lanes]
        dst[32 + t : 33 + t, lanes] = src[10 * t + 8 : 10 * t + 9, lanes]
        dst[36 + t : 37 + t, lanes] = src[10 * t + 9 : 10 * t + 10, lanes]


def product(weights, high, low):
    return jnp.dot(weights, jnp.concatenate([high, low, high], axis=0), preferred_element_type=F32)


def across(a, b):
    dims = (((1,), (1,)), ((), ()))
    dot = lambda p, q: lax.dot_general(p, q, dims, preferred_element_type=F32)
    return dot(a[0], b[0]) + dot(a[0], b[1]) + dot(a[1], b[0])


def to_48(columns, first=0.0):
    more = jnp.where(sub_index(columns.shape[1]) == 0, first, 0.0).astype(F32)
    return jnp.concatenate([columns, more], axis=0)


def wide(bias, values):
    return jnp.concatenate([bias[...]] * (values.shape[1] // COLS), axis=1)


def hidden_layers(z, k1, k2, b2):
    h1 = jnp.tanh(product(k1[...], *z))
    h1s = split(h1)
    h2 = product(k2[...], *h1s)
    return h1, h1s, jnp.tanh(h2 + wide(b2, h2))


def last_layer(h2, k3, b3):
    o = product(k3[...], *split(h2))[0:FEATS]
    return o + wide(b3, o)


def add_weight_terms(acc, z, h1s, h2s, g1s, g2s, gos):
    ones = jnp.ones((16, z[0].shape[1]), BF16)
    acc[0:48, 0:HID] += across(z, g1s)
    acc[48:112, 0:HID] += across(h1s, g2s)
    acc[112:160, 0:HID] += across(gos, h2s)
    acc[160:176, 0:HID] += ones_rows(ones, g2s)
    acc[176:192, 0:48] += ones_rows(ones, gos)


def ones_rows(ones, g):
    dims = (((1,), (1,)), ((), ()))
    dot = lambda q: lax.dot_general(ones, q, dims, preferred_element_type=F32)
    return dot(g[0]) + dot(g[1])


def own_closure_kernel(own, *refs):
    raw, (out, h1_out, h2_out, k1, k2, k3, q1, q2, q3, b2, b3) = refs[:6], refs[6:17]
    w_in, w_mid, w_out, b_in, b_mid, b_out = refs[17:23]
    buffer, spare, stacked, sems = refs[23:]
    copies = [pltpu.make_async_copy(a, b, sems.at[i]) for i, (a, b) in enumerate(zip(raw, refs[17:23]))]
    for copy in copies:
        copy.start()
    for copy in copies:
        copy.wait()
    buffer[...] = jnp.zeros(buffer.shape, F32)
    by_tile(buffer, w_in, slice(0, HID))
    buffer[40:41, 0:HID] = b_in[...]
    stack(q1, buffer[0:48, 0:HID], stacked)
    spare[...] = buffer[...].T
    stack(k1, spare[0:HID, 0:48], stacked)
    buffer[0:HID, 0:HID] = w_mid[...]
    buffer[HID : HID + 1, 0:HID] = b_mid[...]
    stack(q2, buffer[0:HID, 0:HID], stacked)
    spare[...] = buffer[...].T
    stack(k2, spare[0:HID, 0:HID], stacked)
    b2[...] = jnp.broadcast_to(spare[0:HID, HID : HID + 1], (HID, COLS))
    buffer[...] = jnp.zeros(buffer.shape, F32)
    buffer[0:HID, 0:FEATS] = w_out[...]
    buffer[HID : HID + 1, 0:FEATS] = b_out[...]
    spare[...] = buffer[...].T
    buffer[...] = jnp.zeros(buffer.shape, F32)
    by_tile(buffer, spare, slice(0, COLS))
    stack(k3, buffer[0:48, 0:HID], stacked)
    b3[...] = jnp.broadcast_to(buffer[0:FEATS, HID : HID + 1], (FEATS, COLS))
    spare[...] = buffer[...].T
    stack(q3, spare[0:HID, 0:48], stacked)

    for r in range(0, ROWS, 8):
        z = split(to_48(jnp.concatenate([own[r + n, 0:FEATS, :] for n in range(8)], axis=1), 1.0))
        h1, h1s, h2 = hidden_layers(z, k1, k2, b2)
        o = last_layer(h2, k3, b3)
        for n in range(8):
            at = slice(n * COLS, (n + 1) * COLS)
            out[r + n] = o[:, at]
            h1_out[r + n] = h1[:, at]
            h2_out[r + n] = h2[:, at]


class Row:
    def __init__(self, width):
        sub = sub_index(width)
        group = sub % 4
        self.sub = sub
        self.is_t = group == 0
        self.is_s = group == 1
        self.is_u = group == 2
        self.is_v = group == 3
        self.low = sub >= 4
        self.k4 = jnp.where(group < 2, DIFFUSIVITY, VISCOSITY).astype(F32)


def put_state(k, ref, row, tiles):
    for t in range(5):
        ref[row, 8 * t : 8 * t + 8, :] = tiles[t]
    press = 0.4 * tiles[1] - 0.1 * tiles[0]
    for by in (1, 2, 4):
        press = press + jnp.where(k.sub >= by, pltpu.roll(press, by, 0), 0.0)
    ref[row, 40:48, :] = press
    deep_8 = ref[row, 47:48, :] + (0.4 * ref[row, 33:34, :] - 0.1 * ref[row, 32:33, :])
    ref[row, 48:49, :] = deep_8
    ref[row, 49:50, :] = deep_8 + (0.4 * ref[row, 37:38, :] - 0.1 * ref[row, 36:37, :])


def deep_pair(k, ref, row, upper, lower):
    return jnp.where(k.low, ref[row, lower : lower + 1, :], ref[row, upper : upper + 1, :])


def deep_u(k, ref, row):
    return deep_pair(k, ref, row, 34, 38)


def deep_v(k, ref, row):
    return deep_pair(k, ref, row, 35, 39)


def deep_p(k, ref, row):
    return deep_pair(k, ref, row, 48, 49)


def east_of(q):
    return pltpu.roll(q, q.shape[1] - 1, 1)


def west_of(q):
    return pltpu.roll(q, 1, 1)


def gain_of(k, t):
    return k.k4 if t == 4 else (DIFFUSIVITY if t < 2 else VISCOSITY)


def tendency_row(k, ref, row, c, f):
    half = 0.5 * c
    c2 = c * c
    u, v = tile(ref, row, 2), tile(ref, row, 3)
    u4, v4 = deep_u(k, ref, row), deep_v(k, ref, row)
    change = []
    for t in range(5):
        gain = gain_of(k, t)
        if t in (0, 2, 4):
            au, av = (half * u4, 0.5 * v4) if t == 4 else (half * u, 0.5 * v)
            along = gain * c2
            at_e, at_w, at_n, at_s = along - au, along + au, gain - av, gain + av
        q = tile(ref, row, t)
        east, west = at_e * east_of(q), at_w * west_of(q)
        north, south = at_n * tile(ref, row + 1, t), at_s * tile(ref, row - 1, t)
        change.append((east + west) + (north + south) - (gain * (2.0 * c2 + 2.0)) * q)
    p = tile(ref, row, 5)
    change[2] = change[2] + (f * v - half * (east_of(p) - west_of(p)))
    change[3] = change[3] - (f * u + 0.5 * (tile(ref, row + 1, 5) - tile(ref, row - 1, 5)))
    p4 = deep_p(k, ref, row)
    fx = f * v4 - half * (east_of(p4) - west_of(p4))
    fy = f * u4 + 0.5 * (deep_p(k, ref, row + 1) - deep_p(k, ref, row - 1))
    change[4] = change[4] + jnp.where(k.is_u, fx, jnp.where(k.is_v, -fy, 0.0))
    return change


def adjoint_row(k, ref, aref, row, c, f):
    half = 0.5 * c
    c2 = c * c
    u4 = deep_u(k, ref, row)
    qe = [east_of(tile(ref, row, t)) for t in range(5)]
    qw = [west_of(tile(ref, row, t)) for t in range(5)]
    out = []
    to_u = to_v = None
    for t in range(5):
        a = tile(aref, row, t)
        ae, aw = east_of(a), west_of(a)
        an, as_ = tile(aref, row + 1, t), tile(aref, row - 1, t)
        gain = gain_of(k, t)
        if t == 0:
            ue, uw = half * qe[2], half * qw[2]
            vn, vs = 0.5 * tile(ref, row + 1, 3), 0.5 * tile(ref, row - 1, 3)
        if t == 4:
            ue, uw = half * east_of(u4), half * west_of(u4)
            vn, vs = 0.5 * deep_v(k, ref, row + 1), 0.5 * deep_v(k, ref, row - 1)
        if t in (0, 2, 4):
            along = gain * c2
            at_e, at_w, at_n, at_s = along + ue, along - uw, gain + vn, gain - vs
        out.append(
            (at_e * ae + at_w * aw) + (at_n * an + at_s * as_) - (gain * (2.0 * c2 + 2.0)) * a
        )
        px = a * (qe[t] - qw[t])
        py = a * (tile(ref, row + 1, t) - tile(ref, row - 1, t))
        if t < 4:
            to_u = px if to_u is None else to_u + px
            to_v = py if to_v is None else to_v + py
        if t == 2:
            a2, bx = a, half * (ae - aw)
        if t == 3:
            a3, by = a, 0.5 * (an - as_)
        if t == 4:
            a4 = a
            deep_bx, deep_by = half * (ae - aw), 0.5 * (an - as_)
            px4, py4 = px * half, py * 0.5
    out[2] = out[2] - half * to_u - f * a3
    out[3] = out[3] - 0.5 * to_v + f * a2
    sx = px4 + pltpu.roll(px4, 7, 0)
    sx = sx + pltpu.roll(sx, 2, 0)
    sy = py4 + pltpu.roll(py4, 1, 0)
    sy = sy + pltpu.roll(sy, 2, 0)
    at_u = -sx - f * pltpu.roll(a4, 7, 0)
    at_v = f * pltpu.roll(a4, 1, 0) - sy
    deep = jnp.where(k.is_t, pltpu.roll(deep_bx, 6, 0) + pltpu.roll(deep_by, 5, 0), 0.0)
    deep = deep + jnp.where(k.low, 0.0, pltpu.roll(deep, 4, 0))
    press = bx + by
    for shift in (1, 2, 4):
        press = press + jnp.where(k.sub < 8 - shift, pltpu.roll(press, 8 - shift, 0), 0.0)
    press = press + deep[0:1, :]
    out[0] = out[0] - 0.1 * press
    out[1] = out[1] + 0.4 * press
    out[4] = out[4] + jnp.where(
        k.is_t,
        -0.1 * deep,
        jnp.where(k.is_s, 0.4 * pltpu.roll(deep, 1, 0), jnp.where(k.is_u, at_u, at_v)),
    )
    return out


def for_rows(scal, reach, body):
    low, high = PAD - reach * scal[2], PAD + ROWS + reach * scal[3]
    turns = lax.div(high - low + TURN - 1, TURN)
    first = jnp.where(scal[3] == 1, low, high - TURN * turns)

    def turn(i, _):
        for j in range(TURN):
            body(first + TURN * i + j)
        return 0

    lax.fori_loop(0, turns, turn, 0)


def mask_tile(ref, row, t):
    return tile(ref, row, 1 if t == 4 else 0)


def adjoint_third(k, scal, cs, fs, reach, state, masks, abuf, top, hold, bbuf):
    def body(r):
        d = adjoint_row(k, state, abuf, r, cs[r], fs[r])
        for t in range(5):
            ts = (2.0 / 3.0) * tile(top, r, t) + d[t]
            hold[r, 8 * t : 8 * t + 8, :] = ts
            bbuf[r, 8 * t : 8 * t + 8, :] = 0.0625 * mask_tile(masks, r, t) * ts

    for_rows(scal, reach, body)


def adjoint_second(k, scal, cs, fs, reach, state, masks, bbuf, top, hold, left, abuf):
    def body(r):
        d = adjoint_row(k, state, bbuf, r, cs[r], fs[r])
        for t in range(5):
            ts = tile(hold, r, t)
            tf = 0.25 * ts + d[t]
            left[r, 8 * t : 8 * t + 8, :] = (1.0 / 3.0) * tile(top, r, t) + 0.75 * ts + tf
            abuf[r, 8 * t : 8 * t + 8, :] = 0.25 * mask_tile(masks, r, t) * tf

    for_rows(scal, reach, body)


def adjoint_first(k, scal, cs, fs, reach, state, abuf, left, store):
    def body(r):
        d = adjoint_row(k, state, abuf, r, cs[r], fs[r])
        store(r, [tile(left, r, t) + d[t] for t in range(5)])

    for_rows(scal, reach, body)


def edges(reach):
    lane = lax.broadcasted_iota(jnp.int32, (8, COLS), 1)
    return lane < reach, lane >= COLS - reach


def wide_pack(ref, base):
    parts = []
    for t in range(5):
        rows = [ref[base + s, 8 * t : 8 * t + 8, COLS:WIDE] for s in range(8)]
        parts.append(slot_pack(rows, lambda s: 8 + SLOT * s, SLOT))
    return jnp.concatenate(parts, axis=0)

def wide_unpack(ref, base, values):
    for s in range(8):
        ref[base + s, 0:FEATS, COLS:WIDE] = pltpu.roll(values, -(8 + SLOT * s) % COLS, 1)


def section_1(k, cs, fs, masks, src, dst):
    def body(r):
        d = tendency_row(k, src, r, cs[r], fs[r])
        put_state(
            k, dst, r,
            [tile(src, r, t) + 0.25 * mask_tile(masks, r, t) * d[t] for t in range(5)],
        )
    return body

def section_2(k, cs, fs, masks, src, mid, dst):
    def body(r):
        d = tendency_row(k, mid, r, cs[r], fs[r])
        put_state(
            k, dst, r,
            [
                0.75 * tile(src, r, t) + 0.25 * tile(mid, r, t)
                + 0.0625 * mask_tile(masks, r, t) * d[t]
                for t in range(5)
            ],
        )
    return body


def section_3(k, cs, fs, masks, fluxes, mean, src, mid, net, r):
    d = tendency_row(k, mid, r, cs[r], fs[r])
    new = []
    for t in range(5):
        m = mask_tile(masks, r, t)
        o = tile(net, r, t)
        if t == 1:
            force = 2.0 * (mean - fluxes[r, 2:3, :])
            o = o + jnp.where(k.sub == 0, force, 0.0)
        new.append(
            (1.0 / 3.0) * tile(src, r, t) + (2.0 / 3.0) * tile(mid, r, t)
            + m * ((1.0 / 6.0) * d[t] + 0.25 * o)
        )
    return new


def zero_walls(ref):
    for row in (PAD - 1, PAD + ROWS):
        ref[row] = jnp.zeros(ref.shape[1:], F32)


def assemble_kernel(sides, scal, cs, fs, own, own_m, east, west, *rest):
    n = len(sides)
    side_refs = [rest[2 * i : 2 * i + 2] for i in range(n)]
    (k1, k2, k3, b2, b3), rest = rest[2 * n : 2 * n + 5], rest[2 * n + 5 :]
    s0, masks, fluxes, outs = rest
    k = Row(WIDE)
    has_south = scal[2]
    lo = lambda h: PAD - h * has_south

    zero_walls(s0)

    near_e, near_w = edges(REACH)

    def put_packed(row, core, halo):
        both = lambda t: jnp.concatenate([core(t), halo(t)], axis=1)
        put_state(k, s0, row, [both(t) for t in range(5)])
        masks[row, 0:8, :] = both(5)
        last = both(6)
        masks[row, 8:16, :] = jnp.where(k.low, last[1:2, :], last[0:1, :])
        fluxes[row] = last

    for r in range(ROWS):
        at = (r // 8) * PACK
        turn = SLOT * (r % 8)

        def halo(t):
            from_e = pltpu.roll(west[at + 8 * t : at + 8 * t + 8, :], -turn % COLS, 1)
            from_w = pltpu.roll(east[at + 8 * t : at + 8 * t + 8, :], -(turn + SLOT) % COLS, 1)
            return jnp.where(near_e, from_e, jnp.where(near_w, from_w, 0.0))

        put_packed(PAD + r, lambda t: own[r, 8 * t : 8 * t + 8, :], halo)
    for side, (lat, corner) in zip(sides, side_refs):
        base = {"swap": scal[4], "north": PAD - REACH, "south": PAD + ROWS}[side]
        for r in range(REACH):

            def halo(t):
                wrows = slice(8 * t, 8 * t + 8)
                erows = slice(PACK + 40 + 8 * t, PACK + 48 + 8 * t)
                from_e = pltpu.roll(corner[erows, :], -REACH * r % COLS, 1)
                from_w = pltpu.roll(corner[wrows, :], -REACH * (r + 1) % COLS, 1)
                return jnp.where(near_e, from_e, jnp.where(near_w, from_w, 0.0))

            put_packed(base + r, lambda t: lat[PACK * r + 8 * t : PACK * r + 8 * t + 8, :], halo)

    for r in range(ROWS):
        outs[PAD + r, :, 0:COLS] = own_m[r]

    def closure_of(columns):
        _, _, h2 = hidden_layers(split(to_48(columns, 1.0)), k1, k2, b2)
        return last_layer(h2, k3, b3)

    def halo_rows(first):
        o = closure_of(jnp.concatenate([s0[first + i, 0:FEATS, 0:COLS] for i in range(8)], axis=1))
        for i in range(8):
            outs[first + i, :, 0:COLS] = o[:, i * COLS : (i + 1) * COLS]

    if sides == ["swap"]:
        groups = 3
        halo_rows(jnp.where(has_south == 1, PAD - 8, PAD + ROWS))
    else:
        groups = 4
        halo_rows(PAD - 8)
        halo_rows(PAD + ROWS)
    first = lo(8)
    o = closure_of(jnp.concatenate([wide_pack(s0, first + 8 * g) for g in range(groups)], axis=1))
    for g in range(groups):
        wide_unpack(outs, first + 8 * g, o[:, g * COLS : (g + 1) * COLS])


def first_section_kernel(scal, cs, fs, s0, masks, s1):
    zero_walls(s1)
    for_rows(scal, 10, section_1(Row(WIDE), cs, fs, masks, s0, s1))


def second_section_kernel(scal, cs, fs, s0, s1, masks, s2):
    zero_walls(s2)
    for_rows(scal, 9, section_2(Row(WIDE), cs, fs, masks, s0, s1, s2))


def last_section_kernel(scal, cs, fs, sums, s3, t2, masks, fluxes, outs, final):
    k = Row(WIDE)
    mean = sums[0:1, 0:1] / sums[1:2, 0:1]

    def last(r):
        new = section_3(k, cs, fs, masks, fluxes, mean, s3, t2, outs, r)
        put_result(final, r - PAD, [x[:, 0:COLS] for x in new])

    for_rows(scal, 0, last)


def late_kernel(
    sides, scal, cs, fs, sums, own, cown, own_h1, own_h2, s0, s2, masks, fluxes, outs_in, east, west, *rest
):
    n = len(sides)
    side_refs = [rest[2 * i : 2 * i + 2] for i in range(n)]
    (k1, k2, k3, q1, q2, q3, b2, b3), rest = rest[2 * n : 2 * n + 8], rest[2 * n + 8 :]
    grads, s4, abuf, from_closure, s3, t2, outs, t1, cot, gz, bbuf, hold, left, acc = rest
    k = Row(WIDE)
    has_south = scal[2]
    lo = lambda h: PAD - h * has_south
    for ref in (s3, t1, t2, abuf, bbuf):
        zero_walls(ref)
    mean = sums[0:1, 0:1] / sums[1:2, 0:1]

    cnear_e, cnear_w = edges(CREACH)
    for r in range(ROWS):
        for t in range(5):
            rows = slice(2 * PACK + 8 * t, 2 * PACK + 8 * t + 8)
            from_e = pltpu.roll(west[rows, :], -8 * r % COLS, 1)
            from_w = pltpu.roll(east[rows, :], -8 * (r + 1) % COLS, 1)
            side = jnp.where(cnear_e, from_e, jnp.where(cnear_w, from_w, 0.0))
            cot[PAD + r, 8 * t : 8 * t + 8, :] = jnp.concatenate(
                [cown[r, 8 * t : 8 * t + 8, :], side], axis=1
            )
    for side, (lat, corner) in zip(sides, side_refs):
        cbase = {"swap": scal[5], "north": PAD - CREACH, "south": PAD + ROWS}[side]
        crow = {"swap": scal[6], "north": ROWS - CREACH, "south": 0}[side]
        for r in range(CREACH):
            turn = lax.rem(2 * COLS - 8 * (crow + r), COLS)
            turn_w = lax.rem(2 * COLS - 8 * (crow + r + 1), COLS)
            for t in range(5):
                wrows = slice(PACK + 8 * t, PACK + 8 * t + 8)
                erows = slice(2 * PACK + 40 + 8 * t, 2 * PACK + 48 + 8 * t)
                from_e = pltpu.roll(corner[erows, :], turn, 1)
                from_w = pltpu.roll(corner[wrows, :], turn_w, 1)
                part = jnp.where(cnear_e, from_e, jnp.where(cnear_w, from_w, 0.0))
                cot[cbase + r, 8 * t : 8 * t + 8, :] = jnp.concatenate(
                    [lat[LAT_X + FEATS * r + 8 * t : LAT_X + FEATS * r + 8 * t + 8, :], part], axis=1
                )


    def step_1_end(r):
        put_state(k, s3, r, section_3(s0, s2, r))

    def step_1_end(r):
        put_state(k, s3, r, section_3(k, cs, fs, masks, fluxes, mean, s0, s2, outs_in, r))

    for_rows(scal, 8, step_1_end)

    acc[...] = jnp.zeros(acc.shape, F32)

    def closure_adjoint(z, h1, h1s, h2, go, with_weights):
        gos = split(to_48(go))
        g2 = product(q3[...], *gos) * (1.0 - h2 * h2)
        g2s = split(g2)
        g1 = product(q2[...], *g2s) * (1.0 - h1 * h1)
        g1s = split(g1)
        if with_weights:
            add_weight_terms(acc, z, h1s, split(h2), g1s, g2s, gos)
        return product(q1[...], *g1s)[0:FEATS]

    def both_ways(columns, go, with_weights):
        z = split(to_48(columns, 1.0))
        h1, h1s, h2 = hidden_layers(z, k1, k2, b2)
        o = last_layer(h2, k3, b3) if with_weights else None
        return o, closure_adjoint(z, h1, h1s, h2, go, with_weights)

    def masked_core(ref, r):
        m0, m4 = masks[r, 0:8, 0:COLS], masks[r, 8:16, 0:COLS]
        parts = [
            0.25 * (m4 if t == 4 else m0) * ref[r, 8 * t : 8 * t + 8, 0:COLS] for t in range(5)
        ]
        return jnp.concatenate(parts, axis=0)

    def mask_cot(r):
        for t in range(5):
            bbuf[r, 8 * t : 8 * t + 8, :] = 0.25 * mask_tile(masks, r, t) * tile(cot, r, t)
            abuf[r, 8 * t : 8 * t + 8, :] = (1.0 / 6.0) * mask_tile(masks, r, t) * tile(cot, r, t)

    for_rows(scal, 6, mask_cot)

    for first in range(PAD, PAD + ROWS, 8):
        z = jnp.concatenate([s3[first + i, 0:FEATS, 0:COLS] for i in range(8)], axis=1)
        go = jnp.concatenate([bbuf[first + i, 0:FEATS, 0:COLS] for i in range(8)], axis=1)
        o, back = both_ways(z, go, True)
        for i in range(8):
            at = slice(i * COLS, (i + 1) * COLS)
            outs[first + i, :, 0:COLS] = o[:, at]
            gz[first + i, :, 0:COLS] = back[:, at]

    first = lo(4)
    if sides == ["swap"]:
        rows = [jnp.where(has_south == 1, PAD - 4, PAD + ROWS) + i for i in range(4)]
    else:
        rows = [PAD - 4 + i for i in range(4)] + [PAD + ROWS + i for i in range(4)]
    beyond = lambda ref: jnp.concatenate(
        [ref[r, 0:FEATS, 0:COLS] for r in rows] + [wide_pack(ref, first + 8 * g) for g in range(3)], axis=1
    )
    _, back = both_ways(beyond(s3), beyond(bbuf), False)
    for i, r in enumerate(rows):
        gz[r, :, 0:COLS] = back[:, i * COLS : (i + 1) * COLS]
    for g in range(3):
        at = (len(rows) + g) * COLS
        wide_unpack(gz, first + 8 * g, back[:, at : at + COLS])

    for_rows(scal, 7, section_1(k, cs, fs, masks, s3, t1))
    for_rows(scal, 6, section_2(k, cs, fs, masks, s3, t1, t2))

    def store(r, tiles):
        for t in range(5):
            s4[r, 8 * t : 8 * t + 8, :] = tiles[t] + tile(gz, r, t)

    adjoint_third(k, scal, cs, fs, 5, t2, masks, abuf, cot, hold, bbuf)
    adjoint_second(k, scal, cs, fs, 4, t1, masks, bbuf, cot, hold, left, abuf)
    adjoint_first(k, scal, cs, fs, 3, s3, abuf, left, store)

    for r in range(0, ROWS, 8):
        side = lambda read: jnp.concatenate([read(r + j) for j in range(8)], axis=1)
        z = split(to_48(side(lambda j: own[j, 0:FEATS, :]), 1.0))
        h1 = side(lambda j: own_h1[j])
        h2 = side(lambda j: own_h2[j])
        go = side(lambda j: masked_core(s4, PAD + j))
        back = closure_adjoint(z, h1, split(h1), h2, go, True)
        for j in range(8):
            from_closure[r + j] = back[:, j * COLS : (j + 1) * COLS]

    zero_walls(abuf)

    def mask_top(r):
        for t in range(5):
            abuf[r, 8 * t : 8 * t + 8, :] = (1.0 / 6.0) * mask_tile(masks, r, t) * tile(s4, r, t)

    for_rows(scal, 3, mask_top)
    grads[...] = jnp.zeros(grads.shape, F32)
    grads[0:40, 0:HID] = acc[0:40, 0:HID]
    grads[0:40, HID : 2 * HID] = acc[112:152, 0:HID]
    grads[40:72, 0:HID] = acc[48:80, 0:HID]
    grads[40:72, HID : 2 * HID] = acc[80:112, 0:HID]
    grads[72:73, 0:HID] = acc[40:41, 0:HID]
    grads[72:73, HID : 2 * HID] = acc[160:161, 0:HID]
    grads[73:74, 0:HID] = acc[176:177, 0:HID]


def put_result(ref, row, tiles):
    for t in range(4):
        ref[pl.ds(t * 10 * ROWS + row, 8, stride=ROWS), :] = tiles[t]
    ref[pl.ds(8 * ROWS + row, 4, stride=10 * ROWS), :] = tiles[4][0:4, :]
    ref[pl.ds(9 * ROWS + row, 4, stride=10 * ROWS), :] = tiles[4][4:8, :]


def back_third_kernel(scal, cs, fs, state, masks, abuf, top, hold, bbuf):
    zero_walls(bbuf)
    adjoint_third(Row(WIDE), scal, cs, fs, 2, state, masks, abuf, top, hold, bbuf)


def back_second_kernel(scal, cs, fs, state, masks, bbuf, top, hold, left, abuf):
    zero_walls(abuf)
    adjoint_second(Row(WIDE), scal, cs, fs, 1, state, masks, bbuf, top, hold, left, abuf)


def back_first_kernel(scal, cs, fs, state, masks, abuf, left, from_closure, grad):
    def store(r, tiles):
        done = []
        for t in range(5):
            m = masks[r, 8:16, 0:COLS] if t == 4 else masks[r, 0:8, 0:COLS]
            done.append(m * (tiles[t][:, 0:COLS] + from_closure[r - PAD, 8 * t : 8 * t + 8, :]))
        put_result(grad, r - PAD, done)

    adjoint_first(Row(WIDE), scal, cs, fs, 0, state, abuf, left, store)


def unpack_kernel(scale, packed, win, bin_, wmid, bmid, wout, bout):
    for ref, lanes in ((win, slice(0, HID)), (wout, slice(HID, 2 * HID))):
        for t in range(4):
            ref[10 * t : 10 * t + 8, :] = packed[8 * t : 8 * t + 8, lanes] * scale
            ref[10 * t + 8 : 10 * t + 9, :] = packed[32 + t : 33 + t, lanes] * scale
            ref[10 * t + 9 : 10 * t + 10, :] = packed[36 + t : 37 + t, lanes] * scale
    wmid[0:32, :] = packed[40:72, 0:HID] * scale
    wmid[32:64, :] = packed[40:72, HID : 2 * HID] * scale
    bin_[...] = packed[72:73, 0:HID] * scale
    bmid[...] = packed[72:73, HID : 2 * HID] * scale
    for t in range(4):
        bout[:, 10 * t : 10 * t + 8] = packed[73:74, 8 * t : 8 * t + 8] * scale
        bout[:, 10 * t + 8 : 10 * t + 9] = packed[73:74, 32 + t : 33 + t] * scale
        bout[:, 10 * t + 9 : 10 * t + 10] = packed[73:74, 36 + t : 37 + t] * scale


def far_first(axes):
    return [(axis, n, 1 << bit) for axis, n in axes for bit in reversed(range(n.bit_length() - 1))]


def pair_rounds(x, rounds, beside):
    results = []
    for i in range(max(len(rounds), len(beside))):
        if i < len(rounds):
            axis, n, step = rounds[i]
            got = lax.ppermute(x, axis, [(j, j ^ step) for j in range(n)])
        if i < len(beside):
            results.append(beside[i](results))
            if i < len(rounds):
                got, results[-1] = lax.optimization_barrier((got, results[-1]))
        if i < len(rounds):
            x = x + got
    return x, results


def latitude_terms(row_index, row_count):
    latitude = LAT_LIMIT * (2.0 * (jnp.clip(row_index, 0.0, row_count - 1.0) + 0.5) / row_count - 1.0)
    return 1.0 / jnp.cos(latitude), CORIOLIS * jnp.sin(latitude)


def on_device(
    initial_state, land_mask, surface_flux, weight_in, bias_in, weight_mid, bias_mid, weight_out, bias_out, cotangent
):
    lat_n, lon_n = lax.axis_size("lat"), lax.axis_size("lon")
    lat_i = lax.axis_index("lat")
    lat_total, lon_total = ROWS * lat_n, COLS * lon_n
    sides = ["swap"] if lat_n == 2 else ["north", "south"]
    is_low = (lat_i == 0).astype(jnp.int32)
    has_south = (lat_i > 0).astype(jnp.int32)
    has_north = (lat_i < lat_n - 1).astype(jnp.int32)
    scal = jnp.stack(
        [
            is_low * (ROWS - REACH),
            is_low * (ROWS - CREACH),
            has_south,
            has_north,
            jnp.where(is_low == 1, PAD + ROWS, PAD - REACH),
            jnp.where(is_low == 1, PAD + ROWS, PAD - CREACH),
            jnp.where(is_low == 1, 0, ROWS - CREACH),
        ]
    ).astype(jnp.int32)
    rows = (lat_i * ROWS - PAD + jnp.arange(EXT, dtype=jnp.int32)).astype(F32)
    cs, fs = latitude_terms(rows, lat_total)

    hbm = pl.BlockSpec(memory_space=pltpu.HBM)
    packed = pl.pallas_call(
        lambda *refs: pack_kernel(sides, *refs),
        out_shape=[
            sds(ROWS, PACK, COLS), sds(ROWS, FEATS, COLS), sds(STRIP, COLS), sds(STRIP, COLS), sds(8, COLS),
        ]
        + [sds(LAT, COLS)] * len(sides),
        in_specs=[hbm] * 4,
        out_specs=[VMEM] * (5 + len(sides)),
        scratch_shapes=[
            pltpu.VMEM((40 * ROWS, COLS), F32), pltpu.VMEM((10 * ROWS, COLS), jnp.int32),
            pltpu.VMEM((ROWS, COLS), F32), pltpu.VMEM((40 * ROWS, COLS), F32), pltpu.SemaphoreType.DMA((4,)),
        ],
        compiler_params=params(56),
        cost_estimate=pl.CostEstimate(flops=10**9, bytes_accessed=3 * 10**6, transcendentals=0),
        name="pack_halos",
    )(
        initial_state.reshape(40 * ROWS, COLS),
        land_mask.reshape(10 * ROWS, COLS),
        surface_flux,
        cotangent.reshape(40 * ROWS, COLS),
    )
    own, cown, east_pay, west_pay, sums = packed[:5]

    def lat_pairs(side):
        if side == "swap":
            return [(0, 1), (1, 0)]
        if side == "north":
            return [(i, i + 1) for i in range(lat_n - 1)]
        return [(i + 1, i) for i in range(lat_n - 1)]

    east_ring = [(i, (i + 1) % lon_n) for i in range(lon_n)]
    west_ring = [((i + 1) % lon_n, i) for i in range(lon_n)]
    from_west = lax.ppermute(east_pay, "lon", east_ring)
    from_east = lax.ppermute(west_pay, "lon", west_ring)
    row = lambda b: b.reshape(1, -1)
    raw = (weight_in, weight_mid, weight_out, row(bias_in), row(bias_mid), row(bias_out))
    half = lambda *shape: jax.ShapeDtypeStruct(shape, BF16)
    own_closure = pl.pallas_call(
        own_closure_kernel,
        out_shape=[
            sds(ROWS, FEATS, COLS), sds(ROWS, HID, COLS), sds(ROWS, HID, COLS),
            half(HID, 144), half(HID, 192), half(48, 192), half(48, 192), half(HID, 192), half(HID, 144),
            sds(HID, COLS), sds(FEATS, COLS),
        ],
        in_specs=[VMEM] + [hbm] * 6,
        out_specs=[VMEM] * 11,
        scratch_shapes=[pltpu.VMEM(w.shape, F32) for w in raw]
        + [pltpu.VMEM((COLS, COLS), F32), pltpu.VMEM((COLS, COLS), F32), pltpu.VMEM((HID, WIDE), F32)]
        + [pltpu.SemaphoreType.DMA((6,))],
        compiler_params=params(12),
        cost_estimate=pl.CostEstimate(flops=10**9, bytes_accessed=2 * 10**6, transcendentals=0),
        name="own_closure",
    )
    pack_corners = pl.pallas_call(
        lambda *refs: corner_kernel(sides, *refs),
        out_shape=[sds(2 * PACK + 80, COLS)] * len(sides),
        in_specs=[SMEM, VMEM, VMEM],
        out_specs=[VMEM] * len(sides),
        compiler_params=params(8),
        cost_estimate=pl.CostEstimate(flops=10**8, bytes_accessed=10**6, transcendentals=0),
        name="pack_corners",
    )
    total, results = pair_rounds(
        sums,
        far_first((("lat", lat_n),)) + far_first((("lon", lon_n),))[::-1],
        [
            lambda done: packed[5:],
            lambda done: own_closure(own, *raw),
            lambda done: pack_corners(scal, from_west, from_east),
        ],
    )
    lats = [lax.ppermute(pay, "lat", lat_pairs(side)) for side, pay in zip(sides, results[0])]
    corners = [lax.ppermute(pay, "lat", lat_pairs(side)) for side, pay in zip(sides, results[2])]
    received = [ref for pair in zip(lats, corners) for ref in pair]
    own_m, own_h1, own_h2, k1, k2, k3, q1, q2, q3, b2, b3 = results[1]

    geometry = (scal, cs, fs)
    state = sds(EXT, 56, WIDE)
    plain = sds(EXT, FEATS, WIDE)
    marks = sds(EXT, 16, WIDE)
    vmem = lambda shape: pltpu.VMEM(shape.shape, F32)

    def call(kernel, name, out_shape, scratch, args, flops, limit):
        single = not isinstance(out_shape, list)
        return pl.pallas_call(
            kernel,
            out_shape=out_shape,
            in_specs=[SMEM] * 3 + [VMEM] * len(args),
            out_specs=VMEM if single else [VMEM] * len(out_shape),
            scratch_shapes=scratch,
            compiler_params=params(limit),
            cost_estimate=pl.CostEstimate(flops=flops, bytes_accessed=10**7, transcendentals=0),
            name=name,
        )(*geometry, *args)

    s0, masks, fluxes, net = call(
        lambda *refs: assemble_kernel(sides, *refs), "assemble",
        [state, marks, sds(EXT, 8, WIDE), plain], [],
        [own, own_m, from_west, from_east] + received + [k1, k2, k3, b2, b3],
        2 * 10**9, 8,
    )
    s1 = call(first_section_kernel, "first_section", state, [], [s0, masks], 10**9, 8)
    s2 = call(second_section_kernel, "second_section", state, [], [s0, s1, masks], 10**9, 8)
    grads, top, abuf, from_closure, s3, t2, net_2 = call(
        lambda *refs: late_kernel(sides, *refs), "steps_and_adjoint",
        [sds(80, COLS), plain, plain, sds(ROWS, FEATS, COLS), state, state, plain],
        [vmem(state)] + [vmem(plain)] * 5 + [pltpu.VMEM((192, HID), F32)],
        [total, own, cown, own_h1, own_h2, s0, s2, masks, fluxes, net, from_west, from_east]
        + received + [k1, k2, k3, q1, q2, q3, b2, b3],
        4 * 10**9, 18,
    )
    beside = [
        lambda done: call(
            back_third_kernel, "adjoint_third_section", [plain, plain], [], [s2, masks, abuf, top], 10**9, 8
        ),
        lambda done: call(
            back_second_kernel, "adjoint_second_section", [plain, plain], [],
            [s1, masks, done[0][1], top, done[0][0]], 10**9, 8,
        ),
        lambda done: call(
            back_first_kernel, "adjoint_first_section", sds(40 * ROWS, COLS), [],
            [s0, masks, done[1][1], done[1][0], from_closure], 10**9, 8,
        ),
        lambda done: call(
            last_section_kernel, "last_section", sds(40 * ROWS, COLS), [],
            [total, s3, t2, masks, fluxes, net_2], 10**9, 8,
        ),
    ]
    by_lon, by_lat = far_first((("lon", lon_n),)), far_first((("lat", lat_n),))
    summed, results = pair_rounds(grads, by_lon[:-2] + by_lat + by_lon[-2:], beside)
    state_grad, final = results[2:]

    scale = 1.0 / math.sqrt(lat_total * lon_total)
    g_in, g_bin, g_mid, g_bmid, g_out, g_bout = pl.pallas_call(
        lambda *refs: unpack_kernel(scale, *refs),
        out_shape=[sds(40, HID), sds(1, HID), sds(HID, HID), sds(1, HID), sds(40, HID), sds(1, 40)],
        in_specs=[VMEM],
        out_specs=[VMEM] * 6,
        compiler_params=params(8),
        name="unpack_weight_grads",
    )(summed)
    shape = initial_state.shape
    return (
        final.reshape(shape),
        state_grad.reshape(shape),
        g_in,
        g_bin.reshape(-1),
        g_mid,
        g_bmid.reshape(-1),
        g_out.T,
        g_bout.reshape(-1),
    )


def solution(mesh):
    split_state = P(None, None, "lat", "lon")
    return jax.shard_map(
        on_device,
        mesh=mesh,
        in_specs=(split_state, P(None, "lat", "lon"), P("lat", "lon"), P(), P(), P(), P(), P(), P(), split_state),
        out_specs=(split_state, split_state, P(), P(), P(), P(), P(), P()),
        check_vma=False,
    )
```

```python
import math

import jax
import jax.numpy as jnp
from jax import lax
from jax.experimental import pallas as pl
from jax.experimental.pallas import tpu as pltpu
from jax.sharding import PartitionSpec as P

LAT_LIMIT = 1.2
CORIOLIS = 1.0
VISCOSITY = 0.15
DIFFUSIVITY = 0.1

ROWS = 16
COLS = 128
REACH = 11
CREACH = 6
PAD = 16
EXT = 48
TURN = 4
WIDE = 2 * COLS
FEATS = 40
HID = 64
PACK = 56
SUMS = 51
STRIP = 2 * PACK + 40
LAT_X = REACH * PACK
CORNER = 2 * PACK + 80
LAT = LAT_X + CREACH * FEATS
SLOT = 16
F32 = jnp.float32
BF16 = jnp.bfloat16
VMEM = pl.BlockSpec(memory_space=pltpu.VMEM)
SMEM = pl.BlockSpec(memory_space=pltpu.SMEM)


def params(megabytes):
    return pltpu.CompilerParams(vmem_limit_bytes=megabytes * 1024 * 1024)


def sds(*shape):
    return jax.ShapeDtypeStruct(shape, F32)


def sub_index(width):
    return lax.broadcasted_iota(jnp.int32, (8, width), 0)


def tile(ref, row, number):
    return ref[row, 8 * number : 8 * number + 8, :]


def slot_pack(pieces, shift_of, width):
    lane = lax.broadcasted_iota(jnp.int32, (8, COLS), 1)
    packed = None
    for slot, piece in enumerate(pieces):
        turned = pltpu.roll(piece, shift_of(slot) % COLS, 1)
        if packed is None:
            packed = turned
        else:
            packed = jnp.where((lane >= slot * width) & (lane < (slot + 1) * width), turned, packed)
    return packed


def pack_kernel(sides, x_hbm, mask_hbm, flux_hbm, cot_hbm, *outs):
    x, mask, flux, cot, sems = outs[-5:]
    own, cown, east, west, sums = outs[:5]
    per_side = outs[5 : 5 + len(sides)]
    pairs = ((mask_hbm, mask), (x_hbm, x), (flux_hbm, flux), (cot_hbm, cot))
    copies = [pltpu.make_async_copy(a, b, sems.at[i]) for i, (a, b) in enumerate(pairs)]
    for copy in copies:
        copy.start()
    for copy in copies:
        copy.wait()
    top = mask[0:ROWS, :].astype(F32)
    total = jnp.sum(jnp.sum(top * flux[...], axis=1, keepdims=True), axis=0, keepdims=True)
    count = jnp.sum(jnp.sum(top, axis=1, keepdims=True), axis=0, keepdims=True)
    sums[...] = jnp.where(sub_index(COLS) == 0, total, jnp.where(sub_index(COLS) == 1, count, 0.0))
    for r in range(ROWS):
        first = mask[pl.ds(r, 8, stride=ROWS), :].astype(F32)
        m8 = mask[8 * ROWS + r : 8 * ROWS + r + 1, :].astype(F32)
        m9 = mask[9 * ROWS + r : 9 * ROWS + r + 1, :].astype(F32)
        for t in range(4):
            own[r, 8 * t : 8 * t + 8, :] = x[pl.ds(t * 10 * ROWS + r, 8, stride=ROWS), :] * first
            cown[r, 8 * t : 8 * t + 8, :] = cot[pl.ds(t * 10 * ROWS + r, 8, stride=ROWS), :]
        for level, m in ((8, m8), (9, m9)):
            at = 32 + 4 * (level - 8)
            own[r, at : at + 4, :] = x[pl.ds(level * ROWS + r, 4, stride=10 * ROWS), :] * m
            cown[r, at : at + 4, :] = cot[pl.ds(level * ROWS + r, 4, stride=10 * ROWS), :]
        own[r, 40:48, :] = first
        own[r, 48:49, :] = m8
        own[r, 49:50, :] = m9
        own[r, 50:51, :] = flux[r : r + 1, :]
        own[r, SUMS:PACK, :] = sums[0:5, :]
    for half in range(2):
        for t in range(7):
            rows = [own[8 * half + s, 8 * t : 8 * t + 8, :] for s in range(8)]
            at = half * PACK + 8 * t
            east[at : at + 8, :] = slot_pack(rows, lambda s: SLOT * (s + 1), SLOT)
            west[at : at + 8, :] = slot_pack(rows, lambda s: SLOT * s, SLOT)
    for t in range(5):
        rows = [cown[s, 8 * t : 8 * t + 8, :] for s in range(ROWS)]
        at = 2 * PACK + 8 * t
        east[at : at + 8, :] = slot_pack(rows, lambda s: 8 * (s + 1), 8)
        west[at : at + 8, :] = slot_pack(rows, lambda s: 8 * s, 8)
    southern = (lax.axis_index("lat") == 0).astype(jnp.int32)
    for side, lat in zip(sides, per_side):
        start = {"swap": southern * (ROWS - REACH), "north": ROWS - REACH, "south": 0}[side]
        cstart = {"swap": southern * (ROWS - CREACH), "north": ROWS - CREACH, "south": 0}[side]
        for n in range(REACH):
            lat[PACK * n : PACK * (n + 1), :] = own[start + n]
        for n in range(CREACH):
            lat[LAT_X + FEATS * n : LAT_X + FEATS * (n + 1), :] = cown[cstart + n]


def corner_kernel(sides, scal, east, west, *outs):
    for side, corner in zip(sides, outs):
        start = {"swap": scal[0], "north": ROWS - REACH, "south": 0}[side]
        for at, strip, near in ((0, east, 1), (PACK + 40, west, 0)):
            for t in range(7):
                rows = slice(at + 8 * t, at + 8 * t + 8)
                corner[rows, :] = shift_rows(strip, t, start, near)
            corner[at + PACK : at + PACK + 40, :] = strip[2 * PACK : 2 * PACK + 40, :]
        corner[CORNER : CORNER + 8, :] = jnp.zeros((8, COLS), F32)


def shift_rows(strip, t, start, near):
    lane = lax.broadcasted_iota(jnp.int32, (8, COLS), 1)
    halves = [strip[8 * t : 8 * t + 8, :], strip[PACK + 8 * t : PACK + 8 * t + 8, :]]
    if isinstance(start, int):
        out = jnp.zeros((8, COLS), F32)
        for n in range(REACH):
            r = start + n
            turn = REACH * n - (SLOT * (r % 8) + near * (SLOT - REACH))
            turned = pltpu.roll(halves[r // 8], turn % COLS, 1)
            out = jnp.where((lane >= REACH * n) & (lane < REACH * (n + 1)), turned, out)
        return out
    low = shift_rows(strip, t, 0, near)
    high = shift_rows(strip, t, ROWS - REACH, near)
    return jnp.where(start == 0, low, high)


def split(values):
    high = values.astype(BF16)
    return high, (values - high.astype(F32)).astype(BF16)


def stack(out, values, buffer):
    k = values.shape[1]
    rows = slice(0, values.shape[0])
    high, low = split(values)
    buffer[rows, 0:k] = high.astype(F32)
    buffer[rows, k : 2 * k] = high.astype(F32)
    buffer[rows, 2 * k : 3 * k] = low.astype(F32)
    out[...] = buffer[rows, 0 : 3 * k].astype(BF16)


def by_tile(dst, src, lanes):
    for t in range(4):
        dst[8 * t : 8 * t + 8, lanes] = src[10 * t : 10 * t + 8, lanes]
        dst[32 + t : 33 + t, lanes] = src[10 * t + 8 : 10 * t + 9, lanes]
        dst[36 + t : 37 + t, lanes] = src[10 * t + 9 : 10 * t + 10, lanes]


def product(weights, high, low):
    return jnp.dot(weights, jnp.concatenate([high, low, high], axis=0), preferred_element_type=F32)


def across(a, b):
    dims = (((1,), (1,)), ((), ()))
    dot = lambda p, q: lax.dot_general(p, q, dims, preferred_element_type=F32)
    return dot(a[0], b[0]) + dot(a[0], b[1]) + dot(a[1], b[0])


def to_48(columns, first=0.0):
    more = jnp.where(sub_index(columns.shape[1]) == 0, first, 0.0).astype(F32)
    return jnp.concatenate([columns, more], axis=0)


def wide(bias, values):
    return jnp.concatenate([bias[...]] * (values.shape[1] // COLS), axis=1)


def hidden_layers(z, k1, k2, b2):
    h1 = jnp.tanh(product(k1[...], *z))
    h1s = split(h1)
    h2 = product(k2[...], *h1s)
    return h1, h1s, jnp.tanh(h2 + wide(b2, h2))


def last_layer(h2, k3, b3):
    o = product(k3[...], *split(h2))[0:FEATS]
    return o + wide(b3, o)


def add_weight_terms(acc, z, h1s, h2s, g1s, g2s, gos):
    ones = jnp.ones((16, z[0].shape[1]), BF16)
    acc[0:48, 0:HID] += across(z, g1s)
    acc[48:112, 0:HID] += across(h1s, g2s)
    acc[112:160, 0:HID] += across(gos, h2s)
    acc[160:176, 0:HID] += ones_rows(ones, g2s)
    acc[176:192, 0:48] += ones_rows(ones, gos)


def ones_rows(ones, g):
    dims = (((1,), (1,)), ((), ()))
    dot = lambda q: lax.dot_general(ones, q, dims, preferred_element_type=F32)
    return dot(g[0]) + dot(g[1])


def own_closure_kernel(own, *refs):
    raw, (out, h1_out, h2_out, k1, k2, k3, q1, q2, q3, b2, b3) = refs[:6], refs[6:17]
    w_in, w_mid, w_out, b_in, b_mid, b_out = refs[17:23]
    buffer, spare, stacked, sems = refs[23:]
    copies = [pltpu.make_async_copy(a, b, sems.at[i]) for i, (a, b) in enumerate(zip(raw, refs[17:23]))]
    for copy in copies:
        copy.start()
    for copy in copies:
        copy.wait()
    buffer[...] = jnp.zeros(buffer.shape, F32)
    by_tile(buffer, w_in, slice(0, HID))
    buffer[40:41, 0:HID] = b_in[...]
    stack(q1, buffer[0:48, 0:HID], stacked)
    spare[...] = buffer[...].T
    stack(k1, spare[0:HID, 0:48], stacked)
    buffer[0:HID, 0:HID] = w_mid[...]
    buffer[HID : HID + 1, 0:HID] = b_mid[...]
    stack(q2, buffer[0:HID, 0:HID], stacked)
    spare[...] = buffer[...].T
    stack(k2, spare[0:HID, 0:HID], stacked)
    b2[...] = jnp.broadcast_to(spare[0:HID, HID : HID + 1], (HID, COLS))
    buffer[...] = jnp.zeros(buffer.shape, F32)
    buffer[0:HID, 0:FEATS] = w_out[...]
    buffer[HID : HID + 1, 0:FEATS] = b_out[...]
    spare[...] = buffer[...].T
    buffer[...] = jnp.zeros(buffer.shape, F32)
    by_tile(buffer, spare, slice(0, COLS))
    stack(k3, buffer[0:48, 0:HID], stacked)
    b3[...] = jnp.broadcast_to(buffer[0:FEATS, HID : HID + 1], (FEATS, COLS))
    spare[...] = buffer[...].T
    stack(q3, spare[0:HID, 0:48], stacked)

    for r in range(0, ROWS, 8):
        z = split(to_48(jnp.concatenate([own[r + n, 0:FEATS, :] for n in range(8)], axis=1), 1.0))
        h1, h1s, h2 = hidden_layers(z, k1, k2, b2)
        o = last_layer(h2, k3, b3)
        for n in range(8):
            at = slice(n * COLS, (n + 1) * COLS)
            out[r + n] = o[:, at]
            h1_out[r + n] = h1[:, at]
            h2_out[r + n] = h2[:, at]


class Row:
    def __init__(self, width):
        sub = sub_index(width)
        group = sub % 4
        self.sub = sub
        self.is_t = group == 0
        self.is_s = group == 1
        self.is_u = group == 2
        self.is_v = group == 3
        self.low = sub >= 4
        self.k4 = jnp.where(group < 2, DIFFUSIVITY, VISCOSITY).astype(F32)


def put_state(k, ref, row, tiles):
    for t in range(5):
        ref[row, 8 * t : 8 * t + 8, :] = tiles[t]
    press = 0.4 * tiles[1] - 0.1 * tiles[0]
    for by in (1, 2, 4):
        press = press + jnp.where(k.sub >= by, pltpu.roll(press, by, 0), 0.0)
    ref[row, 40:48, :] = press
    deep_8 = ref[row, 47:48, :] + (0.4 * ref[row, 33:34, :] - 0.1 * ref[row, 32:33, :])
    ref[row, 48:49, :] = deep_8
    ref[row, 49:50, :] = deep_8 + (0.4 * ref[row, 37:38, :] - 0.1 * ref[row, 36:37, :])


def deep_pair(k, ref, row, upper, lower):
    return jnp.where(k.low, ref[row, lower : lower + 1, :], ref[row, upper : upper + 1, :])


def deep_u(k, ref, row):
    return deep_pair(k, ref, row, 34, 38)


def deep_v(k, ref, row):
    return deep_pair(k, ref, row, 35, 39)


def deep_p(k, ref, row):
    return deep_pair(k, ref, row, 48, 49)


def east_of(q):
    return pltpu.roll(q, q.shape[1] - 1, 1)


def west_of(q):
    return pltpu.roll(q, 1, 1)


def gain_of(k, t):
    return k.k4 if t == 4 else (DIFFUSIVITY if t < 2 else VISCOSITY)


def tendency_row(k, ref, row, c, f):
    half = 0.5 * c
    c2 = c * c
    u, v = tile(ref, row, 2), tile(ref, row, 3)
    u4, v4 = deep_u(k, ref, row), deep_v(k, ref, row)
    change = []
    for t in range(5):
        gain = gain_of(k, t)
        if t in (0, 2, 4):
            au, av = (half * u4, 0.5 * v4) if t == 4 else (half * u, 0.5 * v)
            along = gain * c2
            at_e, at_w, at_n, at_s = along - au, along + au, gain - av, gain + av
        q = tile(ref, row, t)
        east, west = at_e * east_of(q), at_w * west_of(q)
        north, south = at_n * tile(ref, row + 1, t), at_s * tile(ref, row - 1, t)
        change.append((east + west) + (north + south) - (gain * (2.0 * c2 + 2.0)) * q)
    p = tile(ref, row, 5)
    change[2] = change[2] + (f * v - half * (east_of(p) - west_of(p)))
    change[3] = change[3] - (f * u + 0.5 * (tile(ref, row + 1, 5) - tile(ref, row - 1, 5)))
    p4 = deep_p(k, ref, row)
    fx = f * v4 - half * (east_of(p4) - west_of(p4))
    fy = f * u4 + 0.5 * (deep_p(k, ref, row + 1) - deep_p(k, ref, row - 1))
    change[4] = change[4] + jnp.where(k.is_u, fx, jnp.where(k.is_v, -fy, 0.0))
    return change


def adjoint_row(k, ref, aref, row, c, f):
    half = 0.5 * c
    c2 = c * c
    u4 = deep_u(k, ref, row)
    qe = [east_of(tile(ref, row, t)) for t in range(5)]
    qw = [west_of(tile(ref, row, t)) for t in range(5)]
    out = []
    to_u = to_v = None
    for t in range(5):
        a = tile(aref, row, t)
        ae, aw = east_of(a), west_of(a)
        an, as_ = tile(aref, row + 1, t), tile(aref, row - 1, t)
        gain = gain_of(k, t)
        if t == 0:
            ue, uw = half * qe[2], half * qw[2]
            vn, vs = 0.5 * tile(ref, row + 1, 3), 0.5 * tile(ref, row - 1, 3)
        if t == 4:
            ue, uw = half * east_of(u4), half * west_of(u4)
            vn, vs = 0.5 * deep_v(k, ref, row + 1), 0.5 * deep_v(k, ref, row - 1)
        if t in (0, 2, 4):
            along = gain * c2
            at_e, at_w, at_n, at_s = along + ue, along - uw, gain + vn, gain - vs
        out.append(
            (at_e * ae + at_w * aw) + (at_n * an + at_s * as_) - (gain * (2.0 * c2 + 2.0)) * a
        )
        px = a * (qe[t] - qw[t])
        py = a * (tile(ref, row + 1, t) - tile(ref, row - 1, t))
        if t < 4:
            to_u = px if to_u is None else to_u + px
            to_v = py if to_v is None else to_v + py
        if t == 2:
            a2, bx = a, half * (ae - aw)
        if t == 3:
            a3, by = a, 0.5 * (an - as_)
        if t == 4:
            a4 = a
            deep_bx, deep_by = half * (ae - aw), 0.5 * (an - as_)
            px4, py4 = px * half, py * 0.5
    out[2] = out[2] - half * to_u - f * a3
    out[3] = out[3] - 0.5 * to_v + f * a2
    sx = px4 + pltpu.roll(px4, 7, 0)
    sx = sx + pltpu.roll(sx, 2, 0)
    sy = py4 + pltpu.roll(py4, 1, 0)
    sy = sy + pltpu.roll(sy, 2, 0)
    at_u = -sx - f * pltpu.roll(a4, 7, 0)
    at_v = f * pltpu.roll(a4, 1, 0) - sy
    deep = jnp.where(k.is_t, pltpu.roll(deep_bx, 6, 0) + pltpu.roll(deep_by, 5, 0), 0.0)
    deep = deep + jnp.where(k.low, 0.0, pltpu.roll(deep, 4, 0))
    press = bx + by
    for shift in (1, 2, 4):
        press = press + jnp.where(k.sub < 8 - shift, pltpu.roll(press, 8 - shift, 0), 0.0)
    press = press + deep[0:1, :]
    out[0] = out[0] - 0.1 * press
    out[1] = out[1] + 0.4 * press
    out[4] = out[4] + jnp.where(
        k.is_t,
        -0.1 * deep,
        jnp.where(k.is_s, 0.4 * pltpu.roll(deep, 1, 0), jnp.where(k.is_u, at_u, at_v)),
    )
    return out


def for_span(low, high, up, body):
    turns = lax.div(high - low + TURN - 1, TURN)
    first = jnp.where(up == 1, low, high - TURN * turns)

    def turn(i, _):
        for j in range(TURN):
            body(first + TURN * i + j)
        return 0

    lax.fori_loop(0, turns, turn, 0)


def for_rows(scal, reach, body):
    for_span(PAD - reach * scal[2], PAD + ROWS + reach * scal[3], scal[3], body)


def for_inner(scal, inset, body):
    for_span(PAD + inset * scal[2], PAD + ROWS - inset * scal[3], scal[3], body)


def for_outer(sides, scal, inset, reach, body):
    if sides == ["swap"]:
        low = jnp.where(scal[3] == 1, PAD + ROWS - inset, PAD - reach)
        for_span(low, low + reach + inset, scal[3], body)
    else:
        for_span(PAD - reach * scal[2], PAD + inset * scal[2], 0, body)
        for_span(PAD + ROWS - inset * scal[3], PAD + ROWS + reach * scal[3], 1, body)


def mask_tile(ref, row, t):
    return tile(ref, row, 1 if t == 4 else 0)


def adjoint_third(k, scal, cs, fs, reach, state, masks, abuf, top, hold, bbuf):
    def body(r):
        d = adjoint_row(k, state, abuf, r, cs[r], fs[r])
        for t in range(5):
            ts = (2.0 / 3.0) * tile(top, r, t) + d[t]
            hold[r, 8 * t : 8 * t + 8, :] = ts
            bbuf[r, 8 * t : 8 * t + 8, :] = 0.0625 * mask_tile(masks, r, t) * ts

    for_rows(scal, reach, body)


def adjoint_second(k, scal, cs, fs, reach, state, masks, bbuf, top, hold, left, abuf):
    def body(r):
        d = adjoint_row(k, state, bbuf, r, cs[r], fs[r])
        for t in range(5):
            ts = tile(hold, r, t)
            tf = 0.25 * ts + d[t]
            left[r, 8 * t : 8 * t + 8, :] = (1.0 / 3.0) * tile(top, r, t) + 0.75 * ts + tf
            abuf[r, 8 * t : 8 * t + 8, :] = 0.25 * mask_tile(masks, r, t) * tf

    for_rows(scal, reach, body)


def adjoint_first(k, scal, cs, fs, reach, state, abuf, left, store):
    def body(r):
        d = adjoint_row(k, state, abuf, r, cs[r], fs[r])
        store(r, [tile(left, r, t) + d[t] for t in range(5)])

    for_rows(scal, reach, body)


def edges(reach):
    lane = lax.broadcasted_iota(jnp.int32, (8, COLS), 1)
    return lane < reach, lane >= COLS - reach


def wide_pack(ref, base):
    parts = []
    for t in range(5):
        rows = [ref[base + s, 8 * t : 8 * t + 8, COLS:WIDE] for s in range(8)]
        parts.append(slot_pack(rows, lambda s: 8 + SLOT * s, SLOT))
    return jnp.concatenate(parts, axis=0)

def wide_unpack(ref, base, values):
    for s in range(8):
        ref[base + s, 0:FEATS, COLS:WIDE] = pltpu.roll(values, -(8 + SLOT * s) % COLS, 1)


def section_1(k, cs, fs, masks, src, dst):
    def body(r):
        d = tendency_row(k, src, r, cs[r], fs[r])
        put_state(
            k, dst, r,
            [tile(src, r, t) + 0.25 * mask_tile(masks, r, t) * d[t] for t in range(5)],
        )
    return body

def section_2(k, cs, fs, masks, src, mid, dst):
    def body(r):
        d = tendency_row(k, mid, r, cs[r], fs[r])
        put_state(
            k, dst, r,
            [
                0.75 * tile(src, r, t) + 0.25 * tile(mid, r, t)
                + 0.0625 * mask_tile(masks, r, t) * d[t]
                for t in range(5)
            ],
        )
    return body


def section_3(k, cs, fs, masks, fluxes, mean, src, mid, net, r):
    d = tendency_row(k, mid, r, cs[r], fs[r])
    new = []
    for t in range(5):
        m = mask_tile(masks, r, t)
        o = tile(net, r, t)
        if t == 1:
            force = 2.0 * (mean - fluxes[r, 2:3, :])
            o = o + jnp.where(k.sub == 0, force, 0.0)
        new.append(
            (1.0 / 3.0) * tile(src, r, t) + (2.0 / 3.0) * tile(mid, r, t)
            + m * ((1.0 / 6.0) * d[t] + 0.25 * o)
        )
    return new


def zero_walls(ref):
    for row in (PAD - 1, PAD + ROWS):
        ref[row] = jnp.zeros(ref.shape[1:], F32)


class Block:
    def __init__(self, k, s0, masks, fluxes):
        self.k, self.s0, self.masks, self.fluxes = k, s0, masks, fluxes
        self.near_e, self.near_w = edges(REACH)

    def put(self, row, core, from_e, from_w):
        def both(t):
            halo = jnp.where(self.near_e, from_e(t), jnp.where(self.near_w, from_w(t), 0.0))
            return jnp.concatenate([core(t), halo], axis=1)

        put_state(self.k, self.s0, row, [both(t) for t in range(5)])
        self.masks[row, 0:8, :] = both(5)
        last = both(6)
        self.masks[row, 8:16, :] = jnp.where(self.k.low, last[1:2, :], last[0:1, :])
        self.fluxes[row] = last


def assemble_own_kernel(scal, cs, fs, own, own_m, east, west, k1, k2, k3, b2, b3, s0, masks, fluxes, net):
    k = Row(WIDE)
    zero_walls(s0)
    block = Block(k, s0, masks, fluxes)
    for r in range(ROWS):
        at = (r // 8) * PACK
        turn = SLOT * (r % 8)
        block.put(
            PAD + r,
            lambda t: own[r, 8 * t : 8 * t + 8, :],
            lambda t: pltpu.roll(west[at + 8 * t : at + 8 * t + 8, :], -turn % COLS, 1),
            lambda t: pltpu.roll(east[at + 8 * t : at + 8 * t + 8, :], -(turn + SLOT) % COLS, 1),
        )
        net[PAD + r, :, 0:COLS] = own_m[r]
    columns = jnp.concatenate([wide_pack(s0, PAD), wide_pack(s0, PAD + 8)], axis=1)
    o = closure_of(columns, k1, k2, k3, b2, b3)
    for g in range(2):
        wide_unpack(net, PAD + 8 * g, o[:, g * COLS : (g + 1) * COLS])


def closure_of(columns, k1, k2, k3, b2, b3):
    _, _, h2 = hidden_layers(split(to_48(columns, 1.0)), k1, k2, b2)
    return last_layer(h2, k3, b3)


def first_own_kernel(scal, cs, fs, s0, masks, s1):
    zero_walls(s1)
    for_inner(scal, 1, section_1(Row(WIDE), cs, fs, masks, s0, s1))


def second_own_kernel(scal, cs, fs, s0, s1, masks, s2):
    for_inner(scal, 2, section_2(Row(WIDE), cs, fs, masks, s0, s1, s2))


def halo_kernel(sides, scal, cs, fs, own_s0, own_s1, own_s2, own_masks, own_fluxes, own_net, *rest):
    n = len(sides)
    side_refs = [rest[2 * i : 2 * i + 2] for i in range(n)]
    net_refs, (s0, s1, s2, masks, fluxes, net) = rest[2 * n : 2 * n + 5], rest[2 * n + 5 :]
    k = Row(WIDE)
    for r in range(PAD, PAD + ROWS):
        for src, dst in (
            (own_s0, s0), (own_s1, s1), (own_s2, s2), (own_masks, masks), (own_fluxes, fluxes), (own_net, net)
        ):
            dst[r] = src[r]
    for ref in (s0, s1, s2):
        zero_walls(ref)
    block = Block(k, s0, masks, fluxes)
    firsts = []
    for side, (lat, corner) in zip(sides, side_refs):
        base = {"swap": scal[4], "north": PAD - REACH, "south": PAD + ROWS}[side]
        for r in range(REACH):
            block.put(
                base + r,
                lambda t: lat[PACK * r + 8 * t : PACK * r + 8 * t + 8, :],
                lambda t: pltpu.roll(corner[PACK + 40 + 8 * t : PACK + 48 + 8 * t, :], -REACH * r % COLS, 1),
                lambda t: pltpu.roll(corner[8 * t : 8 * t + 8, :], -REACH * (r + 1) % COLS, 1),
            )
        near = {"swap": jnp.where(scal[2] == 1, PAD - 8, PAD + ROWS), "north": PAD - 8, "south": PAD + ROWS}
        firsts.append(near[side])
    columns = []
    for first in firsts:
        columns += [s0[first + i, 0:FEATS, 0:COLS] for i in range(8)] + [wide_pack(s0, first)]
    o = closure_of(jnp.concatenate(columns, axis=1), *net_refs)
    for g, first in enumerate(firsts):
        for i in range(8):
            at = (9 * g + i) * COLS
            net[first + i, :, 0:COLS] = o[:, at : at + COLS]
        at = (9 * g + 8) * COLS
        wide_unpack(net, first, o[:, at : at + COLS])
    for_outer(sides, scal, 1, 10, section_1(k, cs, fs, masks, s0, s1))
    for_outer(sides, scal, 2, 9, section_2(k, cs, fs, masks, s0, s1, s2))


def last_section_kernel(scal, cs, fs, sums, s3, t2, masks, fluxes, outs, final):
    k = Row(WIDE)
    mean = sums[0:1, 0:1] / sums[1:2, 0:1]

    def last(r):
        new = section_3(k, cs, fs, masks, fluxes, mean, s3, t2, outs, r)
        put_result(final, r - PAD, [x[:, 0:COLS] for x in new])

    for_rows(scal, 0, last)


def late_kernel(
    sides, scal, cs, fs, sums, own, cown, own_h1, own_h2, s0, s2, masks, fluxes, outs_in, east, west, *rest
):
    n = len(sides)
    side_refs = [rest[2 * i : 2 * i + 2] for i in range(n)]
    (k1, k2, k3, q1, q2, q3, b2, b3), rest = rest[2 * n : 2 * n + 8], rest[2 * n + 8 :]
    grads, s4, abuf, from_closure, s3, t2, outs, t1, cot, gz, bbuf, hold, left, acc = rest
    k = Row(WIDE)
    has_south = scal[2]
    lo = lambda h: PAD - h * has_south
    for ref in (s3, t1, t2, abuf, bbuf):
        zero_walls(ref)
    mean = sums[0:1, 0:1] / sums[1:2, 0:1]

    cnear_e, cnear_w = edges(CREACH)
    for r in range(ROWS):
        for t in range(5):
            rows = slice(2 * PACK + 8 * t, 2 * PACK + 8 * t + 8)
            from_e = pltpu.roll(west[rows, :], -8 * r % COLS, 1)
            from_w = pltpu.roll(east[rows, :], -8 * (r + 1) % COLS, 1)
            side = jnp.where(cnear_e, from_e, jnp.where(cnear_w, from_w, 0.0))
            cot[PAD + r, 8 * t : 8 * t + 8, :] = jnp.concatenate(
                [cown[r, 8 * t : 8 * t + 8, :], side], axis=1
            )
    for side, (lat, corner) in zip(sides, side_refs):
        cbase = {"swap": scal[5], "north": PAD - CREACH, "south": PAD + ROWS}[side]
        crow = {"swap": scal[6], "north": ROWS - CREACH, "south": 0}[side]
        for r in range(CREACH):
            turn = lax.rem(2 * COLS - 8 * (crow + r), COLS)
            turn_w = lax.rem(2 * COLS - 8 * (crow + r + 1), COLS)
            for t in range(5):
                wrows = slice(PACK + 8 * t, PACK + 8 * t + 8)
                erows = slice(2 * PACK + 40 + 8 * t, 2 * PACK + 48 + 8 * t)
                from_e = pltpu.roll(corner[erows, :], turn, 1)
                from_w = pltpu.roll(corner[wrows, :], turn_w, 1)
                part = jnp.where(cnear_e, from_e, jnp.where(cnear_w, from_w, 0.0))
                cot[cbase + r, 8 * t : 8 * t + 8, :] = jnp.concatenate(
                    [lat[LAT_X + FEATS * r + 8 * t : LAT_X + FEATS * r + 8 * t + 8, :], part], axis=1
                )


    def step_1_end(r):
        put_state(k, s3, r, section_3(s0, s2, r))

    def step_1_end(r):
        put_state(k, s3, r, section_3(k, cs, fs, masks, fluxes, mean, s0, s2, outs_in, r))

    for_rows(scal, 8, step_1_end)

    acc[...] = jnp.zeros(acc.shape, F32)

    def closure_adjoint(z, h1, h1s, h2, go, with_weights):
        gos = split(to_48(go))
        g2 = product(q3[...], *gos) * (1.0 - h2 * h2)
        g2s = split(g2)
        g1 = product(q2[...], *g2s) * (1.0 - h1 * h1)
        g1s = split(g1)
        if with_weights:
            add_weight_terms(acc, z, h1s, split(h2), g1s, g2s, gos)
        return product(q1[...], *g1s)[0:FEATS]

    def both_ways(columns, go, with_weights):
        z = split(to_48(columns, 1.0))
        h1, h1s, h2 = hidden_layers(z, k1, k2, b2)
        o = last_layer(h2, k3, b3) if with_weights else None
        return o, closure_adjoint(z, h1, h1s, h2, go, with_weights)

    def masked_core(ref, r):
        m0, m4 = masks[r, 0:8, 0:COLS], masks[r, 8:16, 0:COLS]
        parts = [
            0.25 * (m4 if t == 4 else m0) * ref[r, 8 * t : 8 * t + 8, 0:COLS] for t in range(5)
        ]
        return jnp.concatenate(parts, axis=0)

    def mask_cot(r):
        for t in range(5):
            bbuf[r, 8 * t : 8 * t + 8, :] = 0.25 * mask_tile(masks, r, t) * tile(cot, r, t)
            abuf[r, 8 * t : 8 * t + 8, :] = (1.0 / 6.0) * mask_tile(masks, r, t) * tile(cot, r, t)

    for_rows(scal, 6, mask_cot)

    for first in range(PAD, PAD + ROWS, 8):
        z = jnp.concatenate([s3[first + i, 0:FEATS, 0:COLS] for i in range(8)], axis=1)
        go = jnp.concatenate([bbuf[first + i, 0:FEATS, 0:COLS] for i in range(8)], axis=1)
        o, back = both_ways(z, go, True)
        for i in range(8):
            at = slice(i * COLS, (i + 1) * COLS)
            outs[first + i, :, 0:COLS] = o[:, at]
            gz[first + i, :, 0:COLS] = back[:, at]

    first = lo(4)
    if sides == ["swap"]:
        rows = [jnp.where(has_south == 1, PAD - 4, PAD + ROWS) + i for i in range(4)]
    else:
        rows = [PAD - 4 + i for i in range(4)] + [PAD + ROWS + i for i in range(4)]
    beyond = lambda ref: jnp.concatenate(
        [ref[r, 0:FEATS, 0:COLS] for r in rows] + [wide_pack(ref, first + 8 * g) for g in range(3)], axis=1
    )
    _, back = both_ways(beyond(s3), beyond(bbuf), False)
    for i, r in enumerate(rows):
        gz[r, :, 0:COLS] = back[:, i * COLS : (i + 1) * COLS]
    for g in range(3):
        at = (len(rows) + g) * COLS
        wide_unpack(gz, first + 8 * g, back[:, at : at + COLS])

    for_rows(scal, 7, section_1(k, cs, fs, masks, s3, t1))
    for_rows(scal, 6, section_2(k, cs, fs, masks, s3, t1, t2))

    def store(r, tiles):
        for t in range(5):
            s4[r, 8 * t : 8 * t + 8, :] = tiles[t] + tile(gz, r, t)

    adjoint_third(k, scal, cs, fs, 5, t2, masks, abuf, cot, hold, bbuf)
    adjoint_second(k, scal, cs, fs, 4, t1, masks, bbuf, cot, hold, left, abuf)
    adjoint_first(k, scal, cs, fs, 3, s3, abuf, left, store)

    for r in range(0, ROWS, 8):
        side = lambda read: jnp.concatenate([read(r + j) for j in range(8)], axis=1)
        z = split(to_48(side(lambda j: own[j, 0:FEATS, :]), 1.0))
        h1 = side(lambda j: own_h1[j])
        h2 = side(lambda j: own_h2[j])
        go = side(lambda j: masked_core(s4, PAD + j))
        back = closure_adjoint(z, h1, split(h1), h2, go, True)
        for j in range(8):
            from_closure[r + j] = back[:, j * COLS : (j + 1) * COLS]

    zero_walls(abuf)

    def mask_top(r):
        for t in range(5):
            abuf[r, 8 * t : 8 * t + 8, :] = (1.0 / 6.0) * mask_tile(masks, r, t) * tile(s4, r, t)

    for_rows(scal, 3, mask_top)
    grads[...] = jnp.zeros(grads.shape, F32)
    grads[0:40, 0:HID] = acc[0:40, 0:HID]
    grads[0:40, HID : 2 * HID] = acc[112:152, 0:HID]
    grads[40:72, 0:HID] = acc[48:80, 0:HID]
    grads[40:72, HID : 2 * HID] = acc[80:112, 0:HID]
    grads[72:73, 0:HID] = acc[40:41, 0:HID]
    grads[72:73, HID : 2 * HID] = acc[160:161, 0:HID]
    grads[73:74, 0:HID] = acc[176:177, 0:HID]


def put_result(ref, row, tiles):
    for t in range(4):
        ref[pl.ds(t * 10 * ROWS + row, 8, stride=ROWS), :] = tiles[t]
    ref[pl.ds(8 * ROWS + row, 4, stride=10 * ROWS), :] = tiles[4][0:4, :]
    ref[pl.ds(9 * ROWS + row, 4, stride=10 * ROWS), :] = tiles[4][4:8, :]


def back_third_kernel(scal, cs, fs, state, masks, abuf, top, hold, bbuf):
    zero_walls(bbuf)
    adjoint_third(Row(WIDE), scal, cs, fs, 2, state, masks, abuf, top, hold, bbuf)


def back_second_kernel(scal, cs, fs, state, masks, bbuf, top, hold, left, abuf):
    zero_walls(abuf)
    adjoint_second(Row(WIDE), scal, cs, fs, 1, state, masks, bbuf, top, hold, left, abuf)


def back_first_kernel(scal, cs, fs, state, masks, abuf, left, from_closure, grad):
    def store(r, tiles):
        done = []
        for t in range(5):
            m = masks[r, 8:16, 0:COLS] if t == 4 else masks[r, 0:8, 0:COLS]
            done.append(m * (tiles[t][:, 0:COLS] + from_closure[r - PAD, 8 * t : 8 * t + 8, :]))
        put_result(grad, r - PAD, done)

    adjoint_first(Row(WIDE), scal, cs, fs, 0, state, abuf, left, store)


def unpack_kernel(scale, packed, win, bin_, wmid, bmid, wout, bout):
    for ref, lanes in ((win, slice(0, HID)), (wout, slice(HID, 2 * HID))):
        for t in range(4):
            ref[10 * t : 10 * t + 8, :] = packed[8 * t : 8 * t + 8, lanes] * scale
            ref[10 * t + 8 : 10 * t + 9, :] = packed[32 + t : 33 + t, lanes] * scale
            ref[10 * t + 9 : 10 * t + 10, :] = packed[36 + t : 37 + t, lanes] * scale
    wmid[0:32, :] = packed[40:72, 0:HID] * scale
    wmid[32:64, :] = packed[40:72, HID : 2 * HID] * scale
    bin_[...] = packed[72:73, 0:HID] * scale
    bmid[...] = packed[72:73, HID : 2 * HID] * scale
    for t in range(4):
        bout[:, 10 * t : 10 * t + 8] = packed[73:74, 8 * t : 8 * t + 8] * scale
        bout[:, 10 * t + 8 : 10 * t + 9] = packed[73:74, 32 + t : 33 + t] * scale
        bout[:, 10 * t + 9 : 10 * t + 10] = packed[73:74, 36 + t : 37 + t] * scale


def far_first(axes):
    return [(axis, n, 1 << bit) for axis, n in axes for bit in reversed(range(n.bit_length() - 1))]


def pair_rounds(x, rounds, beside):
    results = []
    for i in range(max(len(rounds), len(beside))):
        if i < len(rounds):
            axis, n, step = rounds[i]
            got = lax.ppermute(x, axis, [(j, j ^ step) for j in range(n)])
        if i < len(beside):
            results.append(beside[i](results))
            if i < len(rounds):
                got, results[-1] = lax.optimization_barrier((got, results[-1]))
        if i < len(rounds):
            x = x + got
    return x, results


def latitude_terms(row_index, row_count):
    latitude = LAT_LIMIT * (2.0 * (jnp.clip(row_index, 0.0, row_count - 1.0) + 0.5) / row_count - 1.0)
    return 1.0 / jnp.cos(latitude), CORIOLIS * jnp.sin(latitude)


def on_device(
    initial_state, land_mask, surface_flux, weight_in, bias_in, weight_mid, bias_mid, weight_out, bias_out, cotangent
):
    lat_n, lon_n = lax.axis_size("lat"), lax.axis_size("lon")
    lat_i = lax.axis_index("lat")
    lat_total, lon_total = ROWS * lat_n, COLS * lon_n
    sides = ["swap"] if lat_n == 2 else ["north", "south"]
    is_low = (lat_i == 0).astype(jnp.int32)
    has_south = (lat_i > 0).astype(jnp.int32)
    has_north = (lat_i < lat_n - 1).astype(jnp.int32)
    scal = jnp.stack(
        [
            is_low * (ROWS - REACH),
            is_low * (ROWS - CREACH),
            has_south,
            has_north,
            jnp.where(is_low == 1, PAD + ROWS, PAD - REACH),
            jnp.where(is_low == 1, PAD + ROWS, PAD - CREACH),
            jnp.where(is_low == 1, 0, ROWS - CREACH),
        ]
    ).astype(jnp.int32)
    rows = (lat_i * ROWS - PAD + jnp.arange(EXT, dtype=jnp.int32)).astype(F32)
    cs, fs = latitude_terms(rows, lat_total)

    hbm = pl.BlockSpec(memory_space=pltpu.HBM)
    packed = pl.pallas_call(
        lambda *refs: pack_kernel(sides, *refs),
        out_shape=[
            sds(ROWS, PACK, COLS), sds(ROWS, FEATS, COLS), sds(STRIP, COLS), sds(STRIP, COLS), sds(8, COLS),
        ]
        + [sds(LAT, COLS)] * len(sides),
        in_specs=[hbm] * 4,
        out_specs=[VMEM] * (5 + len(sides)),
        scratch_shapes=[
            pltpu.VMEM((40 * ROWS, COLS), F32), pltpu.VMEM((10 * ROWS, COLS), jnp.int32),
            pltpu.VMEM((ROWS, COLS), F32), pltpu.VMEM((40 * ROWS, COLS), F32), pltpu.SemaphoreType.DMA((4,)),
        ],
        compiler_params=params(56),
        cost_estimate=pl.CostEstimate(flops=10**9, bytes_accessed=3 * 10**6, transcendentals=0),
        name="pack_halos",
    )(
        initial_state.reshape(40 * ROWS, COLS),
        land_mask.reshape(10 * ROWS, COLS),
        surface_flux,
        cotangent.reshape(40 * ROWS, COLS),
    )
    own, cown, east_pay, west_pay, sums = packed[:5]

    def lat_pairs(side):
        if side == "swap":
            return [(0, 1), (1, 0)]
        if side == "north":
            return [(i, i + 1) for i in range(lat_n - 1)]
        return [(i + 1, i) for i in range(lat_n - 1)]

    east_ring = [(i, (i + 1) % lon_n) for i in range(lon_n)]
    west_ring = [((i + 1) % lon_n, i) for i in range(lon_n)]
    from_west = lax.ppermute(east_pay, "lon", east_ring)
    from_east = lax.ppermute(west_pay, "lon", west_ring)
    row = lambda b: b.reshape(1, -1)
    raw = (weight_in, weight_mid, weight_out, row(bias_in), row(bias_mid), row(bias_out))
    half = lambda *shape: jax.ShapeDtypeStruct(shape, BF16)
    own_closure = pl.pallas_call(
        own_closure_kernel,
        out_shape=[
            sds(ROWS, FEATS, COLS), sds(ROWS, HID, COLS), sds(ROWS, HID, COLS),
            half(HID, 144), half(HID, 192), half(48, 192), half(48, 192), half(HID, 192), half(HID, 144),
            sds(HID, COLS), sds(FEATS, COLS),
        ],
        in_specs=[VMEM] + [hbm] * 6,
        out_specs=[VMEM] * 11,
        scratch_shapes=[pltpu.VMEM(w.shape, F32) for w in raw]
        + [pltpu.VMEM((COLS, COLS), F32), pltpu.VMEM((COLS, COLS), F32), pltpu.VMEM((HID, WIDE), F32)]
        + [pltpu.SemaphoreType.DMA((6,))],
        compiler_params=params(12),
        cost_estimate=pl.CostEstimate(flops=10**9, bytes_accessed=2 * 10**6, transcendentals=0),
        name="own_closure",
    )
    pack_corners = pl.pallas_call(
        lambda *refs: corner_kernel(sides, *refs),
        out_shape=[sds(CORNER + 8, COLS)] * len(sides),
        in_specs=[SMEM, VMEM, VMEM],
        out_specs=[VMEM] * len(sides),
        compiler_params=params(8),
        cost_estimate=pl.CostEstimate(flops=10**8, bytes_accessed=10**6, transcendentals=0),
        name="pack_corners",
    )
    lats = [lax.ppermute(pay, "lat", lat_pairs(side)) for side, pay in zip(sides, packed[5:])]
    geometry = (scal, cs, fs)
    state = sds(EXT, 56, WIDE)
    plain = sds(EXT, FEATS, WIDE)
    marks = sds(EXT, 16, WIDE)
    vmem = lambda shape: pltpu.VMEM(shape.shape, F32)

    def call(kernel, name, out_shape, scratch, args, flops, limit):
        single = not isinstance(out_shape, list)
        return pl.pallas_call(
            kernel,
            out_shape=out_shape,
            in_specs=[SMEM] * 3 + [VMEM] * len(args),
            out_specs=VMEM if single else [VMEM] * len(out_shape),
            scratch_shapes=scratch,
            compiler_params=params(limit),
            cost_estimate=pl.CostEstimate(flops=flops, bytes_accessed=10**7, transcendentals=0),
            name=name,
        )(*geometry, *args)

    own_m, own_h1, own_h2, k1, k2, k3, q1, q2, q3, b2, b3 = own_closure(own, *raw)
    net_weights = [k1, k2, k3, b2, b3]
    is_even = lax.axis_index("lon") % 2 == 0
    theirs = jnp.where(is_even, from_east[SUMS:PACK, 0:1], from_west[SUMS:PACK, 0:1])
    pair = sums + jnp.pad(jnp.broadcast_to(theirs, (PACK - SUMS, COLS)), ((0, 8 - PACK + SUMS), (0, 0)))

    def own_sections(done):
        s0, masks, fluxes, _ = done[0]
        return call(first_own_kernel, "first_section_own", state, [], [s0, masks], 10**9, 8)

    def own_second(done):
        s0, masks, fluxes, _ = done[0]
        s2 = call(second_own_kernel, "second_section_own", state, [], [s0, done[1], masks], 10**9, 8)
        return s2, pack_corners(scal, from_west, from_east)

    row_total, results = pair_rounds(
        pair,
        far_first((("lon", lon_n),))[:-1][::-1],
        [
            lambda done: call(
                assemble_own_kernel, "assemble_own", [state, marks, sds(EXT, 8, WIDE), plain], [],
                [own, own_m, from_west, from_east] + net_weights, 10**9, 8,
            ),
            own_sections,
            own_second,
        ],
    )
    (s0, masks, fluxes, net), s1, (s2, corner_pays) = results
    corners = []
    for side, pay in zip(sides, corner_pays):
        pay = lax.dynamic_update_slice(pay, row_total, (CORNER, 0))
        corners.append(lax.ppermute(pay, "lat", lat_pairs(side)))
    if sides == ["swap"]:
        total = row_total + corners[0][CORNER : CORNER + 8]
    else:
        total = lax.psum(row_total, "lat")
    received = [ref for pair in zip(lats, corners) for ref in pair]
    s0, s1, s2, masks, fluxes, net = call(
        lambda *refs: halo_kernel(sides, *refs), "halo_rows",
        [state, state, state, marks, sds(EXT, 8, WIDE), plain], [],
        [s0, s1, s2, masks, fluxes, net] + received + net_weights, 2 * 10**9, 8,
    )
    grads, top, abuf, from_closure, s3, t2, net_2 = call(
        lambda *refs: late_kernel(sides, *refs), "steps_and_adjoint",
        [sds(80, COLS), plain, plain, sds(ROWS, FEATS, COLS), state, state, plain],
        [vmem(state)] + [vmem(plain)] * 5 + [pltpu.VMEM((192, HID), F32)],
        [total, own, cown, own_h1, own_h2, s0, s2, masks, fluxes, net, from_west, from_east]
        + received + [k1, k2, k3, q1, q2, q3, b2, b3],
        4 * 10**9, 18,
    )
    beside = [
        lambda done: call(
            back_third_kernel, "adjoint_third_section", [plain, plain], [], [s2, masks, abuf, top], 10**9, 8
        ),
        lambda done: call(
            back_second_kernel, "adjoint_second_section", [plain, plain], [],
            [s1, masks, done[0][1], top, done[0][0]], 10**9, 8,
        ),
        lambda done: call(
            back_first_kernel, "adjoint_first_section", sds(40 * ROWS, COLS), [],
            [s0, masks, done[1][1], done[1][0], from_closure], 10**9, 8,
        ),
        lambda done: call(
            last_section_kernel, "last_section", sds(40 * ROWS, COLS), [],
            [total, s3, t2, masks, fluxes, net_2], 10**9, 8,
        ),
    ]
    by_lon, by_lat = far_first((("lon", lon_n),)), far_first((("lat", lat_n),))
    summed, results = pair_rounds(grads, by_lon[:-2] + by_lat + by_lon[-2:], beside)
    state_grad, final = results[2:]

    scale = 1.0 / math.sqrt(lat_total * lon_total)
    g_in, g_bin, g_mid, g_bmid, g_out, g_bout = pl.pallas_call(
        lambda *refs: unpack_kernel(scale, *refs),
        out_shape=[sds(40, HID), sds(1, HID), sds(HID, HID), sds(1, HID), sds(40, HID), sds(1, 40)],
        in_specs=[VMEM],
        out_specs=[VMEM] * 6,
        compiler_params=params(8),
        name="unpack_weight_grads",
    )(summed)
    shape = initial_state.shape
    return (
        final.reshape(shape),
        state_grad.reshape(shape),
        g_in,
        g_bin.reshape(-1),
        g_mid,
        g_bmid.reshape(-1),
        g_out.T,
        g_bout.reshape(-1),
    )


def solution(mesh):
    split_state = P(None, None, "lat", "lon")
    return jax.shard_map(
        on_device,
        mesh=mesh,
        in_specs=(split_state, P(None, "lat", "lon"), P("lat", "lon"), P(), P(), P(), P(), P(), P(), split_state),
        out_specs=(split_state, split_state, P(), P(), P(), P(), P(), P()),
        check_vma=False,
    )
```

```python
import math

import jax
import jax.numpy as jnp
from jax import lax
from jax.experimental import pallas as pl
from jax.experimental.pallas import tpu as pltpu
from jax.sharding import PartitionSpec as P

LAT_LIMIT = 1.2
CORIOLIS = 1.0
VISCOSITY = 0.15
DIFFUSIVITY = 0.1

ROWS = 16
COLS = 128
REACH = 11
CREACH = 6
PAD = 16
EXT = 48
TURN = 4
WIDE = 2 * COLS
FEATS = 40
HID = 64
PACK = 56
STRIP = 2 * PACK + 40
LAT_X = REACH * PACK
CORNER = 2 * PACK + 80
LAT = LAT_X + CREACH * FEATS
SLOT = 16
F32 = jnp.float32
BF16 = jnp.bfloat16
VMEM = pl.BlockSpec(memory_space=pltpu.VMEM)
SMEM = pl.BlockSpec(memory_space=pltpu.SMEM)


def params(megabytes):
    return pltpu.CompilerParams(vmem_limit_bytes=megabytes * 1024 * 1024)


def sds(*shape):
    return jax.ShapeDtypeStruct(shape, F32)


def sub_index(width):
    return lax.broadcasted_iota(jnp.int32, (8, width), 0)


def tile(ref, row, number):
    return ref[row, 8 * number : 8 * number + 8, :]


def slot_pack(pieces, shift_of, width):
    lane = lax.broadcasted_iota(jnp.int32, (8, COLS), 1)
    packed = None
    for slot, piece in enumerate(pieces):
        turned = pltpu.roll(piece, shift_of(slot) % COLS, 1)
        if packed is None:
            packed = turned
        else:
            packed = jnp.where((lane >= slot * width) & (lane < (slot + 1) * width), turned, packed)
    return packed


def pack_kernel(sides, x_hbm, mask_hbm, flux_hbm, cot_hbm, *outs):
    x, mask, flux, cot, sems = outs[-5:]
    own, cown, east, west, sums = outs[:5]
    per_side = outs[5 : 5 + len(sides)]
    pairs = ((mask_hbm, mask), (x_hbm, x), (flux_hbm, flux), (cot_hbm, cot))
    copies = [pltpu.make_async_copy(a, b, sems.at[i]) for i, (a, b) in enumerate(pairs)]
    for copy in copies:
        copy.start()
    for copy in copies:
        copy.wait()
    top = mask[0:ROWS, :].astype(F32)
    total = jnp.sum(jnp.sum(top * flux[...], axis=1, keepdims=True), axis=0, keepdims=True)
    count = jnp.sum(jnp.sum(top, axis=1, keepdims=True), axis=0, keepdims=True)
    sums[...] = jnp.where(sub_index(COLS) == 0, total, jnp.where(sub_index(COLS) == 1, count, 0.0))
    for r in range(ROWS):
        first = mask[pl.ds(r, 8, stride=ROWS), :].astype(F32)
        m8 = mask[8 * ROWS + r : 8 * ROWS + r + 1, :].astype(F32)
        m9 = mask[9 * ROWS + r : 9 * ROWS + r + 1, :].astype(F32)
        for t in range(4):
            own[r, 8 * t : 8 * t + 8, :] = x[pl.ds(t * 10 * ROWS + r, 8, stride=ROWS), :] * first
            cown[r, 8 * t : 8 * t + 8, :] = cot[pl.ds(t * 10 * ROWS + r, 8, stride=ROWS), :]
        for level, m in ((8, m8), (9, m9)):
            at = 32 + 4 * (level - 8)
            own[r, at : at + 4, :] = x[pl.ds(level * ROWS + r, 4, stride=10 * ROWS), :] * m
            cown[r, at : at + 4, :] = cot[pl.ds(level * ROWS + r, 4, stride=10 * ROWS), :]
        own[r, 40:48, :] = first
        own[r, 48:49, :] = m8
        own[r, 49:50, :] = m9
        own[r, 50:51, :] = flux[r : r + 1, :]
        own[r, 51:PACK, :] = jnp.zeros((5, COLS), F32)
    for half in range(2):
        for t in range(7):
            rows = [own[8 * half + s, 8 * t : 8 * t + 8, :] for s in range(8)]
            at = half * PACK + 8 * t
            east[at : at + 8, :] = slot_pack(rows, lambda s: SLOT * (s + 1), SLOT)
            west[at : at + 8, :] = slot_pack(rows, lambda s: SLOT * s, SLOT)
    for t in range(5):
        rows = [cown[s, 8 * t : 8 * t + 8, :] for s in range(ROWS)]
        at = 2 * PACK + 8 * t
        east[at : at + 8, :] = slot_pack(rows, lambda s: 8 * (s + 1), 8)
        west[at : at + 8, :] = slot_pack(rows, lambda s: 8 * s, 8)
    southern = (lax.axis_index("lat") == 0).astype(jnp.int32)
    for side, lat in zip(sides, per_side):
        start = {"swap": southern * (ROWS - REACH), "north": ROWS - REACH, "south": 0}[side]
        cstart = {"swap": southern * (ROWS - CREACH), "north": ROWS - CREACH, "south": 0}[side]
        for n in range(REACH):
            lat[PACK * n : PACK * (n + 1), :] = own[start + n]
        for n in range(CREACH):
            lat[LAT_X + FEATS * n : LAT_X + FEATS * (n + 1), :] = cown[cstart + n]


def corner_kernel(sides, scal, east, west, *outs):
    for side, corner in zip(sides, outs):
        start = {"swap": scal[0], "north": ROWS - REACH, "south": 0}[side]
        for at, strip, near in ((0, east, 1), (PACK + 40, west, 0)):
            for t in range(7):
                rows = slice(at + 8 * t, at + 8 * t + 8)
                corner[rows, :] = shift_rows(strip, t, start, near)
            corner[at + PACK : at + PACK + 40, :] = strip[2 * PACK : 2 * PACK + 40, :]
        corner[CORNER : CORNER + 8, :] = jnp.zeros((8, COLS), F32)


def shift_rows(strip, t, start, near):
    lane = lax.broadcasted_iota(jnp.int32, (8, COLS), 1)
    halves = [strip[8 * t : 8 * t + 8, :], strip[PACK + 8 * t : PACK + 8 * t + 8, :]]
    if isinstance(start, int):
        out = jnp.zeros((8, COLS), F32)
        for n in range(REACH):
            r = start + n
            turn = REACH * n - (SLOT * (r % 8) + near * (SLOT - REACH))
            turned = pltpu.roll(halves[r // 8], turn % COLS, 1)
            out = jnp.where((lane >= REACH * n) & (lane < REACH * (n + 1)), turned, out)
        return out
    low = shift_rows(strip, t, 0, near)
    high = shift_rows(strip, t, ROWS - REACH, near)
    return jnp.where(start == 0, low, high)


def split(values):
    high = values.astype(BF16)
    return high, (values - high.astype(F32)).astype(BF16)


def stack(out, values, buffer):
    k = values.shape[1]
    rows = slice(0, values.shape[0])
    high, low = split(values)
    buffer[rows, 0:k] = high.astype(F32)
    buffer[rows, k : 2 * k] = high.astype(F32)
    buffer[rows, 2 * k : 3 * k] = low.astype(F32)
    out[...] = buffer[rows, 0 : 3 * k].astype(BF16)


def by_tile(dst, src, lanes):
    for t in range(4):
        dst[8 * t : 8 * t + 8, lanes] = src[10 * t : 10 * t + 8, lanes]
        dst[32 + t : 33 + t, lanes] = src[10 * t + 8 : 10 * t + 9, lanes]
        dst[36 + t : 37 + t, lanes] = src[10 * t + 9 : 10 * t + 10, lanes]


def product(weights, high, low):
    return jnp.dot(weights, jnp.concatenate([high, low, high], axis=0), preferred_element_type=F32)


def across(a, b):
    dims = (((1,), (1,)), ((), ()))
    dot = lambda p, q: lax.dot_general(p, q, dims, preferred_element_type=F32)
    return dot(a[0], b[0]) + dot(a[0], b[1]) + dot(a[1], b[0])


def to_48(columns, first=0.0):
    more = jnp.where(sub_index(columns.shape[1]) == 0, first, 0.0).astype(F32)
    return jnp.concatenate([columns, more], axis=0)


def wide(bias, values):
    return jnp.concatenate([bias[...]] * (values.shape[1] // COLS), axis=1)


def hidden_layers(z, k1, k2, b2):
    h1 = jnp.tanh(product(k1[...], *z))
    h1s = split(h1)
    h2 = product(k2[...], *h1s)
    return h1, h1s, jnp.tanh(h2 + wide(b2, h2))


def last_layer(h2, k3, b3):
    o = product(k3[...], *split(h2))[0:FEATS]
    return o + wide(b3, o)


def add_weight_terms(acc, z, h1s, h2s, g1s, g2s, gos):
    ones = jnp.ones((16, z[0].shape[1]), BF16)
    acc[0:48, 0:HID] += across(z, g1s)
    acc[48:112, 0:HID] += across(h1s, g2s)
    acc[112:160, 0:HID] += across(gos, h2s)
    acc[160:176, 0:HID] += ones_rows(ones, g2s)
    acc[176:192, 0:48] += ones_rows(ones, gos)


def ones_rows(ones, g):
    dims = (((1,), (1,)), ((), ()))
    dot = lambda q: lax.dot_general(ones, q, dims, preferred_element_type=F32)
    return dot(g[0]) + dot(g[1])


def own_closure_kernel(own, *refs):
    raw, (out, h1_out, h2_out, k1, k2, k3, q1, q2, q3, b2, b3) = refs[:6], refs[6:17]
    w_in, w_mid, w_out, b_in, b_mid, b_out = refs[17:23]
    buffer, spare, stacked, sems = refs[23:]
    copies = [pltpu.make_async_copy(a, b, sems.at[i]) for i, (a, b) in enumerate(zip(raw, refs[17:23]))]
    for copy in copies:
        copy.start()
    for copy in copies:
        copy.wait()
    buffer[...] = jnp.zeros(buffer.shape, F32)
    by_tile(buffer, w_in, slice(0, HID))
    buffer[40:41, 0:HID] = b_in[...]
    stack(q1, buffer[0:48, 0:HID], stacked)
    spare[...] = buffer[...].T
    stack(k1, spare[0:HID, 0:48], stacked)
    buffer[0:HID, 0:HID] = w_mid[...]
    buffer[HID : HID + 1, 0:HID] = b_mid[...]
    stack(q2, buffer[0:HID, 0:HID], stacked)
    spare[...] = buffer[...].T
    stack(k2, spare[0:HID, 0:HID], stacked)
    b2[...] = jnp.broadcast_to(spare[0:HID, HID : HID + 1], (HID, COLS))
    buffer[...] = jnp.zeros(buffer.shape, F32)
    buffer[0:HID, 0:FEATS] = w_out[...]
    buffer[HID : HID + 1, 0:FEATS] = b_out[...]
    spare[...] = buffer[...].T
    buffer[...] = jnp.zeros(buffer.shape, F32)
    by_tile(buffer, spare, slice(0, COLS))
    stack(k3, buffer[0:48, 0:HID], stacked)
    b3[...] = jnp.broadcast_to(buffer[0:FEATS, HID : HID + 1], (FEATS, COLS))
    spare[...] = buffer[...].T
    stack(q3, spare[0:HID, 0:48], stacked)

    for r in range(0, ROWS, 8):
        z = split(to_48(jnp.concatenate([own[r + n, 0:FEATS, :] for n in range(8)], axis=1), 1.0))
        h1, h1s, h2 = hidden_layers(z, k1, k2, b2)
        o = last_layer(h2, k3, b3)
        for n in range(8):
            at = slice(n * COLS, (n + 1) * COLS)
            out[r + n] = o[:, at]
            h1_out[r + n] = h1[:, at]
            h2_out[r + n] = h2[:, at]


class Row:
    def __init__(self, width):
        sub = sub_index(width)
        group = sub % 4
        self.sub = sub
        self.is_t = group == 0
        self.is_s = group == 1
        self.is_u = group == 2
        self.is_v = group == 3
        self.low = sub >= 4
        self.k4 = jnp.where(group < 2, DIFFUSIVITY, VISCOSITY).astype(F32)


def put_state(k, ref, row, tiles):
    for t in range(5):
        ref[row, 8 * t : 8 * t + 8, :] = tiles[t]
    press = 0.4 * tiles[1] - 0.1 * tiles[0]
    for by in (1, 2, 4):
        press = press + jnp.where(k.sub >= by, pltpu.roll(press, by, 0), 0.0)
    ref[row, 40:48, :] = press
    deep_8 = ref[row, 47:48, :] + (0.4 * ref[row, 33:34, :] - 0.1 * ref[row, 32:33, :])
    ref[row, 48:49, :] = deep_8
    ref[row, 49:50, :] = deep_8 + (0.4 * ref[row, 37:38, :] - 0.1 * ref[row, 36:37, :])


def deep_pair(k, ref, row, upper, lower):
    return jnp.where(k.low, ref[row, lower : lower + 1, :], ref[row, upper : upper + 1, :])


def deep_u(k, ref, row):
    return deep_pair(k, ref, row, 34, 38)


def deep_v(k, ref, row):
    return deep_pair(k, ref, row, 35, 39)


def deep_p(k, ref, row):
    return deep_pair(k, ref, row, 48, 49)


def east_of(q):
    return pltpu.roll(q, q.shape[1] - 1, 1)


def west_of(q):
    return pltpu.roll(q, 1, 1)


def gain_of(k, t):
    return k.k4 if t == 4 else (DIFFUSIVITY if t < 2 else VISCOSITY)


def tendency_row(k, ref, row, c, f):
    half = 0.5 * c
    c2 = c * c
    u, v = tile(ref, row, 2), tile(ref, row, 3)
    u4, v4 = deep_u(k, ref, row), deep_v(k, ref, row)
    change = []
    for t in range(5):
        gain = gain_of(k, t)
        if t in (0, 2, 4):
            au, av = (half * u4, 0.5 * v4) if t == 4 else (half * u, 0.5 * v)
            along = gain * c2
            at_e, at_w, at_n, at_s = along - au, along + au, gain - av, gain + av
        q = tile(ref, row, t)
        east, west = at_e * east_of(q), at_w * west_of(q)
        north, south = at_n * tile(ref, row + 1, t), at_s * tile(ref, row - 1, t)
        change.append((east + west) + (north + south) - (gain * (2.0 * c2 + 2.0)) * q)
    p = tile(ref, row, 5)
    change[2] = change[2] + (f * v - half * (east_of(p) - west_of(p)))
    change[3] = change[3] - (f * u + 0.5 * (tile(ref, row + 1, 5) - tile(ref, row - 1, 5)))
    p4 = deep_p(k, ref, row)
    fx = f * v4 - half * (east_of(p4) - west_of(p4))
    fy = f * u4 + 0.5 * (deep_p(k, ref, row + 1) - deep_p(k, ref, row - 1))
    change[4] = change[4] + jnp.where(k.is_u, fx, jnp.where(k.is_v, -fy, 0.0))
    return change


def adjoint_row(k, ref, aref, row, c, f):
    half = 0.5 * c
    c2 = c * c
    u4 = deep_u(k, ref, row)
    qe = [east_of(tile(ref, row, t)) for t in range(5)]
    qw = [west_of(tile(ref, row, t)) for t in range(5)]
    out = []
    to_u = to_v = None
    for t in range(5):
        a = tile(aref, row, t)
        ae, aw = east_of(a), west_of(a)
        an, as_ = tile(aref, row + 1, t), tile(aref, row - 1, t)
        gain = gain_of(k, t)
        if t == 0:
            ue, uw = half * qe[2], half * qw[2]
            vn, vs = 0.5 * tile(ref, row + 1, 3), 0.5 * tile(ref, row - 1, 3)
        if t == 4:
            ue, uw = half * east_of(u4), half * west_of(u4)
            vn, vs = 0.5 * deep_v(k, ref, row + 1), 0.5 * deep_v(k, ref, row - 1)
        if t in (0, 2, 4):
            along = gain * c2
            at_e, at_w, at_n, at_s = along + ue, along - uw, gain + vn, gain - vs
        out.append(
            (at_e * ae + at_w * aw) + (at_n * an + at_s * as_) - (gain * (2.0 * c2 + 2.0)) * a
        )
        px = a * (qe[t] - qw[t])
        py = a * (tile(ref, row + 1, t) - tile(ref, row - 1, t))
        if t < 4:
            to_u = px if to_u is None else to_u + px
            to_v = py if to_v is None else to_v + py
        if t == 2:
            a2, bx = a, half * (ae - aw)
        if t == 3:
            a3, by = a, 0.5 * (an - as_)
        if t == 4:
            a4 = a
            deep_bx, deep_by = half * (ae - aw), 0.5 * (an - as_)
            px4, py4 = px * half, py * 0.5
    out[2] = out[2] - half * to_u - f * a3
    out[3] = out[3] - 0.5 * to_v + f * a2
    sx = px4 + pltpu.roll(px4, 7, 0)
    sx = sx + pltpu.roll(sx, 2, 0)
    sy = py4 + pltpu.roll(py4, 1, 0)
    sy = sy + pltpu.roll(sy, 2, 0)
    at_u = -sx - f * pltpu.roll(a4, 7, 0)
    at_v = f * pltpu.roll(a4, 1, 0) - sy
    deep = jnp.where(k.is_t, pltpu.roll(deep_bx, 6, 0) + pltpu.roll(deep_by, 5, 0), 0.0)
    deep = deep + jnp.where(k.low, 0.0, pltpu.roll(deep, 4, 0))
    press = bx + by
    for shift in (1, 2, 4):
        press = press + jnp.where(k.sub < 8 - shift, pltpu.roll(press, 8 - shift, 0), 0.0)
    press = press + deep[0:1, :]
    out[0] = out[0] - 0.1 * press
    out[1] = out[1] + 0.4 * press
    out[4] = out[4] + jnp.where(
        k.is_t,
        -0.1 * deep,
        jnp.where(k.is_s, 0.4 * pltpu.roll(deep, 1, 0), jnp.where(k.is_u, at_u, at_v)),
    )
    return out


def for_span(low, high, up, body):
    turns = lax.div(high - low + TURN - 1, TURN)
    first = jnp.where(up == 1, low, high - TURN * turns)

    def turn(i, _):
        for j in range(TURN):
            body(first + TURN * i + j)
        return 0

    lax.fori_loop(0, turns, turn, 0)


def for_rows(scal, reach, body):
    for_span(PAD - reach * scal[2], PAD + ROWS + reach * scal[3], scal[3], body)


def for_inner(scal, inset, body):
    for_span(PAD + inset * scal[2], PAD + ROWS - inset * scal[3], scal[3], body)


def for_outer(sides, scal, inset, reach, body):
    if sides == ["swap"]:
        low = jnp.where(scal[3] == 1, PAD + ROWS - inset, PAD - reach)
        for_span(low, low + reach + inset, scal[3], body)
    else:
        for_span(PAD - reach * scal[2], PAD + inset * scal[2], 0, body)
        for_span(PAD + ROWS - inset * scal[3], PAD + ROWS + reach * scal[3], 1, body)


def mask_tile(ref, row, t):
    return tile(ref, row, 1 if t == 4 else 0)


def adjoint_third(k, scal, cs, fs, reach, state, masks, abuf, top, hold, bbuf):
    def body(r):
        d = adjoint_row(k, state, abuf, r, cs[r], fs[r])
        for t in range(5):
            ts = (2.0 / 3.0) * tile(top, r, t) + d[t]
            hold[r, 8 * t : 8 * t + 8, :] = ts
            bbuf[r, 8 * t : 8 * t + 8, :] = 0.0625 * mask_tile(masks, r, t) * ts

    for_rows(scal, reach, body)


def adjoint_second(k, scal, cs, fs, reach, state, masks, bbuf, top, hold, left, abuf):
    def body(r):
        d = adjoint_row(k, state, bbuf, r, cs[r], fs[r])
        for t in range(5):
            ts = tile(hold, r, t)
            tf = 0.25 * ts + d[t]
            left[r, 8 * t : 8 * t + 8, :] = (1.0 / 3.0) * tile(top, r, t) + 0.75 * ts + tf
            abuf[r, 8 * t : 8 * t + 8, :] = 0.25 * mask_tile(masks, r, t) * tf

    for_rows(scal, reach, body)


def adjoint_first(k, scal, cs, fs, reach, state, abuf, left, store):
    def body(r):
        d = adjoint_row(k, state, abuf, r, cs[r], fs[r])
        store(r, [tile(left, r, t) + d[t] for t in range(5)])

    for_rows(scal, reach, body)


def edges(reach):
    lane = lax.broadcasted_iota(jnp.int32, (8, COLS), 1)
    return lane < reach, lane >= COLS - reach


def wide_pack(ref, base):
    parts = []
    for t in range(5):
        rows = [ref[base + s, 8 * t : 8 * t + 8, COLS:WIDE] for s in range(8)]
        parts.append(slot_pack(rows, lambda s: 8 + SLOT * s, SLOT))
    return jnp.concatenate(parts, axis=0)

def wide_unpack(ref, base, values):
    for s in range(8):
        ref[base + s, 0:FEATS, COLS:WIDE] = pltpu.roll(values, -(8 + SLOT * s) % COLS, 1)


def section_1(k, cs, fs, masks, src, dst):
    def body(r):
        d = tendency_row(k, src, r, cs[r], fs[r])
        put_state(
            k, dst, r,
            [tile(src, r, t) + 0.25 * mask_tile(masks, r, t) * d[t] for t in range(5)],
        )
    return body

def section_2(k, cs, fs, masks, src, mid, dst):
    def body(r):
        d = tendency_row(k, mid, r, cs[r], fs[r])
        put_state(
            k, dst, r,
            [
                0.75 * tile(src, r, t) + 0.25 * tile(mid, r, t)
                + 0.0625 * mask_tile(masks, r, t) * d[t]
                for t in range(5)
            ],
        )
    return body


def section_3(k, cs, fs, masks, fluxes, mean, src, mid, net, r):
    d = tendency_row(k, mid, r, cs[r], fs[r])
    new = []
    for t in range(5):
        m = mask_tile(masks, r, t)
        o = tile(net, r, t)
        if t == 1:
            force = 2.0 * (mean - fluxes[r, 2:3, :])
            o = o + jnp.where(k.sub == 0, force, 0.0)
        new.append(
            (1.0 / 3.0) * tile(src, r, t) + (2.0 / 3.0) * tile(mid, r, t)
            + m * ((1.0 / 6.0) * d[t] + 0.25 * o)
        )
    return new


def zero_walls(ref):
    for row in (PAD - 1, PAD + ROWS):
        ref[row] = jnp.zeros(ref.shape[1:], F32)


class Block:
    def __init__(self, k, s0, masks, fluxes):
        self.k, self.s0, self.masks, self.fluxes = k, s0, masks, fluxes
        self.near_e, self.near_w = edges(REACH)

    def put(self, row, core, from_e, from_w):
        def both(t):
            halo = jnp.where(self.near_e, from_e(t), jnp.where(self.near_w, from_w(t), 0.0))
            return jnp.concatenate([core(t), halo], axis=1)

        put_state(self.k, self.s0, row, [both(t) for t in range(5)])
        self.masks[row, 0:8, :] = both(5)
        last = both(6)
        self.masks[row, 8:16, :] = jnp.where(self.k.low, last[1:2, :], last[0:1, :])
        self.fluxes[row] = last


def assemble_own_kernel(scal, cs, fs, own, own_m, east, west, k1, k2, k3, b2, b3, s0, masks, fluxes, net):
    k = Row(WIDE)
    zero_walls(s0)
    block = Block(k, s0, masks, fluxes)
    for r in range(ROWS):
        at = (r // 8) * PACK
        turn = SLOT * (r % 8)
        block.put(
            PAD + r,
            lambda t: own[r, 8 * t : 8 * t + 8, :],
            lambda t: pltpu.roll(west[at + 8 * t : at + 8 * t + 8, :], -turn % COLS, 1),
            lambda t: pltpu.roll(east[at + 8 * t : at + 8 * t + 8, :], -(turn + SLOT) % COLS, 1),
        )
        net[PAD + r, :, 0:COLS] = own_m[r]
    columns = jnp.concatenate([wide_pack(s0, PAD), wide_pack(s0, PAD + 8)], axis=1)
    o = closure_of(columns, k1, k2, k3, b2, b3)
    for g in range(2):
        wide_unpack(net, PAD + 8 * g, o[:, g * COLS : (g + 1) * COLS])


def closure_of(columns, k1, k2, k3, b2, b3):
    _, _, h2 = hidden_layers(split(to_48(columns, 1.0)), k1, k2, b2)
    return last_layer(h2, k3, b3)


def first_own_kernel(scal, cs, fs, s0, masks, s1):
    zero_walls(s1)
    for_inner(scal, 1, section_1(Row(WIDE), cs, fs, masks, s0, s1))


def second_own_kernel(scal, cs, fs, s0, s1, masks, s2):
    for_inner(scal, 2, section_2(Row(WIDE), cs, fs, masks, s0, s1, s2))


def halo_kernel(sides, scal, cs, fs, own_s0, own_s1, own_s2, own_masks, own_fluxes, own_net, *rest):
    n = len(sides)
    side_refs = [rest[2 * i : 2 * i + 2] for i in range(n)]
    net_refs, (s0, s1, s2, masks, fluxes, net) = rest[2 * n : 2 * n + 5], rest[2 * n + 5 :]
    k = Row(WIDE)
    for r in range(PAD, PAD + ROWS):
        for src, dst in (
            (own_s0, s0), (own_s1, s1), (own_s2, s2), (own_masks, masks), (own_fluxes, fluxes), (own_net, net)
        ):
            dst[r] = src[r]
    for ref in (s0, s1, s2):
        zero_walls(ref)
    block = Block(k, s0, masks, fluxes)
    firsts = []
    for side, (lat, corner) in zip(sides, side_refs):
        base = {"swap": scal[4], "north": PAD - REACH, "south": PAD + ROWS}[side]
        for r in range(REACH):
            block.put(
                base + r,
                lambda t: lat[PACK * r + 8 * t : PACK * r + 8 * t + 8, :],
                lambda t: pltpu.roll(corner[PACK + 40 + 8 * t : PACK + 48 + 8 * t, :], -REACH * r % COLS, 1),
                lambda t: pltpu.roll(corner[8 * t : 8 * t + 8, :], -REACH * (r + 1) % COLS, 1),
            )
        near = {"swap": jnp.where(scal[2] == 1, PAD - 8, PAD + ROWS), "north": PAD - 8, "south": PAD + ROWS}
        firsts.append(near[side])
    columns = []
    for first in firsts:
        columns += [s0[first + i, 0:FEATS, 0:COLS] for i in range(8)] + [wide_pack(s0, first)]
    o = closure_of(jnp.concatenate(columns, axis=1), *net_refs)
    for g, first in enumerate(firsts):
        for i in range(8):
            at = (9 * g + i) * COLS
            net[first + i, :, 0:COLS] = o[:, at : at + COLS]
        at = (9 * g + 8) * COLS
        wide_unpack(net, first, o[:, at : at + COLS])
    for_outer(sides, scal, 1, 10, section_1(k, cs, fs, masks, s0, s1))
    for_outer(sides, scal, 2, 9, section_2(k, cs, fs, masks, s0, s1, s2))


def last_section_kernel(scal, cs, fs, sums, s3, t2, masks, fluxes, outs, final):
    k = Row(WIDE)
    mean = sums[0:1, 0:1] / sums[1:2, 0:1]

    def last(r):
        new = section_3(k, cs, fs, masks, fluxes, mean, s3, t2, outs, r)
        put_result(final, r - PAD, [x[:, 0:COLS] for x in new])

    for_rows(scal, 0, last)


def late_kernel(
    sides, scal, cs, fs, sums, own, cown, own_h1, own_h2, s0, s2, masks, fluxes, outs_in, east, west, *rest
):
    n = len(sides)
    side_refs = [rest[2 * i : 2 * i + 2] for i in range(n)]
    (k1, k2, k3, q1, q2, q3, b2, b3), rest = rest[2 * n : 2 * n + 8], rest[2 * n + 8 :]
    grads, s4, abuf, from_closure, s3, t2, outs, t1, cot, gz, bbuf, hold, left, acc = rest
    k = Row(WIDE)
    has_south = scal[2]
    lo = lambda h: PAD - h * has_south
    for ref in (s3, t1, t2, abuf, bbuf):
        zero_walls(ref)
    mean = sums[0:1, 0:1] / sums[1:2, 0:1]

    cnear_e, cnear_w = edges(CREACH)
    for r in range(ROWS):
        for t in range(5):
            rows = slice(2 * PACK + 8 * t, 2 * PACK + 8 * t + 8)
            from_e = pltpu.roll(west[rows, :], -8 * r % COLS, 1)
            from_w = pltpu.roll(east[rows, :], -8 * (r + 1) % COLS, 1)
            side = jnp.where(cnear_e, from_e, jnp.where(cnear_w, from_w, 0.0))
            cot[PAD + r, 8 * t : 8 * t + 8, :] = jnp.concatenate(
                [cown[r, 8 * t : 8 * t + 8, :], side], axis=1
            )
    for side, (lat, corner) in zip(sides, side_refs):
        cbase = {"swap": scal[5], "north": PAD - CREACH, "south": PAD + ROWS}[side]
        crow = {"swap": scal[6], "north": ROWS - CREACH, "south": 0}[side]
        for r in range(CREACH):
            turn = lax.rem(2 * COLS - 8 * (crow + r), COLS)
            turn_w = lax.rem(2 * COLS - 8 * (crow + r + 1), COLS)
            for t in range(5):
                wrows = slice(PACK + 8 * t, PACK + 8 * t + 8)
                erows = slice(2 * PACK + 40 + 8 * t, 2 * PACK + 48 + 8 * t)
                from_e = pltpu.roll(corner[erows, :], turn, 1)
                from_w = pltpu.roll(corner[wrows, :], turn_w, 1)
                part = jnp.where(cnear_e, from_e, jnp.where(cnear_w, from_w, 0.0))
                cot[cbase + r, 8 * t : 8 * t + 8, :] = jnp.concatenate(
                    [lat[LAT_X + FEATS * r + 8 * t : LAT_X + FEATS * r + 8 * t + 8, :], part], axis=1
                )


    def step_1_end(r):
        put_state(k, s3, r, section_3(s0, s2, r))

    def step_1_end(r):
        put_state(k, s3, r, section_3(k, cs, fs, masks, fluxes, mean, s0, s2, outs_in, r))

    for_rows(scal, 8, step_1_end)

    acc[...] = jnp.zeros(acc.shape, F32)

    def closure_adjoint(z, h1, h1s, h2, go, with_weights):
        gos = split(to_48(go))
        g2 = product(q3[...], *gos) * (1.0 - h2 * h2)
        g2s = split(g2)
        g1 = product(q2[...], *g2s) * (1.0 - h1 * h1)
        g1s = split(g1)
        if with_weights:
            add_weight_terms(acc, z, h1s, split(h2), g1s, g2s, gos)
        return product(q1[...], *g1s)[0:FEATS]

    def both_ways(columns, go, with_weights):
        z = split(to_48(columns, 1.0))
        h1, h1s, h2 = hidden_layers(z, k1, k2, b2)
        o = last_layer(h2, k3, b3) if with_weights else None
        return o, closure_adjoint(z, h1, h1s, h2, go, with_weights)

    def masked_core(ref, r):
        m0, m4 = masks[r, 0:8, 0:COLS], masks[r, 8:16, 0:COLS]
        parts = [
            0.25 * (m4 if t == 4 else m0) * ref[r, 8 * t : 8 * t + 8, 0:COLS] for t in range(5)
        ]
        return jnp.concatenate(parts, axis=0)

    def mask_cot(r):
        for t in range(5):
            bbuf[r, 8 * t : 8 * t + 8, :] = 0.25 * mask_tile(masks, r, t) * tile(cot, r, t)
            abuf[r, 8 * t : 8 * t + 8, :] = (1.0 / 6.0) * mask_tile(masks, r, t) * tile(cot, r, t)

    for_rows(scal, 6, mask_cot)

    for first in range(PAD, PAD + ROWS, 8):
        z = jnp.concatenate([s3[first + i, 0:FEATS, 0:COLS] for i in range(8)], axis=1)
        go = jnp.concatenate([bbuf[first + i, 0:FEATS, 0:COLS] for i in range(8)], axis=1)
        o, back = both_ways(z, go, True)
        for i in range(8):
            at = slice(i * COLS, (i + 1) * COLS)
            outs[first + i, :, 0:COLS] = o[:, at]
            gz[first + i, :, 0:COLS] = back[:, at]

    first = lo(4)
    if sides == ["swap"]:
        rows = [jnp.where(has_south == 1, PAD - 4, PAD + ROWS) + i for i in range(4)]
    else:
        rows = [PAD - 4 + i for i in range(4)] + [PAD + ROWS + i for i in range(4)]
    beyond = lambda ref: jnp.concatenate(
        [ref[r, 0:FEATS, 0:COLS] for r in rows] + [wide_pack(ref, first + 8 * g) for g in range(3)], axis=1
    )
    _, back = both_ways(beyond(s3), beyond(bbuf), False)
    for i, r in enumerate(rows):
        gz[r, :, 0:COLS] = back[:, i * COLS : (i + 1) * COLS]
    for g in range(3):
        at = (len(rows) + g) * COLS
        wide_unpack(gz, first + 8 * g, back[:, at : at + COLS])

    for_rows(scal, 7, section_1(k, cs, fs, masks, s3, t1))
    for_rows(scal, 6, section_2(k, cs, fs, masks, s3, t1, t2))

    def store(r, tiles):
        for t in range(5):
            s4[r, 8 * t : 8 * t + 8, :] = tiles[t] + tile(gz, r, t)

    adjoint_third(k, scal, cs, fs, 5, t2, masks, abuf, cot, hold, bbuf)
    adjoint_second(k, scal, cs, fs, 4, t1, masks, bbuf, cot, hold, left, abuf)
    adjoint_first(k, scal, cs, fs, 3, s3, abuf, left, store)

    for r in range(0, ROWS, 8):
        side = lambda read: jnp.concatenate([read(r + j) for j in range(8)], axis=1)
        z = split(to_48(side(lambda j: own[j, 0:FEATS, :]), 1.0))
        h1 = side(lambda j: own_h1[j])
        h2 = side(lambda j: own_h2[j])
        go = side(lambda j: masked_core(s4, PAD + j))
        back = closure_adjoint(z, h1, split(h1), h2, go, True)
        for j in range(8):
            from_closure[r + j] = back[:, j * COLS : (j + 1) * COLS]

    zero_walls(abuf)

    def mask_top(r):
        for t in range(5):
            abuf[r, 8 * t : 8 * t + 8, :] = (1.0 / 6.0) * mask_tile(masks, r, t) * tile(s4, r, t)

    for_rows(scal, 3, mask_top)
    grads[...] = jnp.zeros(grads.shape, F32)
    grads[0:40, 0:HID] = acc[0:40, 0:HID]
    grads[0:40, HID : 2 * HID] = acc[112:152, 0:HID]
    grads[40:72, 0:HID] = acc[48:80, 0:HID]
    grads[40:72, HID : 2 * HID] = acc[80:112, 0:HID]
    grads[72:73, 0:HID] = acc[40:41, 0:HID]
    grads[72:73, HID : 2 * HID] = acc[160:161, 0:HID]
    grads[73:74, 0:HID] = acc[176:177, 0:HID]


def put_result(ref, row, tiles):
    for t in range(4):
        ref[pl.ds(t * 10 * ROWS + row, 8, stride=ROWS), :] = tiles[t]
    ref[pl.ds(8 * ROWS + row, 4, stride=10 * ROWS), :] = tiles[4][0:4, :]
    ref[pl.ds(9 * ROWS + row, 4, stride=10 * ROWS), :] = tiles[4][4:8, :]


def back_third_kernel(scal, cs, fs, state, masks, abuf, top, hold, bbuf):
    zero_walls(bbuf)
    adjoint_third(Row(WIDE), scal, cs, fs, 2, state, masks, abuf, top, hold, bbuf)


def back_second_kernel(scal, cs, fs, state, masks, bbuf, top, hold, left, abuf):
    zero_walls(abuf)
    adjoint_second(Row(WIDE), scal, cs, fs, 1, state, masks, bbuf, top, hold, left, abuf)


def back_first_kernel(scal, cs, fs, state, masks, abuf, left, from_closure, grad):
    def store(r, tiles):
        done = []
        for t in range(5):
            m = masks[r, 8:16, 0:COLS] if t == 4 else masks[r, 0:8, 0:COLS]
            done.append(m * (tiles[t][:, 0:COLS] + from_closure[r - PAD, 8 * t : 8 * t + 8, :]))
        put_result(grad, r - PAD, done)

    adjoint_first(Row(WIDE), scal, cs, fs, 0, state, abuf, left, store)


def unpack_kernel(scale, packed, win, bin_, wmid, bmid, wout, bout):
    for ref, lanes in ((win, slice(0, HID)), (wout, slice(HID, 2 * HID))):
        for t in range(4):
            ref[10 * t : 10 * t + 8, :] = packed[8 * t : 8 * t + 8, lanes] * scale
            ref[10 * t + 8 : 10 * t + 9, :] = packed[32 + t : 33 + t, lanes] * scale
            ref[10 * t + 9 : 10 * t + 10, :] = packed[36 + t : 37 + t, lanes] * scale
    wmid[0:32, :] = packed[40:72, 0:HID] * scale
    wmid[32:64, :] = packed[40:72, HID : 2 * HID] * scale
    bin_[...] = packed[72:73, 0:HID] * scale
    bmid[...] = packed[72:73, HID : 2 * HID] * scale
    for t in range(4):
        bout[:, 10 * t : 10 * t + 8] = packed[73:74, 8 * t : 8 * t + 8] * scale
        bout[:, 10 * t + 8 : 10 * t + 9] = packed[73:74, 32 + t : 33 + t] * scale
        bout[:, 10 * t + 9 : 10 * t + 10] = packed[73:74, 36 + t : 37 + t] * scale


def far_first(axes):
    return [(axis, n, 1 << bit) for axis, n in axes for bit in reversed(range(n.bit_length() - 1))]


def pair_rounds(x, rounds, beside):
    results = []
    for i in range(max(len(rounds), len(beside))):
        if i < len(rounds):
            axis, n, step = rounds[i]
            got = lax.ppermute(x, axis, [(j, j ^ step) for j in range(n)])
        if i < len(beside):
            results.append(beside[i](results))
            if i < len(rounds):
                got, results[-1] = lax.optimization_barrier((got, results[-1]))
        if i < len(rounds):
            x = x + got
    return x, results


def latitude_terms(row_index, row_count):
    latitude = LAT_LIMIT * (2.0 * (jnp.clip(row_index, 0.0, row_count - 1.0) + 0.5) / row_count - 1.0)
    return 1.0 / jnp.cos(latitude), CORIOLIS * jnp.sin(latitude)


def on_device(
    initial_state, land_mask, surface_flux, weight_in, bias_in, weight_mid, bias_mid, weight_out, bias_out, cotangent
):
    lat_n, lon_n = lax.axis_size("lat"), lax.axis_size("lon")
    lat_i = lax.axis_index("lat")
    lat_total, lon_total = ROWS * lat_n, COLS * lon_n
    sides = ["swap"] if lat_n == 2 else ["north", "south"]
    is_low = (lat_i == 0).astype(jnp.int32)
    has_south = (lat_i > 0).astype(jnp.int32)
    has_north = (lat_i < lat_n - 1).astype(jnp.int32)
    scal = jnp.stack(
        [
            is_low * (ROWS - REACH),
            is_low * (ROWS - CREACH),
            has_south,
            has_north,
            jnp.where(is_low == 1, PAD + ROWS, PAD - REACH),
            jnp.where(is_low == 1, PAD + ROWS, PAD - CREACH),
            jnp.where(is_low == 1, 0, ROWS - CREACH),
        ]
    ).astype(jnp.int32)
    rows = (lat_i * ROWS - PAD + jnp.arange(EXT, dtype=jnp.int32)).astype(F32)
    cs, fs = latitude_terms(rows, lat_total)

    hbm = pl.BlockSpec(memory_space=pltpu.HBM)
    packed = pl.pallas_call(
        lambda *refs: pack_kernel(sides, *refs),
        out_shape=[
            sds(ROWS, PACK, COLS), sds(ROWS, FEATS, COLS), sds(STRIP, COLS), sds(STRIP, COLS), sds(8, COLS),
        ]
        + [sds(LAT, COLS)] * len(sides),
        in_specs=[hbm] * 4,
        out_specs=[VMEM] * (5 + len(sides)),
        scratch_shapes=[
            pltpu.VMEM((40 * ROWS, COLS), F32), pltpu.VMEM((10 * ROWS, COLS), jnp.int32),
            pltpu.VMEM((ROWS, COLS), F32), pltpu.VMEM((40 * ROWS, COLS), F32), pltpu.SemaphoreType.DMA((4,)),
        ],
        compiler_params=params(56),
        cost_estimate=pl.CostEstimate(flops=10**9, bytes_accessed=3 * 10**6, transcendentals=0),
        name="pack_halos",
    )(
        initial_state.reshape(40 * ROWS, COLS),
        land_mask.reshape(10 * ROWS, COLS),
        surface_flux,
        cotangent.reshape(40 * ROWS, COLS),
    )
    own, cown, east_pay, west_pay, sums = packed[:5]

    def lat_pairs(side):
        if side == "swap":
            return [(0, 1), (1, 0)]
        if side == "north":
            return [(i, i + 1) for i in range(lat_n - 1)]
        return [(i + 1, i) for i in range(lat_n - 1)]

    east_ring = [(i, (i + 1) % lon_n) for i in range(lon_n)]
    west_ring = [((i + 1) % lon_n, i) for i in range(lon_n)]
    from_west = lax.ppermute(east_pay, "lon", east_ring)
    from_east = lax.ppermute(west_pay, "lon", west_ring)
    row = lambda b: b.reshape(1, -1)
    raw = (weight_in, weight_mid, weight_out, row(bias_in), row(bias_mid), row(bias_out))
    half = lambda *shape: jax.ShapeDtypeStruct(shape, BF16)
    own_closure = pl.pallas_call(
        own_closure_kernel,
        out_shape=[
            sds(ROWS, FEATS, COLS), sds(ROWS, HID, COLS), sds(ROWS, HID, COLS),
            half(HID, 144), half(HID, 192), half(48, 192), half(48, 192), half(HID, 192), half(HID, 144),
            sds(HID, COLS), sds(FEATS, COLS),
        ],
        in_specs=[VMEM] + [hbm] * 6,
        out_specs=[VMEM] * 11,
        scratch_shapes=[pltpu.VMEM(w.shape, F32) for w in raw]
        + [pltpu.VMEM((COLS, COLS), F32), pltpu.VMEM((COLS, COLS), F32), pltpu.VMEM((HID, WIDE), F32)]
        + [pltpu.SemaphoreType.DMA((6,))],
        compiler_params=params(12),
        cost_estimate=pl.CostEstimate(flops=10**9, bytes_accessed=2 * 10**6, transcendentals=0),
        name="own_closure",
    )
    pack_corners = pl.pallas_call(
        lambda *refs: corner_kernel(sides, *refs),
        out_shape=[sds(CORNER + 8, COLS)] * len(sides),
        in_specs=[SMEM, VMEM, VMEM],
        out_specs=[VMEM] * len(sides),
        compiler_params=params(8),
        cost_estimate=pl.CostEstimate(flops=10**8, bytes_accessed=10**6, transcendentals=0),
        name="pack_corners",
    )
    lats = [lax.ppermute(pay, "lat", lat_pairs(side)) for side, pay in zip(sides, packed[5:])]
    geometry = (scal, cs, fs)
    state = sds(EXT, 56, WIDE)
    plain = sds(EXT, FEATS, WIDE)
    marks = sds(EXT, 16, WIDE)
    vmem = lambda shape: pltpu.VMEM(shape.shape, F32)

    def call(kernel, name, out_shape, scratch, args, flops, limit):
        single = not isinstance(out_shape, list)
        return pl.pallas_call(
            kernel,
            out_shape=out_shape,
            in_specs=[SMEM] * 3 + [VMEM] * len(args),
            out_specs=VMEM if single else [VMEM] * len(out_shape),
            scratch_shapes=scratch,
            compiler_params=params(limit),
            cost_estimate=pl.CostEstimate(flops=flops, bytes_accessed=10**7, transcendentals=0),
            name=name,
        )(*geometry, *args)


    def last_round(done):
        own_m, _, _, k1, k2, k3, _, _, _, b2, b3 = done[1]
        blocks = call(
            assemble_own_kernel, "assemble_own", [state, marks, sds(EXT, 8, WIDE), plain], [],
            [own, own_m, from_west, from_east, k1, k2, k3, b2, b3], 10**9, 8,
        )
        return blocks, pack_corners(scal, from_west, from_east)

    rounds = far_first((("lon", lon_n),))[::-1]
    row_total, results = pair_rounds(
        sums,
        rounds,
        [lambda done: sums, lambda done: own_closure(own, *raw)]
        + [lambda done: sums] * (len(rounds) - 3)
        + [last_round],
    )
    own_m, own_h1, own_h2, k1, k2, k3, q1, q2, q3, b2, b3 = results[1]
    net_weights = [k1, k2, k3, b2, b3]
    (s0, masks, fluxes, net), corner_pays = results[-1]
    corners = []
    for side, pay in zip(sides, corner_pays):
        pay = lax.dynamic_update_slice(pay, row_total, (CORNER, 0))
        corners.append(lax.ppermute(pay, "lat", lat_pairs(side)))
    s1 = call(first_own_kernel, "first_section_own", state, [], [s0, masks], 10**9, 8)
    s2 = call(second_own_kernel, "second_section_own", state, [], [s0, s1, masks], 10**9, 8)
    corners, s2 = lax.optimization_barrier((corners, s2))
    if sides == ["swap"]:
        total = row_total + corners[0][CORNER : CORNER + 8]
    else:
        total = lax.psum(row_total, "lat")
    received = [ref for pair in zip(lats, corners) for ref in pair]
    s0, s1, s2, masks, fluxes, net = call(
        lambda *refs: halo_kernel(sides, *refs), "halo_rows",
        [state, state, state, marks, sds(EXT, 8, WIDE), plain], [],
        [s0, s1, s2, masks, fluxes, net] + received + net_weights, 2 * 10**9, 8,
    )
    grads, top, abuf, from_closure, s3, t2, net_2 = call(
        lambda *refs: late_kernel(sides, *refs), "steps_and_adjoint",
        [sds(80, COLS), plain, plain, sds(ROWS, FEATS, COLS), state, state, plain],
        [vmem(state)] + [vmem(plain)] * 5 + [pltpu.VMEM((192, HID), F32)],
        [total, own, cown, own_h1, own_h2, s0, s2, masks, fluxes, net, from_west, from_east]
        + received + [k1, k2, k3, q1, q2, q3, b2, b3],
        4 * 10**9, 18,
    )
    beside = [
        lambda done: call(
            back_third_kernel, "adjoint_third_section", [plain, plain], [], [s2, masks, abuf, top], 10**9, 8
        ),
        lambda done: call(
            back_second_kernel, "adjoint_second_section", [plain, plain], [],
            [s1, masks, done[0][1], top, done[0][0]], 10**9, 8,
        ),
        lambda done: call(
            back_first_kernel, "adjoint_first_section", sds(40 * ROWS, COLS), [],
            [s0, masks, done[1][1], done[1][0], from_closure], 10**9, 8,
        ),
        lambda done: call(
            last_section_kernel, "last_section", sds(40 * ROWS, COLS), [],
            [total, s3, t2, masks, fluxes, net_2], 10**9, 8,
        ),
    ]
    by_lon, by_lat = far_first((("lon", lon_n),)), far_first((("lat", lat_n),))
    summed, results = pair_rounds(grads, by_lon[:-2] + by_lat + by_lon[-2:], beside)
    state_grad, final = results[2:]

    scale = 1.0 / math.sqrt(lat_total * lon_total)
    g_in, g_bin, g_mid, g_bmid, g_out, g_bout = pl.pallas_call(
        lambda *refs: unpack_kernel(scale, *refs),
        out_shape=[sds(40, HID), sds(1, HID), sds(HID, HID), sds(1, HID), sds(40, HID), sds(1, 40)],
        in_specs=[VMEM],
        out_specs=[VMEM] * 6,
        compiler_params=params(8),
        name="unpack_weight_grads",
    )(summed)
    shape = initial_state.shape
    return (
        final.reshape(shape),
        state_grad.reshape(shape),
        g_in,
        g_bin.reshape(-1),
        g_mid,
        g_bmid.reshape(-1),
        g_out.T,
        g_bout.reshape(-1),
    )


def solution(mesh):
    split_state = P(None, None, "lat", "lon")
    return jax.shard_map(
        on_device,
        mesh=mesh,
        in_specs=(split_state, P(None, "lat", "lon"), P("lat", "lon"), P(), P(), P(), P(), P(), P(), split_state),
        out_specs=(split_state, split_state, P(), P(), P(), P(), P(), P()),
        check_vma=False,
    )
```

```python
import math

import jax
import jax.numpy as jnp
from jax import lax
from jax.experimental import pallas as pl
from jax.experimental.pallas import tpu as pltpu
from jax.sharding import PartitionSpec as P

LAT_LIMIT = 1.2
CORIOLIS = 1.0
VISCOSITY = 0.15
DIFFUSIVITY = 0.1

ROWS = 16
COLS = 128
REACH = 11
CREACH = 6
PAD = 16
EXT = 48
TURN = 4
WIDE = 2 * COLS
FEATS = 40
HID = 64
PACK = 56
STRIP = 2 * PACK + 40
LAT_X = REACH * PACK
CORNER = 2 * PACK + 80
LAT = LAT_X + CREACH * FEATS
SLOT = 16
F32 = jnp.float32
BF16 = jnp.bfloat16
VMEM = pl.BlockSpec(memory_space=pltpu.VMEM)
SMEM = pl.BlockSpec(memory_space=pltpu.SMEM)


def params(megabytes):
    return pltpu.CompilerParams(vmem_limit_bytes=megabytes * 1024 * 1024)


def sds(*shape):
    return jax.ShapeDtypeStruct(shape, F32)


def sub_index(width):
    return lax.broadcasted_iota(jnp.int32, (8, width), 0)


def tile(ref, row, number):
    return ref[row, 8 * number : 8 * number + 8, :]


def slot_pack(pieces, shift_of, width):
    lane = lax.broadcasted_iota(jnp.int32, (8, COLS), 1)
    packed = None
    for slot, piece in enumerate(pieces):
        turned = pltpu.roll(piece, shift_of(slot) % COLS, 1)
        if packed is None:
            packed = turned
        else:
            packed = jnp.where((lane >= slot * width) & (lane < (slot + 1) * width), turned, packed)
    return packed


def pack_kernel(sides, x_hbm, mask_hbm, flux_hbm, cot_hbm, *outs):
    x, mask, flux, cot, sems = outs[-5:]
    own, cown, east, west, sums = outs[:5]
    per_side = outs[5 : 5 + len(sides)]
    pairs = ((mask_hbm, mask), (x_hbm, x), (flux_hbm, flux), (cot_hbm, cot))
    copies = [pltpu.make_async_copy(a, b, sems.at[i]) for i, (a, b) in enumerate(pairs)]
    for copy in copies:
        copy.start()
    for copy in copies:
        copy.wait()
    top = mask[0:ROWS, :].astype(F32)
    total = jnp.sum(jnp.sum(top * flux[...], axis=1, keepdims=True), axis=0, keepdims=True)
    count = jnp.sum(jnp.sum(top, axis=1, keepdims=True), axis=0, keepdims=True)
    sums[...] = jnp.where(sub_index(COLS) == 0, total, jnp.where(sub_index(COLS) == 1, count, 0.0))
    for r in range(ROWS):
        first = mask[pl.ds(r, 8, stride=ROWS), :].astype(F32)
        m8 = mask[8 * ROWS + r : 8 * ROWS + r + 1, :].astype(F32)
        m9 = mask[9 * ROWS + r : 9 * ROWS + r + 1, :].astype(F32)
        for t in range(4):
            own[r, 8 * t : 8 * t + 8, :] = x[pl.ds(t * 10 * ROWS + r, 8, stride=ROWS), :] * first
            cown[r, 8 * t : 8 * t + 8, :] = cot[pl.ds(t * 10 * ROWS + r, 8, stride=ROWS), :]
        for level, m in ((8, m8), (9, m9)):
            at = 32 + 4 * (level - 8)
            own[r, at : at + 4, :] = x[pl.ds(level * ROWS + r, 4, stride=10 * ROWS), :] * m
            cown[r, at : at + 4, :] = cot[pl.ds(level * ROWS + r, 4, stride=10 * ROWS), :]
        own[r, 40:48, :] = first
        own[r, 48:49, :] = m8
        own[r, 49:50, :] = m9
        own[r, 50:51, :] = flux[r : r + 1, :]
        own[r, 51:PACK, :] = jnp.zeros((5, COLS), F32)
    for half in range(2):
        for t in range(7):
            rows = [own[8 * half + s, 8 * t : 8 * t + 8, :] for s in range(8)]
            at = half * PACK + 8 * t
            east[at : at + 8, :] = slot_pack(rows, lambda s: SLOT * (s + 1), SLOT)
            west[at : at + 8, :] = slot_pack(rows, lambda s: SLOT * s, SLOT)
    for t in range(5):
        rows = [cown[s, 8 * t : 8 * t + 8, :] for s in range(ROWS)]
        at = 2 * PACK + 8 * t
        east[at : at + 8, :] = slot_pack(rows, lambda s: 8 * (s + 1), 8)
        west[at : at + 8, :] = slot_pack(rows, lambda s: 8 * s, 8)
    southern = (lax.axis_index("lat") == 0).astype(jnp.int32)
    for side, lat in zip(sides, per_side):
        start = {"swap": southern * (ROWS - REACH), "north": ROWS - REACH, "south": 0}[side]
        cstart = {"swap": southern * (ROWS - CREACH), "north": ROWS - CREACH, "south": 0}[side]
        for n in range(REACH):
            lat[PACK * n : PACK * (n + 1), :] = own[start + n]
        for n in range(CREACH):
            lat[LAT_X + FEATS * n : LAT_X + FEATS * (n + 1), :] = cown[cstart + n]


def corner_kernel(sides, scal, east, west, *outs):
    for side, corner in zip(sides, outs):
        start = {"swap": scal[0], "north": ROWS - REACH, "south": 0}[side]
        for at, strip, near in ((0, east, 1), (PACK + 40, west, 0)):
            for t in range(7):
                rows = slice(at + 8 * t, at + 8 * t + 8)
                corner[rows, :] = shift_rows(strip, t, start, near)
            corner[at + PACK : at + PACK + 40, :] = strip[2 * PACK : 2 * PACK + 40, :]
        corner[CORNER : CORNER + 8, :] = jnp.zeros((8, COLS), F32)


def shift_rows(strip, t, start, near):
    lane = lax.broadcasted_iota(jnp.int32, (8, COLS), 1)
    halves = [strip[8 * t : 8 * t + 8, :], strip[PACK + 8 * t : PACK + 8 * t + 8, :]]
    if isinstance(start, int):
        out = jnp.zeros((8, COLS), F32)
        for n in range(REACH):
            r = start + n
            turn = REACH * n - (SLOT * (r % 8) + near * (SLOT - REACH))
            turned = pltpu.roll(halves[r // 8], turn % COLS, 1)
            out = jnp.where((lane >= REACH * n) & (lane < REACH * (n + 1)), turned, out)
        return out
    low = shift_rows(strip, t, 0, near)
    high = shift_rows(strip, t, ROWS - REACH, near)
    return jnp.where(start == 0, low, high)


def split(values):
    high = values.astype(BF16)
    return high, (values - high.astype(F32)).astype(BF16)


def stack(out, values, buffer):
    k = values.shape[1]
    rows = slice(0, values.shape[0])
    high, low = split(values)
    buffer[rows, 0:k] = high.astype(F32)
    buffer[rows, k : 2 * k] = high.astype(F32)
    buffer[rows, 2 * k : 3 * k] = low.astype(F32)
    out[...] = buffer[rows, 0 : 3 * k].astype(BF16)


def by_tile(dst, src, lanes):
    for t in range(4):
        dst[8 * t : 8 * t + 8, lanes] = src[10 * t : 10 * t + 8, lanes]
        dst[32 + t : 33 + t, lanes] = src[10 * t + 8 : 10 * t + 9, lanes]
        dst[36 + t : 37 + t, lanes] = src[10 * t + 9 : 10 * t + 10, lanes]


def product(weights, high, low):
    return jnp.dot(weights, jnp.concatenate([high, low, high], axis=0), preferred_element_type=F32)


def across(a, b):
    dims = (((1,), (1,)), ((), ()))
    dot = lambda p, q: lax.dot_general(p, q, dims, preferred_element_type=F32)
    return dot(a[0], b[0]) + dot(a[0], b[1]) + dot(a[1], b[0])


def to_48(columns, first=0.0):
    more = jnp.where(sub_index(columns.shape[1]) == 0, first, 0.0).astype(F32)
    return jnp.concatenate([columns, more], axis=0)


def wide(bias, values):
    return jnp.concatenate([bias[...]] * (values.shape[1] // COLS), axis=1)


def hidden_layers(z, k1, k2, b2):
    h1 = jnp.tanh(product(k1[...], *z))
    h1s = split(h1)
    h2 = product(k2[...], *h1s)
    return h1, h1s, jnp.tanh(h2 + wide(b2, h2))


def last_layer(h2, k3, b3):
    o = product(k3[...], *split(h2))[0:FEATS]
    return o + wide(b3, o)


def add_weight_terms(acc, z, h1s, h2s, g1s, g2s, gos):
    ones = jnp.ones((16, z[0].shape[1]), BF16)
    acc[0:48, 0:HID] += across(z, g1s)
    acc[48:112, 0:HID] += across(h1s, g2s)
    acc[112:160, 0:HID] += across(gos, h2s)
    acc[160:176, 0:HID] += ones_rows(ones, g2s)
    acc[176:192, 0:48] += ones_rows(ones, gos)


def ones_rows(ones, g):
    dims = (((1,), (1,)), ((), ()))
    dot = lambda q: lax.dot_general(ones, q, dims, preferred_element_type=F32)
    return dot(g[0]) + dot(g[1])


def own_closure_kernel(own, *refs):
    raw, (out, h1_out, h2_out, k1, k2, k3, q1, q2, q3, b2, b3) = refs[:6], refs[6:17]
    w_in, w_mid, w_out, b_in, b_mid, b_out = refs[17:23]
    buffer, spare, stacked, sems = refs[23:]
    copies = [pltpu.make_async_copy(a, b, sems.at[i]) for i, (a, b) in enumerate(zip(raw, refs[17:23]))]
    for copy in copies:
        copy.start()
    for copy in copies:
        copy.wait()
    buffer[...] = jnp.zeros(buffer.shape, F32)
    by_tile(buffer, w_in, slice(0, HID))
    buffer[40:41, 0:HID] = b_in[...]
    stack(q1, buffer[0:48, 0:HID], stacked)
    spare[...] = buffer[...].T
    stack(k1, spare[0:HID, 0:48], stacked)
    buffer[0:HID, 0:HID] = w_mid[...]
    buffer[HID : HID + 1, 0:HID] = b_mid[...]
    stack(q2, buffer[0:HID, 0:HID], stacked)
    spare[...] = buffer[...].T
    stack(k2, spare[0:HID, 0:HID], stacked)
    b2[...] = jnp.broadcast_to(spare[0:HID, HID : HID + 1], (HID, COLS))
    buffer[...] = jnp.zeros(buffer.shape, F32)
    buffer[0:HID, 0:FEATS] = w_out[...]
    buffer[HID : HID + 1, 0:FEATS] = b_out[...]
    spare[...] = buffer[...].T
    buffer[...] = jnp.zeros(buffer.shape, F32)
    by_tile(buffer, spare, slice(0, COLS))
    stack(k3, buffer[0:48, 0:HID], stacked)
    b3[...] = jnp.broadcast_to(buffer[0:FEATS, HID : HID + 1], (FEATS, COLS))
    spare[...] = buffer[...].T
    stack(q3, spare[0:HID, 0:48], stacked)

    for r in range(0, ROWS, 8):
        z = split(to_48(jnp.concatenate([own[r + n, 0:FEATS, :] for n in range(8)], axis=1), 1.0))
        h1, h1s, h2 = hidden_layers(z, k1, k2, b2)
        o = last_layer(h2, k3, b3)
        for n in range(8):
            at = slice(n * COLS, (n + 1) * COLS)
            out[r + n] = o[:, at]
            h1_out[r + n] = h1[:, at]
            h2_out[r + n] = h2[:, at]


class Row:
    def __init__(self, width):
        sub = sub_index(width)
        group = sub % 4
        self.sub = sub
        self.is_t = group == 0
        self.is_s = group == 1
        self.is_u = group == 2
        self.is_v = group == 3
        self.low = sub >= 4
        self.k4 = jnp.where(group < 2, DIFFUSIVITY, VISCOSITY).astype(F32)


def put_state(k, ref, row, tiles):
    for t in range(5):
        ref[row, 8 * t : 8 * t + 8, :] = tiles[t]
    press = 0.4 * tiles[1] - 0.1 * tiles[0]
    for by in (1, 2, 4):
        press = press + jnp.where(k.sub >= by, pltpu.roll(press, by, 0), 0.0)
    ref[row, 40:48, :] = press
    mixed = tiles[4]
    over = lambda values, n: jnp.broadcast_to(values[n : n + 1, :], values.shape)
    deep_8 = over(press, 7) + (0.4 * over(mixed, 1) - 0.1 * over(mixed, 0))
    deep_9 = deep_8 + (0.4 * over(mixed, 5) - 0.1 * over(mixed, 4))
    ref[row, 48:56, :] = jnp.where(k.low, deep_9, deep_8)


def deep_pair(k, ref, row, upper, lower):
    return jnp.where(k.low, ref[row, lower : lower + 1, :], ref[row, upper : upper + 1, :])


def deep_u(k, ref, row):
    return deep_pair(k, ref, row, 34, 38)


def deep_v(k, ref, row):
    return deep_pair(k, ref, row, 35, 39)


def east_of(q):
    return pltpu.roll(q, q.shape[1] - 1, 1)


def west_of(q):
    return pltpu.roll(q, 1, 1)


def gain_of(k, t):
    return k.k4 if t == 4 else (DIFFUSIVITY if t < 2 else VISCOSITY)


def tendency_row(k, ref, row, c, f):
    half = 0.5 * c
    c2 = c * c
    u, v = tile(ref, row, 2), tile(ref, row, 3)
    u4, v4 = deep_u(k, ref, row), deep_v(k, ref, row)
    change = []
    for t in range(5):
        gain = gain_of(k, t)
        if t in (0, 2, 4):
            au, av = (half * u4, 0.5 * v4) if t == 4 else (half * u, 0.5 * v)
            along = gain * c2
            at_e, at_w, at_n, at_s = along - au, along + au, gain - av, gain + av
        q = tile(ref, row, t)
        east, west = at_e * east_of(q), at_w * west_of(q)
        north, south = at_n * tile(ref, row + 1, t), at_s * tile(ref, row - 1, t)
        change.append((east + west) + (north + south) - (gain * (2.0 * c2 + 2.0)) * q)
    p = tile(ref, row, 5)
    change[2] = change[2] + (f * v - half * (east_of(p) - west_of(p)))
    change[3] = change[3] - (f * u + 0.5 * (tile(ref, row + 1, 5) - tile(ref, row - 1, 5)))
    p4 = tile(ref, row, 6)
    fx = f * v4 - half * (east_of(p4) - west_of(p4))
    fy = f * u4 + 0.5 * (tile(ref, row + 1, 6) - tile(ref, row - 1, 6))
    change[4] = change[4] + jnp.where(k.is_u, fx, jnp.where(k.is_v, -fy, 0.0))
    return change


def adjoint_row(k, ref, aref, row, c, f):
    half = 0.5 * c
    c2 = c * c
    u4 = deep_u(k, ref, row)
    qe = [east_of(tile(ref, row, t)) for t in range(5)]
    qw = [west_of(tile(ref, row, t)) for t in range(5)]
    out = []
    to_u = to_v = None
    for t in range(5):
        a = tile(aref, row, t)
        ae, aw = east_of(a), west_of(a)
        an, as_ = tile(aref, row + 1, t), tile(aref, row - 1, t)
        gain = gain_of(k, t)
        if t == 0:
            ue, uw = half * qe[2], half * qw[2]
            vn, vs = 0.5 * tile(ref, row + 1, 3), 0.5 * tile(ref, row - 1, 3)
        if t == 4:
            ue, uw = half * east_of(u4), half * west_of(u4)
            vn, vs = 0.5 * deep_v(k, ref, row + 1), 0.5 * deep_v(k, ref, row - 1)
        if t in (0, 2, 4):
            along = gain * c2
            at_e, at_w, at_n, at_s = along + ue, along - uw, gain + vn, gain - vs
        out.append(
            (at_e * ae + at_w * aw) + (at_n * an + at_s * as_) - (gain * (2.0 * c2 + 2.0)) * a
        )
        px = a * (qe[t] - qw[t])
        py = a * (tile(ref, row + 1, t) - tile(ref, row - 1, t))
        if t < 4:
            to_u = px if to_u is None else to_u + px
            to_v = py if to_v is None else to_v + py
        if t == 2:
            a2, bx = a, half * (ae - aw)
        if t == 3:
            a3, by = a, 0.5 * (an - as_)
        if t == 4:
            a4 = a
            deep_bx, deep_by = half * (ae - aw), 0.5 * (an - as_)
            px4, py4 = px * half, py * 0.5
    out[2] = out[2] - half * to_u - f * a3
    out[3] = out[3] - 0.5 * to_v + f * a2
    sx = px4 + pltpu.roll(px4, 7, 0)
    sx = sx + pltpu.roll(sx, 2, 0)
    sy = py4 + pltpu.roll(py4, 1, 0)
    sy = sy + pltpu.roll(sy, 2, 0)
    at_u = -sx - f * pltpu.roll(a4, 7, 0)
    at_v = f * pltpu.roll(a4, 1, 0) - sy
    deep = jnp.where(k.is_t, pltpu.roll(deep_bx, 6, 0) + pltpu.roll(deep_by, 5, 0), 0.0)
    deep = deep + jnp.where(k.low, 0.0, pltpu.roll(deep, 4, 0))
    press = bx + by
    for shift in (1, 2, 4):
        press = press + jnp.where(k.sub < 8 - shift, pltpu.roll(press, 8 - shift, 0), 0.0)
    press = press + deep[0:1, :]
    out[0] = out[0] - 0.1 * press
    out[1] = out[1] + 0.4 * press
    out[4] = out[4] + jnp.where(
        k.is_t,
        -0.1 * deep,
        jnp.where(k.is_s, 0.4 * pltpu.roll(deep, 1, 0), jnp.where(k.is_u, at_u, at_v)),
    )
    return out


def for_span(low, high, up, body):
    turns = lax.div(high - low + TURN - 1, TURN)
    first = jnp.where(up == 1, low, high - TURN * turns)

    def turn(i, _):
        stores = [body(first + TURN * i + j) for j in range(TURN)]
        for store in stores:
            store()
        return 0

    lax.fori_loop(0, turns, turn, 0)


def for_rows(scal, reach, body):
    for_span(PAD - reach * scal[2], PAD + ROWS + reach * scal[3], scal[3], body)


def for_inner(scal, inset, body):
    for_span(PAD + inset * scal[2], PAD + ROWS - inset * scal[3], scal[3], body)


def for_outer(sides, scal, inset, reach, body):
    if sides == ["swap"]:
        low = jnp.where(scal[3] == 1, PAD + ROWS - inset, PAD - reach)
        for_span(low, low + reach + inset, scal[3], body)
    else:
        for_span(PAD - reach * scal[2], PAD + inset * scal[2], 0, body)
        for_span(PAD + ROWS - inset * scal[3], PAD + ROWS + reach * scal[3], 1, body)


def mask_tile(ref, row, t):
    return tile(ref, row, 1 if t == 4 else 0)


def put_tiles(ref, row, tiles):
    for t in range(5):
        ref[row, 8 * t : 8 * t + 8, :] = tiles[t]


def adjoint_third(k, scal, cs, fs, reach, state, masks, abuf, top, hold, bbuf):
    def body(r):
        d = adjoint_row(k, state, abuf, r, cs[r], fs[r])
        ts = [(2.0 / 3.0) * tile(top, r, t) + d[t] for t in range(5)]
        masked = [0.0625 * mask_tile(masks, r, t) * ts[t] for t in range(5)]
        return lambda: (put_tiles(hold, r, ts), put_tiles(bbuf, r, masked))

    for_rows(scal, reach, body)


def adjoint_second(k, scal, cs, fs, reach, state, masks, bbuf, top, hold, left, abuf):
    def body(r):
        d = adjoint_row(k, state, bbuf, r, cs[r], fs[r])
        ts = [tile(hold, r, t) for t in range(5)]
        tf = [0.25 * ts[t] + d[t] for t in range(5)]
        new = [(1.0 / 3.0) * tile(top, r, t) + 0.75 * ts[t] + tf[t] for t in range(5)]
        masked = [0.25 * mask_tile(masks, r, t) * tf[t] for t in range(5)]
        return lambda: (put_tiles(left, r, new), put_tiles(abuf, r, masked))

    for_rows(scal, reach, body)


def adjoint_first(k, scal, cs, fs, reach, state, abuf, left, store):
    def body(r):
        d = adjoint_row(k, state, abuf, r, cs[r], fs[r])
        return store(r, [tile(left, r, t) + d[t] for t in range(5)])

    for_rows(scal, reach, body)


def edges(reach):
    lane = lax.broadcasted_iota(jnp.int32, (8, COLS), 1)
    return lane < reach, lane >= COLS - reach


def wide_pack(ref, base):
    parts = []
    for t in range(5):
        rows = [ref[base + s, 8 * t : 8 * t + 8, COLS:WIDE] for s in range(8)]
        parts.append(slot_pack(rows, lambda s: 8 + SLOT * s, SLOT))
    return jnp.concatenate(parts, axis=0)

def wide_unpack(ref, base, values):
    for s in range(8):
        ref[base + s, 0:FEATS, COLS:WIDE] = pltpu.roll(values, -(8 + SLOT * s) % COLS, 1)


def section_1(k, cs, fs, masks, src, dst):
    def body(r):
        d = tendency_row(k, src, r, cs[r], fs[r])
        new = [tile(src, r, t) + 0.25 * mask_tile(masks, r, t) * d[t] for t in range(5)]
        return lambda: put_state(k, dst, r, new)

    return body


def section_2(k, cs, fs, masks, src, mid, dst):
    def body(r):
        d = tendency_row(k, mid, r, cs[r], fs[r])
        new = [
            0.75 * tile(src, r, t) + 0.25 * tile(mid, r, t) + 0.0625 * mask_tile(masks, r, t) * d[t]
            for t in range(5)
        ]
        return lambda: put_state(k, dst, r, new)

    return body


def section_3(k, cs, fs, masks, fluxes, mean, src, mid, net, r):
    d = tendency_row(k, mid, r, cs[r], fs[r])
    new = []
    for t in range(5):
        m = mask_tile(masks, r, t)
        o = tile(net, r, t)
        if t == 1:
            force = 2.0 * (mean - fluxes[r, 2:3, :])
            o = o + jnp.where(k.sub == 0, force, 0.0)
        new.append(
            (1.0 / 3.0) * tile(src, r, t) + (2.0 / 3.0) * tile(mid, r, t)
            + m * ((1.0 / 6.0) * d[t] + 0.25 * o)
        )
    return new


def zero_walls(ref):
    for row in (PAD - 1, PAD + ROWS):
        ref[row] = jnp.zeros(ref.shape[1:], F32)


class Block:
    def __init__(self, k, s0, masks, fluxes):
        self.k, self.s0, self.masks, self.fluxes = k, s0, masks, fluxes
        self.near_e, self.near_w = edges(REACH)

    def put(self, row, core, from_e, from_w):
        def both(t):
            halo = jnp.where(self.near_e, from_e(t), jnp.where(self.near_w, from_w(t), 0.0))
            return jnp.concatenate([core(t), halo], axis=1)

        put_state(self.k, self.s0, row, [both(t) for t in range(5)])
        self.masks[row, 0:8, :] = both(5)
        last = both(6)
        self.masks[row, 8:16, :] = jnp.where(self.k.low, last[1:2, :], last[0:1, :])
        self.fluxes[row] = last


def assemble_own_kernel(scal, cs, fs, own, own_m, east, west, k1, k2, k3, b2, b3, s0, masks, fluxes, net):
    k = Row(WIDE)
    zero_walls(s0)
    block = Block(k, s0, masks, fluxes)
    for r in range(ROWS):
        at = (r // 8) * PACK
        turn = SLOT * (r % 8)
        block.put(
            PAD + r,
            lambda t: own[r, 8 * t : 8 * t + 8, :],
            lambda t: pltpu.roll(west[at + 8 * t : at + 8 * t + 8, :], -turn % COLS, 1),
            lambda t: pltpu.roll(east[at + 8 * t : at + 8 * t + 8, :], -(turn + SLOT) % COLS, 1),
        )
        net[PAD + r, :, 0:COLS] = own_m[r]
    columns = jnp.concatenate([wide_pack(s0, PAD), wide_pack(s0, PAD + 8)], axis=1)
    o = closure_of(columns, k1, k2, k3, b2, b3)
    for g in range(2):
        wide_unpack(net, PAD + 8 * g, o[:, g * COLS : (g + 1) * COLS])


def closure_of(columns, k1, k2, k3, b2, b3):
    _, _, h2 = hidden_layers(split(to_48(columns, 1.0)), k1, k2, b2)
    return last_layer(h2, k3, b3)


def first_own_kernel(scal, cs, fs, s0, masks, s1):
    zero_walls(s1)
    for_inner(scal, 1, section_1(Row(WIDE), cs, fs, masks, s0, s1))


def second_own_kernel(scal, cs, fs, s0, s1, masks, s2):
    for_inner(scal, 2, section_2(Row(WIDE), cs, fs, masks, s0, s1, s2))


def halo_kernel(sides, scal, cs, fs, own_s0, own_s1, own_s2, own_masks, own_fluxes, own_net, *rest):
    n = len(sides)
    side_refs = [rest[2 * i : 2 * i + 2] for i in range(n)]
    net_refs, (s0, s1, s2, masks, fluxes, net) = rest[2 * n : 2 * n + 5], rest[2 * n + 5 :]
    k = Row(WIDE)
    for r in range(PAD, PAD + ROWS):
        for src, dst in (
            (own_s0, s0), (own_s1, s1), (own_s2, s2), (own_masks, masks), (own_fluxes, fluxes), (own_net, net)
        ):
            dst[r] = src[r]
    for ref in (s0, s1, s2):
        zero_walls(ref)
    block = Block(k, s0, masks, fluxes)
    firsts = []
    for side, (lat, corner) in zip(sides, side_refs):
        base = {"swap": scal[4], "north": PAD - REACH, "south": PAD + ROWS}[side]
        for r in range(REACH):
            block.put(
                base + r,
                lambda t: lat[PACK * r + 8 * t : PACK * r + 8 * t + 8, :],
                lambda t: pltpu.roll(corner[PACK + 40 + 8 * t : PACK + 48 + 8 * t, :], -REACH * r % COLS, 1),
                lambda t: pltpu.roll(corner[8 * t : 8 * t + 8, :], -REACH * (r + 1) % COLS, 1),
            )
        near = {"swap": jnp.where(scal[2] == 1, PAD - 8, PAD + ROWS), "north": PAD - 8, "south": PAD + ROWS}
        firsts.append(near[side])
    columns = []
    for first in firsts:
        columns += [s0[first + i, 0:FEATS, 0:COLS] for i in range(8)] + [wide_pack(s0, first)]
    o = closure_of(jnp.concatenate(columns, axis=1), *net_refs)
    for g, first in enumerate(firsts):
        for i in range(8):
            at = (9 * g + i) * COLS
            net[first + i, :, 0:COLS] = o[:, at : at + COLS]
        at = (9 * g + 8) * COLS
        wide_unpack(net, first, o[:, at : at + COLS])
    for_outer(sides, scal, 1, 10, section_1(k, cs, fs, masks, s0, s1))
    for_outer(sides, scal, 2, 9, section_2(k, cs, fs, masks, s0, s1, s2))


def last_section_kernel(scal, cs, fs, sums, s3, t2, masks, fluxes, outs, final):
    k = Row(WIDE)
    mean = sums[0:1, 0:1] / sums[1:2, 0:1]

    def last(r):
        new = section_3(k, cs, fs, masks, fluxes, mean, s3, t2, outs, r)
        return lambda: put_result(final, r - PAD, [x[:, 0:COLS] for x in new])

    for_rows(scal, 0, last)


def late_kernel(
    sides, scal, cs, fs, sums, own, cown, own_h1, own_h2, s0, s2, masks, fluxes, outs_in, east, west, *rest
):
    n = len(sides)
    side_refs = [rest[2 * i : 2 * i + 2] for i in range(n)]
    (k1, k2, k3, q1, q2, q3, b2, b3), rest = rest[2 * n : 2 * n + 8], rest[2 * n + 8 :]
    grads, s4, abuf, from_closure, s3, t2, outs, t1, cot, gz, bbuf, hold, left, acc = rest
    k = Row(WIDE)
    has_south = scal[2]
    lo = lambda h: PAD - h * has_south
    for ref in (s3, t1, t2, abuf, bbuf):
        zero_walls(ref)
    mean = sums[0:1, 0:1] / sums[1:2, 0:1]

    cnear_e, cnear_w = edges(CREACH)
    for r in range(ROWS):
        for t in range(5):
            rows = slice(2 * PACK + 8 * t, 2 * PACK + 8 * t + 8)
            from_e = pltpu.roll(west[rows, :], -8 * r % COLS, 1)
            from_w = pltpu.roll(east[rows, :], -8 * (r + 1) % COLS, 1)
            side = jnp.where(cnear_e, from_e, jnp.where(cnear_w, from_w, 0.0))
            cot[PAD + r, 8 * t : 8 * t + 8, :] = jnp.concatenate(
                [cown[r, 8 * t : 8 * t + 8, :], side], axis=1
            )
    for side, (lat, corner) in zip(sides, side_refs):
        cbase = {"swap": scal[5], "north": PAD - CREACH, "south": PAD + ROWS}[side]
        crow = {"swap": scal[6], "north": ROWS - CREACH, "south": 0}[side]
        for r in range(CREACH):
            turn = lax.rem(2 * COLS - 8 * (crow + r), COLS)
            turn_w = lax.rem(2 * COLS - 8 * (crow + r + 1), COLS)
            for t in range(5):
                wrows = slice(PACK + 8 * t, PACK + 8 * t + 8)
                erows = slice(2 * PACK + 40 + 8 * t, 2 * PACK + 48 + 8 * t)
                from_e = pltpu.roll(corner[erows, :], turn, 1)
                from_w = pltpu.roll(corner[wrows, :], turn_w, 1)
                part = jnp.where(cnear_e, from_e, jnp.where(cnear_w, from_w, 0.0))
                cot[cbase + r, 8 * t : 8 * t + 8, :] = jnp.concatenate(
                    [lat[LAT_X + FEATS * r + 8 * t : LAT_X + FEATS * r + 8 * t + 8, :], part], axis=1
                )


    def step_1_end(r):
        put_state(k, s3, r, section_3(s0, s2, r))

    def step_1_end(r):
        new = section_3(k, cs, fs, masks, fluxes, mean, s0, s2, outs_in, r)
        return lambda: put_state(k, s3, r, new)

    for_rows(scal, 8, step_1_end)

    acc[...] = jnp.zeros(acc.shape, F32)

    def closure_adjoint(z, h1, h1s, h2, go, with_weights):
        gos = split(to_48(go))
        g2 = product(q3[...], *gos) * (1.0 - h2 * h2)
        g2s = split(g2)
        g1 = product(q2[...], *g2s) * (1.0 - h1 * h1)
        g1s = split(g1)
        if with_weights:
            add_weight_terms(acc, z, h1s, split(h2), g1s, g2s, gos)
        return product(q1[...], *g1s)[0:FEATS]

    def both_ways(columns, go, with_weights):
        z = split(to_48(columns, 1.0))
        h1, h1s, h2 = hidden_layers(z, k1, k2, b2)
        o = last_layer(h2, k3, b3) if with_weights else None
        return o, closure_adjoint(z, h1, h1s, h2, go, with_weights)

    def masked_core(ref, r):
        m0, m4 = masks[r, 0:8, 0:COLS], masks[r, 8:16, 0:COLS]
        parts = [
            0.25 * (m4 if t == 4 else m0) * ref[r, 8 * t : 8 * t + 8, 0:COLS] for t in range(5)
        ]
        return jnp.concatenate(parts, axis=0)

    def mask_cot(r):
        seen = [mask_tile(masks, r, t) * tile(cot, r, t) for t in range(5)]
        quarter, sixth = [0.25 * x for x in seen], [(1.0 / 6.0) * x for x in seen]
        return lambda: (put_tiles(bbuf, r, quarter), put_tiles(abuf, r, sixth))

    for_rows(scal, 6, mask_cot)

    for first in range(PAD, PAD + ROWS, 8):
        z = jnp.concatenate([s3[first + i, 0:FEATS, 0:COLS] for i in range(8)], axis=1)
        go = jnp.concatenate([bbuf[first + i, 0:FEATS, 0:COLS] for i in range(8)], axis=1)
        o, back = both_ways(z, go, True)
        for i in range(8):
            at = slice(i * COLS, (i + 1) * COLS)
            outs[first + i, :, 0:COLS] = o[:, at]
            gz[first + i, :, 0:COLS] = back[:, at]

    first = lo(4)
    if sides == ["swap"]:
        rows = [jnp.where(has_south == 1, PAD - 4, PAD + ROWS) + i for i in range(4)]
    else:
        rows = [PAD - 4 + i for i in range(4)] + [PAD + ROWS + i for i in range(4)]
    beyond = lambda ref: jnp.concatenate(
        [ref[r, 0:FEATS, 0:COLS] for r in rows] + [wide_pack(ref, first + 8 * g) for g in range(3)], axis=1
    )
    _, back = both_ways(beyond(s3), beyond(bbuf), False)
    for i, r in enumerate(rows):
        gz[r, :, 0:COLS] = back[:, i * COLS : (i + 1) * COLS]
    for g in range(3):
        at = (len(rows) + g) * COLS
        wide_unpack(gz, first + 8 * g, back[:, at : at + COLS])

    for_rows(scal, 7, section_1(k, cs, fs, masks, s3, t1))
    for_rows(scal, 6, section_2(k, cs, fs, masks, s3, t1, t2))

    def store(r, tiles):
        new = [tiles[t] + tile(gz, r, t) for t in range(5)]
        return lambda: put_tiles(s4, r, new)

    adjoint_third(k, scal, cs, fs, 5, t2, masks, abuf, cot, hold, bbuf)
    adjoint_second(k, scal, cs, fs, 4, t1, masks, bbuf, cot, hold, left, abuf)
    adjoint_first(k, scal, cs, fs, 3, s3, abuf, left, store)

    for r in range(0, ROWS, 8):
        side = lambda read: jnp.concatenate([read(r + j) for j in range(8)], axis=1)
        z = split(to_48(side(lambda j: own[j, 0:FEATS, :]), 1.0))
        h1 = side(lambda j: own_h1[j])
        h2 = side(lambda j: own_h2[j])
        go = side(lambda j: masked_core(s4, PAD + j))
        back = closure_adjoint(z, h1, split(h1), h2, go, True)
        for j in range(8):
            from_closure[r + j] = back[:, j * COLS : (j + 1) * COLS]

    zero_walls(abuf)

    def mask_top(r):
        new = [(1.0 / 6.0) * mask_tile(masks, r, t) * tile(s4, r, t) for t in range(5)]
        return lambda: put_tiles(abuf, r, new)

    for_rows(scal, 3, mask_top)
    grads[...] = jnp.zeros(grads.shape, F32)
    grads[0:40, 0:HID] = acc[0:40, 0:HID]
    grads[0:40, HID : 2 * HID] = acc[112:152, 0:HID]
    grads[40:72, 0:HID] = acc[48:80, 0:HID]
    grads[40:72, HID : 2 * HID] = acc[80:112, 0:HID]
    grads[72:73, 0:HID] = acc[40:41, 0:HID]
    grads[72:73, HID : 2 * HID] = acc[160:161, 0:HID]
    grads[73:74, 0:HID] = acc[176:177, 0:HID]


def put_result(ref, row, tiles):
    for t in range(4):
        ref[pl.ds(t * 10 * ROWS + row, 8, stride=ROWS), :] = tiles[t]
    ref[pl.ds(8 * ROWS + row, 4, stride=10 * ROWS), :] = tiles[4][0:4, :]
    ref[pl.ds(9 * ROWS + row, 4, stride=10 * ROWS), :] = tiles[4][4:8, :]


def back_third_kernel(scal, cs, fs, state, masks, abuf, top, hold, bbuf):
    zero_walls(bbuf)
    adjoint_third(Row(WIDE), scal, cs, fs, 2, state, masks, abuf, top, hold, bbuf)


def back_second_kernel(scal, cs, fs, state, masks, bbuf, top, hold, left, abuf):
    zero_walls(abuf)
    adjoint_second(Row(WIDE), scal, cs, fs, 1, state, masks, bbuf, top, hold, left, abuf)


def back_first_kernel(scal, cs, fs, state, masks, abuf, left, from_closure, grad):
    def store(r, tiles):
        done = []
        for t in range(5):
            m = masks[r, 8:16, 0:COLS] if t == 4 else masks[r, 0:8, 0:COLS]
            done.append(m * (tiles[t][:, 0:COLS] + from_closure[r - PAD, 8 * t : 8 * t + 8, :]))
        return lambda: put_result(grad, r - PAD, done)

    adjoint_first(Row(WIDE), scal, cs, fs, 0, state, abuf, left, store)


def unpack_kernel(scale, packed, win, bin_, wmid, bmid, wout, bout):
    for ref, lanes in ((win, slice(0, HID)), (wout, slice(HID, 2 * HID))):
        for t in range(4):
            ref[10 * t : 10 * t + 8, :] = packed[8 * t : 8 * t + 8, lanes] * scale
            ref[10 * t + 8 : 10 * t + 9, :] = packed[32 + t : 33 + t, lanes] * scale
            ref[10 * t + 9 : 10 * t + 10, :] = packed[36 + t : 37 + t, lanes] * scale
    wmid[0:32, :] = packed[40:72, 0:HID] * scale
    wmid[32:64, :] = packed[40:72, HID : 2 * HID] * scale
    bin_[...] = packed[72:73, 0:HID] * scale
    bmid[...] = packed[72:73, HID : 2 * HID] * scale
    for t in range(4):
        bout[:, 10 * t : 10 * t + 8] = packed[73:74, 8 * t : 8 * t + 8] * scale
        bout[:, 10 * t + 8 : 10 * t + 9] = packed[73:74, 32 + t : 33 + t] * scale
        bout[:, 10 * t + 9 : 10 * t + 10] = packed[73:74, 36 + t : 37 + t] * scale


def far_first(axes):
    return [(axis, n, 1 << bit) for axis, n in axes for bit in reversed(range(n.bit_length() - 1))]


def pair_rounds(x, rounds, beside):
    results = []
    for i in range(max(len(rounds), len(beside))):
        if i < len(rounds):
            axis, n, step = rounds[i]
            got = lax.ppermute(x, axis, [(j, j ^ step) for j in range(n)])
        if i < len(beside):
            results.append(beside[i](results))
            if i < len(rounds):
                got, results[-1] = lax.optimization_barrier((got, results[-1]))
        if i < len(rounds):
            x = x + got
    return x, results


def latitude_terms(row_index, row_count):
    latitude = LAT_LIMIT * (2.0 * (jnp.clip(row_index, 0.0, row_count - 1.0) + 0.5) / row_count - 1.0)
    return 1.0 / jnp.cos(latitude), CORIOLIS * jnp.sin(latitude)


def on_device(
    initial_state, land_mask, surface_flux, weight_in, bias_in, weight_mid, bias_mid, weight_out, bias_out, cotangent
):
    lat_n, lon_n = lax.axis_size("lat"), lax.axis_size("lon")
    lat_i = lax.axis_index("lat")
    lat_total, lon_total = ROWS * lat_n, COLS * lon_n
    sides = ["swap"] if lat_n == 2 else ["north", "south"]
    is_low = (lat_i == 0).astype(jnp.int32)
    has_south = (lat_i > 0).astype(jnp.int32)
    has_north = (lat_i < lat_n - 1).astype(jnp.int32)
    scal = jnp.stack(
        [
            is_low * (ROWS - REACH),
            is_low * (ROWS - CREACH),
            has_south,
            has_north,
            jnp.where(is_low == 1, PAD + ROWS, PAD - REACH),
            jnp.where(is_low == 1, PAD + ROWS, PAD - CREACH),
            jnp.where(is_low == 1, 0, ROWS - CREACH),
        ]
    ).astype(jnp.int32)
    rows = (lat_i * ROWS - PAD + jnp.arange(EXT, dtype=jnp.int32)).astype(F32)
    cs, fs = latitude_terms(rows, lat_total)

    hbm = pl.BlockSpec(memory_space=pltpu.HBM)
    packed = pl.pallas_call(
        lambda *refs: pack_kernel(sides, *refs),
        out_shape=[
            sds(ROWS, PACK, COLS), sds(ROWS, FEATS, COLS), sds(STRIP, COLS), sds(STRIP, COLS), sds(8, COLS),
        ]
        + [sds(LAT, COLS)] * len(sides),
        in_specs=[hbm] * 4,
        out_specs=[VMEM] * (5 + len(sides)),
        scratch_shapes=[
            pltpu.VMEM((40 * ROWS, COLS), F32), pltpu.VMEM((10 * ROWS, COLS), jnp.int32),
            pltpu.VMEM((ROWS, COLS), F32), pltpu.VMEM((40 * ROWS, COLS), F32), pltpu.SemaphoreType.DMA((4,)),
        ],
        compiler_params=params(56),
        cost_estimate=pl.CostEstimate(flops=10**9, bytes_accessed=3 * 10**6, transcendentals=0),
        name="pack_halos",
    )(
        initial_state.reshape(40 * ROWS, COLS),
        land_mask.reshape(10 * ROWS, COLS),
        surface_flux,
        cotangent.reshape(40 * ROWS, COLS),
    )
    own, cown, east_pay, west_pay, sums = packed[:5]

    def lat_pairs(side):
        if side == "swap":
            return [(0, 1), (1, 0)]
        if side == "north":
            return [(i, i + 1) for i in range(lat_n - 1)]
        return [(i + 1, i) for i in range(lat_n - 1)]

    east_ring = [(i, (i + 1) % lon_n) for i in range(lon_n)]
    west_ring = [((i + 1) % lon_n, i) for i in range(lon_n)]
    from_west = lax.ppermute(east_pay, "lon", east_ring)
    from_east = lax.ppermute(west_pay, "lon", west_ring)
    row = lambda b: b.reshape(1, -1)
    raw = (weight_in, weight_mid, weight_out, row(bias_in), row(bias_mid), row(bias_out))
    half = lambda *shape: jax.ShapeDtypeStruct(shape, BF16)
    own_closure = pl.pallas_call(
        own_closure_kernel,
        out_shape=[
            sds(ROWS, FEATS, COLS), sds(ROWS, HID, COLS), sds(ROWS, HID, COLS),
            half(HID, 144), half(HID, 192), half(48, 192), half(48, 192), half(HID, 192), half(HID, 144),
            sds(HID, COLS), sds(FEATS, COLS),
        ],
        in_specs=[VMEM] + [hbm] * 6,
        out_specs=[VMEM] * 11,
        scratch_shapes=[pltpu.VMEM(w.shape, F32) for w in raw]
        + [pltpu.VMEM((COLS, COLS), F32), pltpu.VMEM((COLS, COLS), F32), pltpu.VMEM((HID, WIDE), F32)]
        + [pltpu.SemaphoreType.DMA((6,))],
        compiler_params=params(12),
        cost_estimate=pl.CostEstimate(flops=10**9, bytes_accessed=2 * 10**6, transcendentals=0),
        name="own_closure",
    )
    pack_corners = pl.pallas_call(
        lambda *refs: corner_kernel(sides, *refs),
        out_shape=[sds(CORNER + 8, COLS)] * len(sides),
        in_specs=[SMEM, VMEM, VMEM],
        out_specs=[VMEM] * len(sides),
        compiler_params=params(8),
        cost_estimate=pl.CostEstimate(flops=10**8, bytes_accessed=10**6, transcendentals=0),
        name="pack_corners",
    )
    lats = [lax.ppermute(pay, "lat", lat_pairs(side)) for side, pay in zip(sides, packed[5:])]
    geometry = (scal, cs, fs)
    state = sds(EXT, 56, WIDE)
    plain = sds(EXT, FEATS, WIDE)
    marks = sds(EXT, 16, WIDE)
    vmem = lambda shape: pltpu.VMEM(shape.shape, F32)

    def call(kernel, name, out_shape, scratch, args, flops, limit):
        single = not isinstance(out_shape, list)
        return pl.pallas_call(
            kernel,
            out_shape=out_shape,
            in_specs=[SMEM] * 3 + [VMEM] * len(args),
            out_specs=VMEM if single else [VMEM] * len(out_shape),
            scratch_shapes=scratch,
            compiler_params=params(limit),
            cost_estimate=pl.CostEstimate(flops=flops, bytes_accessed=10**7, transcendentals=0),
            name=name,
        )(*geometry, *args)


    def last_round(done):
        own_m, _, _, k1, k2, k3, _, _, _, b2, b3 = done[1]
        blocks = call(
            assemble_own_kernel, "assemble_own", [state, marks, sds(EXT, 8, WIDE), plain], [],
            [own, own_m, from_west, from_east, k1, k2, k3, b2, b3], 10**9, 8,
        )
        return blocks, pack_corners(scal, from_west, from_east)

    rounds = far_first((("lon", lon_n),))[::-1]
    row_total, results = pair_rounds(
        sums,
        rounds,
        [lambda done: sums, lambda done: own_closure(own, *raw)]
        + [lambda done: sums] * (len(rounds) - 3)
        + [last_round],
    )
    own_m, own_h1, own_h2, k1, k2, k3, q1, q2, q3, b2, b3 = results[1]
    net_weights = [k1, k2, k3, b2, b3]
    (s0, masks, fluxes, net), corner_pays = results[-1]
    corners = []
    for side, pay in zip(sides, corner_pays):
        pay = lax.dynamic_update_slice(pay, row_total, (CORNER, 0))
        corners.append(lax.ppermute(pay, "lat", lat_pairs(side)))
    s1 = call(first_own_kernel, "first_section_own", state, [], [s0, masks], 10**9, 8)
    s2 = call(second_own_kernel, "second_section_own", state, [], [s0, s1, masks], 10**9, 8)
    corners, s2 = lax.optimization_barrier((corners, s2))
    if sides == ["swap"]:
        total = row_total + corners[0][CORNER : CORNER + 8]
    else:
        total = lax.psum(row_total, "lat")
    received = [ref for pair in zip(lats, corners) for ref in pair]
    s0, s1, s2, masks, fluxes, net = call(
        lambda *refs: halo_kernel(sides, *refs), "halo_rows",
        [state, state, state, marks, sds(EXT, 8, WIDE), plain], [],
        [s0, s1, s2, masks, fluxes, net] + received + net_weights, 2 * 10**9, 8,
    )
    grads, top, abuf, from_closure, s3, t2, net_2 = call(
        lambda *refs: late_kernel(sides, *refs), "steps_and_adjoint",
        [sds(80, COLS), plain, plain, sds(ROWS, FEATS, COLS), state, state, plain],
        [vmem(state)] + [vmem(plain)] * 5 + [pltpu.VMEM((192, HID), F32)],
        [total, own, cown, own_h1, own_h2, s0, s2, masks, fluxes, net, from_west, from_east]
        + received + [k1, k2, k3, q1, q2, q3, b2, b3],
        4 * 10**9, 18,
    )
    beside = [
        lambda done: call(
            back_third_kernel, "adjoint_third_section", [plain, plain], [], [s2, masks, abuf, top], 10**9, 8
        ),
        lambda done: call(
            back_second_kernel, "adjoint_second_section", [plain, plain], [],
            [s1, masks, done[0][1], top, done[0][0]], 10**9, 8,
        ),
        lambda done: call(
            back_first_kernel, "adjoint_first_section", sds(40 * ROWS, COLS), [],
            [s0, masks, done[1][1], done[1][0], from_closure], 10**9, 8,
        ),
        lambda done: call(
            last_section_kernel, "last_section", sds(40 * ROWS, COLS), [],
            [total, s3, t2, masks, fluxes, net_2], 10**9, 8,
        ),
    ]
    by_lon, by_lat = far_first((("lon", lon_n),)), far_first((("lat", lat_n),))
    summed, results = pair_rounds(grads, by_lon[:-2] + by_lat + by_lon[-2:], beside)
    state_grad, final = results[2:]

    scale = 1.0 / math.sqrt(lat_total * lon_total)
    g_in, g_bin, g_mid, g_bmid, g_out, g_bout = pl.pallas_call(
        lambda *refs: unpack_kernel(scale, *refs),
        out_shape=[sds(40, HID), sds(1, HID), sds(HID, HID), sds(1, HID), sds(40, HID), sds(1, 40)],
        in_specs=[VMEM],
        out_specs=[VMEM] * 6,
        compiler_params=params(8),
        name="unpack_weight_grads",
    )(summed)
    shape = initial_state.shape
    return (
        final.reshape(shape),
        state_grad.reshape(shape),
        g_in,
        g_bin.reshape(-1),
        g_mid,
        g_bmid.reshape(-1),
        g_out.T,
        g_bout.reshape(-1),
    )


def solution(mesh):
    split_state = P(None, None, "lat", "lon")
    return jax.shard_map(
        on_device,
        mesh=mesh,
        in_specs=(split_state, P(None, "lat", "lon"), P("lat", "lon"), P(), P(), P(), P(), P(), P(), split_state),
        out_specs=(split_state, split_state, P(), P(), P(), P(), P(), P()),
        check_vma=False,
    )
```

```python
import math

import jax
import jax.numpy as jnp
from jax import lax
from jax.experimental import pallas as pl
from jax.experimental.pallas import tpu as pltpu
from jax.sharding import PartitionSpec as P

LAT_LIMIT = 1.2
CORIOLIS = 1.0
VISCOSITY = 0.15
DIFFUSIVITY = 0.1

ROWS = 16
COLS = 128
REACH = 11
CREACH = 6
PAD = 16
EXT = 48
TURN = 4
WIDE = 2 * COLS
FEATS = 40
HID = 64
PACK = 56
STRIP = 2 * PACK + 40
LAT_X = REACH * PACK
CORNER = 2 * PACK + 80
LAT = LAT_X + CREACH * FEATS
SLOT = 16
F32 = jnp.float32
BF16 = jnp.bfloat16
VMEM = pl.BlockSpec(memory_space=pltpu.VMEM)


def params(megabytes):
    return pltpu.CompilerParams(vmem_limit_bytes=megabytes * 1024 * 1024)


def sds(*shape):
    return jax.ShapeDtypeStruct(shape, F32)


def sub_index(width):
    return lax.broadcasted_iota(jnp.int32, (8, width), 0)


def tile(ref, row, number):
    return ref[row, 8 * number : 8 * number + 8, :]


def slot_pack(pieces, shift_of, width):
    lane = lax.broadcasted_iota(jnp.int32, (8, COLS), 1)
    packed = None
    for slot, piece in enumerate(pieces):
        turned = pltpu.roll(piece, shift_of(slot) % COLS, 1)
        if packed is None:
            packed = turned
        else:
            packed = jnp.where((lane >= slot * width) & (lane < (slot + 1) * width), turned, packed)
    return packed


def pack_kernel(sides, x_hbm, mask_hbm, flux_hbm, cot_hbm, *outs):
    x, mask, flux, cot, sems = outs[-5:]
    own, cown, east, west, sums = outs[:5]
    per_side = outs[5 : 5 + len(sides)]
    pairs = ((mask_hbm, mask), (x_hbm, x), (flux_hbm, flux), (cot_hbm, cot))
    copies = [pltpu.make_async_copy(a, b, sems.at[i]) for i, (a, b) in enumerate(pairs)]
    for copy in copies:
        copy.start()
    for copy in copies:
        copy.wait()
    top = mask[0:ROWS, :].astype(F32)
    total = jnp.sum(jnp.sum(top * flux[...], axis=1, keepdims=True), axis=0, keepdims=True)
    count = jnp.sum(jnp.sum(top, axis=1, keepdims=True), axis=0, keepdims=True)
    sums[...] = jnp.where(sub_index(COLS) == 0, total, jnp.where(sub_index(COLS) == 1, count, 0.0))
    for r in range(ROWS):
        first = mask[pl.ds(r, 8, stride=ROWS), :].astype(F32)
        m8 = mask[8 * ROWS + r : 8 * ROWS + r + 1, :].astype(F32)
        m9 = mask[9 * ROWS + r : 9 * ROWS + r + 1, :].astype(F32)
        for t in range(4):
            own[r, 8 * t : 8 * t + 8, :] = x[pl.ds(t * 10 * ROWS + r, 8, stride=ROWS), :] * first
            cown[r, 8 * t : 8 * t + 8, :] = cot[pl.ds(t * 10 * ROWS + r, 8, stride=ROWS), :]
        for level, m in ((8, m8), (9, m9)):
            at = 32 + 4 * (level - 8)
            own[r, at : at + 4, :] = x[pl.ds(level * ROWS + r, 4, stride=10 * ROWS), :] * m
            cown[r, at : at + 4, :] = cot[pl.ds(level * ROWS + r, 4, stride=10 * ROWS), :]
        own[r, 40:48, :] = first
        own[r, 48:49, :] = m8
        own[r, 49:50, :] = m9
        own[r, 50:51, :] = flux[r : r + 1, :]
        own[r, 51:PACK, :] = jnp.zeros((5, COLS), F32)
    for half in range(2):
        for t in range(7):
            rows = [own[8 * half + s, 8 * t : 8 * t + 8, :] for s in range(8)]
            at = half * PACK + 8 * t
            east[at : at + 8, :] = slot_pack(rows, lambda s: SLOT * (s + 1), SLOT)
            west[at : at + 8, :] = slot_pack(rows, lambda s: SLOT * s, SLOT)
    for t in range(5):
        rows = [cown[s, 8 * t : 8 * t + 8, :] for s in range(ROWS)]
        at = 2 * PACK + 8 * t
        east[at : at + 8, :] = slot_pack(rows, lambda s: 8 * (s + 1), 8)
        west[at : at + 8, :] = slot_pack(rows, lambda s: 8 * s, 8)
    southern = (lax.axis_index("lat") == 0).astype(jnp.int32)
    for side, lat in zip(sides, per_side):
        start = {"swap": southern * (ROWS - REACH), "north": ROWS - REACH, "south": 0}[side]
        cstart = {"swap": southern * (ROWS - CREACH), "north": ROWS - CREACH, "south": 0}[side]
        for n in range(REACH):
            lat[PACK * n : PACK * (n + 1), :] = own[start + n]
        for n in range(CREACH):
            lat[LAT_X + FEATS * n : LAT_X + FEATS * (n + 1), :] = cown[cstart + n]


def corner_kernel(sides, east, west, *outs):
    southern = (lax.axis_index("lat") == 0).astype(jnp.int32)
    for side, corner in zip(sides, outs):
        start = {"swap": southern * (ROWS - REACH), "north": ROWS - REACH, "south": 0}[side]
        for at, strip, near in ((0, east, 1), (PACK + 40, west, 0)):
            for t in range(7):
                rows = slice(at + 8 * t, at + 8 * t + 8)
                corner[rows, :] = shift_rows(strip, t, start, near)
            corner[at + PACK : at + PACK + 40, :] = strip[2 * PACK : 2 * PACK + 40, :]
        corner[CORNER : CORNER + 8, :] = jnp.zeros((8, COLS), F32)


def shift_rows(strip, t, start, near):
    lane = lax.broadcasted_iota(jnp.int32, (8, COLS), 1)
    halves = [strip[8 * t : 8 * t + 8, :], strip[PACK + 8 * t : PACK + 8 * t + 8, :]]
    if isinstance(start, int):
        out = jnp.zeros((8, COLS), F32)
        for n in range(REACH):
            r = start + n
            turn = REACH * n - (SLOT * (r % 8) + near * (SLOT - REACH))
            turned = pltpu.roll(halves[r // 8], turn % COLS, 1)
            out = jnp.where((lane >= REACH * n) & (lane < REACH * (n + 1)), turned, out)
        return out
    low = shift_rows(strip, t, 0, near)
    high = shift_rows(strip, t, ROWS - REACH, near)
    return jnp.where(start == 0, low, high)


def split(values):
    high = values.astype(BF16)
    return high, (values - high.astype(F32)).astype(BF16)


def stack(out, values, buffer):
    k = values.shape[1]
    rows = slice(0, values.shape[0])
    high, low = split(values)
    buffer[rows, 0:k] = high.astype(F32)
    buffer[rows, k : 2 * k] = high.astype(F32)
    buffer[rows, 2 * k : 3 * k] = low.astype(F32)
    out[...] = buffer[rows, 0 : 3 * k].astype(BF16)


def by_tile(dst, src, lanes):
    for t in range(4):
        dst[8 * t : 8 * t + 8, lanes] = src[10 * t : 10 * t + 8, lanes]
        dst[32 + t : 33 + t, lanes] = src[10 * t + 8 : 10 * t + 9, lanes]
        dst[36 + t : 37 + t, lanes] = src[10 * t + 9 : 10 * t + 10, lanes]


def product(weights, high, low):
    return jnp.dot(weights, jnp.concatenate([high, low, high], axis=0), preferred_element_type=F32)


def across(a, b):
    dims = (((1,), (1,)), ((), ()))
    dot = lambda p, q: lax.dot_general(p, q, dims, preferred_element_type=F32)
    return dot(a[0], b[0]) + dot(a[0], b[1]) + dot(a[1], b[0])


def to_48(columns, first=0.0):
    more = jnp.where(sub_index(columns.shape[1]) == 0, first, 0.0).astype(F32)
    return jnp.concatenate([columns, more], axis=0)


def wide(bias, values):
    return jnp.concatenate([bias[...]] * (values.shape[1] // COLS), axis=1)


def hidden_layers(z, k1, k2, b2):
    h1 = jnp.tanh(product(k1[...], *z))
    h1s = split(h1)
    h2 = product(k2[...], *h1s)
    return h1, h1s, jnp.tanh(h2 + wide(b2, h2))


def last_layer(h2, k3, b3):
    o = product(k3[...], *split(h2))[0:FEATS]
    return o + wide(b3, o)


def add_weight_terms(acc, z, h1s, h2s, g1s, g2s, gos):
    ones = jnp.ones((16, z[0].shape[1]), BF16)
    acc[0:48, 0:HID] += across(z, g1s)
    acc[48:112, 0:HID] += across(h1s, g2s)
    acc[112:160, 0:HID] += across(gos, h2s)
    acc[160:176, 0:HID] += ones_rows(ones, g2s)
    acc[176:192, 0:48] += ones_rows(ones, gos)


def ones_rows(ones, g):
    dims = (((1,), (1,)), ((), ()))
    dot = lambda q: lax.dot_general(ones, q, dims, preferred_element_type=F32)
    return dot(g[0]) + dot(g[1])


def own_closure_kernel(own, *refs):
    raw, (out, h1_out, h2_out, k1, k2, k3, q1, q2, q3, b2, b3) = refs[:6], refs[6:17]
    w_in, w_mid, w_out, b_in, b_mid, b_out = refs[17:23]
    buffer, spare, stacked, sems = refs[23:]
    copies = [pltpu.make_async_copy(a, b, sems.at[i]) for i, (a, b) in enumerate(zip(raw, refs[17:23]))]
    for copy in copies:
        copy.start()
    for copy in copies:
        copy.wait()
    buffer[...] = jnp.zeros(buffer.shape, F32)
    by_tile(buffer, w_in, slice(0, HID))
    buffer[40:41, 0:HID] = b_in[...]
    stack(q1, buffer[0:48, 0:HID], stacked)
    spare[...] = buffer[...].T
    stack(k1, spare[0:HID, 0:48], stacked)
    buffer[0:HID, 0:HID] = w_mid[...]
    buffer[HID : HID + 1, 0:HID] = b_mid[...]
    stack(q2, buffer[0:HID, 0:HID], stacked)
    spare[...] = buffer[...].T
    stack(k2, spare[0:HID, 0:HID], stacked)
    b2[...] = jnp.broadcast_to(spare[0:HID, HID : HID + 1], (HID, COLS))
    buffer[...] = jnp.zeros(buffer.shape, F32)
    buffer[0:HID, 0:FEATS] = w_out[...]
    buffer[HID : HID + 1, 0:FEATS] = b_out[...]
    spare[...] = buffer[...].T
    buffer[...] = jnp.zeros(buffer.shape, F32)
    by_tile(buffer, spare, slice(0, COLS))
    stack(k3, buffer[0:48, 0:HID], stacked)
    b3[...] = jnp.broadcast_to(buffer[0:FEATS, HID : HID + 1], (FEATS, COLS))
    spare[...] = buffer[...].T
    stack(q3, spare[0:HID, 0:48], stacked)

    for r in range(0, ROWS, 8):
        z = split(to_48(jnp.concatenate([own[r + n, 0:FEATS, :] for n in range(8)], axis=1), 1.0))
        h1, h1s, h2 = hidden_layers(z, k1, k2, b2)
        o = last_layer(h2, k3, b3)
        for n in range(8):
            at = slice(n * COLS, (n + 1) * COLS)
            out[r + n] = o[:, at]
            h1_out[r + n] = h1[:, at]
            h2_out[r + n] = h2[:, at]


class Row:
    def __init__(self, width):
        sub = sub_index(width)
        group = sub % 4
        self.sub = sub
        self.is_t = group == 0
        self.is_s = group == 1
        self.is_u = group == 2
        self.is_v = group == 3
        self.low = sub >= 4
        self.k4 = jnp.where(group < 2, DIFFUSIVITY, VISCOSITY).astype(F32)


def put_state(k, ref, row, tiles):
    for t in range(5):
        ref[row, 8 * t : 8 * t + 8, :] = tiles[t]
    press = 0.4 * tiles[1] - 0.1 * tiles[0]
    for by in (1, 2, 4):
        press = press + jnp.where(k.sub >= by, pltpu.roll(press, by, 0), 0.0)
    ref[row, 40:48, :] = press
    mixed = tiles[4]
    over = lambda values, n: jnp.broadcast_to(values[n : n + 1, :], values.shape)
    deep_8 = over(press, 7) + (0.4 * over(mixed, 1) - 0.1 * over(mixed, 0))
    deep_9 = deep_8 + (0.4 * over(mixed, 5) - 0.1 * over(mixed, 4))
    ref[row, 48:56, :] = jnp.where(k.low, deep_9, deep_8)


def deep_pair(k, ref, row, upper, lower):
    return jnp.where(k.low, ref[row, lower : lower + 1, :], ref[row, upper : upper + 1, :])


def deep_u(k, ref, row):
    return deep_pair(k, ref, row, 34, 38)


def deep_v(k, ref, row):
    return deep_pair(k, ref, row, 35, 39)


def east_of(q):
    return pltpu.roll(q, q.shape[1] - 1, 1)


def west_of(q):
    return pltpu.roll(q, 1, 1)


def gain_of(k, t):
    return k.k4 if t == 4 else (DIFFUSIVITY if t < 2 else VISCOSITY)


def tendency_row(k, ref, row, c, f):
    half = 0.5 * c
    c2 = c * c
    u, v = tile(ref, row, 2), tile(ref, row, 3)
    u4, v4 = deep_u(k, ref, row), deep_v(k, ref, row)
    change = []
    for t in range(5):
        gain = gain_of(k, t)
        if t in (0, 2, 4):
            au, av = (half * u4, 0.5 * v4) if t == 4 else (half * u, 0.5 * v)
            along = gain * c2
            at_e, at_w, at_n, at_s = along - au, along + au, gain - av, gain + av
        q = tile(ref, row, t)
        east, west = at_e * east_of(q), at_w * west_of(q)
        north, south = at_n * tile(ref, row + 1, t), at_s * tile(ref, row - 1, t)
        change.append((east + west) + (north + south) - (gain * (2.0 * c2 + 2.0)) * q)
    p = tile(ref, row, 5)
    change[2] = change[2] + (f * v - half * (east_of(p) - west_of(p)))
    change[3] = change[3] - (f * u + 0.5 * (tile(ref, row + 1, 5) - tile(ref, row - 1, 5)))
    p4 = tile(ref, row, 6)
    fx = f * v4 - half * (east_of(p4) - west_of(p4))
    fy = f * u4 + 0.5 * (tile(ref, row + 1, 6) - tile(ref, row - 1, 6))
    change[4] = change[4] + jnp.where(k.is_u, fx, jnp.where(k.is_v, -fy, 0.0))
    return change


def adjoint_row(k, ref, aref, row, c, f):
    half = 0.5 * c
    c2 = c * c
    u4 = deep_u(k, ref, row)
    qe = [east_of(tile(ref, row, t)) for t in range(5)]
    qw = [west_of(tile(ref, row, t)) for t in range(5)]
    out = []
    to_u = to_v = None
    for t in range(5):
        a = tile(aref, row, t)
        ae, aw = east_of(a), west_of(a)
        an, as_ = tile(aref, row + 1, t), tile(aref, row - 1, t)
        gain = gain_of(k, t)
        if t == 0:
            ue, uw = half * qe[2], half * qw[2]
            vn, vs = 0.5 * tile(ref, row + 1, 3), 0.5 * tile(ref, row - 1, 3)
        if t == 4:
            ue, uw = half * east_of(u4), half * west_of(u4)
            vn, vs = 0.5 * deep_v(k, ref, row + 1), 0.5 * deep_v(k, ref, row - 1)
        if t in (0, 2, 4):
            along = gain * c2
            at_e, at_w, at_n, at_s = along + ue, along - uw, gain + vn, gain - vs
        out.append(
            (at_e * ae + at_w * aw) + (at_n * an + at_s * as_) - (gain * (2.0 * c2 + 2.0)) * a
        )
        px = a * (qe[t] - qw[t])
        py = a * (tile(ref, row + 1, t) - tile(ref, row - 1, t))
        if t < 4:
            to_u = px if to_u is None else to_u + px
            to_v = py if to_v is None else to_v + py
        if t == 2:
            a2, bx = a, half * (ae - aw)
        if t == 3:
            a3, by = a, 0.5 * (an - as_)
        if t == 4:
            a4 = a
            deep_bx, deep_by = half * (ae - aw), 0.5 * (an - as_)
            px4, py4 = px * half, py * 0.5
    out[2] = out[2] - half * to_u - f * a3
    out[3] = out[3] - 0.5 * to_v + f * a2
    sx = px4 + pltpu.roll(px4, 7, 0)
    sx = sx + pltpu.roll(sx, 2, 0)
    sy = py4 + pltpu.roll(py4, 1, 0)
    sy = sy + pltpu.roll(sy, 2, 0)
    at_u = -sx - f * pltpu.roll(a4, 7, 0)
    at_v = f * pltpu.roll(a4, 1, 0) - sy
    deep = jnp.where(k.is_t, pltpu.roll(deep_bx, 6, 0) + pltpu.roll(deep_by, 5, 0), 0.0)
    deep = deep + jnp.where(k.low, 0.0, pltpu.roll(deep, 4, 0))
    press = bx + by
    for shift in (1, 2, 4):
        press = press + jnp.where(k.sub < 8 - shift, pltpu.roll(press, 8 - shift, 0), 0.0)
    press = press + deep[0:1, :]
    out[0] = out[0] - 0.1 * press
    out[1] = out[1] + 0.4 * press
    out[4] = out[4] + jnp.where(
        k.is_t,
        -0.1 * deep,
        jnp.where(k.is_s, 0.4 * pltpu.roll(deep, 1, 0), jnp.where(k.is_u, at_u, at_v)),
    )
    return out


def for_span(low, high, up, body):
    turns = lax.div(high - low + TURN - 1, TURN)
    first = jnp.where(up == 1, low, high - TURN * turns)

    def turn(i, _):
        stores = [body(first + TURN * i + j) for j in range(TURN)]
        for store in stores:
            store()
        return 0

    lax.fori_loop(0, turns, turn, 0)


def for_rows(scal, reach, body):
    for_span(PAD - reach * scal[2], PAD + ROWS + reach * scal[3], scal[3], body)


def for_inner(scal, inset, body):
    for_span(PAD + inset * scal[2], PAD + ROWS - inset * scal[3], scal[3], body)


def for_outer(sides, scal, inset, reach, body):
    if sides == ["swap"]:
        low = jnp.where(scal[3] == 1, PAD + ROWS - inset, PAD - reach)
        for_span(low, low + reach + inset, scal[3], body)
    else:
        for_span(PAD - reach * scal[2], PAD + inset * scal[2], 0, body)
        for_span(PAD + ROWS - inset * scal[3], PAD + ROWS + reach * scal[3], 1, body)


def mask_tile(ref, row, t):
    return tile(ref, row, 1 if t == 4 else 0)


def put_tiles(ref, row, tiles):
    for t in range(5):
        ref[row, 8 * t : 8 * t + 8, :] = tiles[t]


def adjoint_third(k, scal, cs, fs, reach, state, masks, abuf, top, hold, bbuf):
    def body(r):
        d = adjoint_row(k, state, abuf, r, cs[r], fs[r])
        ts = [(2.0 / 3.0) * tile(top, r, t) + d[t] for t in range(5)]
        masked = [0.0625 * mask_tile(masks, r, t) * ts[t] for t in range(5)]
        return lambda: (put_tiles(hold, r, ts), put_tiles(bbuf, r, masked))

    for_rows(scal, reach, body)


def adjoint_second(k, scal, cs, fs, reach, state, masks, bbuf, top, hold, left, abuf):
    def body(r):
        d = adjoint_row(k, state, bbuf, r, cs[r], fs[r])
        ts = [tile(hold, r, t) for t in range(5)]
        tf = [0.25 * ts[t] + d[t] for t in range(5)]
        new = [(1.0 / 3.0) * tile(top, r, t) + 0.75 * ts[t] + tf[t] for t in range(5)]
        masked = [0.25 * mask_tile(masks, r, t) * tf[t] for t in range(5)]
        return lambda: (put_tiles(left, r, new), put_tiles(abuf, r, masked))

    for_rows(scal, reach, body)


def adjoint_first(k, scal, cs, fs, reach, state, abuf, left, store):
    def body(r):
        d = adjoint_row(k, state, abuf, r, cs[r], fs[r])
        return store(r, [tile(left, r, t) + d[t] for t in range(5)])

    for_rows(scal, reach, body)


def edges(reach):
    lane = lax.broadcasted_iota(jnp.int32, (8, COLS), 1)
    return lane < reach, lane >= COLS - reach


def wide_pack(ref, base):
    parts = []
    for t in range(5):
        rows = [ref[base + s, 8 * t : 8 * t + 8, COLS:WIDE] for s in range(8)]
        parts.append(slot_pack(rows, lambda s: 8 + SLOT * s, SLOT))
    return jnp.concatenate(parts, axis=0)

def wide_unpack(ref, base, values):
    for s in range(8):
        ref[base + s, 0:FEATS, COLS:WIDE] = pltpu.roll(values, -(8 + SLOT * s) % COLS, 1)


def section_1(k, cs, fs, masks, src, dst):
    def body(r):
        d = tendency_row(k, src, r, cs[r], fs[r])
        new = [tile(src, r, t) + 0.25 * mask_tile(masks, r, t) * d[t] for t in range(5)]
        return lambda: put_state(k, dst, r, new)

    return body


def section_2(k, cs, fs, masks, src, mid, dst):
    def body(r):
        d = tendency_row(k, mid, r, cs[r], fs[r])
        new = [
            0.75 * tile(src, r, t) + 0.25 * tile(mid, r, t) + 0.0625 * mask_tile(masks, r, t) * d[t]
            for t in range(5)
        ]
        return lambda: put_state(k, dst, r, new)

    return body


def section_3(k, cs, fs, masks, fluxes, mean, src, mid, net, r):
    d = tendency_row(k, mid, r, cs[r], fs[r])
    new = []
    for t in range(5):
        m = mask_tile(masks, r, t)
        o = tile(net, r, t)
        if t == 1:
            force = 2.0 * (mean - fluxes[r, 2:3, :])
            o = o + jnp.where(k.sub == 0, force, 0.0)
        new.append(
            (1.0 / 3.0) * tile(src, r, t) + (2.0 / 3.0) * tile(mid, r, t)
            + m * ((1.0 / 6.0) * d[t] + 0.25 * o)
        )
    return new


def zero_walls(ref):
    for row in (PAD - 1, PAD + ROWS):
        ref[row] = jnp.zeros(ref.shape[1:], F32)


class Block:
    def __init__(self, k, s0, masks, fluxes):
        self.k, self.s0, self.masks, self.fluxes = k, s0, masks, fluxes
        self.near_e, self.near_w = edges(REACH)

    def put(self, row, core, from_e, from_w):
        def both(t):
            halo = jnp.where(self.near_e, from_e(t), jnp.where(self.near_w, from_w(t), 0.0))
            return jnp.concatenate([core(t), halo], axis=1)

        put_state(self.k, self.s0, row, [both(t) for t in range(5)])
        self.masks[row, 0:8, :] = both(5)
        last = both(6)
        self.masks[row, 8:16, :] = jnp.where(self.k.low, last[1:2, :], last[0:1, :])
        self.fluxes[row] = last


def assemble_own_kernel(scal, cs, fs, own, own_m, east, west, k1, k2, k3, b2, b3, s0, masks, fluxes, net):
    k = Row(WIDE)
    zero_walls(s0)
    block = Block(k, s0, masks, fluxes)
    for r in range(ROWS):
        at = (r // 8) * PACK
        turn = SLOT * (r % 8)
        block.put(
            PAD + r,
            lambda t: own[r, 8 * t : 8 * t + 8, :],
            lambda t: pltpu.roll(west[at + 8 * t : at + 8 * t + 8, :], -turn % COLS, 1),
            lambda t: pltpu.roll(east[at + 8 * t : at + 8 * t + 8, :], -(turn + SLOT) % COLS, 1),
        )
        net[PAD + r, :, 0:COLS] = own_m[r]
    columns = jnp.concatenate([wide_pack(s0, PAD), wide_pack(s0, PAD + 8)], axis=1)
    o = closure_of(columns, k1, k2, k3, b2, b3)
    for g in range(2):
        wide_unpack(net, PAD + 8 * g, o[:, g * COLS : (g + 1) * COLS])


def closure_of(columns, k1, k2, k3, b2, b3):
    _, _, h2 = hidden_layers(split(to_48(columns, 1.0)), k1, k2, b2)
    return last_layer(h2, k3, b3)


def first_own_kernel(scal, cs, fs, s0, masks, s1):
    zero_walls(s1)
    for_inner(scal, 1, section_1(Row(WIDE), cs, fs, masks, s0, s1))


def second_own_kernel(scal, cs, fs, s0, s1, masks, s2):
    for_inner(scal, 2, section_2(Row(WIDE), cs, fs, masks, s0, s1, s2))


def halo_kernel(sides, scal, cs, fs, own_s0, own_s1, own_s2, own_masks, own_fluxes, own_net, *rest):
    n = len(sides)
    side_refs = [rest[2 * i : 2 * i + 2] for i in range(n)]
    net_refs, (s0, s1, s2, masks, fluxes, net) = rest[2 * n : 2 * n + 5], rest[2 * n + 5 :]
    k = Row(WIDE)
    for r in range(PAD, PAD + ROWS):
        for src, dst in (
            (own_s0, s0), (own_s1, s1), (own_s2, s2), (own_masks, masks), (own_fluxes, fluxes), (own_net, net)
        ):
            dst[r] = src[r]
    for ref in (s0, s1, s2):
        zero_walls(ref)
    block = Block(k, s0, masks, fluxes)
    firsts = []
    for side, (lat, corner) in zip(sides, side_refs):
        base = {"swap": scal[4], "north": PAD - REACH, "south": PAD + ROWS}[side]
        for r in range(REACH):
            block.put(
                base + r,
                lambda t: lat[PACK * r + 8 * t : PACK * r + 8 * t + 8, :],
                lambda t: pltpu.roll(corner[PACK + 40 + 8 * t : PACK + 48 + 8 * t, :], -REACH * r % COLS, 1),
                lambda t: pltpu.roll(corner[8 * t : 8 * t + 8, :], -REACH * (r + 1) % COLS, 1),
            )
        near = {"swap": jnp.where(scal[2] == 1, PAD - 8, PAD + ROWS), "north": PAD - 8, "south": PAD + ROWS}
        firsts.append(near[side])
    columns = []
    for first in firsts:
        columns += [s0[first + i, 0:FEATS, 0:COLS] for i in range(8)] + [wide_pack(s0, first)]
    o = closure_of(jnp.concatenate(columns, axis=1), *net_refs)
    for g, first in enumerate(firsts):
        for i in range(8):
            at = (9 * g + i) * COLS
            net[first + i, :, 0:COLS] = o[:, at : at + COLS]
        at = (9 * g + 8) * COLS
        wide_unpack(net, first, o[:, at : at + COLS])
    for_outer(sides, scal, 1, 10, section_1(k, cs, fs, masks, s0, s1))
    for_outer(sides, scal, 2, 9, section_2(k, cs, fs, masks, s0, s1, s2))


def last_section_kernel(scal, cs, fs, sums, s3, t2, masks, fluxes, outs, final):
    k = Row(WIDE)
    mean = sums[0:1, 0:1] / sums[1:2, 0:1]

    def last(r):
        new = section_3(k, cs, fs, masks, fluxes, mean, s3, t2, outs, r)
        return lambda: put_result(final, r - PAD, [x[:, 0:COLS] for x in new])

    for_rows(scal, 0, last)


def late_kernel(
    sides, scal, cs, fs, sums, own, cown, own_h1, own_h2, s0, s2, masks, fluxes, outs_in, east, west, *rest
):
    n = len(sides)
    side_refs = [rest[2 * i : 2 * i + 2] for i in range(n)]
    (k1, k2, k3, q1, q2, q3, b2, b3), rest = rest[2 * n : 2 * n + 8], rest[2 * n + 8 :]
    grads, s4, abuf, from_closure, s3, t2, outs, t1, cot, gz, bbuf, hold, left, acc = rest
    k = Row(WIDE)
    has_south = scal[2]
    lo = lambda h: PAD - h * has_south
    for ref in (s3, t1, t2, abuf, bbuf):
        zero_walls(ref)
    mean = sums[0:1, 0:1] / sums[1:2, 0:1]

    cnear_e, cnear_w = edges(CREACH)
    for r in range(ROWS):
        for t in range(5):
            rows = slice(2 * PACK + 8 * t, 2 * PACK + 8 * t + 8)
            from_e = pltpu.roll(west[rows, :], -8 * r % COLS, 1)
            from_w = pltpu.roll(east[rows, :], -8 * (r + 1) % COLS, 1)
            side = jnp.where(cnear_e, from_e, jnp.where(cnear_w, from_w, 0.0))
            cot[PAD + r, 8 * t : 8 * t + 8, :] = jnp.concatenate(
                [cown[r, 8 * t : 8 * t + 8, :], side], axis=1
            )
    for side, (lat, corner) in zip(sides, side_refs):
        cbase = {"swap": scal[5], "north": PAD - CREACH, "south": PAD + ROWS}[side]
        crow = {"swap": scal[6], "north": ROWS - CREACH, "south": 0}[side]
        for r in range(CREACH):
            turn = lax.rem(2 * COLS - 8 * (crow + r), COLS)
            turn_w = lax.rem(2 * COLS - 8 * (crow + r + 1), COLS)
            for t in range(5):
                wrows = slice(PACK + 8 * t, PACK + 8 * t + 8)
                erows = slice(2 * PACK + 40 + 8 * t, 2 * PACK + 48 + 8 * t)
                from_e = pltpu.roll(corner[erows, :], turn, 1)
                from_w = pltpu.roll(corner[wrows, :], turn_w, 1)
                part = jnp.where(cnear_e, from_e, jnp.where(cnear_w, from_w, 0.0))
                cot[cbase + r, 8 * t : 8 * t + 8, :] = jnp.concatenate(
                    [lat[LAT_X + FEATS * r + 8 * t : LAT_X + FEATS * r + 8 * t + 8, :], part], axis=1
                )


    def step_1_end(r):
        put_state(k, s3, r, section_3(s0, s2, r))

    def step_1_end(r):
        new = section_3(k, cs, fs, masks, fluxes, mean, s0, s2, outs_in, r)
        return lambda: put_state(k, s3, r, new)

    for_rows(scal, 8, step_1_end)

    acc[...] = jnp.zeros(acc.shape, F32)

    def closure_adjoint(z, h1, h1s, h2, go, with_weights):
        gos = split(to_48(go))
        g2 = product(q3[...], *gos) * (1.0 - h2 * h2)
        g2s = split(g2)
        g1 = product(q2[...], *g2s) * (1.0 - h1 * h1)
        g1s = split(g1)
        if with_weights:
            add_weight_terms(acc, z, h1s, split(h2), g1s, g2s, gos)
        return product(q1[...], *g1s)[0:FEATS]

    def both_ways(columns, go, with_weights):
        z = split(to_48(columns, 1.0))
        h1, h1s, h2 = hidden_layers(z, k1, k2, b2)
        o = last_layer(h2, k3, b3) if with_weights else None
        return o, closure_adjoint(z, h1, h1s, h2, go, with_weights)

    def masked_core(ref, r):
        m0, m4 = masks[r, 0:8, 0:COLS], masks[r, 8:16, 0:COLS]
        parts = [
            0.25 * (m4 if t == 4 else m0) * ref[r, 8 * t : 8 * t + 8, 0:COLS] for t in range(5)
        ]
        return jnp.concatenate(parts, axis=0)

    def mask_cot(r):
        seen = [mask_tile(masks, r, t) * tile(cot, r, t) for t in range(5)]
        quarter, sixth = [0.25 * x for x in seen], [(1.0 / 6.0) * x for x in seen]
        return lambda: (put_tiles(bbuf, r, quarter), put_tiles(abuf, r, sixth))

    for_rows(scal, 6, mask_cot)

    for first in range(PAD, PAD + ROWS, 8):
        z = jnp.concatenate([s3[first + i, 0:FEATS, 0:COLS] for i in range(8)], axis=1)
        go = jnp.concatenate([bbuf[first + i, 0:FEATS, 0:COLS] for i in range(8)], axis=1)
        o, back = both_ways(z, go, True)
        for i in range(8):
            at = slice(i * COLS, (i + 1) * COLS)
            outs[first + i, :, 0:COLS] = o[:, at]
            gz[first + i, :, 0:COLS] = back[:, at]

    first = lo(4)
    if sides == ["swap"]:
        rows = [jnp.where(has_south == 1, PAD - 4, PAD + ROWS) + i for i in range(4)]
    else:
        rows = [PAD - 4 + i for i in range(4)] + [PAD + ROWS + i for i in range(4)]
    beyond = lambda ref: jnp.concatenate(
        [ref[r, 0:FEATS, 0:COLS] for r in rows] + [wide_pack(ref, first + 8 * g) for g in range(3)], axis=1
    )
    _, back = both_ways(beyond(s3), beyond(bbuf), False)
    for i, r in enumerate(rows):
        gz[r, :, 0:COLS] = back[:, i * COLS : (i + 1) * COLS]
    for g in range(3):
        at = (len(rows) + g) * COLS
        wide_unpack(gz, first + 8 * g, back[:, at : at + COLS])

    for_rows(scal, 7, section_1(k, cs, fs, masks, s3, t1))
    for_rows(scal, 6, section_2(k, cs, fs, masks, s3, t1, t2))

    def store(r, tiles):
        new = [tiles[t] + tile(gz, r, t) for t in range(5)]
        return lambda: put_tiles(s4, r, new)

    adjoint_third(k, scal, cs, fs, 5, t2, masks, abuf, cot, hold, bbuf)
    adjoint_second(k, scal, cs, fs, 4, t1, masks, bbuf, cot, hold, left, abuf)
    adjoint_first(k, scal, cs, fs, 3, s3, abuf, left, store)

    for r in range(0, ROWS, 8):
        side = lambda read: jnp.concatenate([read(r + j) for j in range(8)], axis=1)
        z = split(to_48(side(lambda j: own[j, 0:FEATS, :]), 1.0))
        h1 = side(lambda j: own_h1[j])
        h2 = side(lambda j: own_h2[j])
        go = side(lambda j: masked_core(s4, PAD + j))
        back = closure_adjoint(z, h1, split(h1), h2, go, True)
        for j in range(8):
            from_closure[r + j] = back[:, j * COLS : (j + 1) * COLS]

    zero_walls(abuf)

    def mask_top(r):
        new = [(1.0 / 6.0) * mask_tile(masks, r, t) * tile(s4, r, t) for t in range(5)]
        return lambda: put_tiles(abuf, r, new)

    for_rows(scal, 3, mask_top)
    grads[...] = jnp.zeros(grads.shape, F32)
    grads[0:40, 0:HID] = acc[0:40, 0:HID]
    grads[0:40, HID : 2 * HID] = acc[112:152, 0:HID]
    grads[40:72, 0:HID] = acc[48:80, 0:HID]
    grads[40:72, HID : 2 * HID] = acc[80:112, 0:HID]
    grads[72:73, 0:HID] = acc[40:41, 0:HID]
    grads[72:73, HID : 2 * HID] = acc[160:161, 0:HID]
    grads[73:74, 0:HID] = acc[176:177, 0:HID]


def put_result(ref, row, tiles):
    for t in range(4):
        ref[pl.ds(t * 10 * ROWS + row, 8, stride=ROWS), :] = tiles[t]
    ref[pl.ds(8 * ROWS + row, 4, stride=10 * ROWS), :] = tiles[4][0:4, :]
    ref[pl.ds(9 * ROWS + row, 4, stride=10 * ROWS), :] = tiles[4][4:8, :]


def back_third_kernel(scal, cs, fs, state, masks, abuf, top, hold, bbuf):
    zero_walls(bbuf)
    adjoint_third(Row(WIDE), scal, cs, fs, 2, state, masks, abuf, top, hold, bbuf)


def back_second_kernel(scal, cs, fs, state, masks, bbuf, top, hold, left, abuf):
    zero_walls(abuf)
    adjoint_second(Row(WIDE), scal, cs, fs, 1, state, masks, bbuf, top, hold, left, abuf)


def back_first_kernel(scal, cs, fs, state, masks, abuf, left, from_closure, grad):
    def store(r, tiles):
        done = []
        for t in range(5):
            m = masks[r, 8:16, 0:COLS] if t == 4 else masks[r, 0:8, 0:COLS]
            done.append(m * (tiles[t][:, 0:COLS] + from_closure[r - PAD, 8 * t : 8 * t + 8, :]))
        return lambda: put_result(grad, r - PAD, done)

    adjoint_first(Row(WIDE), scal, cs, fs, 0, state, abuf, left, store)


def unpack_kernel(scale, packed, win, bin_, wmid, bmid, wout, bout):
    for ref, lanes in ((win, slice(0, HID)), (wout, slice(HID, 2 * HID))):
        for t in range(4):
            ref[10 * t : 10 * t + 8, :] = packed[8 * t : 8 * t + 8, lanes] * scale
            ref[10 * t + 8 : 10 * t + 9, :] = packed[32 + t : 33 + t, lanes] * scale
            ref[10 * t + 9 : 10 * t + 10, :] = packed[36 + t : 37 + t, lanes] * scale
    wmid[0:32, :] = packed[40:72, 0:HID] * scale
    wmid[32:64, :] = packed[40:72, HID : 2 * HID] * scale
    bin_[...] = packed[72:73, 0:HID] * scale
    bmid[...] = packed[72:73, HID : 2 * HID] * scale
    for t in range(4):
        bout[:, 10 * t : 10 * t + 8] = packed[73:74, 8 * t : 8 * t + 8] * scale
        bout[:, 10 * t + 8 : 10 * t + 9] = packed[73:74, 32 + t : 33 + t] * scale
        bout[:, 10 * t + 9 : 10 * t + 10] = packed[73:74, 36 + t : 37 + t] * scale


def position(lat_n):
    lat_i = lax.axis_index("lat")
    low = (lat_i == 0).astype(jnp.int32)
    return (
        low * (ROWS - REACH),
        low * (ROWS - CREACH),
        (lat_i > 0).astype(jnp.int32),
        (lat_i < lat_n - 1).astype(jnp.int32),
        jnp.where(low == 1, PAD + ROWS, PAD - REACH),
        jnp.where(low == 1, PAD + ROWS, PAD - CREACH),
        jnp.where(low == 1, 0, ROWS - CREACH),
    )


class RowTable:
    def __init__(self, ref, number):
        self.ref, self.number = ref, number

    def __getitem__(self, row):
        part = tile(self.ref, row, self.number)
        return jnp.concatenate([part, part], axis=1)


def far_first(axes):
    return [(axis, n, 1 << bit) for axis, n in axes for bit in reversed(range(n.bit_length() - 1))]


def pair_rounds(x, rounds, beside):
    results = []
    for i in range(max(len(rounds), len(beside))):
        if i < len(rounds):
            axis, n, step = rounds[i]
            got = lax.ppermute(x, axis, [(j, j ^ step) for j in range(n)])
        if i < len(beside):
            results.append(beside[i](results))
            if i < len(rounds):
                got, results[-1] = lax.optimization_barrier((got, results[-1]))
        if i < len(rounds):
            x = x + got
    return x, results


def latitude_terms(row_index, row_count):
    latitude = LAT_LIMIT * (2.0 * (jnp.clip(row_index, 0.0, row_count - 1.0) + 0.5) / row_count - 1.0)
    return 1.0 / jnp.cos(latitude), CORIOLIS * jnp.sin(latitude)


def on_device(
    initial_state, land_mask, surface_flux, weight_in, bias_in, weight_mid, bias_mid, weight_out, bias_out, cotangent
):
    lat_n, lon_n = lax.axis_size("lat"), lax.axis_size("lon")
    lat_i = lax.axis_index("lat")
    lat_total, lon_total = ROWS * lat_n, COLS * lon_n
    sides = ["swap"] if lat_n == 2 else ["north", "south"]
    rows = (lat_i * ROWS - PAD + jnp.arange(EXT, dtype=jnp.int32)).astype(F32)
    tiles = [jnp.broadcast_to(x[:, None, None], (EXT, 8, COLS)) for x in latitude_terms(rows, lat_total)]
    geometry = jnp.concatenate(tiles, axis=1)

    hbm = pl.BlockSpec(memory_space=pltpu.HBM)
    packed = pl.pallas_call(
        lambda *refs: pack_kernel(sides, *refs),
        out_shape=[
            sds(ROWS, PACK, COLS), sds(ROWS, FEATS, COLS), sds(STRIP, COLS), sds(STRIP, COLS), sds(8, COLS),
        ]
        + [sds(LAT, COLS)] * len(sides),
        in_specs=[hbm] * 4,
        out_specs=[VMEM] * (5 + len(sides)),
        scratch_shapes=[
            pltpu.VMEM((40 * ROWS, COLS), F32), pltpu.VMEM((10 * ROWS, COLS), jnp.int32),
            pltpu.VMEM((ROWS, COLS), F32), pltpu.VMEM((40 * ROWS, COLS), F32), pltpu.SemaphoreType.DMA((4,)),
        ],
        compiler_params=params(56),
        cost_estimate=pl.CostEstimate(flops=10**9, bytes_accessed=3 * 10**6, transcendentals=0),
        name="pack_halos",
    )(
        initial_state.reshape(40 * ROWS, COLS),
        land_mask.reshape(10 * ROWS, COLS),
        surface_flux,
        cotangent.reshape(40 * ROWS, COLS),
    )
    own, cown, east_pay, west_pay, sums = packed[:5]

    def lat_pairs(side):
        if side == "swap":
            return [(0, 1), (1, 0)]
        if side == "north":
            return [(i, i + 1) for i in range(lat_n - 1)]
        return [(i + 1, i) for i in range(lat_n - 1)]

    east_ring = [(i, (i + 1) % lon_n) for i in range(lon_n)]
    west_ring = [((i + 1) % lon_n, i) for i in range(lon_n)]
    from_west = lax.ppermute(east_pay, "lon", east_ring)
    from_east = lax.ppermute(west_pay, "lon", west_ring)
    row = lambda b: b.reshape(1, -1)
    raw = (weight_in, weight_mid, weight_out, row(bias_in), row(bias_mid), row(bias_out))
    half = lambda *shape: jax.ShapeDtypeStruct(shape, BF16)
    own_closure = pl.pallas_call(
        own_closure_kernel,
        out_shape=[
            sds(ROWS, FEATS, COLS), sds(ROWS, HID, COLS), sds(ROWS, HID, COLS),
            half(HID, 144), half(HID, 192), half(48, 192), half(48, 192), half(HID, 192), half(HID, 144),
            sds(HID, COLS), sds(FEATS, COLS),
        ],
        in_specs=[VMEM] + [hbm] * 6,
        out_specs=[VMEM] * 11,
        scratch_shapes=[pltpu.VMEM(w.shape, F32) for w in raw]
        + [pltpu.VMEM((COLS, COLS), F32), pltpu.VMEM((COLS, COLS), F32), pltpu.VMEM((HID, WIDE), F32)]
        + [pltpu.SemaphoreType.DMA((6,))],
        compiler_params=params(12),
        cost_estimate=pl.CostEstimate(flops=10**9, bytes_accessed=2 * 10**6, transcendentals=0),
        name="own_closure",
    )
    pack_corners = pl.pallas_call(
        lambda *refs: corner_kernel(sides, *refs),
        out_shape=[sds(CORNER + 8, COLS)] * len(sides),
        in_specs=[VMEM, VMEM],
        out_specs=[VMEM] * len(sides),
        compiler_params=params(8),
        cost_estimate=pl.CostEstimate(flops=10**8, bytes_accessed=10**6, transcendentals=0),
        name="pack_corners",
    )
    lats = [lax.ppermute(pay, "lat", lat_pairs(side)) for side, pay in zip(sides, packed[5:])]
    state = sds(EXT, 56, WIDE)
    plain = sds(EXT, FEATS, WIDE)
    marks = sds(EXT, 16, WIDE)
    vmem = lambda shape: pltpu.VMEM(shape.shape, F32)

    def call(kernel, name, out_shape, scratch, args, flops, limit):
        single = not isinstance(out_shape, list)
        return pl.pallas_call(
            lambda geo, *refs: kernel(position(lat_n), RowTable(geo, 0), RowTable(geo, 1), *refs),
            out_shape=out_shape,
            in_specs=[VMEM] * (1 + len(args)),
            out_specs=VMEM if single else [VMEM] * len(out_shape),
            scratch_shapes=scratch,
            compiler_params=params(limit),
            cost_estimate=pl.CostEstimate(flops=flops, bytes_accessed=10**7, transcendentals=0),
            name=name,
        )(geometry, *args)


    def last_round(done):
        own_m, _, _, k1, k2, k3, _, _, _, b2, b3 = done[1]
        blocks = call(
            assemble_own_kernel, "assemble_own", [state, marks, sds(EXT, 8, WIDE), plain], [],
            [own, own_m, from_west, from_east, k1, k2, k3, b2, b3], 10**9, 8,
        )
        return blocks, pack_corners(from_west, from_east)

    rounds = far_first((("lon", lon_n),))[::-1]
    row_total, results = pair_rounds(
        sums,
        rounds,
        [lambda done: sums, lambda done: own_closure(own, *raw)]
        + [lambda done: sums] * (len(rounds) - 3)
        + [last_round],
    )
    own_m, own_h1, own_h2, k1, k2, k3, q1, q2, q3, b2, b3 = results[1]
    net_weights = [k1, k2, k3, b2, b3]
    (s0, masks, fluxes, net), corner_pays = results[-1]
    corners = []
    for side, pay in zip(sides, corner_pays):
        pay = lax.dynamic_update_slice(pay, row_total, (CORNER, 0))
        corners.append(lax.ppermute(pay, "lat", lat_pairs(side)))
    s1 = call(first_own_kernel, "first_section_own", state, [], [s0, masks], 10**9, 8)
    s2 = call(second_own_kernel, "second_section_own", state, [], [s0, s1, masks], 10**9, 8)
    corners, s2 = lax.optimization_barrier((corners, s2))
    if sides == ["swap"]:
        total = row_total + corners[0][CORNER : CORNER + 8]
    else:
        total = lax.psum(row_total, "lat")
    received = [ref for pair in zip(lats, corners) for ref in pair]
    s0, s1, s2, masks, fluxes, net = call(
        lambda *refs: halo_kernel(sides, *refs), "halo_rows",
        [state, state, state, marks, sds(EXT, 8, WIDE), plain], [],
        [s0, s1, s2, masks, fluxes, net] + received + net_weights, 2 * 10**9, 8,
    )
    grads, top, abuf, from_closure, s3, t2, net_2 = call(
        lambda *refs: late_kernel(sides, *refs), "steps_and_adjoint",
        [sds(80, COLS), plain, plain, sds(ROWS, FEATS, COLS), state, state, plain],
        [vmem(state)] + [vmem(plain)] * 5 + [pltpu.VMEM((192, HID), F32)],
        [total, own, cown, own_h1, own_h2, s0, s2, masks, fluxes, net, from_west, from_east]
        + received + [k1, k2, k3, q1, q2, q3, b2, b3],
        4 * 10**9, 18,
    )
    beside = [
        lambda done: call(
            back_third_kernel, "adjoint_third_section", [plain, plain], [], [s2, masks, abuf, top], 10**9, 8
        ),
        lambda done: call(
            back_second_kernel, "adjoint_second_section", [plain, plain], [],
            [s1, masks, done[0][1], top, done[0][0]], 10**9, 8,
        ),
        lambda done: call(
            back_first_kernel, "adjoint_first_section", sds(40 * ROWS, COLS), [],
            [s0, masks, done[1][1], done[1][0], from_closure], 10**9, 8,
        ),
        lambda done: call(
            last_section_kernel, "last_section", sds(40 * ROWS, COLS), [],
            [total, s3, t2, masks, fluxes, net_2], 10**9, 8,
        ),
    ]
    by_lon, by_lat = far_first((("lon", lon_n),)), far_first((("lat", lat_n),))
    summed, results = pair_rounds(grads, by_lon[:-2] + by_lat + by_lon[-2:], beside)
    state_grad, final = results[2:]

    scale = 1.0 / math.sqrt(lat_total * lon_total)
    g_in, g_bin, g_mid, g_bmid, g_out, g_bout = pl.pallas_call(
        lambda *refs: unpack_kernel(scale, *refs),
        out_shape=[sds(40, HID), sds(1, HID), sds(HID, HID), sds(1, HID), sds(40, HID), sds(1, 40)],
        in_specs=[VMEM],
        out_specs=[VMEM] * 6,
        compiler_params=params(8),
        name="unpack_weight_grads",
    )(summed)
    shape = initial_state.shape
    return (
        final.reshape(shape),
        state_grad.reshape(shape),
        g_in,
        g_bin.reshape(-1),
        g_mid,
        g_bmid.reshape(-1),
        g_out.T,
        g_bout.reshape(-1),
    )


def solution(mesh):
    split_state = P(None, None, "lat", "lon")
    return jax.shard_map(
        on_device,
        mesh=mesh,
        in_specs=(split_state, P(None, "lat", "lon"), P("lat", "lon"), P(), P(), P(), P(), P(), P(), split_state),
        out_specs=(split_state, split_state, P(), P(), P(), P(), P(), P()),
        check_vma=False,
    )
```

```python
import math

import jax
import jax.numpy as jnp
from jax import lax
from jax.experimental import pallas as pl
from jax.experimental.pallas import tpu as pltpu
from jax.sharding import PartitionSpec as P

LAT_LIMIT = 1.2
CORIOLIS = 1.0
VISCOSITY = 0.15
DIFFUSIVITY = 0.1

ROWS = 16
COLS = 128
REACH = 11
CREACH = 6
PAD = 16
EXT = 48
TURN = 4
WIDE = 2 * COLS
FEATS = 40
HID = 64
PACK = 56
STRIP = 2 * PACK + 40
LAT_X = REACH * PACK
CORNER = 2 * PACK + 80
LAT = LAT_X + CREACH * FEATS
SLOT = 16
F32 = jnp.float32
BF16 = jnp.bfloat16
VMEM = pl.BlockSpec(memory_space=pltpu.VMEM)


def params(megabytes):
    return pltpu.CompilerParams(vmem_limit_bytes=megabytes * 1024 * 1024)


def sds(*shape):
    return jax.ShapeDtypeStruct(shape, F32)


def sub_index(width):
    return lax.broadcasted_iota(jnp.int32, (8, width), 0)


def tile(ref, row, number):
    return ref[row, 8 * number : 8 * number + 8, :]


def slot_pack(pieces, shift_of, width):
    lane = lax.broadcasted_iota(jnp.int32, (8, COLS), 1)
    packed = None
    for slot, piece in enumerate(pieces):
        turned = pltpu.roll(piece, shift_of(slot) % COLS, 1)
        if packed is None:
            packed = turned
        else:
            packed = jnp.where((lane >= slot * width) & (lane < (slot + 1) * width), turned, packed)
    return packed


def pack_kernel(sides, x_hbm, mask_hbm, flux_hbm, cot_hbm, *outs):
    x, mask, flux, cot, sems = outs[-5:]
    own, cown, east, west, sums = outs[:5]
    per_side = outs[5 : 5 + len(sides)]
    pairs = ((mask_hbm, mask), (x_hbm, x), (flux_hbm, flux), (cot_hbm, cot))
    copies = [pltpu.make_async_copy(a, b, sems.at[i]) for i, (a, b) in enumerate(pairs)]
    for copy in copies:
        copy.start()
    for copy in copies:
        copy.wait()
    top = mask[0:ROWS, :].astype(F32)
    total = jnp.sum(jnp.sum(top * flux[...], axis=1, keepdims=True), axis=0, keepdims=True)
    count = jnp.sum(jnp.sum(top, axis=1, keepdims=True), axis=0, keepdims=True)
    sums[...] = jnp.where(sub_index(COLS) == 0, total, jnp.where(sub_index(COLS) == 1, count, 0.0))
    for r in range(ROWS):
        first = mask[pl.ds(r, 8, stride=ROWS), :].astype(F32)
        m8 = mask[8 * ROWS + r : 8 * ROWS + r + 1, :].astype(F32)
        m9 = mask[9 * ROWS + r : 9 * ROWS + r + 1, :].astype(F32)
        for t in range(4):
            own[r, 8 * t : 8 * t + 8, :] = x[pl.ds(t * 10 * ROWS + r, 8, stride=ROWS), :] * first
            cown[r, 8 * t : 8 * t + 8, :] = cot[pl.ds(t * 10 * ROWS + r, 8, stride=ROWS), :]
        for level, m in ((8, m8), (9, m9)):
            at = 32 + 4 * (level - 8)
            own[r, at : at + 4, :] = x[pl.ds(level * ROWS + r, 4, stride=10 * ROWS), :] * m
            cown[r, at : at + 4, :] = cot[pl.ds(level * ROWS + r, 4, stride=10 * ROWS), :]
        own[r, 40:48, :] = first
        own[r, 48:49, :] = m8
        own[r, 49:50, :] = m9
        own[r, 50:51, :] = flux[r : r + 1, :]
        own[r, 51:PACK, :] = jnp.zeros((5, COLS), F32)
    for half in range(2):
        for t in range(7):
            rows = [own[8 * half + s, 8 * t : 8 * t + 8, :] for s in range(8)]
            at = half * PACK + 8 * t
            east[at : at + 8, :] = slot_pack(rows, lambda s: SLOT * (s + 1), SLOT)
            west[at : at + 8, :] = slot_pack(rows, lambda s: SLOT * s, SLOT)
    for t in range(5):
        rows = [cown[s, 8 * t : 8 * t + 8, :] for s in range(ROWS)]
        at = 2 * PACK + 8 * t
        east[at : at + 8, :] = slot_pack(rows, lambda s: 8 * (s + 1), 8)
        west[at : at + 8, :] = slot_pack(rows, lambda s: 8 * s, 8)
    southern = (lax.axis_index("lat") == 0).astype(jnp.int32)
    for side, lat in zip(sides, per_side):
        start = {"swap": southern * (ROWS - REACH), "north": ROWS - REACH, "south": 0}[side]
        cstart = {"swap": southern * (ROWS - CREACH), "north": ROWS - CREACH, "south": 0}[side]
        for n in range(REACH):
            lat[PACK * n : PACK * (n + 1), :] = own[start + n]
        for n in range(CREACH):
            lat[LAT_X + FEATS * n : LAT_X + FEATS * (n + 1), :] = cown[cstart + n]


def corner_kernel(sides, east, west, *outs):
    southern = (lax.axis_index("lat") == 0).astype(jnp.int32)
    for side, corner in zip(sides, outs):
        start = {"swap": southern * (ROWS - REACH), "north": ROWS - REACH, "south": 0}[side]
        for at, strip, near in ((0, east, 1), (PACK + 40, west, 0)):
            for t in range(7):
                rows = slice(at + 8 * t, at + 8 * t + 8)
                corner[rows, :] = shift_rows(strip, t, start, near)
            corner[at + PACK : at + PACK + 40, :] = strip[2 * PACK : 2 * PACK + 40, :]
        corner[CORNER : CORNER + 8, :] = jnp.zeros((8, COLS), F32)


def shift_rows(strip, t, start, near):
    lane = lax.broadcasted_iota(jnp.int32, (8, COLS), 1)
    halves = [strip[8 * t : 8 * t + 8, :], strip[PACK + 8 * t : PACK + 8 * t + 8, :]]
    if isinstance(start, int):
        out = jnp.zeros((8, COLS), F32)
        for n in range(REACH):
            r = start + n
            turn = REACH * n - (SLOT * (r % 8) + near * (SLOT - REACH))
            turned = pltpu.roll(halves[r // 8], turn % COLS, 1)
            out = jnp.where((lane >= REACH * n) & (lane < REACH * (n + 1)), turned, out)
        return out
    low = shift_rows(strip, t, 0, near)
    high = shift_rows(strip, t, ROWS - REACH, near)
    return jnp.where(start == 0, low, high)


def split(values):
    high = values.astype(BF16)
    return high, (values - high.astype(F32)).astype(BF16)


def stack(out, values, buffer):
    k = values.shape[1]
    rows = slice(0, values.shape[0])
    high, low = split(values)
    buffer[rows, 0:k] = high.astype(F32)
    buffer[rows, k : 2 * k] = high.astype(F32)
    buffer[rows, 2 * k : 3 * k] = low.astype(F32)
    out[...] = buffer[rows, 0 : 3 * k].astype(BF16)


def by_tile(dst, src, lanes):
    for t in range(4):
        dst[8 * t : 8 * t + 8, lanes] = src[10 * t : 10 * t + 8, lanes]
        dst[32 + t : 33 + t, lanes] = src[10 * t + 8 : 10 * t + 9, lanes]
        dst[36 + t : 37 + t, lanes] = src[10 * t + 9 : 10 * t + 10, lanes]


def product(weights, high, low):
    return jnp.dot(weights, jnp.concatenate([high, low, high], axis=0), preferred_element_type=F32)


def across(a, b):
    dims = (((1,), (1,)), ((), ()))
    dot = lambda p, q: lax.dot_general(p, q, dims, preferred_element_type=F32)
    return dot(a[0], b[0]) + dot(a[0], b[1]) + dot(a[1], b[0])


def to_48(columns, first=0.0):
    more = jnp.where(sub_index(columns.shape[1]) == 0, first, 0.0).astype(F32)
    return jnp.concatenate([columns, more], axis=0)


def wide(bias, values):
    return jnp.concatenate([bias[...]] * (values.shape[1] // COLS), axis=1)


def hidden_layers(z, k1, k2, b2):
    h1 = jnp.tanh(product(k1[...], *z))
    h1s = split(h1)
    h2 = product(k2[...], *h1s)
    return h1, h1s, jnp.tanh(h2 + wide(b2, h2))


def last_layer(h2, k3, b3):
    o = product(k3[...], *split(h2))[0:FEATS]
    return o + wide(b3, o)


def add_weight_terms(acc, z, h1s, h2s, g1s, g2s, gos):
    ones = jnp.ones((16, z[0].shape[1]), BF16)
    acc[0:48, 0:HID] += across(z, g1s)
    acc[48:112, 0:HID] += across(h1s, g2s)
    acc[112:160, 0:HID] += across(gos, h2s)
    acc[160:176, 0:HID] += ones_rows(ones, g2s)
    acc[176:192, 0:48] += ones_rows(ones, gos)


def ones_rows(ones, g):
    dims = (((1,), (1,)), ((), ()))
    dot = lambda q: lax.dot_general(ones, q, dims, preferred_element_type=F32)
    return dot(g[0]) + dot(g[1])


def own_closure_kernel(own, *refs):
    raw, (out, h1_out, h2_out, k1, k2, k3, q1, q2, q3, b2, b3) = refs[:6], refs[6:17]
    w_in, w_mid, w_out, b_in, b_mid, b_out = refs[17:23]
    buffer, spare, stacked, sems = refs[23:]
    copies = [pltpu.make_async_copy(a, b, sems.at[i]) for i, (a, b) in enumerate(zip(raw, refs[17:23]))]
    for copy in copies:
        copy.start()
    for copy in copies:
        copy.wait()
    buffer[...] = jnp.zeros(buffer.shape, F32)
    by_tile(buffer, w_in, slice(0, HID))
    buffer[40:41, 0:HID] = b_in[...]
    stack(q1, buffer[0:48, 0:HID], stacked)
    spare[...] = buffer[...].T
    stack(k1, spare[0:HID, 0:48], stacked)
    buffer[0:HID, 0:HID] = w_mid[...]
    buffer[HID : HID + 1, 0:HID] = b_mid[...]
    stack(q2, buffer[0:HID, 0:HID], stacked)
    spare[...] = buffer[...].T
    stack(k2, spare[0:HID, 0:HID], stacked)
    b2[...] = jnp.broadcast_to(spare[0:HID, HID : HID + 1], (HID, COLS))
    buffer[...] = jnp.zeros(buffer.shape, F32)
    buffer[0:HID, 0:FEATS] = w_out[...]
    buffer[HID : HID + 1, 0:FEATS] = b_out[...]
    spare[...] = buffer[...].T
    buffer[...] = jnp.zeros(buffer.shape, F32)
    by_tile(buffer, spare, slice(0, COLS))
    stack(k3, buffer[0:48, 0:HID], stacked)
    b3[...] = jnp.broadcast_to(buffer[0:FEATS, HID : HID + 1], (FEATS, COLS))
    spare[...] = buffer[...].T
    stack(q3, spare[0:HID, 0:48], stacked)

    for r in range(0, ROWS, 8):
        z = split(to_48(jnp.concatenate([own[r + n, 0:FEATS, :] for n in range(8)], axis=1), 1.0))
        h1, h1s, h2 = hidden_layers(z, k1, k2, b2)
        o = last_layer(h2, k3, b3)
        for n in range(8):
            at = slice(n * COLS, (n + 1) * COLS)
            out[r + n] = o[:, at]
            h1_out[r + n] = h1[:, at]
            h2_out[r + n] = h2[:, at]


class Row:
    def __init__(self, width):
        sub = sub_index(width)
        group = sub % 4
        self.sub = sub
        self.is_t = group == 0
        self.is_s = group == 1
        self.is_u = group == 2
        self.is_v = group == 3
        self.low = sub >= 4
        self.k4 = jnp.where(group < 2, DIFFUSIVITY, VISCOSITY).astype(F32)


def put_state(k, ref, row, tiles):
    for t in range(5):
        ref[row, 8 * t : 8 * t + 8, :] = tiles[t]
    press = 0.4 * tiles[1] - 0.1 * tiles[0]
    for by in (1, 2, 4):
        press = press + jnp.where(k.sub >= by, pltpu.roll(press, by, 0), 0.0)
    ref[row, 40:48, :] = press
    mixed = tiles[4]
    over = lambda values, n: jnp.broadcast_to(values[n : n + 1, :], values.shape)
    deep_8 = over(press, 7) + (0.4 * over(mixed, 1) - 0.1 * over(mixed, 0))
    deep_9 = deep_8 + (0.4 * over(mixed, 5) - 0.1 * over(mixed, 4))
    ref[row, 48:56, :] = jnp.where(k.low, deep_9, deep_8)


def deep_pair(k, ref, row, upper, lower):
    return jnp.where(k.low, ref[row, lower : lower + 1, :], ref[row, upper : upper + 1, :])


def deep_u(k, ref, row):
    return deep_pair(k, ref, row, 34, 38)


def deep_v(k, ref, row):
    return deep_pair(k, ref, row, 35, 39)


def east_of(q):
    return pltpu.roll(q, q.shape[1] - 1, 1)


def west_of(q):
    return pltpu.roll(q, 1, 1)


def gain_of(k, t):
    return k.k4 if t == 4 else (DIFFUSIVITY if t < 2 else VISCOSITY)


def tendency_row(k, ref, row, c, f):
    half = 0.5 * c
    c2 = c * c
    u, v = tile(ref, row, 2), tile(ref, row, 3)
    u4, v4 = deep_u(k, ref, row), deep_v(k, ref, row)
    change = []
    for t in range(5):
        gain = gain_of(k, t)
        if t in (0, 2, 4):
            au, av = (half * u4, 0.5 * v4) if t == 4 else (half * u, 0.5 * v)
            along = gain * c2
            at_e, at_w, at_n, at_s = along - au, along + au, gain - av, gain + av
        q = tile(ref, row, t)
        east, west = at_e * east_of(q), at_w * west_of(q)
        north, south = at_n * tile(ref, row + 1, t), at_s * tile(ref, row - 1, t)
        change.append((east + west) + (north + south) - (gain * (2.0 * c2 + 2.0)) * q)
    p = tile(ref, row, 5)
    change[2] = change[2] + (f * v - half * (east_of(p) - west_of(p)))
    change[3] = change[3] - (f * u + 0.5 * (tile(ref, row + 1, 5) - tile(ref, row - 1, 5)))
    p4 = tile(ref, row, 6)
    fx = f * v4 - half * (east_of(p4) - west_of(p4))
    fy = f * u4 + 0.5 * (tile(ref, row + 1, 6) - tile(ref, row - 1, 6))
    change[4] = change[4] + jnp.where(k.is_u, fx, jnp.where(k.is_v, -fy, 0.0))
    return change


def adjoint_row(k, ref, aref, row, c, f):
    half = 0.5 * c
    c2 = c * c
    u4 = deep_u(k, ref, row)
    qe = [east_of(tile(ref, row, t)) for t in range(5)]
    qw = [west_of(tile(ref, row, t)) for t in range(5)]
    out = []
    to_u = to_v = None
    for t in range(5):
        a = tile(aref, row, t)
        ae, aw = east_of(a), west_of(a)
        an, as_ = tile(aref, row + 1, t), tile(aref, row - 1, t)
        gain = gain_of(k, t)
        if t == 0:
            ue, uw = half * qe[2], half * qw[2]
            vn, vs = 0.5 * tile(ref, row + 1, 3), 0.5 * tile(ref, row - 1, 3)
        if t == 4:
            ue, uw = half * east_of(u4), half * west_of(u4)
            vn, vs = 0.5 * deep_v(k, ref, row + 1), 0.5 * deep_v(k, ref, row - 1)
        if t in (0, 2, 4):
            along = gain * c2
            at_e, at_w, at_n, at_s = along + ue, along - uw, gain + vn, gain - vs
        out.append(
            (at_e * ae + at_w * aw) + (at_n * an + at_s * as_) - (gain * (2.0 * c2 + 2.0)) * a
        )
        px = a * (qe[t] - qw[t])
        py = a * (tile(ref, row + 1, t) - tile(ref, row - 1, t))
        if t < 4:
            to_u = px if to_u is None else to_u + px
            to_v = py if to_v is None else to_v + py
        if t == 2:
            a2, bx = a, half * (ae - aw)
        if t == 3:
            a3, by = a, 0.5 * (an - as_)
        if t == 4:
            a4 = a
            deep_bx, deep_by = half * (ae - aw), 0.5 * (an - as_)
            px4, py4 = px * half, py * 0.5
    out[2] = out[2] - half * to_u - f * a3
    out[3] = out[3] - 0.5 * to_v + f * a2
    sx = px4 + pltpu.roll(px4, 7, 0)
    sx = sx + pltpu.roll(sx, 2, 0)
    sy = py4 + pltpu.roll(py4, 1, 0)
    sy = sy + pltpu.roll(sy, 2, 0)
    at_u = -sx - f * pltpu.roll(a4, 7, 0)
    at_v = f * pltpu.roll(a4, 1, 0) - sy
    deep = jnp.where(k.is_t, pltpu.roll(deep_bx, 6, 0) + pltpu.roll(deep_by, 5, 0), 0.0)
    deep = deep + jnp.where(k.low, 0.0, pltpu.roll(deep, 4, 0))
    press = bx + by
    for shift in (1, 2, 4):
        press = press + jnp.where(k.sub < 8 - shift, pltpu.roll(press, 8 - shift, 0), 0.0)
    press = press + deep[0:1, :]
    out[0] = out[0] - 0.1 * press
    out[1] = out[1] + 0.4 * press
    out[4] = out[4] + jnp.where(
        k.is_t,
        -0.1 * deep,
        jnp.where(k.is_s, 0.4 * pltpu.roll(deep, 1, 0), jnp.where(k.is_u, at_u, at_v)),
    )
    return out


def for_span(low, high, up, body):
    turns = lax.div(high - low + TURN - 1, TURN)
    first = jnp.where(up == 1, low, high - TURN * turns)

    def turn(i, _):
        stores = [body(first + TURN * i + j) for j in range(TURN)]
        for store in stores:
            store()
        return 0

    lax.fori_loop(0, turns, turn, 0)


def for_rows(scal, reach, body):
    for_span(PAD - reach * scal[2], PAD + ROWS + reach * scal[3], scal[3], body)


def for_inner(scal, inset, body):
    for_span(PAD + inset * scal[2], PAD + ROWS - inset * scal[3], scal[3], body)


def for_outer(sides, scal, inset, reach, body):
    if sides == ["swap"]:
        low = jnp.where(scal[3] == 1, PAD + ROWS - inset, PAD - reach)
        for_span(low, low + reach + inset, scal[3], body)
    else:
        for_span(PAD - reach * scal[2], PAD + inset * scal[2], 0, body)
        for_span(PAD + ROWS - inset * scal[3], PAD + ROWS + reach * scal[3], 1, body)


def mask_tile(ref, row, t):
    return tile(ref, row, 1 if t == 4 else 0)


def put_tiles(ref, row, tiles):
    for t in range(5):
        ref[row, 8 * t : 8 * t + 8, :] = tiles[t]


def adjoint_third(k, scal, cs, fs, reach, state, masks, abuf, top, hold, bbuf):
    def body(r):
        d = adjoint_row(k, state, abuf, r, cs[r], fs[r])
        ts = [(2.0 / 3.0) * tile(top, r, t) + d[t] for t in range(5)]
        masked = [0.0625 * mask_tile(masks, r, t) * ts[t] for t in range(5)]
        return lambda: (put_tiles(hold, r, ts), put_tiles(bbuf, r, masked))

    for_rows(scal, reach, body)


def adjoint_second(k, scal, cs, fs, reach, state, masks, bbuf, top, hold, left, abuf):
    def body(r):
        d = adjoint_row(k, state, bbuf, r, cs[r], fs[r])
        ts = [tile(hold, r, t) for t in range(5)]
        tf = [0.25 * ts[t] + d[t] for t in range(5)]
        new = [(1.0 / 3.0) * tile(top, r, t) + 0.75 * ts[t] + tf[t] for t in range(5)]
        masked = [0.25 * mask_tile(masks, r, t) * tf[t] for t in range(5)]
        return lambda: (put_tiles(left, r, new), put_tiles(abuf, r, masked))

    for_rows(scal, reach, body)


def adjoint_first(k, scal, cs, fs, reach, state, abuf, left, store):
    def body(r):
        d = adjoint_row(k, state, abuf, r, cs[r], fs[r])
        return store(r, [tile(left, r, t) + d[t] for t in range(5)])

    for_rows(scal, reach, body)


def edges(reach):
    lane = lax.broadcasted_iota(jnp.int32, (8, COLS), 1)
    return lane < reach, lane >= COLS - reach


def wide_pack(ref, base):
    parts = []
    for t in range(5):
        rows = [ref[base + s, 8 * t : 8 * t + 8, COLS:WIDE] for s in range(8)]
        parts.append(slot_pack(rows, lambda s: 8 + SLOT * s, SLOT))
    return jnp.concatenate(parts, axis=0)

def wide_unpack(ref, base, values):
    for s in range(8):
        ref[base + s, 0:FEATS, COLS:WIDE] = pltpu.roll(values, -(8 + SLOT * s) % COLS, 1)


def section_1(k, cs, fs, masks, src, dst):
    def body(r):
        d = tendency_row(k, src, r, cs[r], fs[r])
        new = [tile(src, r, t) + 0.25 * mask_tile(masks, r, t) * d[t] for t in range(5)]
        return lambda: put_state(k, dst, r, new)

    return body


def section_2(k, cs, fs, masks, src, mid, dst):
    def body(r):
        d = tendency_row(k, mid, r, cs[r], fs[r])
        new = [
            0.75 * tile(src, r, t) + 0.25 * tile(mid, r, t) + 0.0625 * mask_tile(masks, r, t) * d[t]
            for t in range(5)
        ]
        return lambda: put_state(k, dst, r, new)

    return body


def section_3(k, cs, fs, masks, fluxes, mean, src, mid, net, r):
    d = tendency_row(k, mid, r, cs[r], fs[r])
    new = []
    for t in range(5):
        m = mask_tile(masks, r, t)
        o = tile(net, r, t)
        if t == 1:
            force = 2.0 * (mean - fluxes[r, 2:3, :])
            o = o + jnp.where(k.sub == 0, force, 0.0)
        new.append(
            (1.0 / 3.0) * tile(src, r, t) + (2.0 / 3.0) * tile(mid, r, t)
            + m * ((1.0 / 6.0) * d[t] + 0.25 * o)
        )
    return new


def zero_walls(ref):
    for row in (PAD - 1, PAD + ROWS):
        ref[row] = jnp.zeros(ref.shape[1:], F32)


class Block:
    def __init__(self, k, s0, masks, fluxes):
        self.k, self.s0, self.masks, self.fluxes = k, s0, masks, fluxes
        self.near_e, self.near_w = edges(REACH)

    def put(self, row, core, from_e, from_w):
        def both(t):
            halo = jnp.where(self.near_e, from_e(t), jnp.where(self.near_w, from_w(t), 0.0))
            return jnp.concatenate([core(t), halo], axis=1)

        put_state(self.k, self.s0, row, [both(t) for t in range(5)])
        self.masks[row, 0:8, :] = both(5)
        last = both(6)
        self.masks[row, 8:16, :] = jnp.where(self.k.low, last[1:2, :], last[0:1, :])
        self.fluxes[row] = last


def assemble_own_kernel(scal, cs, fs, own, own_m, east, west, k1, k2, k3, b2, b3, s0, masks, fluxes, net):
    k = Row(WIDE)
    zero_walls(s0)
    block = Block(k, s0, masks, fluxes)
    for r in range(ROWS):
        at = (r // 8) * PACK
        turn = SLOT * (r % 8)
        block.put(
            PAD + r,
            lambda t: own[r, 8 * t : 8 * t + 8, :],
            lambda t: pltpu.roll(west[at + 8 * t : at + 8 * t + 8, :], -turn % COLS, 1),
            lambda t: pltpu.roll(east[at + 8 * t : at + 8 * t + 8, :], -(turn + SLOT) % COLS, 1),
        )
        net[PAD + r, :, 0:COLS] = own_m[r]
    columns = jnp.concatenate([wide_pack(s0, PAD), wide_pack(s0, PAD + 8)], axis=1)
    o = closure_of(columns, k1, k2, k3, b2, b3)
    for g in range(2):
        wide_unpack(net, PAD + 8 * g, o[:, g * COLS : (g + 1) * COLS])


def closure_of(columns, k1, k2, k3, b2, b3):
    _, _, h2 = hidden_layers(split(to_48(columns, 1.0)), k1, k2, b2)
    return last_layer(h2, k3, b3)


def first_own_kernel(scal, cs, fs, s0, masks, s1):
    zero_walls(s1)
    for_inner(scal, 1, section_1(Row(WIDE), cs, fs, masks, s0, s1))


def second_own_kernel(scal, cs, fs, s0, s1, masks, s2):
    for_inner(scal, 2, section_2(Row(WIDE), cs, fs, masks, s0, s1, s2))


def halo_kernel(sides, scal, cs, fs, own_s0, own_s1, own_s2, own_masks, own_fluxes, own_net, *rest):
    n = len(sides)
    side_refs = [rest[2 * i : 2 * i + 2] for i in range(n)]
    net_refs, (s0, s1, s2, masks, fluxes, net) = rest[2 * n : 2 * n + 5], rest[2 * n + 5 :]
    k = Row(WIDE)
    for r in range(PAD, PAD + ROWS):
        for src, dst in (
            (own_s0, s0), (own_s1, s1), (own_s2, s2), (own_masks, masks), (own_fluxes, fluxes), (own_net, net)
        ):
            dst[r] = src[r]
    for ref in (s0, s1, s2):
        zero_walls(ref)
    block = Block(k, s0, masks, fluxes)
    firsts = []
    for side, (lat, corner) in zip(sides, side_refs):
        base = {"swap": scal[4], "north": PAD - REACH, "south": PAD + ROWS}[side]
        for r in range(REACH):
            block.put(
                base + r,
                lambda t: lat[PACK * r + 8 * t : PACK * r + 8 * t + 8, :],
                lambda t: pltpu.roll(corner[PACK + 40 + 8 * t : PACK + 48 + 8 * t, :], -REACH * r % COLS, 1),
                lambda t: pltpu.roll(corner[8 * t : 8 * t + 8, :], -REACH * (r + 1) % COLS, 1),
            )
        near = {"swap": jnp.where(scal[2] == 1, PAD - 8, PAD + ROWS), "north": PAD - 8, "south": PAD + ROWS}
        firsts.append(near[side])
    columns = []
    for first in firsts:
        columns += [s0[first + i, 0:FEATS, 0:COLS] for i in range(8)] + [wide_pack(s0, first)]
    o = closure_of(jnp.concatenate(columns, axis=1), *net_refs)
    for g, first in enumerate(firsts):
        for i in range(8):
            at = (9 * g + i) * COLS
            net[first + i, :, 0:COLS] = o[:, at : at + COLS]
        at = (9 * g + 8) * COLS
        wide_unpack(net, first, o[:, at : at + COLS])
    for_outer(sides, scal, 1, 10, section_1(k, cs, fs, masks, s0, s1))
    for_outer(sides, scal, 2, 9, section_2(k, cs, fs, masks, s0, s1, s2))


def last_section_kernel(scal, cs, fs, sums, s3, t2, masks, fluxes, outs, final):
    k = Row(WIDE)
    mean = sums[0:1, 0:1] / sums[1:2, 0:1]

    def last(r):
        new = section_3(k, cs, fs, masks, fluxes, mean, s3, t2, outs, r)
        return lambda: put_result(final, r - PAD, [x[:, 0:COLS] for x in new])

    for_rows(scal, 0, last)


def late_kernel(
    sides, scal, cs, fs, sums, own, cown, own_h1, own_h2, s0, s2, masks, fluxes, outs_in, east, west, *rest
):
    n = len(sides)
    side_refs = [rest[2 * i : 2 * i + 2] for i in range(n)]
    (k1, k2, k3, q1, q2, q3, b2, b3), rest = rest[2 * n : 2 * n + 8], rest[2 * n + 8 :]
    grads, s4, abuf, from_closure, s3, t2, outs, t1, cot, gz, bbuf, hold, left, acc = rest
    k = Row(WIDE)
    has_south = scal[2]
    lo = lambda h: PAD - h * has_south
    for ref in (s3, t1, t2, abuf, bbuf):
        zero_walls(ref)
    mean = sums[0:1, 0:1] / sums[1:2, 0:1]

    cnear_e, cnear_w = edges(CREACH)
    for r in range(ROWS):
        for t in range(5):
            rows = slice(2 * PACK + 8 * t, 2 * PACK + 8 * t + 8)
            from_e = pltpu.roll(west[rows, :], -8 * r % COLS, 1)
            from_w = pltpu.roll(east[rows, :], -8 * (r + 1) % COLS, 1)
            side = jnp.where(cnear_e, from_e, jnp.where(cnear_w, from_w, 0.0))
            cot[PAD + r, 8 * t : 8 * t + 8, :] = jnp.concatenate(
                [cown[r, 8 * t : 8 * t + 8, :], side], axis=1
            )
    for side, (lat, corner) in zip(sides, side_refs):
        cbase = {"swap": scal[5], "north": PAD - CREACH, "south": PAD + ROWS}[side]
        crow = {"swap": scal[6], "north": ROWS - CREACH, "south": 0}[side]
        for r in range(CREACH):
            turn = lax.rem(2 * COLS - 8 * (crow + r), COLS)
            turn_w = lax.rem(2 * COLS - 8 * (crow + r + 1), COLS)
            for t in range(5):
                wrows = slice(PACK + 8 * t, PACK + 8 * t + 8)
                erows = slice(2 * PACK + 40 + 8 * t, 2 * PACK + 48 + 8 * t)
                from_e = pltpu.roll(corner[erows, :], turn, 1)
                from_w = pltpu.roll(corner[wrows, :], turn_w, 1)
                part = jnp.where(cnear_e, from_e, jnp.where(cnear_w, from_w, 0.0))
                cot[cbase + r, 8 * t : 8 * t + 8, :] = jnp.concatenate(
                    [lat[LAT_X + FEATS * r + 8 * t : LAT_X + FEATS * r + 8 * t + 8, :], part], axis=1
                )


    def step_1_end(r):
        put_state(k, s3, r, section_3(s0, s2, r))

    def step_1_end(r):
        new = section_3(k, cs, fs, masks, fluxes, mean, s0, s2, outs_in, r)
        return lambda: put_state(k, s3, r, new)

    for_rows(scal, 8, step_1_end)

    acc[...] = jnp.zeros(acc.shape, F32)

    def closure_adjoint(z, h1, h1s, h2, go, with_weights):
        gos = split(to_48(go))
        g2 = product(q3[...], *gos) * (1.0 - h2 * h2)
        g2s = split(g2)
        g1 = product(q2[...], *g2s) * (1.0 - h1 * h1)
        g1s = split(g1)
        if with_weights:
            add_weight_terms(acc, z, h1s, split(h2), g1s, g2s, gos)
        return product(q1[...], *g1s)[0:FEATS]

    def both_ways(columns, go, with_weights):
        z = split(to_48(columns, 1.0))
        h1, h1s, h2 = hidden_layers(z, k1, k2, b2)
        o = last_layer(h2, k3, b3) if with_weights else None
        return o, closure_adjoint(z, h1, h1s, h2, go, with_weights)

    def masked_core(ref, r):
        m0, m4 = masks[r, 0:8, 0:COLS], masks[r, 8:16, 0:COLS]
        parts = [
            0.25 * (m4 if t == 4 else m0) * ref[r, 8 * t : 8 * t + 8, 0:COLS] for t in range(5)
        ]
        return jnp.concatenate(parts, axis=0)

    def mask_cot(r):
        seen = [mask_tile(masks, r, t) * tile(cot, r, t) for t in range(5)]
        quarter, sixth = [0.25 * x for x in seen], [(1.0 / 6.0) * x for x in seen]
        return lambda: (put_tiles(bbuf, r, quarter), put_tiles(abuf, r, sixth))

    for_rows(scal, 6, mask_cot)

    for first in range(PAD, PAD + ROWS, 8):
        z = jnp.concatenate([s3[first + i, 0:FEATS, 0:COLS] for i in range(8)], axis=1)
        go = jnp.concatenate([bbuf[first + i, 0:FEATS, 0:COLS] for i in range(8)], axis=1)
        o, back = both_ways(z, go, True)
        for i in range(8):
            at = slice(i * COLS, (i + 1) * COLS)
            outs[first + i, :, 0:COLS] = o[:, at]
            gz[first + i, :, 0:COLS] = back[:, at]

    first = lo(4)
    if sides == ["swap"]:
        rows = [jnp.where(has_south == 1, PAD - 4, PAD + ROWS) + i for i in range(4)]
    else:
        rows = [PAD - 4 + i for i in range(4)] + [PAD + ROWS + i for i in range(4)]
    beyond = lambda ref: jnp.concatenate(
        [ref[r, 0:FEATS, 0:COLS] for r in rows] + [wide_pack(ref, first + 8 * g) for g in range(3)], axis=1
    )
    _, back = both_ways(beyond(s3), beyond(bbuf), False)
    for i, r in enumerate(rows):
        gz[r, :, 0:COLS] = back[:, i * COLS : (i + 1) * COLS]
    for g in range(3):
        at = (len(rows) + g) * COLS
        wide_unpack(gz, first + 8 * g, back[:, at : at + COLS])

    for_rows(scal, 7, section_1(k, cs, fs, masks, s3, t1))
    for_rows(scal, 6, section_2(k, cs, fs, masks, s3, t1, t2))

    def store(r, tiles):
        new = [tiles[t] + tile(gz, r, t) for t in range(5)]
        return lambda: put_tiles(s4, r, new)

    adjoint_third(k, scal, cs, fs, 5, t2, masks, abuf, cot, hold, bbuf)
    adjoint_second(k, scal, cs, fs, 4, t1, masks, bbuf, cot, hold, left, abuf)
    adjoint_first(k, scal, cs, fs, 3, s3, abuf, left, store)

    for r in range(0, ROWS, 8):
        side = lambda read: jnp.concatenate([read(r + j) for j in range(8)], axis=1)
        z = split(to_48(side(lambda j: own[j, 0:FEATS, :]), 1.0))
        h1 = side(lambda j: own_h1[j])
        h2 = side(lambda j: own_h2[j])
        go = side(lambda j: masked_core(s4, PAD + j))
        back = closure_adjoint(z, h1, split(h1), h2, go, True)
        for j in range(8):
            from_closure[r + j] = back[:, j * COLS : (j + 1) * COLS]

    zero_walls(abuf)

    def mask_top(r):
        new = [(1.0 / 6.0) * mask_tile(masks, r, t) * tile(s4, r, t) for t in range(5)]
        return lambda: put_tiles(abuf, r, new)

    for_rows(scal, 3, mask_top)
    grads[...] = jnp.zeros(grads.shape, F32)
    grads[0:40, 0:HID] = acc[0:40, 0:HID]
    grads[0:40, HID : 2 * HID] = acc[112:152, 0:HID]
    grads[40:72, 0:HID] = acc[48:80, 0:HID]
    grads[40:72, HID : 2 * HID] = acc[80:112, 0:HID]
    grads[72:73, 0:HID] = acc[40:41, 0:HID]
    grads[72:73, HID : 2 * HID] = acc[160:161, 0:HID]
    grads[73:74, 0:HID] = acc[176:177, 0:HID]


def put_result(ref, row, tiles):
    for t in range(4):
        ref[pl.ds(t * 10 * ROWS + row, 8, stride=ROWS), :] = tiles[t]
    ref[pl.ds(8 * ROWS + row, 4, stride=10 * ROWS), :] = tiles[4][0:4, :]
    ref[pl.ds(9 * ROWS + row, 4, stride=10 * ROWS), :] = tiles[4][4:8, :]


def back_third_kernel(scal, cs, fs, state, masks, abuf, top, hold, bbuf):
    zero_walls(bbuf)
    adjoint_third(Row(WIDE), scal, cs, fs, 2, state, masks, abuf, top, hold, bbuf)


def back_second_kernel(scal, cs, fs, state, masks, bbuf, top, hold, left, abuf):
    zero_walls(abuf)
    adjoint_second(Row(WIDE), scal, cs, fs, 1, state, masks, bbuf, top, hold, left, abuf)


def back_first_kernel(scal, cs, fs, state, masks, abuf, left, from_closure, grad):
    def store(r, tiles):
        done = []
        for t in range(5):
            m = masks[r, 8:16, 0:COLS] if t == 4 else masks[r, 0:8, 0:COLS]
            done.append(m * (tiles[t][:, 0:COLS] + from_closure[r - PAD, 8 * t : 8 * t + 8, :]))
        return lambda: put_result(grad, r - PAD, done)

    adjoint_first(Row(WIDE), scal, cs, fs, 0, state, abuf, left, store)


def unpack_kernel(scale, packed, win, bin_, wmid, bmid, wout, bout):
    for ref, lanes in ((win, slice(0, HID)), (wout, slice(HID, 2 * HID))):
        for t in range(4):
            ref[10 * t : 10 * t + 8, :] = packed[8 * t : 8 * t + 8, lanes] * scale
            ref[10 * t + 8 : 10 * t + 9, :] = packed[32 + t : 33 + t, lanes] * scale
            ref[10 * t + 9 : 10 * t + 10, :] = packed[36 + t : 37 + t, lanes] * scale
    wmid[0:32, :] = packed[40:72, 0:HID] * scale
    wmid[32:64, :] = packed[40:72, HID : 2 * HID] * scale
    bin_[...] = packed[72:73, 0:HID] * scale
    bmid[...] = packed[72:73, HID : 2 * HID] * scale
    for t in range(4):
        bout[:, 10 * t : 10 * t + 8] = packed[73:74, 8 * t : 8 * t + 8] * scale
        bout[:, 10 * t + 8 : 10 * t + 9] = packed[73:74, 32 + t : 33 + t] * scale
        bout[:, 10 * t + 9 : 10 * t + 10] = packed[73:74, 36 + t : 37 + t] * scale


def position(lat_n):
    lat_i = lax.axis_index("lat")
    low = (lat_i == 0).astype(jnp.int32)
    return (
        low * (ROWS - REACH),
        low * (ROWS - CREACH),
        (lat_i > 0).astype(jnp.int32),
        (lat_i < lat_n - 1).astype(jnp.int32),
        jnp.where(low == 1, PAD + ROWS, PAD - REACH),
        jnp.where(low == 1, PAD + ROWS, PAD - CREACH),
        jnp.where(low == 1, 0, ROWS - CREACH),
    )


class RowTable:
    def __init__(self, ref, number):
        self.ref, self.number = ref, number

    def __getitem__(self, row):
        part = tile(self.ref, row, self.number)
        return jnp.concatenate([part, part], axis=1)


def far_first(axes):
    return [(axis, n, 1 << bit) for axis, n in axes for bit in reversed(range(n.bit_length() - 1))]


def pair_rounds(x, rounds, beside):
    results = []
    for i in range(max(len(rounds), len(beside))):
        if i < len(rounds):
            axis, n, step = rounds[i]
            got = lax.ppermute(x, axis, [(j, j ^ step) for j in range(n)])
        if i < len(beside):
            results.append(beside[i](results))
            if i < len(rounds):
                got, results[-1] = lax.optimization_barrier((got, results[-1]))
        if i < len(rounds):
            x = x + got
    return x, results


def latitude_terms(row_index, row_count):
    latitude = LAT_LIMIT * (2.0 * (jnp.clip(row_index, 0.0, row_count - 1.0) + 0.5) / row_count - 1.0)
    return 1.0 / jnp.cos(latitude), CORIOLIS * jnp.sin(latitude)


def on_device(
    initial_state, land_mask, surface_flux, weight_in, bias_in, weight_mid, bias_mid, weight_out, bias_out, cotangent
):
    lat_n, lon_n = lax.axis_size("lat"), lax.axis_size("lon")
    lat_i = lax.axis_index("lat")
    lat_total, lon_total = ROWS * lat_n, COLS * lon_n
    sides = ["swap"] if lat_n == 2 else ["north", "south"]
    rows = (lat_i * ROWS - PAD + jnp.arange(EXT, dtype=jnp.int32)).astype(F32)
    tiles = [jnp.broadcast_to(x[:, None, None], (EXT, 8, COLS)) for x in latitude_terms(rows, lat_total)]
    geometry = jnp.concatenate(tiles, axis=1)

    hbm = pl.BlockSpec(memory_space=pltpu.HBM)
    packed = pl.pallas_call(
        lambda *refs: pack_kernel(sides, *refs),
        out_shape=[
            sds(ROWS, PACK, COLS), sds(ROWS, FEATS, COLS), sds(STRIP, COLS), sds(STRIP, COLS), sds(8, COLS),
        ]
        + [sds(LAT, COLS)] * len(sides),
        in_specs=[hbm] * 4,
        out_specs=[VMEM] * (5 + len(sides)),
        scratch_shapes=[
            pltpu.VMEM((40 * ROWS, COLS), F32), pltpu.VMEM((10 * ROWS, COLS), jnp.int32),
            pltpu.VMEM((ROWS, COLS), F32), pltpu.VMEM((40 * ROWS, COLS), F32), pltpu.SemaphoreType.DMA((4,)),
        ],
        compiler_params=params(56),
        cost_estimate=pl.CostEstimate(flops=10**9, bytes_accessed=3 * 10**6, transcendentals=0),
        name="pack_halos",
    )(
        initial_state.reshape(40 * ROWS, COLS),
        land_mask.reshape(10 * ROWS, COLS),
        surface_flux,
        cotangent.reshape(40 * ROWS, COLS),
    )
    own, cown, east_pay, west_pay, sums = packed[:5]

    def lat_pairs(side):
        if side == "swap":
            return [(0, 1), (1, 0)]
        if side == "north":
            return [(i, i + 1) for i in range(lat_n - 1)]
        return [(i + 1, i) for i in range(lat_n - 1)]

    east_ring = [(i, (i + 1) % lon_n) for i in range(lon_n)]
    west_ring = [((i + 1) % lon_n, i) for i in range(lon_n)]
    from_west = lax.ppermute(east_pay, "lon", east_ring)
    from_east = lax.ppermute(west_pay, "lon", west_ring)
    row = lambda b: b.reshape(1, -1)
    raw = (weight_in, weight_mid, weight_out, row(bias_in), row(bias_mid), row(bias_out))
    half = lambda *shape: jax.ShapeDtypeStruct(shape, BF16)
    own_closure = pl.pallas_call(
        own_closure_kernel,
        out_shape=[
            sds(ROWS, FEATS, COLS), sds(ROWS, HID, COLS), sds(ROWS, HID, COLS),
            half(HID, 144), half(HID, 192), half(48, 192), half(48, 192), half(HID, 192), half(HID, 144),
            sds(HID, COLS), sds(FEATS, COLS),
        ],
        in_specs=[VMEM] + [hbm] * 6,
        out_specs=[VMEM] * 11,
        scratch_shapes=[pltpu.VMEM(w.shape, F32) for w in raw]
        + [pltpu.VMEM((COLS, COLS), F32), pltpu.VMEM((COLS, COLS), F32), pltpu.VMEM((HID, WIDE), F32)]
        + [pltpu.SemaphoreType.DMA((6,))],
        compiler_params=params(12),
        cost_estimate=pl.CostEstimate(flops=10**9, bytes_accessed=2 * 10**6, transcendentals=0),
        name="own_closure",
    )
    pack_corners = pl.pallas_call(
        lambda *refs: corner_kernel(sides, *refs),
        out_shape=[sds(CORNER + 8, COLS)] * len(sides),
        in_specs=[VMEM, VMEM],
        out_specs=[VMEM] * len(sides),
        compiler_params=params(8),
        cost_estimate=pl.CostEstimate(flops=10**8, bytes_accessed=10**6, transcendentals=0),
        name="pack_corners",
    )
    lats = [lax.ppermute(pay, "lat", lat_pairs(side)) for side, pay in zip(sides, packed[5:])]
    state = sds(EXT, 56, WIDE)
    plain = sds(EXT, FEATS, WIDE)
    marks = sds(EXT, 16, WIDE)
    vmem = lambda shape: pltpu.VMEM(shape.shape, F32)

    def call(kernel, name, out_shape, scratch, args, flops, limit):
        single = not isinstance(out_shape, list)
        return pl.pallas_call(
            lambda geo, *refs: kernel(position(lat_n), RowTable(geo, 0), RowTable(geo, 1), *refs),
            out_shape=out_shape,
            in_specs=[VMEM] * (1 + len(args)),
            out_specs=VMEM if single else [VMEM] * len(out_shape),
            scratch_shapes=scratch,
            compiler_params=params(limit),
            cost_estimate=pl.CostEstimate(flops=flops, bytes_accessed=10**7, transcendentals=0),
            name=name,
        )(geometry, *args)


    rounds = far_first((("lon", lon_n),))[::-1]
    row_total, results = pair_rounds(
        sums,
        rounds,
        [lambda done: sums] * (len(rounds) - 1)
        + [lambda done: (own_closure(own, *raw), pack_corners(from_west, from_east))],
    )
    (own_m, own_h1, own_h2, k1, k2, k3, q1, q2, q3, b2, b3), corner_pays = results[-1]
    net_weights = [k1, k2, k3, b2, b3]
    corners = []
    for side, pay in zip(sides, corner_pays):
        pay = lax.dynamic_update_slice(pay, row_total, (CORNER, 0))
        corners.append(lax.ppermute(pay, "lat", lat_pairs(side)))
    s0, masks, fluxes, net = call(
        assemble_own_kernel, "assemble_own", [state, marks, sds(EXT, 8, WIDE), plain], [],
        [own, own_m, from_west, from_east] + net_weights, 10**9, 8,
    )
    s1 = call(first_own_kernel, "first_section_own", state, [], [s0, masks], 10**9, 8)
    s2 = call(second_own_kernel, "second_section_own", state, [], [s0, s1, masks], 10**9, 8)
    corners, s2 = lax.optimization_barrier((corners, s2))
    if sides == ["swap"]:
        total = row_total + corners[0][CORNER : CORNER + 8]
    else:
        total = lax.psum(row_total, "lat")
    received = [ref for pair in zip(lats, corners) for ref in pair]
    s0, s1, s2, masks, fluxes, net = call(
        lambda *refs: halo_kernel(sides, *refs), "halo_rows",
        [state, state, state, marks, sds(EXT, 8, WIDE), plain], [],
        [s0, s1, s2, masks, fluxes, net] + received + net_weights, 2 * 10**9, 8,
    )
    grads, top, abuf, from_closure, s3, t2, net_2 = call(
        lambda *refs: late_kernel(sides, *refs), "steps_and_adjoint",
        [sds(80, COLS), plain, plain, sds(ROWS, FEATS, COLS), state, state, plain],
        [vmem(state)] + [vmem(plain)] * 5 + [pltpu.VMEM((192, HID), F32)],
        [total, own, cown, own_h1, own_h2, s0, s2, masks, fluxes, net, from_west, from_east]
        + received + [k1, k2, k3, q1, q2, q3, b2, b3],
        4 * 10**9, 18,
    )
    beside = [
        lambda done: call(
            back_third_kernel, "adjoint_third_section", [plain, plain], [], [s2, masks, abuf, top], 10**9, 8
        ),
        lambda done: call(
            back_second_kernel, "adjoint_second_section", [plain, plain], [],
            [s1, masks, done[0][1], top, done[0][0]], 10**9, 8,
        ),
        lambda done: call(
            back_first_kernel, "adjoint_first_section", sds(40 * ROWS, COLS), [],
            [s0, masks, done[1][1], done[1][0], from_closure], 10**9, 8,
        ),
        lambda done: call(
            last_section_kernel, "last_section", sds(40 * ROWS, COLS), [],
            [total, s3, t2, masks, fluxes, net_2], 10**9, 8,
        ),
    ]
    by_lon, by_lat = far_first((("lon", lon_n),)), far_first((("lat", lat_n),))
    summed, results = pair_rounds(grads, by_lon[:-2] + by_lat + by_lon[-2:], beside)
    state_grad, final = results[2:]

    scale = 1.0 / math.sqrt(lat_total * lon_total)
    g_in, g_bin, g_mid, g_bmid, g_out, g_bout = pl.pallas_call(
        lambda *refs: unpack_kernel(scale, *refs),
        out_shape=[sds(40, HID), sds(1, HID), sds(HID, HID), sds(1, HID), sds(40, HID), sds(1, 40)],
        in_specs=[VMEM],
        out_specs=[VMEM] * 6,
        compiler_params=params(8),
        name="unpack_weight_grads",
    )(summed)
    shape = initial_state.shape
    return (
        final.reshape(shape),
        state_grad.reshape(shape),
        g_in,
        g_bin.reshape(-1),
        g_mid,
        g_bmid.reshape(-1),
        g_out.T,
        g_bout.reshape(-1),
    )


def solution(mesh):
    split_state = P(None, None, "lat", "lon")
    return jax.shard_map(
        on_device,
        mesh=mesh,
        in_specs=(split_state, P(None, "lat", "lon"), P("lat", "lon"), P(), P(), P(), P(), P(), P(), split_state),
        out_specs=(split_state, split_state, P(), P(), P(), P(), P(), P()),
        check_vma=False,
    )
```
